32 devices in a mesh: grp: 2 (over x), sx: 16 (over z, y, core).
Axes of the slice: x: 2, y: 2, z: 4, core: 2. Of those that a mesh axis runs over, the one named last changes fastest.
Arguments:
- pieces: bfloat16 [6144, 4096], P(('grp', 'sx')), parts along dimension 0, may hold values from -6 to 6
- potential: float32 [128, 1024], P(('grp', 'sx')), parts along dimension 0, may hold values from -1.5 to 1.5
- centers: int32 [2048, 4], P('grp'), parts along dimension 0, may hold values from 0 to 63, as said below
- pattern: int32 [32, 2], P('grp'), parts along dimension 0, may hold values 0 or 1
Outputs:
- direction: bfloat16 [6144, 4096], P(('grp', 'sx')), parts along dimension 0
The draws below stay inside these ranges and needn't reach their ends.
There are 2 independent parts, one for each index of `grp`. The reference program is written for one: setup_inputs(seed, part) draws one part's arguments, and reference() takes and returns one part's arrays. A program takes and returns all parts, laid end to end along the dimension named above; each array names one. Nothing has to cross between parts.
Inputs may be any that keep to these rules, and one draw needn't show every extreme that they name: `centers`: row j holds orbital j's center (x, y, z) and sphere radius r: 4 * (j // 64) <= x < 4 * (j // 64 + 1), 0 <= y < 32, 0 <= z < 32, and 2 <= r <= 4, so orbital j is zero outside slabs j // 64 - 1 to j // 64 + 1.
All inputs are finite; a program needn't handle non-finite values.
Results may differ from the reference program's by a relative error of at most 0.0097.
Values may be sent and summed in bfloat16 or wider, within the bound.
No kernel may reach another device: no remote copies, remote signals or barrier semaphores. Data moves between devices by JAX's collectives and lax.ppermute only.
A program may use at most 64 MiB of HBM per device.

```python
import jax
import jax.numpy as jnp
from jax import lax

ORB = 64
CX = 4
NY = 32
NZ = 32
SLABS = 16
CELLS = 4096


def draw_centers(key, part):
    key = jax.random.fold_in(key, 7)
    streams = jax.random.split(key, 4)
    orbital_count = ORB * SLABS
    owner_block = jnp.arange(orbital_count, dtype=jnp.int32) // ORB
    coord_x = owner_block * CX + jax.random.randint(streams[0], (orbital_count,), 0, CX, dtype=jnp.int32)
    coord_y = jax.random.randint(streams[1], (orbital_count,), 0, NY, dtype=jnp.int32)
    coord_z = jax.random.randint(streams[2], (orbital_count,), 0, NZ, dtype=jnp.int32)
    radius = jax.random.randint(streams[3], (orbital_count,), (CX + 1) // 2, CX + 1, dtype=jnp.int32)
    table = jnp.stack([coord_x, coord_y, coord_z, radius], axis=1)
    first_row = jnp.array([0, 0, 0, CX], dtype=jnp.int32)
    last_row = jnp.array([SLABS * CX - 1, NY - 1, NZ - 1, CX], dtype=jnp.int32)
    table = table.at[0].set(first_row)
    table = table.at[orbital_count - 1].set(last_row)
    return table


def with_ends(values, own_key, least, top_value):
    longest = values.shape.index(max(values.shape))
    spots = []
    for shift in (0, 1):
        where = [jax.random.randint(jax.random.fold_in(own_key, axis), (), 0, length) for axis, length in enumerate(values.shape)]
        where[longest] = (where[longest] + shift) % values.shape[longest]
        spots.append(tuple(where))
    return values.at[spots[0]].set(least).at[spots[1]].set(top_value)


def block_scale(own_key, shape, cuts, least, high):
    def one(axis_at, shards_of):
        steps = jax.random.uniform(jax.random.fold_in(jax.random.fold_in(own_key, 6), axis_at), (shards_of,), jnp.float32, least / len(cuts), high / len(cuts))
        return jnp.repeat(jnp.exp(steps), shape[axis_at] // shards_of).reshape((-1,) + (1,) * (len(shape) - axis_at - 1))

    level = one(*cuts[0])
    for cut in cuts[1:]:
        level = level * one(*cut)
    return level


def noise(rng, extent, deviation, bound, cuts=(), kind=jnp.bfloat16):
    loudness = block_scale(rng, extent, cuts, -0.22, 0.18) if cuts else 1.0
    values = jax.random.normal(rng, extent, jnp.float32) * deviation * loudness
    return jnp.minimum(jnp.maximum(values, -bound), bound).astype(kind)


def setup_inputs(seed: int = 0, part: int = 0) -> dict:
    arg_keys = jax.random.split(jax.random.key(seed), 5)
    part_splits = jax.random.split(jax.random.fold_in(arg_keys[4], part), 5)
    pieces = noise(part_splits[0], (3 * ORB * SLABS, CELLS), 1.0, 6.0, ((0, 16),))
    potential = jnp.clip(jax.random.uniform(part_splits[1], (SLABS * CX, NY * NZ), jnp.float32, -1.5, 1.5) * block_scale(part_splits[1], (SLABS * CX, NY * NZ), ((0, 16),), -0.4, 0.0), -1.5, 1.5)
    centers = draw_centers(jax.random.fold_in(jax.random.fold_in(arg_keys[4], part), 71), part)
    pattern = with_ends((jax.random.randint(part_splits[3], (SLABS, 2), 0, 4) < 3).astype(jnp.int32), jax.random.fold_in(part_splits[3], 1), 0, 1)
    return dict(pieces=pieces, potential=potential, centers=centers, pattern=pattern)


mass_term = 1.0
jacobi_diag = 3.0 + mass_term


def sphere_mask(centers, slab_id, slab_count):
    padded = jnp.pad(centers, ((ORB, ORB), (0, 0)))
    nearby = lax.dynamic_slice_in_dim(padded, (slab_id * ORB).astype(jnp.int32), 3 * ORB, 0)
    blocks = slab_id - 1 + jnp.arange(3 * ORB, dtype=jnp.int32) // ORB
    in_range = (blocks >= 0) & (blocks < slab_count)
    plane_x = slab_id * CX + jnp.arange(CX, dtype=jnp.int32)
    dist_x = (plane_x[None, :] - nearby[:, 0:1]) ** 2
    dist_y = (jnp.arange(NY, dtype=jnp.int32)[None, :] - nearby[:, 1:2]) ** 2
    dist_z = (jnp.arange(NZ, dtype=jnp.int32)[None, :] - nearby[:, 2:3]) ** 2
    reach_sq = dist_x[:, :, None, None] + dist_y[:, None, :, None] + dist_z[:, None, None, :]
    radius_sq = (nearby[:, 3] ** 2)[:, None, None, None]
    inside = (reach_sq <= radius_sq) & in_range[:, None, None, None]
    return inside.reshape(3 * ORB, CX, NY * NZ)


def kinetic(values, plane_low, plane_high):
    row_count = values.shape[0]
    extended = jnp.concatenate([plane_low[:, None], values, plane_high[:, None]], axis=1)
    beside_all = extended[:, :-2] + extended[:, 2:]
    cube_view = values.reshape(row_count, CX, NY, NZ)
    padded_y = jnp.pad(cube_view, ((0, 0), (0, 0), (1, 1), (0, 0)))
    padded_z = jnp.pad(cube_view, ((0, 0), (0, 0), (0, 0), (1, 1)))
    sideways = padded_y[:, :, :-2] + padded_y[:, :, 2:] + padded_z[:, :, :, :-2] + padded_z[:, :, :, 2:]
    beside_all = beside_all + sideways.reshape(row_count, CX, NY * NZ)
    return 0.5 * (6.0 * values - beside_all)


def align_planes(firsts, lasts):
    slab_count = firsts.shape[0]
    section = firsts.shape[-1]
    first_planes = firsts.reshape(slab_count, 3, ORB, section)
    last_planes = lasts.reshape(slab_count, 3, ORB, section)
    plane_high = jnp.pad(first_planes, ((0, 1), (1, 0), (0, 0), (0, 0)))[1:, :3]
    plane_low = jnp.pad(last_planes, ((1, 0), (0, 1), (0, 0), (0, 0)))[:slab_count, 1:]
    return plane_low.reshape(slab_count, 3 * ORB, section), plane_high.reshape(slab_count, 3 * ORB, section)


def gather_band(local):
    blocks = local.reshape(SLABS, 3, ORB, 3, ORB)
    framed = jnp.pad(blocks, ((1, 1), (0, 0), (0, 0), (0, 0), (0, 0)))
    from_below = jnp.pad(framed[:-2, 2], ((0, 0), (0, 0), (0, 2), (0, 0)))
    from_self = jnp.pad(framed[1:-1, 1], ((0, 0), (0, 0), (1, 1), (0, 0)))
    from_above = jnp.pad(framed[2:, 0], ((0, 0), (0, 0), (2, 0), (0, 0)))
    return from_below + from_self + from_above


def reference(pieces, potential, centers, pattern):
    row_count = 3 * ORB
    section = NY * NZ
    volume = 1.0 / (4.0 * CX ** 3)
    raw_pieces = pieces.reshape(SLABS, row_count, CX, section)
    fields = potential.reshape(SLABS, CX, section)
    slab_ids = jnp.arange(SLABS, dtype=jnp.int32)
    zero_half = jnp.zeros((), pieces.dtype)

    def masked(slab_id):
        return jnp.where(sphere_mask(centers, slab_id, SLABS), raw_pieces[slab_id], zero_half)

    def edge_planes(slab_id):
        orbitals = masked(slab_id)
        return orbitals[:, 0], orbitals[:, CX - 1]

    firsts, lasts = lax.map(edge_planes, slab_ids)
    plane_low, plane_high = align_planes(firsts, lasts)

    def energies(slab_id):
        orbitals = masked(slab_id)
        values = orbitals.astype(jnp.float32)
        applied = kinetic(values, plane_low[slab_id].astype(jnp.float32), plane_high[slab_id].astype(jnp.float32)) + fields[slab_id][None] * values
        inside = sphere_mask(centers, slab_id, SLABS)
        return orbitals, jnp.where(inside, applied, 0.0).astype(jnp.bfloat16)

    def gram_terms(slab_id):
        orbitals, energy = energies(slab_id)
        flat_orbit = orbitals.reshape(row_count, -1)
        flat_energy = energy.reshape(row_count, -1)
        contract_cells = (((1,), (1,)), ((), ()))
        correlation_part = lax.dot_general(flat_orbit, flat_orbit, contract_cells, preferred_element_type=jnp.float32) * volume
        ham_part = lax.dot_general(flat_orbit, flat_energy, contract_cells, preferred_element_type=jnp.float32) * volume
        return correlation_part, ham_part

    correlation_local, ham_local = lax.map(gram_terms, slab_ids)
    padded_pattern = jnp.pad(pattern, ((2, 2), (0, 0))).astype(jnp.float32)
    keep_mask = jnp.stack([padded_pattern[0:SLABS, 1], padded_pattern[1:SLABS + 1, 0], jnp.ones((SLABS,), jnp.float32), padded_pattern[2:SLABS + 2, 0], padded_pattern[2:SLABS + 2, 1]], axis=1)
    correlation_band = gather_band(correlation_local) * keep_mask[:, None, :, None]
    ham_band = gather_band(ham_local) * keep_mask[:, None, :, None]
    inverse_band = (-correlation_band).at[:, :, 2, :].add(2.0 * jnp.eye(ORB, dtype=jnp.float32))
    inverse_pad = jnp.pad(inverse_band, ((3, 3), (0, 0), (0, 0), (0, 0)))
    ham_pad = jnp.pad(ham_band, ((3, 3), (0, 0), (0, 0), (0, 0)))
    theta_rows = []
    for row_slot in range(3):
        theta_cols = []
        for col_slot in range(3):
            summed = jnp.zeros((SLABS, ORB, ORB), jnp.float32)
            for step_off in range(-2, 3):
                band_off = col_slot - row_slot - step_off
                if abs(band_off) > 2:
                    continue
                x_block = inverse_pad[row_slot + 2:row_slot + 2 + SLABS, :, step_off + 2, :]
                h_block = ham_pad[row_slot + 2 + step_off:row_slot + 2 + step_off + SLABS, :, band_off + 2, :]
                summed = summed + jnp.einsum("sij,sjk->sik", x_block, h_block, precision=lax.Precision.HIGHEST)
            theta_cols.append(summed)
        theta_rows.append(jnp.stack(theta_cols, axis=2))
    theta_all = jnp.stack(theta_rows, axis=1).astype(jnp.bfloat16).reshape(SLABS, row_count, row_count)

    def gradients(slab_id):
        orbitals, energy = energies(slab_id)
        correction = lax.dot_general(theta_all[slab_id], orbitals.reshape(row_count, -1), (((0,), (0,)), ((), ())), preferred_element_type=jnp.float32)
        inside = sphere_mask(centers, slab_id, SLABS).reshape(row_count, -1)
        result = jnp.where(inside, energy.reshape(row_count, -1).astype(jnp.float32) - correction, 0.0)
        return result.astype(jnp.bfloat16).reshape(row_count, CX, section)

    gradient = lax.map(gradients, slab_ids)
    grad_low, grad_high = align_planes(gradient[:, :, 0], gradient[:, :, CX - 1])

    def precondition(slab_id):
        values = gradient[slab_id].astype(jnp.float32)
        applied = kinetic(values, grad_low[slab_id].astype(jnp.float32), grad_high[slab_id].astype(jnp.float32)) + mass_term * values
        smoothed = (2.0 * values - applied / jacobi_diag) / jacobi_diag
        inside = sphere_mask(centers, slab_id, SLABS)
        return jnp.where(inside, smoothed, 0.0).astype(jnp.bfloat16)

    direction = lax.map(precondition, slab_ids)
    return direction.reshape(SLABS * row_count, CX * section)
```

```python
import functools

import jax
import jax.numpy as jnp
from jax import lax
from jax.experimental import pallas as pl
from jax.experimental.pallas import tpu as pltpu
from jax.sharding import PartitionSpec as P

ORB = 64
CX = 4
NY = 32
NZ = 32
ROWS = 3 * ORB
PLANE = NY * NZ
TILE = 256
HALF = PLANE // 4
F32 = jnp.float32
BF16 = jnp.bfloat16


def iota(shape, dim):
    return lax.broadcasted_iota(jnp.int32, shape, dim)


def row_features(ct_ref):
    slab = lax.axis_index("sx")
    count = lax.axis_size("sx")
    width = ct_ref.shape[1]
    first = jnp.clip(slab * ORB - ORB, 0, width - 4 * ORB) // 128 * 128
    first = pl.multiple_of(first, 128)
    window = ct_ref[:, pl.ds(first, 4 * ORB)]
    shift = slab * ORB - ORB - first
    window = pltpu.roll(jnp.concatenate([window, window], axis=0), lax.rem(4 * ORB - shift, 4 * ORB), 1)
    lane = iota((1, 4 * ORB), 1)
    block = slab - 1 + lane // ORB
    valid = (block >= 0) & (block < count)
    cx = window[0:1] - slab * CX
    cy = window[1:2]
    cz = window[2:3]
    r = window[3:4]
    const = cx * cx + cy * cy + cz * cz - r * r
    const = jnp.where(valid, const, 65535)
    cx = jnp.where(valid, cx, 0)
    cy = jnp.where(valid, cy, 0)
    cz = jnp.where(valid, cz, 0)
    k = iota((16, 4 * ORB), 0)
    feats = jnp.where(k == 0, 1, 0)
    feats = jnp.where(k == 1, 256, feats)
    feats = jnp.where(k == 2, cy, feats)
    feats = jnp.where(k == 3, cz, feats)
    feats = jnp.where(k == 4, const & 255, feats)
    feats = jnp.where(k == 5, const >> 8, feats)
    feats = jnp.where(k == 6, cx, feats)
    return jnp.transpose(feats.astype(F32))[:ROWS].astype(BF16)


def cell_features(plane):
    k = iota((16, PLANE), 0)
    cell = iota((16, PLANE), 1)
    y = cell >> 5
    z = cell & 31
    sq = y * y + z * z + plane * plane
    feats = jnp.where(k == 0, sq & 255, 0)
    feats = jnp.where(k == 1, sq >> 8, feats)
    feats = jnp.where(k == 2, -2 * y, feats)
    feats = jnp.where(k == 3, -2 * z, feats)
    feats = jnp.where(k == 4, 1, feats)
    feats = jnp.where(k == 5, 256, feats)
    feats = jnp.where(k == 6, -2 * plane, feats)
    return feats.astype(F32).astype(BF16)


def sphere(rows, plane):
    reach = jnp.dot(rows, cell_features(plane), preferred_element_type=F32)
    return jnp.where(reach <= 0.0, 1.0, 0.0).astype(BF16)


def in_plane(center, beside):
    k = iota((2 * TILE, TILE), 0) - 128
    n = iota((2 * TILE, TILE), 1)
    diff = k - n
    near_y = (diff == NZ) | (diff == -NZ)
    near_z = ((diff == 1) | (diff == -1)) & ((k >> 5) == (n >> 5))
    w = jnp.where(near_y | near_z, float(beside), 0.0)
    return jnp.where(diff == 0, float(center), w).astype(BF16)


def plane_product(values, weights, t):
    low = max(0, TILE * t - 128)
    high = min(PLANE, TILE * t + TILE + 128)
    shift = 128 - TILE * t
    return jnp.dot(
        values[:, low:high], weights[low + shift : high + shift], preferred_element_type=F32
    )


def fold(values):
    half = values[:, : PLANE // 2] + values[:, PLANE // 2 :]
    low_z = (iota((1, 128), 1) & 31) < 16
    out = []
    for i in range(2):
        a = half[:, 256 * i : 256 * i + 128]
        b = half[:, 256 * i + 128 : 256 * i + 256]
        out.append(jnp.where(low_z, a + pltpu.roll(a, 112, 1), b + pltpu.roll(b, 16, 1)))
    return out


def unfold(packed):
    low_z = (iota((1, 128), 1) & 31) < 16
    tiles = []
    for i in range(2):
        p = packed[:, 128 * i : 128 * i + 128]
        tiles.append(jnp.where(low_z, p, pltpu.roll(p, 16, 1)))
        tiles.append(jnp.where(low_z, pltpu.roll(p, 112, 1), p))
    return tiles


def put_fold(ref, values):
    a, b = fold(values)
    ref[:, 0:128] = a.astype(BF16)
    ref[:, 128:256] = b.astype(BF16)


def edges_kernel(ct_ref, first_ref, last_ref, phi_ref, mask_ref, up_ref, down_ref):
    rows = row_features(ct_ref)
    for i, (plane, ref) in enumerate(((0, first_ref), (CX - 1, last_ref))):
        mask = sphere(rows, plane)
        value = ref[...] * mask
        mask_ref[i] = mask
        phi_ref[i] = value
        if i == 0:
            put_fold(down_ref, value[: 2 * ORB].astype(F32))
        else:
            put_fold(up_ref, value[ORB:].astype(F32))


def rows_product(a, b):
    return lax.dot_general(a, b, (((1,), (1,)), ((), ())), preferred_element_type=F32)


def energy_kernel(
    ct_ref, mid1_ref, mid2_ref, pot_ref, edge_ref,
    phi_ref, mask_ref, energy_ref, part_ref, corr_ref, ham_ref,
):
    rows = row_features(ct_ref)
    for i, ref in enumerate((mid1_ref, mid2_ref)):
        mask = sphere(rows, 1 + i)
        mask_ref[i] = mask
        phi_ref[i] = ref[...] * mask
    weights = in_plane(6, -1)
    for t in range(PLANE // TILE):
        lanes = slice(TILE * t, TILE * t + TILE)
        edge = edge_ref[:, :, lanes].astype(F32)
        mid = phi_ref[:, :, lanes].astype(F32)
        inner = plane_product(phi_ref[...].reshape(2 * ROWS, PLANE), weights, t).reshape(2, ROWS, TILE)
        outer = plane_product(edge_ref[...].reshape(2 * ROWS, PLANE), weights, t).reshape(2, ROWS, TILE)
        for i in range(2):
            value = 0.5 * (inner[i] - (edge[i] + mid[1 - i])) + pot_ref[1 + i : 2 + i, lanes] * mid[i]
            energy_ref[i, :, lanes] = value.astype(BF16) * mask_ref[i, :, lanes]
            plane = (CX - 1) * i
            part_ref[i, :, lanes] = 0.5 * (outer[i] - mid[i]) + pot_ref[plane : plane + 1, lanes] * edge[i]
    corr = jnp.zeros((ROWS, ROWS), F32)
    ham = jnp.zeros((ROWS, ROWS), F32)
    for i in range(2):
        corr = corr + rows_product(phi_ref[i], phi_ref[i]) + rows_product(edge_ref[i], edge_ref[i])
        ham = ham + rows_product(energy_ref[i], phi_ref[i])
    corr_ref[...] = corr
    ham_ref[...] = ham


def halo_rows(i):
    return slice(0, 2 * ORB) if i == 0 else slice(ORB, ROWS)


def bands_kernel(
    below_ref, above_ref, part_ref, mask_ref, phi_ref, corr_ref, ham_ref,
    energy_ref, own_ref, up1_ref, down1_ref, up2_ref, down2_ref,
):
    volume = 1.0 / (4.0 * CX**3)
    ham = ham_ref[...]
    for i, ref in enumerate((below_ref, above_ref)):
        tiles = unfold(ref[...].astype(F32))
        rest = slice(2 * ORB, ROWS) if i == 0 else slice(0, ORB)
        for t in range(PLANE // 128):
            lanes = slice(128 * t, 128 * t + 128)
            value = part_ref[i, halo_rows(i), lanes] - 0.5 * tiles[t % 4]
            energy_ref[i, halo_rows(i), lanes] = value.astype(BF16) * mask_ref[i, halo_rows(i), lanes]
            energy_ref[i, rest, lanes] = part_ref[i, rest, lanes].astype(BF16) * mask_ref[i, rest, lanes]
        ham = ham + rows_product(energy_ref[i], phi_ref[i])
    own_ref[:, :, ROWS:] = jnp.zeros((2, ROWS, TILE - ROWS), F32)
    own_ref[0, :, :ROWS] = ham * volume
    own_ref[1, :, :ROWS] = corr_ref[...] * volume
    low = iota((1, 128), 1) < 64
    h0 = own_ref[0, :, 0:128]
    h1 = own_ref[0, :, 128:256]
    c0 = own_ref[1, :, 0:128]
    c1 = own_ref[1, :, 128:256]
    h0r = pltpu.roll(h0, 64, 1)
    h1r = pltpu.roll(h1, 64, 1)
    c1r = pltpu.roll(c1, 64, 1)
    near = (
        jnp.where(low, h0r, h1r),
        jnp.where(low, pltpu.roll(c0, 64, 1), c1r),
        jnp.where(low, c0, h0r),
    )
    far = (h0, c0, jnp.where(low, h1, c1r))
    for i in range(3):
        value = near[i].astype(BF16)
        up1_ref[i] = value[ORB:]
        down1_ref[i] = value[: 2 * ORB]
        value = far[i].astype(BF16)
        up2_ref[i] = value[2 * ORB :]
        down2_ref[i] = value[:ORB]


def gradient_kernel(
    pattern_ref, own_ref, below1_ref, above1_ref, below2_ref, above2_ref,
    edge_ref, phi_ref, edge_energy_ref, energy_ref, edge_mask_ref, mask_ref,
    edge_grad_ref, grad_ref, up_ref, down_ref,
    ham_ref, inv_ref,
):
    slab = lax.axis_index("sx")
    last = pattern_ref.shape[1] - 1
    low = iota((1, 128), 1) < 64
    for which, band_ref in enumerate((ham_ref, inv_ref)):

        def near(ref):
            head = ref[2].astype(F32)
            if which == 1:
                head = pltpu.roll(head, 64, 1)
            return (jnp.where(low, 0.0, head), ref[which].astype(F32))

        def far(ref):
            tail = ref[2].astype(F32)
            if which == 1:
                tail = pltpu.roll(tail, 64, 1)
            return (ref[which].astype(F32), jnp.where(low, tail, 0.0))

        own = (own_ref[which, :, 0:128], own_ref[which, :, 128:256])
        below1 = near(below1_ref)
        above1 = near(above1_ref)
        below2 = far(below2_ref)
        above2 = far(above2_ref)
        zero = jnp.zeros((ORB, 128), F32)
        s0, s1, s2 = (slice(ORB * i, ORB * i + ORB) for i in range(3))
        tiles = (
            (
                below1[0][s0] + below2[0],
                own[0][s0] + below1[1][s0] + below2[1],
                own[1][s0],
                zero,
            ),
            (
                below1[0][s1],
                own[0][s1] + below1[1][s1] + above1[0][s0],
                own[1][s1] + above1[1][s0],
                zero,
            ),
            (
                zero,
                own[0][s2] + above1[0][s1],
                own[1][s2] + above1[1][s1] + above2[0],
                above2[1],
            ),
        )
        for r in range(3):
            for q in range(4):
                kept = []
                for col in (2 * q, 2 * q + 1):
                    apart = abs(col - r - 2)
                    if apart == 0:
                        kept.append(1.0)
                    elif apart > 2:
                        kept.append(0.0)
                    else:
                        at = jnp.clip(slab - 3 + min(col, r + 2), 0, last)
                        kept.append(pattern_ref[apart - 1, at].astype(F32))
                value = tiles[r][q] * jnp.where(low, kept[0], kept[1])
                if which == 1:
                    on = iota((ORB, 128), 0) + (ORB * (r + 2) - 128 * q) == iota((ORB, 128), 1)
                    value = jnp.where(on, 2.0, 0.0) - value
                band_ref[ORB * r : ORB * r + ORB, 128 * q : 128 * q + 128] = value
    theta = lax.dot_general(
        ham_ref[...], inv_ref[...], (((1,), (1,)), ((), ())),
        precision=lax.Precision.HIGHEST, preferred_element_type=F32,
    ).astype(BF16)
    for orb_ref, en_ref, m_ref, out_ref in (
        (edge_ref, edge_energy_ref, edge_mask_ref, edge_grad_ref),
        (phi_ref, energy_ref, mask_ref, grad_ref),
    ):
        for i in range(2):
            for t in range(PLANE // TILE):
                lanes = slice(TILE * t, TILE * t + TILE)
                fix = jnp.dot(theta, orb_ref[i, :, lanes], preferred_element_type=F32)
                value = en_ref[i, :, lanes].astype(F32) - fix
                out_ref[i, :, lanes] = value.astype(BF16) * m_ref[i, :, lanes]
    put_fold(down_ref, edge_grad_ref[0, : 2 * ORB].astype(F32))
    put_fold(up_ref, edge_grad_ref[1, ORB:].astype(F32))


def smooth_kernel(edge_ref, grad_ref, edge_mask_ref, mask_ref, out_ref, part_ref):
    weights = in_plane(8, 1)
    for t in range(PLANE // TILE):
        lanes = slice(TILE * t, TILE * t + TILE)
        edge = edge_ref[:, :, lanes].astype(F32)
        mid = grad_ref[:, :, lanes].astype(F32)
        inner = plane_product(grad_ref[...].reshape(2 * ROWS, PLANE), weights, t).reshape(2, ROWS, TILE)
        outer = plane_product(edge_ref[...].reshape(2 * ROWS, PLANE), weights, t).reshape(2, ROWS, TILE)
        for i in range(2):
            value = (inner[i] + (edge[i] + mid[1 - i])) * (1.0 / 32.0)
            start = PLANE * (1 + i) + TILE * t
            out_ref[:, start : start + TILE] = value.astype(BF16) * mask_ref[i, :, lanes]
            part_ref[i, :, lanes] = outer[i] + mid[i]


def finish_kernel(below_ref, above_ref, part_ref, mask_ref, inner_ref, out_ref):
    for i, ref in enumerate((below_ref, above_ref)):
        tiles = unfold(ref[...].astype(F32))
        rest = slice(2 * ORB, ROWS) if i == 0 else slice(0, ORB)
        for t in range(PLANE // 128):
            lanes = slice(128 * t, 128 * t + 128)
            start = PLANE * (CX - 1) * i + 128 * t
            put = slice(start, start + 128)
            value = (part_ref[i, halo_rows(i), lanes] + tiles[t % 4]) * (1.0 / 32.0)
            out_ref[halo_rows(i), put] = value.astype(BF16) * mask_ref[i, halo_rows(i), lanes]
            value = part_ref[i, rest, lanes] * (1.0 / 32.0)
            out_ref[rest, put] = value.astype(BF16) * mask_ref[i, rest, lanes]
    out_ref[:, PLANE : (CX - 1) * PLANE] = inner_ref[:, PLANE : (CX - 1) * PLANE]


def shape(*dims, dtype=BF16):
    return jax.ShapeDtypeStruct(dims, dtype)


def cost(flops, moved):
    return pl.CostEstimate(flops=flops, bytes_accessed=moved, transcendentals=0)


PARAMS = pltpu.CompilerParams(vmem_limit_bytes=32 * 1024 * 1024)
WHOLE = pl.BlockSpec(memory_space=pltpu.VMEM)


def per_device(pieces, potential, centers, pattern):
    count = lax.axis_size("sx")

    def moved(value, steps):
        first, end = max(0, -steps), min(count, count - steps)
        return lax.ppermute(value, "sx", [(i, i + steps) for i in range(first, end)])

    table = centers.T
    pair = shape(2, ROWS, PLANE)

    def plane_spec(plane):
        return pl.BlockSpec((ROWS, PLANE), lambda i: (0, plane))

    def whole_spec(*dims):
        return pl.BlockSpec(dims, lambda i: (0,) * len(dims))

    edge, edge_mask, up, down = pl.pallas_call(
        edges_kernel,
        grid=(1,),
        out_shape=(pair, pair, shape(2 * ORB, HALF), shape(2 * ORB, HALF)),
        in_specs=[whole_spec(*table.shape), plane_spec(0), plane_spec(CX - 1)],
        out_specs=(
            whole_spec(2, ROWS, PLANE), whole_spec(2, ROWS, PLANE),
            whole_spec(2 * ORB, HALF), whole_spec(2 * ORB, HALF),
        ),
        compiler_params=PARAMS,
        cost_estimate=cost(10**8, 10**6),
        name="edges",
    )(table, pieces, pieces)
    below = moved(up, 1)
    above = moved(down, -1)

    mid, mid_mask, mid_energy, part, corr, ham = pl.pallas_call(
        energy_kernel,
        grid=(1,),
        out_shape=(
            pair, pair, pair, shape(2, ROWS, PLANE, dtype=F32),
            shape(ROWS, ROWS, dtype=F32), shape(ROWS, ROWS, dtype=F32),
        ),
        in_specs=[
            whole_spec(*table.shape), plane_spec(1), plane_spec(2),
            whole_spec(CX, PLANE), whole_spec(2, ROWS, PLANE),
        ],
        out_specs=(
            whole_spec(2, ROWS, PLANE), whole_spec(2, ROWS, PLANE), whole_spec(2, ROWS, PLANE),
            whole_spec(2, ROWS, PLANE), whole_spec(ROWS, ROWS), whole_spec(ROWS, ROWS),
        ),
        compiler_params=PARAMS,
        cost_estimate=cost(4 * 10**9, 10**7),
        name="energy",
    )(table, pieces, pieces, potential, edge)

    edge_energy, own, up1, down1, up2, down2 = pl.pallas_call(
        bands_kernel,
        out_shape=(
            pair, shape(2, ROWS, TILE, dtype=F32),
            shape(3, 2 * ORB, 128), shape(3, 2 * ORB, 128),
            shape(3, ORB, 128), shape(3, ORB, 128),
        ),
        in_specs=[WHOLE] * 7,
        out_specs=(WHOLE,) * 6,
        compiler_params=PARAMS,
        cost_estimate=cost(10**9, 10**7),
        name="bands",
    )(below, above, part, edge_mask, edge, corr, ham)
    below1 = moved(up1, 1)
    above1 = moved(down1, -1)
    below2 = moved(up2, 2)
    above2 = moved(down2, -2)

    edge_grad, mid_grad, up, down = pl.pallas_call(
        gradient_kernel,
        out_shape=(pair, pair, shape(2 * ORB, HALF), shape(2 * ORB, HALF)),
        in_specs=[pl.BlockSpec(memory_space=pltpu.SMEM)] + [WHOLE] * 11,
        out_specs=(WHOLE,) * 4,
        scratch_shapes=[pltpu.VMEM((ROWS, 512), F32), pltpu.VMEM((ROWS, 512), F32)],
        compiler_params=PARAMS,
        cost_estimate=cost(10**9, 10**7),
        name="gradient",
    )(
        pattern.T, own, below1, above1, below2, above2,
        edge, mid, edge_energy, mid_energy, edge_mask, mid_mask,
    )
    below = moved(up, 1)
    above = moved(down, -1)

    inner, part = pl.pallas_call(
        smooth_kernel,
        out_shape=(shape(ROWS, CX * PLANE), shape(2, ROWS, PLANE, dtype=F32)),
        in_specs=[WHOLE] * 4,
        out_specs=(WHOLE,) * 2,
        compiler_params=PARAMS,
        cost_estimate=cost(2 * 10**9, 10**7),
        name="smooth",
    )(edge_grad, mid_grad, edge_mask, mid_mask)

    return pl.pallas_call(
        finish_kernel,
        out_shape=shape(ROWS, CX * PLANE),
        in_specs=[WHOLE] * 5,
        out_specs=WHOLE,
        compiler_params=PARAMS,
        cost_estimate=cost(10**7, 10**7),
        name="finish",
    )(below, above, part, edge_mask, inner)


def solution(mesh):
    return jax.shard_map(
        per_device,
        mesh=mesh,
        in_specs=(P(("grp", "sx"), None), P(("grp", "sx"), None), P("grp", None), P("grp", None)),
        out_specs=P(("grp", "sx"), None),
        check_vma=False,
    )
```

```python
import functools

import jax
import jax.numpy as jnp
from jax import lax
from jax.experimental import pallas as pl
from jax.experimental.pallas import tpu as pltpu
from jax.sharding import PartitionSpec as P

ORB = 64
CX = 4
NY = 32
NZ = 32
ROWS = 3 * ORB
PLANE = NY * NZ
TILE = 256
HALF = PLANE // 4
F32 = jnp.float32
BF16 = jnp.bfloat16


def iota(shape, dim):
    return lax.broadcasted_iota(jnp.int32, shape, dim)


def row_features(ct_ref):
    slab = lax.axis_index("sx")
    count = lax.axis_size("sx")
    width = ct_ref.shape[1]
    first = jnp.clip(slab * ORB - ORB, 0, width - 4 * ORB) // 128 * 128
    first = pl.multiple_of(first, 128)
    window = ct_ref[:, pl.ds(first, 4 * ORB)]
    shift = slab * ORB - ORB - first
    window = pltpu.roll(jnp.concatenate([window, window], axis=0), lax.rem(4 * ORB - shift, 4 * ORB), 1)
    lane = iota((1, 4 * ORB), 1)
    block = slab - 1 + lane // ORB
    valid = (block >= 0) & (block < count)
    cx = window[0:1] - slab * CX
    cy = window[1:2]
    cz = window[2:3]
    r = window[3:4]
    const = cx * cx + cy * cy + cz * cz - r * r
    const = jnp.where(valid, const, 65535)
    cx = jnp.where(valid, cx, 0)
    cy = jnp.where(valid, cy, 0)
    cz = jnp.where(valid, cz, 0)
    k = iota((16, 4 * ORB), 0)
    feats = jnp.where(k == 0, 1, 0)
    feats = jnp.where(k == 1, 256, feats)
    feats = jnp.where(k == 2, cy, feats)
    feats = jnp.where(k == 3, cz, feats)
    feats = jnp.where(k == 4, const & 255, feats)
    feats = jnp.where(k == 5, const >> 8, feats)
    feats = jnp.where(k == 6, cx, feats)
    return jnp.transpose(feats.astype(F32))[:ROWS].astype(BF16)


def cell_features(plane):
    k = iota((16, PLANE), 0)
    cell = iota((16, PLANE), 1)
    y = cell >> 5
    z = cell & 31
    sq = y * y + z * z + plane * plane
    feats = jnp.where(k == 0, sq & 255, 0)
    feats = jnp.where(k == 1, sq >> 8, feats)
    feats = jnp.where(k == 2, -2 * y, feats)
    feats = jnp.where(k == 3, -2 * z, feats)
    feats = jnp.where(k == 4, 1, feats)
    feats = jnp.where(k == 5, 256, feats)
    feats = jnp.where(k == 6, -2 * plane, feats)
    return feats.astype(F32).astype(BF16)


def sphere(rows, plane):
    reach = jnp.dot(rows, cell_features(plane), preferred_element_type=F32)
    return jnp.where(reach <= 0.0, 1.0, 0.0).astype(BF16)


def in_plane(center, beside):
    k = iota((2 * TILE, TILE), 0) - 128
    n = iota((2 * TILE, TILE), 1)
    diff = k - n
    near_y = (diff == NZ) | (diff == -NZ)
    near_z = ((diff == 1) | (diff == -1)) & ((k >> 5) == (n >> 5))
    w = jnp.where(near_y | near_z, float(beside), 0.0)
    return jnp.where(diff == 0, float(center), w).astype(BF16)


def plane_product(values, weights, t):
    low = max(0, TILE * t - 128)
    high = min(PLANE, TILE * t + TILE + 128)
    shift = 128 - TILE * t
    return jnp.dot(
        values[:, low:high], weights[low + shift : high + shift], preferred_element_type=F32
    )


def fold(values):
    half = values[:, : PLANE // 2] + values[:, PLANE // 2 :]
    low_z = (iota((1, 128), 1) & 31) < 16
    out = []
    for i in range(2):
        a = half[:, 256 * i : 256 * i + 128]
        b = half[:, 256 * i + 128 : 256 * i + 256]
        out.append(jnp.where(low_z, a + pltpu.roll(a, 112, 1), b + pltpu.roll(b, 16, 1)))
    return out


def unfold(packed):
    low_z = (iota((1, 128), 1) & 31) < 16
    tiles = []
    for i in range(2):
        p = packed[:, 128 * i : 128 * i + 128]
        tiles.append(jnp.where(low_z, p, pltpu.roll(p, 16, 1)))
        tiles.append(jnp.where(low_z, pltpu.roll(p, 112, 1), p))
    return tiles


def is_even():
    return lax.rem(lax.axis_index("sx"), 2) == 0


def put_messages(planes, mate_ref, across_ref):
    down = fold(planes[0, : 2 * ORB].astype(F32))
    up = fold(planes[1, ORB:].astype(F32))
    even = is_even()
    for i in range(2):
        lanes = slice(128 * i, 128 * i + 128)
        mate_ref[:, lanes] = jnp.where(even, up[i], down[i]).astype(BF16)
        across_ref[:, lanes] = jnp.where(even, down[i], up[i]).astype(BF16)


def sides(mate_ref, across_ref):
    mate = mate_ref[...].astype(F32)
    across = across_ref[...].astype(F32)
    even = is_even()
    return (jnp.where(even, across, mate), jnp.where(even, mate, across))


def edges_kernel(ct_ref, first_ref, last_ref, phi_ref, mask_ref, mate_ref, across_ref):
    rows = row_features(ct_ref)
    for i, (plane, ref) in enumerate(((0, first_ref), (CX - 1, last_ref))):
        mask = sphere(rows, plane)
        mask_ref[i] = mask
        phi_ref[i] = ref[...] * mask
    put_messages(phi_ref, mate_ref, across_ref)


def rows_product(a, b):
    return lax.dot_general(a, b, (((1,), (1,)), ((), ())), preferred_element_type=F32)


def energy_kernel(
    ct_ref, mid1_ref, mid2_ref, pot_ref, edge_ref,
    phi_ref, mask_ref, energy_ref, part_ref, corr_ref, ham_ref,
):
    rows = row_features(ct_ref)
    for i, ref in enumerate((mid1_ref, mid2_ref)):
        mask = sphere(rows, 1 + i)
        mask_ref[i] = mask
        phi_ref[i] = ref[...] * mask
    weights = in_plane(6, -1)
    for t in range(PLANE // TILE):
        lanes = slice(TILE * t, TILE * t + TILE)
        edge = edge_ref[:, :, lanes].astype(F32)
        mid = phi_ref[:, :, lanes].astype(F32)
        inner = plane_product(phi_ref[...].reshape(2 * ROWS, PLANE), weights, t).reshape(2, ROWS, TILE)
        outer = plane_product(edge_ref[...].reshape(2 * ROWS, PLANE), weights, t).reshape(2, ROWS, TILE)
        for i in range(2):
            value = 0.5 * (inner[i] - (edge[i] + mid[1 - i])) + pot_ref[1 + i : 2 + i, lanes] * mid[i]
            energy_ref[i, :, lanes] = value.astype(BF16) * mask_ref[i, :, lanes]
            plane = (CX - 1) * i
            part_ref[i, :, lanes] = 0.5 * (outer[i] - mid[i]) + pot_ref[plane : plane + 1, lanes] * edge[i]
    corr = jnp.zeros((ROWS, ROWS), F32)
    ham = jnp.zeros((ROWS, ROWS), F32)
    for i in range(2):
        corr = corr + rows_product(phi_ref[i], phi_ref[i]) + rows_product(edge_ref[i], edge_ref[i])
        ham = ham + rows_product(energy_ref[i], phi_ref[i])
    corr_ref[...] = corr
    ham_ref[...] = ham


def halo_rows(i):
    return slice(0, 2 * ORB) if i == 0 else slice(ORB, ROWS)


def bands_kernel(
    mate_ref, across_ref, part_ref, mask_ref, phi_ref, corr_ref, ham_ref,
    energy_ref, own_ref, rows_ref,
):
    volume = 1.0 / (4.0 * CX**3)
    ham = ham_ref[...]
    for i, side in enumerate(sides(mate_ref, across_ref)):
        tiles = unfold(side)
        rest = slice(2 * ORB, ROWS) if i == 0 else slice(0, ORB)
        for t in range(PLANE // 128):
            lanes = slice(128 * t, 128 * t + 128)
            value = part_ref[i, halo_rows(i), lanes] - 0.5 * tiles[t % 4]
            energy_ref[i, halo_rows(i), lanes] = value.astype(BF16) * mask_ref[i, halo_rows(i), lanes]
            energy_ref[i, rest, lanes] = part_ref[i, rest, lanes].astype(BF16) * mask_ref[i, rest, lanes]
        ham = ham + rows_product(energy_ref[i], phi_ref[i])
    own_ref[:, :, ROWS:] = jnp.zeros((2, ROWS, TILE - ROWS), F32)
    own_ref[0, :, :ROWS] = ham * volume
    own_ref[1, :, :ROWS] = corr_ref[...] * volume
    tail = jnp.where(low_half(), own_ref[0, :, 128:256], swapped(own_ref[1, :, 128:256]))
    even = is_even()
    for i, value in enumerate((own_ref[0, :, 0:128], own_ref[1, :, 0:128], tail)):
        rows_ref[i] = jnp.where(even, value[ORB:], value[: 2 * ORB]).astype(BF16)


def low_half():
    return iota((1, 128), 1) < 64


def swapped(value):
    return pltpu.roll(value, 64, 1)


def mate_blocks(rows_ref, which):
    tail = rows_ref[2].astype(F32)
    if which == 1:
        tail = swapped(tail)
    return rows_ref[which].astype(F32), jnp.where(low_half(), tail, 0.0)


def shifted(c01, c2x):
    low = low_half()
    turned = swapped(c01)
    return jnp.where(low, 0.0, turned), jnp.where(low, turned, swapped(c2x))


def relay_kernel(own_ref, rows_ref, out_ref):
    even = is_even()
    for which in range(2):
        head, rest = shifted(own_ref[which, :, 0:128], own_ref[which, :, 128:256])
        c01, c2x = mate_blocks(rows_ref, which)
        c01 = jnp.where(even, c01[:ORB], c01[ORB:])
        c2x = jnp.where(even, c2x[:ORB], c2x[ORB:])
        own = slice(ORB, 2 * ORB)
        out_ref[which, :ORB, 0:128] = (head[own] + jnp.where(even, c2x, c01)).astype(BF16)
        out_ref[which, :ORB, 128:256] = (rest[own] + jnp.where(even, c01, c2x)).astype(BF16)
        out_ref[which, ORB:, 0:128] = jnp.where(even, head[:ORB], head[2 * ORB :]).astype(BF16)
        out_ref[which, ORB:, 128:256] = jnp.where(even, rest[:ORB], rest[2 * ORB :]).astype(BF16)


def gradient_kernel(
    pattern_ref, own_ref, rows_ref, across_in_ref, relayed_ref,
    edge_ref, phi_ref, edge_energy_ref, energy_ref, edge_mask_ref, mask_ref,
    edge_grad_ref, grad_ref, mate_ref, across_ref,
    ham_ref, inv_ref,
):
    slab = lax.axis_index("sx")
    even = is_even()
    last = pattern_ref.shape[1] - 1
    low = low_half()
    zero = jnp.zeros((ORB, 128), F32)
    for which, band_ref in enumerate((ham_ref, inv_ref)):
        near, rest = shifted(*mate_blocks(rows_ref, which))
        ahead = across_in_ref[which, :, 0:128].astype(F32)
        beside = across_in_ref[which, :, 128:256].astype(F32)
        turned = swapped(relayed_ref[which, ORB:, 128:256].astype(F32))
        far0 = jnp.where(low, swapped(relayed_ref[which, ORB:, 0:128].astype(F32)), turned)
        far1 = jnp.where(low, turned, 0.0)
        got_even = (
            (ahead[:ORB], beside[:ORB], zero, zero),
            (ahead[ORB:], beside[ORB:] + near[:ORB], rest[:ORB], zero),
            (zero, near[ORB:], rest[ORB:] + far0, far1),
        )
        ahead_high = jnp.where(low, 0.0, ahead)
        ahead_low = jnp.where(low, ahead, 0.0)
        got_odd = (
            (near[:ORB] + far0, rest[:ORB] + far1, zero, zero),
            (near[ORB:], rest[ORB:] + ahead_high[ORB:], beside[ORB:], zero),
            (zero, ahead_high[:ORB], beside[:ORB], ahead_low[:ORB]),
        )
        for r in range(3):
            for q in range(4):
                kept = []
                for col in (2 * q, 2 * q + 1):
                    apart = abs(col - r - 2)
                    if apart == 0:
                        kept.append(1.0)
                    elif apart > 2:
                        kept.append(0.0)
                    else:
                        at = jnp.clip(slab - 3 + min(col, r + 2), 0, last)
                        kept.append(pattern_ref[apart - 1, at].astype(F32))
                value = jnp.where(even, got_even[r][q], got_odd[r][q])
                if q in (1, 2):
                    value = value + own_ref[which, ORB * r : ORB * r + ORB, 128 * q - 128 : 128 * q]
                value = value * jnp.where(low, kept[0], kept[1])
                if which == 1:
                    on = iota((ORB, 128), 0) + (ORB * (r + 2) - 128 * q) == iota((ORB, 128), 1)
                    value = jnp.where(on, 2.0, 0.0) - value
                band_ref[ORB * r : ORB * r + ORB, 128 * q : 128 * q + 128] = value
    theta = lax.dot_general(
        ham_ref[...], inv_ref[...], (((1,), (1,)), ((), ())),
        precision=lax.Precision.HIGHEST, preferred_element_type=F32,
    ).astype(BF16)
    for orb_ref, en_ref, m_ref, out_ref in (
        (edge_ref, edge_energy_ref, edge_mask_ref, edge_grad_ref),
        (phi_ref, energy_ref, mask_ref, grad_ref),
    ):
        for i in range(2):
            for t in range(PLANE // TILE):
                lanes = slice(TILE * t, TILE * t + TILE)
                fix = jnp.dot(theta, orb_ref[i, :, lanes], preferred_element_type=F32)
                value = en_ref[i, :, lanes].astype(F32) - fix
                out_ref[i, :, lanes] = value.astype(BF16) * m_ref[i, :, lanes]
    put_messages(edge_grad_ref, mate_ref, across_ref)


def smooth_kernel(edge_ref, grad_ref, edge_mask_ref, mask_ref, out_ref, part_ref):
    weights = in_plane(8, 1)
    for t in range(PLANE // TILE):
        lanes = slice(TILE * t, TILE * t + TILE)
        edge = edge_ref[:, :, lanes].astype(F32)
        mid = grad_ref[:, :, lanes].astype(F32)
        inner = plane_product(grad_ref[...].reshape(2 * ROWS, PLANE), weights, t).reshape(2, ROWS, TILE)
        outer = plane_product(edge_ref[...].reshape(2 * ROWS, PLANE), weights, t).reshape(2, ROWS, TILE)
        for i in range(2):
            value = (inner[i] + (edge[i] + mid[1 - i])) * (1.0 / 32.0)
            start = PLANE * (1 + i) + TILE * t
            out_ref[:, start : start + TILE] = value.astype(BF16) * mask_ref[i, :, lanes]
            part_ref[i, :, lanes] = outer[i] + mid[i]


def finish_kernel(mate_ref, across_ref, part_ref, mask_ref, inner_ref, out_ref):
    for i, side in enumerate(sides(mate_ref, across_ref)):
        tiles = unfold(side)
        rest = slice(2 * ORB, ROWS) if i == 0 else slice(0, ORB)
        for t in range(PLANE // 128):
            lanes = slice(128 * t, 128 * t + 128)
            start = PLANE * (CX - 1) * i + 128 * t
            put = slice(start, start + 128)
            value = (part_ref[i, halo_rows(i), lanes] + tiles[t % 4]) * (1.0 / 32.0)
            out_ref[halo_rows(i), put] = value.astype(BF16) * mask_ref[i, halo_rows(i), lanes]
            value = part_ref[i, rest, lanes] * (1.0 / 32.0)
            out_ref[rest, put] = value.astype(BF16) * mask_ref[i, rest, lanes]
    out_ref[:, PLANE : (CX - 1) * PLANE] = inner_ref[:, PLANE : (CX - 1) * PLANE]


def shape(*dims, dtype=BF16):
    return jax.ShapeDtypeStruct(dims, dtype)


def cost(flops, moved):
    return pl.CostEstimate(flops=flops, bytes_accessed=moved, transcendentals=0)


PARAMS = pltpu.CompilerParams(vmem_limit_bytes=32 * 1024 * 1024)
WHOLE = pl.BlockSpec(memory_space=pltpu.VMEM)


def per_device(pieces, potential, centers, pattern):
    count = lax.axis_size("sx")
    mates = [(i, i ^ 1) for i in range(count)]
    others = [(i, i + 1 if i % 2 else i - 1) for i in range(1, count - 1)]

    def to_mate(value):
        return lax.ppermute(value, "sx", mates)

    def across(value):
        return lax.ppermute(value, "sx", others)

    table = centers.T
    pair = shape(2, ROWS, PLANE)

    def plane_spec(plane):
        return pl.BlockSpec((ROWS, PLANE), lambda i: (0, plane))

    def whole_spec(*dims):
        return pl.BlockSpec(dims, lambda i: (0,) * len(dims))

    edge, edge_mask, for_mate, for_other = pl.pallas_call(
        edges_kernel,
        grid=(1,),
        out_shape=(pair, pair, shape(2 * ORB, HALF), shape(2 * ORB, HALF)),
        in_specs=[whole_spec(*table.shape), plane_spec(0), plane_spec(CX - 1)],
        out_specs=(
            whole_spec(2, ROWS, PLANE), whole_spec(2, ROWS, PLANE),
            whole_spec(2 * ORB, HALF), whole_spec(2 * ORB, HALF),
        ),
        compiler_params=PARAMS,
        cost_estimate=cost(10**8, 10**6),
        name="edges",
    )(table, pieces, pieces)
    other_side = across(for_other)
    mate_side = to_mate(for_mate)

    mid, mid_mask, mid_energy, part, corr, ham = pl.pallas_call(
        energy_kernel,
        grid=(1,),
        out_shape=(
            pair, pair, pair, shape(2, ROWS, PLANE, dtype=F32),
            shape(ROWS, ROWS, dtype=F32), shape(ROWS, ROWS, dtype=F32),
        ),
        in_specs=[
            whole_spec(*table.shape), plane_spec(1), plane_spec(2),
            whole_spec(CX, PLANE), whole_spec(2, ROWS, PLANE),
        ],
        out_specs=(
            whole_spec(2, ROWS, PLANE), whole_spec(2, ROWS, PLANE), whole_spec(2, ROWS, PLANE),
            whole_spec(2, ROWS, PLANE), whole_spec(ROWS, ROWS), whole_spec(ROWS, ROWS),
        ),
        compiler_params=PARAMS,
        cost_estimate=cost(4 * 10**9, 10**7),
        name="energy",
    )(table, pieces, pieces, potential, edge)

    edge_energy, own, for_mate = pl.pallas_call(
        bands_kernel,
        out_shape=(pair, shape(2, ROWS, TILE, dtype=F32), shape(3, 2 * ORB, 128)),
        in_specs=[WHOLE] * 7,
        out_specs=(WHOLE,) * 3,
        compiler_params=PARAMS,
        cost_estimate=cost(10**9, 10**7),
        name="bands",
    )(mate_side, other_side, part, edge_mask, edge, corr, ham)
    mate_rows = to_mate(for_mate)
    for_other = pl.pallas_call(
        relay_kernel,
        out_shape=shape(2, 2 * ORB, TILE),
        in_specs=[WHOLE] * 2,
        out_specs=WHOLE,
        compiler_params=PARAMS,
        cost_estimate=cost(10**6, 10**6),
        name="relay",
    )(own, mate_rows)
    other_rows = across(for_other)
    relayed = to_mate(other_rows)

    edge_grad, mid_grad, for_mate, for_other = pl.pallas_call(
        gradient_kernel,
        out_shape=(pair, pair, shape(2 * ORB, HALF), shape(2 * ORB, HALF)),
        in_specs=[pl.BlockSpec(memory_space=pltpu.SMEM)] + [WHOLE] * 10,
        out_specs=(WHOLE,) * 4,
        scratch_shapes=[pltpu.VMEM((ROWS, 512), F32), pltpu.VMEM((ROWS, 512), F32)],
        compiler_params=PARAMS,
        cost_estimate=cost(10**9, 10**7),
        name="gradient",
    )(
        pattern.T, own, mate_rows, other_rows, relayed,
        edge, mid, edge_energy, mid_energy, edge_mask, mid_mask,
    )
    other_side = across(for_other)
    mate_side = to_mate(for_mate)

    inner, part = pl.pallas_call(
        smooth_kernel,
        out_shape=(shape(ROWS, CX * PLANE), shape(2, ROWS, PLANE, dtype=F32)),
        in_specs=[WHOLE] * 4,
        out_specs=(WHOLE,) * 2,
        compiler_params=PARAMS,
        cost_estimate=cost(2 * 10**9, 10**7),
        name="smooth",
    )(edge_grad, mid_grad, edge_mask, mid_mask)

    return pl.pallas_call(
        finish_kernel,
        out_shape=shape(ROWS, CX * PLANE),
        in_specs=[WHOLE] * 5,
        out_specs=WHOLE,
        compiler_params=PARAMS,
        cost_estimate=cost(10**7, 10**7),
        name="finish",
    )(mate_side, other_side, part, edge_mask, inner)


def solution(mesh):
    return jax.shard_map(
        per_device,
        mesh=mesh,
        in_specs=(P(("grp", "sx"), None), P(("grp", "sx"), None), P("grp", None), P("grp", None)),
        out_specs=P(("grp", "sx"), None),
        check_vma=False,
    )
```

```python
import functools

import jax
import jax.numpy as jnp
from jax import lax
from jax.experimental import pallas as pl
from jax.experimental.pallas import tpu as pltpu
from jax.sharding import PartitionSpec as P

ORB = 64
CX = 4
NY = 32
NZ = 32
ROWS = 3 * ORB
PLANE = NY * NZ
TILE = 256
HALF = PLANE // 4
F32 = jnp.float32
BF16 = jnp.bfloat16


def iota(shape, dim):
    return lax.broadcasted_iota(jnp.int32, shape, dim)


def window_start(width):
    slab = lax.axis_index("sx")
    first = jnp.clip(slab * ORB - ORB, 0, width - 4 * ORB) // 128 * 128
    return pl.multiple_of(first, 128)


def row_features(window_ref, first):
    slab = lax.axis_index("sx")
    count = lax.axis_size("sx")
    window = window_ref[...]
    shift = slab * ORB - ORB - first
    window = pltpu.roll(jnp.concatenate([window, window], axis=0), lax.rem(4 * ORB - shift, 4 * ORB), 1)
    lane = iota((1, 4 * ORB), 1)
    block = slab - 1 + lane // ORB
    valid = (block >= 0) & (block < count)
    cx = window[0:1] - slab * CX
    cy = window[1:2]
    cz = window[2:3]
    r = window[3:4]
    const = cx * cx + cy * cy + cz * cz - r * r
    const = jnp.where(valid, const, 65535)
    cx = jnp.where(valid, cx, 0)
    cy = jnp.where(valid, cy, 0)
    cz = jnp.where(valid, cz, 0)
    k = iota((16, 4 * ORB), 0)
    feats = jnp.where(k == 0, 1, 0)
    feats = jnp.where(k == 1, 256, feats)
    feats = jnp.where(k == 2, cy, feats)
    feats = jnp.where(k == 3, cz, feats)
    feats = jnp.where(k == 4, const & 255, feats)
    feats = jnp.where(k == 5, const >> 8, feats)
    feats = jnp.where(k == 6, cx, feats)
    return jnp.transpose(feats.astype(F32))[:ROWS].astype(BF16)


def cell_features(plane):
    k = iota((16, PLANE), 0)
    cell = iota((16, PLANE), 1)
    y = cell >> 5
    z = cell & 31
    sq = y * y + z * z + plane * plane
    feats = jnp.where(k == 0, sq & 255, 0)
    feats = jnp.where(k == 1, sq >> 8, feats)
    feats = jnp.where(k == 2, -2 * y, feats)
    feats = jnp.where(k == 3, -2 * z, feats)
    feats = jnp.where(k == 4, 1, feats)
    feats = jnp.where(k == 5, 256, feats)
    feats = jnp.where(k == 6, -2 * plane, feats)
    return feats.astype(F32).astype(BF16)


def sphere(rows, plane):
    reach = jnp.dot(rows, cell_features(plane), preferred_element_type=F32)
    return jnp.where(reach <= 0.0, 1.0, 0.0).astype(BF16)


def in_plane(center, beside):
    k = iota((2 * TILE, TILE), 0) - 128
    n = iota((2 * TILE, TILE), 1)
    diff = k - n
    near_y = (diff == NZ) | (diff == -NZ)
    near_z = ((diff == 1) | (diff == -1)) & ((k >> 5) == (n >> 5))
    w = jnp.where(near_y | near_z, float(beside), 0.0)
    return jnp.where(diff == 0, float(center), w).astype(BF16)


def plane_product(values, weights, t):
    low = max(0, TILE * t - 128)
    high = min(PLANE, TILE * t + TILE + 128)
    shift = 128 - TILE * t
    return jnp.dot(
        values[:, low:high], weights[low + shift : high + shift], preferred_element_type=F32
    )


def fold(values):
    half = values[:, : PLANE // 2] + values[:, PLANE // 2 :]
    low_z = (iota((1, 128), 1) & 31) < 16
    out = []
    for i in range(2):
        a = half[:, 256 * i : 256 * i + 128]
        b = half[:, 256 * i + 128 : 256 * i + 256]
        out.append(jnp.where(low_z, a + pltpu.roll(a, 112, 1), b + pltpu.roll(b, 16, 1)))
    return out


def unfold(packed):
    low_z = (iota((1, 128), 1) & 31) < 16
    tiles = []
    for i in range(2):
        p = packed[:, 128 * i : 128 * i + 128]
        tiles.append(jnp.where(low_z, p, pltpu.roll(p, 16, 1)))
        tiles.append(jnp.where(low_z, pltpu.roll(p, 112, 1), p))
    return tiles


def is_even():
    return lax.rem(lax.axis_index("sx"), 2) == 0


def at_end():
    slab = lax.axis_index("sx")
    return (slab == 0) | (slab == lax.axis_size("sx") - 1)


def put_messages(planes, mate_ref, across_ref):
    down = fold(planes[0, : 2 * ORB].astype(F32))
    up = fold(planes[1, ORB:].astype(F32))
    even = is_even()
    for i in range(2):
        lanes = slice(128 * i, 128 * i + 128)
        mate_ref[:, lanes] = jnp.where(even, up[i], down[i]).astype(BF16)
        across_ref[:, lanes] = jnp.where(even, down[i], up[i]).astype(BF16)


def sides(mate_ref, across_ref):
    mate = mate_ref[...].astype(F32)
    across = jnp.where(at_end(), 0.0, across_ref[...].astype(F32))
    even = is_even()
    return (jnp.where(even, across, mate), jnp.where(even, mate, across))


def edges_kernel(
    table_ref, pieces_ref,
    phi_ref, mask_ref, rows_ref, mate_ref, across_ref,
    window_ref, raw_ref, sems,
):
    first = window_start(table_ref.shape[1])
    table_copy = pltpu.make_async_copy(table_ref.at[:, pl.ds(first, 4 * ORB)], window_ref, sems.at[2])
    table_copy.start()
    copies = []
    for i in range(2):
        start = (CX - 1) * PLANE * i
        copies.append(
            pltpu.make_async_copy(pieces_ref.at[:, start : start + PLANE], raw_ref.at[i], sems.at[i])
        )
        copies[i].start()
    table_copy.wait()
    rows = row_features(window_ref, first)
    rows_ref[...] = rows
    for i in range(2):
        mask_ref[i] = sphere(rows, (CX - 1) * i)
    for i in range(2):
        copies[i].wait()
        phi_ref[i] = raw_ref[i] * mask_ref[i]
    put_messages(phi_ref, mate_ref, across_ref)


def rows_product(a, b):
    return lax.dot_general(a, b, (((1,), (1,)), ((), ())), preferred_element_type=F32)


def energy_kernel(
    rows_ref, pieces_ref, pot_ref, edge_ref,
    phi_ref, mask_ref, energy_ref, part_ref, corr_ref, ham_ref,
):
    rows = rows_ref[...]
    for i in range(2):
        mask = sphere(rows, 1 + i)
        mask_ref[i] = mask
        phi_ref[i] = pieces_ref[:, PLANE * (1 + i) : PLANE * (2 + i)] * mask
    weights = in_plane(6, -1)
    for t in range(PLANE // TILE):
        lanes = slice(TILE * t, TILE * t + TILE)
        edge = edge_ref[:, :, lanes].astype(F32)
        mid = phi_ref[:, :, lanes].astype(F32)
        inner = plane_product(phi_ref[...].reshape(2 * ROWS, PLANE), weights, t).reshape(2, ROWS, TILE)
        outer = plane_product(edge_ref[...].reshape(2 * ROWS, PLANE), weights, t).reshape(2, ROWS, TILE)
        for i in range(2):
            value = 0.5 * (inner[i] - (edge[i] + mid[1 - i])) + pot_ref[1 + i : 2 + i, lanes] * mid[i]
            energy_ref[i, :, lanes] = value.astype(BF16) * mask_ref[i, :, lanes]
            plane = (CX - 1) * i
            part_ref[i, :, lanes] = 0.5 * (outer[i] - mid[i]) + pot_ref[plane : plane + 1, lanes] * edge[i]
    corr = jnp.zeros((ROWS, ROWS), F32)
    ham = jnp.zeros((ROWS, ROWS), F32)
    for i in range(2):
        corr = corr + rows_product(phi_ref[i], phi_ref[i]) + rows_product(edge_ref[i], edge_ref[i])
        ham = ham + rows_product(energy_ref[i], phi_ref[i])
    corr_ref[...] = corr
    ham_ref[...] = ham


def halo_rows(i):
    return slice(0, 2 * ORB) if i == 0 else slice(ORB, ROWS)


def bands_kernel(
    across_ref, mate_ref, part_ref, mask_ref, phi_ref, corr_ref, ham_ref,
    energy_ref, own_ref, rows_ref,
):
    volume = 1.0 / (4.0 * CX**3)
    ham = ham_ref[...]
    for i, side in enumerate(sides(mate_ref, across_ref)):
        tiles = unfold(side)
        rest = slice(2 * ORB, ROWS) if i == 0 else slice(0, ORB)
        for t in range(PLANE // 128):
            lanes = slice(128 * t, 128 * t + 128)
            value = part_ref[i, halo_rows(i), lanes] - 0.5 * tiles[t % 4]
            energy_ref[i, halo_rows(i), lanes] = value.astype(BF16) * mask_ref[i, halo_rows(i), lanes]
            energy_ref[i, rest, lanes] = part_ref[i, rest, lanes].astype(BF16) * mask_ref[i, rest, lanes]
        ham = ham + rows_product(energy_ref[i], phi_ref[i])
    own_ref[:, :, ROWS:] = jnp.zeros((2, ROWS, TILE - ROWS), F32)
    own_ref[0, :, :ROWS] = ham * volume
    own_ref[1, :, :ROWS] = corr_ref[...] * volume
    tail = jnp.where(low_half(), own_ref[0, :, 128:256], swapped(own_ref[1, :, 128:256]))
    even = is_even()
    for i, value in enumerate((own_ref[0, :, 0:128], own_ref[1, :, 0:128], tail)):
        rows_ref[i] = jnp.where(even, value[ORB:], value[: 2 * ORB]).astype(BF16)


def low_half():
    return iota((1, 128), 1) < 64


def swapped(value):
    return pltpu.roll(value, 64, 1)


def mate_blocks(rows_ref, which):
    tail = rows_ref[2].astype(F32)
    if which == 1:
        tail = swapped(tail)
    return rows_ref[which].astype(F32), jnp.where(low_half(), tail, 0.0)


def shifted(c01, c2x):
    low = low_half()
    turned = swapped(c01)
    return jnp.where(low, 0.0, turned), jnp.where(low, turned, swapped(c2x))


def relay_kernel(own_ref, rows_ref, out_ref):
    even = is_even()
    for which in range(2):
        head, rest = shifted(own_ref[which, :, 0:128], own_ref[which, :, 128:256])
        c01, c2x = mate_blocks(rows_ref, which)
        c01 = jnp.where(even, c01[:ORB], c01[ORB:])
        c2x = jnp.where(even, c2x[:ORB], c2x[ORB:])
        own = slice(ORB, 2 * ORB)
        parts = (
            (head[own] + jnp.where(even, c2x, c01), rest[own] + jnp.where(even, c01, c2x)),
            (jnp.where(even, head[:ORB], head[2 * ORB :]), jnp.where(even, rest[:ORB], rest[2 * ORB :])),
        )
        for i in range(2):
            for q in range(2):
                value = jnp.where(at_end(), 0.0, parts[i][q]).astype(BF16)
                out_ref[which, ORB * i : ORB * i + ORB, 128 * q : 128 * q + 128] = value


def put_gradient(theta, orbital_ref, energy_ref, mask_ref, out_ref):
    for i in range(2):
        for t in range(PLANE // TILE):
            lanes = slice(TILE * t, TILE * t + TILE)
            fix = jnp.dot(theta, orbital_ref[i, :, lanes], preferred_element_type=F32)
            value = energy_ref[i, :, lanes].astype(F32) - fix
            out_ref[i, :, lanes] = value.astype(BF16) * mask_ref[i, :, lanes]


def gradient_kernel(
    pattern_ref, own_ref, rows_ref, across_in_ref, relayed_ref,
    edge_ref, edge_energy_ref, edge_mask_ref,
    edge_grad_ref, theta_ref, mate_ref, across_ref,
    ham_ref, inv_ref,
):
    slab = lax.axis_index("sx")
    even = is_even()
    last = pattern_ref.shape[1] - 1
    low = low_half()
    zero = jnp.zeros((ORB, 128), F32)
    for which, band_ref in enumerate((ham_ref, inv_ref)):
        near, rest = shifted(*mate_blocks(rows_ref, which))
        ahead = across_in_ref[which, :, 0:128].astype(F32)
        beside = across_in_ref[which, :, 128:256].astype(F32)
        turned = swapped(relayed_ref[which, ORB:, 128:256].astype(F32))
        far0 = jnp.where(low, swapped(relayed_ref[which, ORB:, 0:128].astype(F32)), turned)
        far1 = jnp.where(low, turned, 0.0)
        got_even = (
            (ahead[:ORB], beside[:ORB], zero, zero),
            (ahead[ORB:], beside[ORB:] + near[:ORB], rest[:ORB], zero),
            (zero, near[ORB:], rest[ORB:] + far0, far1),
        )
        ahead_high = jnp.where(low, 0.0, ahead)
        ahead_low = jnp.where(low, ahead, 0.0)
        got_odd = (
            (near[:ORB] + far0, rest[:ORB] + far1, zero, zero),
            (near[ORB:], rest[ORB:] + ahead_high[ORB:], beside[ORB:], zero),
            (zero, ahead_high[:ORB], beside[:ORB], ahead_low[:ORB]),
        )
        for r in range(3):
            for q in range(4):
                kept = []
                for col in (2 * q, 2 * q + 1):
                    apart = abs(col - r - 2)
                    if apart == 0:
                        kept.append(1.0)
                    elif apart > 2:
                        kept.append(0.0)
                    else:
                        at = jnp.clip(slab - 3 + min(col, r + 2), 0, last)
                        kept.append(pattern_ref[apart - 1, at].astype(F32))
                value = jnp.where(even, got_even[r][q], got_odd[r][q])
                if q in (1, 2):
                    value = value + own_ref[which, ORB * r : ORB * r + ORB, 128 * q - 128 : 128 * q]
                value = value * jnp.where(low, kept[0], kept[1])
                if which == 1:
                    on = iota((ORB, 128), 0) + (ORB * (r + 2) - 128 * q) == iota((ORB, 128), 1)
                    value = jnp.where(on, 2.0, 0.0) - value
                band_ref[ORB * r : ORB * r + ORB, 128 * q : 128 * q + 128] = value
    theta = lax.dot_general(
        ham_ref[...], inv_ref[...], (((1,), (1,)), ((), ())),
        precision=lax.Precision.HIGHEST, preferred_element_type=F32,
    ).astype(BF16)
    theta_ref[...] = theta
    put_gradient(theta, edge_ref, edge_energy_ref, edge_mask_ref, edge_grad_ref)
    put_messages(edge_grad_ref, mate_ref, across_ref)


def smooth_kernel(
    theta_ref, phi_ref, energy_ref, edge_ref, mask_ref,
    out_ref, part_ref,
    grad_ref, done_ref, sems,
):
    put_gradient(theta_ref[...], phi_ref, energy_ref, mask_ref, grad_ref)
    weights = in_plane(8, 1)
    for t in range(PLANE // TILE):
        lanes = slice(TILE * t, TILE * t + TILE)
        edge = edge_ref[:, :, lanes].astype(F32)
        mid = grad_ref[:, :, lanes].astype(F32)
        inner = plane_product(grad_ref[...].reshape(2 * ROWS, PLANE), weights, t).reshape(2, ROWS, TILE)
        outer = plane_product(edge_ref[...].reshape(2 * ROWS, PLANE), weights, t).reshape(2, ROWS, TILE)
        for i in range(2):
            value = (inner[i] + (edge[i] + mid[1 - i])) * (1.0 / 32.0)
            done_ref[i, :, lanes] = value.astype(BF16) * mask_ref[i, :, lanes]
            part_ref[i, :, lanes] = outer[i] + mid[i]
    copies = []
    for i in range(2):
        start = PLANE * (1 + i)
        copies.append(
            pltpu.make_async_copy(done_ref.at[i], out_ref.at[:, start : start + PLANE], sems.at[i])
        )
        copies[i].start()
    for copy in copies:
        copy.wait()


def finish_kernel(across_ref, mate_ref, part_ref, mask_ref, inner_ref, out_ref, done_ref, sems):
    copies = []
    for i, side in enumerate(sides(mate_ref, across_ref)):
        tiles = unfold(side)
        rest = slice(2 * ORB, ROWS) if i == 0 else slice(0, ORB)
        for t in range(PLANE // 128):
            lanes = slice(128 * t, 128 * t + 128)
            value = (part_ref[i, halo_rows(i), lanes] + tiles[t % 4]) * (1.0 / 32.0)
            done_ref[i, halo_rows(i), lanes] = value.astype(BF16) * mask_ref[i, halo_rows(i), lanes]
            value = part_ref[i, rest, lanes] * (1.0 / 32.0)
            done_ref[i, rest, lanes] = value.astype(BF16) * mask_ref[i, rest, lanes]
        start = PLANE * (CX - 1) * i
        copies.append(
            pltpu.make_async_copy(done_ref.at[i], out_ref.at[:, start : start + PLANE], sems.at[i])
        )
        copies[i].start()
    for copy in copies:
        copy.wait()


def shape(*dims, dtype=BF16):
    return jax.ShapeDtypeStruct(dims, dtype)


def cost(flops, moved):
    return pl.CostEstimate(flops=flops, bytes_accessed=moved, transcendentals=0)


PARAMS = pltpu.CompilerParams(vmem_limit_bytes=32 * 1024 * 1024)
WHOLE = pl.BlockSpec(memory_space=pltpu.VMEM)
FAR = pl.BlockSpec(memory_space=pltpu.HBM)


def far(value):
    return pltpu.with_memory_space_constraint(value, pltpu.HBM)


def per_device(pieces, potential, centers, pattern):
    count = lax.axis_size("sx")
    mates = [(i, i ^ 1) for i in range(count)]
    others = [(0, 0), (count - 1, count - 1)]
    others += [(i, i + 1 if i % 2 else i - 1) for i in range(1, count - 1)]

    def to_mate(value):
        return lax.ppermute(value, "sx", mates)

    def across(value):
        return lax.ppermute(value, "sx", others)

    table = centers.T
    pair = shape(2, ROWS, PLANE)

    edge, edge_mask, rows, for_mate, for_other = pl.pallas_call(
        edges_kernel,
        out_shape=(pair, pair, shape(ROWS, 16), shape(2 * ORB, HALF), shape(2 * ORB, HALF)),
        in_specs=[FAR, FAR],
        out_specs=(WHOLE,) * 5,
        scratch_shapes=[
            pltpu.VMEM((4, 4 * ORB), jnp.int32),
            pltpu.VMEM((2, ROWS, PLANE), BF16),
            pltpu.SemaphoreType.DMA((3,)),
        ],
        compiler_params=PARAMS,
        cost_estimate=cost(10**8, 10**6),
        name="edges",
    )(far(table), far(pieces))
    other_side = across(for_other)
    mate_side = to_mate(for_mate)

    mid, mid_mask, mid_energy, part, corr, ham = pl.pallas_call(
        energy_kernel,
        out_shape=(
            pair, pair, pair, shape(2, ROWS, PLANE, dtype=F32),
            shape(ROWS, ROWS, dtype=F32), shape(ROWS, ROWS, dtype=F32),
        ),
        in_specs=[WHOLE] * 4,
        out_specs=(WHOLE,) * 6,
        compiler_params=PARAMS,
        cost_estimate=cost(4 * 10**9, 10**7),
        name="energy",
    )(rows, pieces, potential, edge)

    edge_energy, own, for_mate = pl.pallas_call(
        bands_kernel,
        out_shape=(pair, shape(2, ROWS, TILE, dtype=F32), shape(3, 2 * ORB, 128)),
        in_specs=[WHOLE] * 7,
        out_specs=(WHOLE,) * 3,
        compiler_params=PARAMS,
        cost_estimate=cost(10**9, 10**7),
        name="bands",
    )(other_side, mate_side, part, edge_mask, edge, corr, ham)
    mate_rows = to_mate(for_mate)
    for_other = pl.pallas_call(
        relay_kernel,
        out_shape=shape(2, 2 * ORB, TILE),
        in_specs=[WHOLE] * 2,
        out_specs=WHOLE,
        compiler_params=PARAMS,
        cost_estimate=cost(10**6, 10**6),
        name="relay",
    )(own, mate_rows)
    other_rows = across(for_other)
    relayed = to_mate(other_rows)

    edge_grad, theta, for_mate, for_other = pl.pallas_call(
        gradient_kernel,
        out_shape=(pair, shape(ROWS, ROWS), shape(2 * ORB, HALF), shape(2 * ORB, HALF)),
        in_specs=[pl.BlockSpec(memory_space=pltpu.SMEM)] + [WHOLE] * 7,
        out_specs=(WHOLE,) * 4,
        scratch_shapes=[pltpu.VMEM((ROWS, 512), F32), pltpu.VMEM((ROWS, 512), F32)],
        compiler_params=PARAMS,
        cost_estimate=cost(10**9, 10**7),
        name="gradient",
    )(pattern.T, own, mate_rows, other_rows, relayed, edge, edge_energy, edge_mask)
    other_side = across(for_other)
    mate_side = to_mate(for_mate)

    inner, part = pl.pallas_call(
        smooth_kernel,
        out_shape=(pltpu.HBM((ROWS, CX * PLANE), BF16), shape(2, ROWS, PLANE, dtype=F32)),
        in_specs=[WHOLE] * 5,
        out_specs=(FAR, WHOLE),
        scratch_shapes=[
            pltpu.VMEM((2, ROWS, PLANE), BF16),
            pltpu.VMEM((2, ROWS, PLANE), BF16),
            pltpu.SemaphoreType.DMA((2,)),
        ],
        compiler_params=PARAMS,
        cost_estimate=cost(2 * 10**9, 10**7),
        name="smooth",
    )(theta, mid, mid_energy, edge_grad, mid_mask)

    return pl.pallas_call(
        finish_kernel,
        out_shape=pltpu.HBM((ROWS, CX * PLANE), BF16),
        in_specs=[WHOLE] * 4 + [FAR],
        out_specs=FAR,
        scratch_shapes=[pltpu.VMEM((2, ROWS, PLANE), BF16), pltpu.SemaphoreType.DMA((2,))],
        input_output_aliases={4: 0},
        compiler_params=PARAMS,
        cost_estimate=cost(10**7, 10**7),
        name="finish",
    )(other_side, mate_side, part, edge_mask, inner)


def solution(mesh):
    return jax.shard_map(
        per_device,
        mesh=mesh,
        in_specs=(P(("grp", "sx"), None), P(("grp", "sx"), None), P("grp", None), P("grp", None)),
        out_specs=P(("grp", "sx"), None),
        check_vma=False,
    )
```

```python
import functools

import jax
import jax.numpy as jnp
from jax import lax
from jax.experimental import pallas as pl
from jax.experimental.pallas import tpu as pltpu
from jax.sharding import PartitionSpec as P

ORB = 64
CX = 4
NY = 32
NZ = 32
ROWS = 3 * ORB
PLANE = NY * NZ
TILE = 256
HALF = PLANE // 4
F32 = jnp.float32
BF16 = jnp.bfloat16


def iota(shape, dim):
    return lax.broadcasted_iota(jnp.int32, shape, dim)


def window_start(width):
    slab = lax.axis_index("sx")
    first = jnp.clip(slab * ORB - ORB, 0, width - 4 * ORB) // 128 * 128
    return pl.multiple_of(first, 128)


def row_features(window_ref, first):
    slab = lax.axis_index("sx")
    count = lax.axis_size("sx")
    window = window_ref[...]
    shift = slab * ORB - ORB - first
    window = pltpu.roll(jnp.concatenate([window, window], axis=0), lax.rem(4 * ORB - shift, 4 * ORB), 1)
    lane = iota((1, 4 * ORB), 1)
    block = slab - 1 + lane // ORB
    valid = (block >= 0) & (block < count)
    cx = window[0:1] - slab * CX
    cy = window[1:2]
    cz = window[2:3]
    r = window[3:4]
    const = cx * cx + cy * cy + cz * cz - r * r
    const = jnp.where(valid, const, 65535)
    cx = jnp.where(valid, cx, 0)
    cy = jnp.where(valid, cy, 0)
    cz = jnp.where(valid, cz, 0)
    k = iota((16, 4 * ORB), 0)
    feats = jnp.where(k == 0, 1, 0)
    feats = jnp.where(k == 1, 256, feats)
    feats = jnp.where(k == 2, cy, feats)
    feats = jnp.where(k == 3, cz, feats)
    feats = jnp.where(k == 4, const & 255, feats)
    feats = jnp.where(k == 5, const >> 8, feats)
    feats = jnp.where(k == 6, cx, feats)
    return jnp.transpose(feats.astype(F32))[:ROWS].astype(BF16)


def cell_features(plane):
    k = iota((16, PLANE), 0)
    cell = iota((16, PLANE), 1)
    y = cell >> 5
    z = cell & 31
    sq = y * y + z * z + plane * plane
    feats = jnp.where(k == 0, sq & 255, 0)
    feats = jnp.where(k == 1, sq >> 8, feats)
    feats = jnp.where(k == 2, -2 * y, feats)
    feats = jnp.where(k == 3, -2 * z, feats)
    feats = jnp.where(k == 4, 1, feats)
    feats = jnp.where(k == 5, 256, feats)
    feats = jnp.where(k == 6, -2 * plane, feats)
    return feats.astype(F32).astype(BF16)


def sphere(rows, plane):
    reach = jnp.dot(rows, cell_features(plane), preferred_element_type=F32)
    return jnp.where(reach <= 0.0, 1.0, 0.0).astype(BF16)


def in_plane(center, beside):
    k = iota((2 * TILE, TILE), 0) - 128
    n = iota((2 * TILE, TILE), 1)
    diff = k - n
    near_y = (diff == NZ) | (diff == -NZ)
    near_z = ((diff == 1) | (diff == -1)) & ((k >> 5) == (n >> 5))
    w = jnp.where(near_y | near_z, float(beside), 0.0)
    return jnp.where(diff == 0, float(center), w).astype(BF16)


def plane_product(values, weights, t):
    low = max(0, TILE * t - 128)
    high = min(PLANE, TILE * t + TILE + 128)
    shift = 128 - TILE * t
    return jnp.dot(
        values[:, low:high], weights[low + shift : high + shift], preferred_element_type=F32
    )


def fold(values):
    half = values[:, : PLANE // 2] + values[:, PLANE // 2 :]
    low_z = (iota((1, 128), 1) & 31) < 16
    out = []
    for i in range(2):
        a = half[:, 256 * i : 256 * i + 128]
        b = half[:, 256 * i + 128 : 256 * i + 256]
        out.append(jnp.where(low_z, a + pltpu.roll(a, 112, 1), b + pltpu.roll(b, 16, 1)))
    return out


def unfold(packed):
    low_z = (iota((1, 128), 1) & 31) < 16
    tiles = []
    for i in range(2):
        p = packed[:, 128 * i : 128 * i + 128]
        tiles.append(jnp.where(low_z, p, pltpu.roll(p, 16, 1)))
        tiles.append(jnp.where(low_z, pltpu.roll(p, 112, 1), p))
    return tiles


def is_even():
    return lax.rem(lax.axis_index("sx"), 2) == 0


def at_end():
    slab = lax.axis_index("sx")
    return (slab == 0) | (slab == lax.axis_size("sx") - 1)


def put_messages(planes, mate_ref, across_ref):
    down = fold(planes[0, : 2 * ORB].astype(F32))
    up = fold(planes[1, ORB:].astype(F32))
    even = is_even()
    for i in range(2):
        lanes = slice(128 * i, 128 * i + 128)
        mate_ref[:, lanes] = jnp.where(even, up[i], down[i]).astype(BF16)
        across_ref[:, lanes] = jnp.where(even, down[i], up[i]).astype(BF16)


def sides(mate_ref, across_ref):
    mate = mate_ref[...].astype(F32)
    across = jnp.where(at_end(), 0.0, across_ref[...].astype(F32))
    even = is_even()
    return (jnp.where(even, across, mate), jnp.where(even, mate, across))


def edges_kernel(
    table_ref, pieces_ref,
    phi_ref, mask_ref, rows_ref, mate_ref, across_ref,
    window_ref, raw_ref, sems,
):
    first = window_start(table_ref.shape[1])
    table_copy = pltpu.make_async_copy(table_ref.at[:, pl.ds(first, 4 * ORB)], window_ref, sems.at[2])
    table_copy.start()
    copies = []
    for i in range(2):
        start = (CX - 1) * PLANE * i
        copies.append(
            pltpu.make_async_copy(pieces_ref.at[:, start : start + PLANE], raw_ref.at[i], sems.at[i])
        )
        copies[i].start()
    table_copy.wait()
    rows = row_features(window_ref, first)
    rows_ref[...] = rows
    for i in range(2):
        mask_ref[i] = sphere(rows, (CX - 1) * i)
    for i in range(2):
        copies[i].wait()
        phi_ref[i] = raw_ref[i] * mask_ref[i]
    put_messages(phi_ref, mate_ref, across_ref)


def rows_product(a, b):
    return lax.dot_general(a, b, (((1,), (1,)), ((), ())), preferred_element_type=F32)


def energy_kernel(
    rows_ref, pieces_ref, pot_ref, edge_ref,
    phi_ref, mask_ref, energy_ref, part_ref, corr_ref, ham_ref,
):
    rows = rows_ref[...]
    for i in range(2):
        mask = sphere(rows, 1 + i)
        mask_ref[i] = mask
        phi_ref[i] = pieces_ref[:, PLANE * (1 + i) : PLANE * (2 + i)] * mask
    weights = in_plane(6, -1)
    for t in range(PLANE // TILE):
        lanes = slice(TILE * t, TILE * t + TILE)
        edge = edge_ref[:, :, lanes].astype(F32)
        mid = phi_ref[:, :, lanes].astype(F32)
        inner = plane_product(phi_ref[...].reshape(2 * ROWS, PLANE), weights, t).reshape(2, ROWS, TILE)
        outer = plane_product(edge_ref[...].reshape(2 * ROWS, PLANE), weights, t).reshape(2, ROWS, TILE)
        for i in range(2):
            value = 0.5 * (inner[i] - (edge[i] + mid[1 - i])) + pot_ref[1 + i : 2 + i, lanes] * mid[i]
            energy_ref[i, :, lanes] = value.astype(BF16) * mask_ref[i, :, lanes]
            plane = (CX - 1) * i
            part_ref[i, :, lanes] = 0.5 * (outer[i] - mid[i]) + pot_ref[plane : plane + 1, lanes] * edge[i]
    corr = jnp.zeros((ROWS, ROWS), F32)
    ham = jnp.zeros((ROWS, ROWS), F32)
    for i in range(2):
        corr = corr + rows_product(phi_ref[i], phi_ref[i]) + rows_product(edge_ref[i], edge_ref[i])
        ham = ham + rows_product(energy_ref[i], phi_ref[i])
    corr_ref[...] = corr
    ham_ref[...] = ham


def halo_rows(i):
    return slice(0, 2 * ORB) if i == 0 else slice(ORB, ROWS)


def bands_kernel(
    across_ref, mate_ref, part_ref, mask_ref, phi_ref, corr_ref, ham_ref,
    energy_ref, own_ref, rows_ref,
):
    volume = 1.0 / (4.0 * CX**3)
    ham = ham_ref[...]
    for i, side in enumerate(sides(mate_ref, across_ref)):
        tiles = unfold(side)
        rest = slice(2 * ORB, ROWS) if i == 0 else slice(0, ORB)
        for t in range(PLANE // 128):
            lanes = slice(128 * t, 128 * t + 128)
            value = part_ref[i, halo_rows(i), lanes] - 0.5 * tiles[t % 4]
            energy_ref[i, halo_rows(i), lanes] = value.astype(BF16) * mask_ref[i, halo_rows(i), lanes]
            energy_ref[i, rest, lanes] = part_ref[i, rest, lanes].astype(BF16) * mask_ref[i, rest, lanes]
        ham = ham + rows_product(energy_ref[i], phi_ref[i])
    own_ref[:, :, ROWS:] = jnp.zeros((2, ROWS, TILE - ROWS), F32)
    own_ref[0, :, :ROWS] = ham * volume
    own_ref[1, :, :ROWS] = corr_ref[...] * volume
    tail = jnp.where(low_half(), own_ref[0, :, 128:256], swapped(own_ref[1, :, 128:256]))
    even = is_even()
    for i, value in enumerate((own_ref[0, :, 0:128], own_ref[1, :, 0:128], tail)):
        rows_ref[i] = jnp.where(even, value[ORB:], value[: 2 * ORB]).astype(BF16)


def low_half():
    return iota((1, 128), 1) < 64


def swapped(value):
    return pltpu.roll(value, 64, 1)


def mate_blocks(rows_ref, which):
    tail = rows_ref[2].astype(F32)
    if which == 1:
        tail = swapped(tail)
    return rows_ref[which].astype(F32), jnp.where(low_half(), tail, 0.0)


def shifted(c01, c2x):
    low = low_half()
    turned = swapped(c01)
    return jnp.where(low, 0.0, turned), jnp.where(low, turned, swapped(c2x))


def relay_kernel(own_ref, rows_ref, out_ref):
    even = is_even()
    for which in range(2):
        head, rest = shifted(own_ref[which, :, 0:128], own_ref[which, :, 128:256])
        c01, c2x = mate_blocks(rows_ref, which)
        c01 = jnp.where(even, c01[:ORB], c01[ORB:])
        c2x = jnp.where(even, c2x[:ORB], c2x[ORB:])
        own = slice(ORB, 2 * ORB)
        parts = (
            (head[own] + jnp.where(even, c2x, c01), rest[own] + jnp.where(even, c01, c2x)),
            (jnp.where(even, head[:ORB], head[2 * ORB :]), jnp.where(even, rest[:ORB], rest[2 * ORB :])),
        )
        for i in range(2):
            for q in range(2):
                value = jnp.where(at_end(), 0.0, parts[i][q]).astype(BF16)
                out_ref[which, ORB * i : ORB * i + ORB, 128 * q : 128 * q + 128] = value


def put_gradient(theta, orbital_ref, energy_ref, mask_ref, out_ref):
    for i in range(2):
        for t in range(PLANE // TILE):
            lanes = slice(TILE * t, TILE * t + TILE)
            fix = jnp.dot(theta, orbital_ref[i, :, lanes], preferred_element_type=F32)
            value = energy_ref[i, :, lanes].astype(F32) - fix
            out_ref[i, :, lanes] = value.astype(BF16) * mask_ref[i, :, lanes]


def gradient_kernel(
    pattern_ref, own_ref, rows_ref, across_in_ref, relayed_ref,
    edge_ref, edge_energy_ref, edge_mask_ref,
    edge_grad_ref, theta_ref, mate_ref, across_ref,
    ham_ref, inv_ref,
):
    slab = lax.axis_index("sx")
    even = is_even()
    last = pattern_ref.shape[1] - 1
    low = low_half()
    zero = jnp.zeros((ORB, 128), F32)
    for which, band_ref in enumerate((ham_ref, inv_ref)):
        near, rest = shifted(*mate_blocks(rows_ref, which))
        ahead = across_in_ref[which, :, 0:128].astype(F32)
        beside = across_in_ref[which, :, 128:256].astype(F32)
        turned = swapped(relayed_ref[which, ORB:, 128:256].astype(F32))
        far0 = jnp.where(low, swapped(relayed_ref[which, ORB:, 0:128].astype(F32)), turned)
        far1 = jnp.where(low, turned, 0.0)
        got_even = (
            (ahead[:ORB], beside[:ORB], zero, zero),
            (ahead[ORB:], beside[ORB:] + near[:ORB], rest[:ORB], zero),
            (zero, near[ORB:], rest[ORB:] + far0, far1),
        )
        ahead_high = jnp.where(low, 0.0, ahead)
        ahead_low = jnp.where(low, ahead, 0.0)
        got_odd = (
            (near[:ORB] + far0, rest[:ORB] + far1, zero, zero),
            (near[ORB:], rest[ORB:] + ahead_high[ORB:], beside[ORB:], zero),
            (zero, ahead_high[:ORB], beside[:ORB], ahead_low[:ORB]),
        )
        for r in range(3):
            for q in range(4):
                kept = []
                for col in (2 * q, 2 * q + 1):
                    apart = abs(col - r - 2)
                    if apart == 0:
                        kept.append(1.0)
                    elif apart > 2:
                        kept.append(0.0)
                    else:
                        at = jnp.clip(slab - 3 + min(col, r + 2), 0, last)
                        kept.append(pattern_ref[apart - 1, at].astype(F32))
                value = jnp.where(even, got_even[r][q], got_odd[r][q])
                if q in (1, 2):
                    value = value + own_ref[which, ORB * r : ORB * r + ORB, 128 * q - 128 : 128 * q]
                value = value * jnp.where(low, kept[0], kept[1])
                if which == 1:
                    on = iota((ORB, 128), 0) + (ORB * (r + 2) - 128 * q) == iota((ORB, 128), 1)
                    value = jnp.where(on, 2.0, 0.0) - value
                band_ref[ORB * r : ORB * r + ORB, 128 * q : 128 * q + 128] = value
    theta = lax.dot_general(
        ham_ref[...], inv_ref[...], (((1,), (1,)), ((), ())),
        precision=lax.Precision.HIGHEST, preferred_element_type=F32,
    ).astype(BF16)
    theta_ref[...] = theta
    put_gradient(theta, edge_ref, edge_energy_ref, edge_mask_ref, edge_grad_ref)
    put_messages(edge_grad_ref, mate_ref, across_ref)


def smooth_kernel(
    theta_ref, phi_ref, energy_ref, edge_ref, mask_ref,
    out_ref, part_ref,
    grad_ref, done_ref, sems,
):
    put_gradient(theta_ref[...], phi_ref, energy_ref, mask_ref, grad_ref)
    weights = in_plane(8, 1)
    for t in range(PLANE // TILE):
        lanes = slice(TILE * t, TILE * t + TILE)
        edge = edge_ref[:, :, lanes].astype(F32)
        mid = grad_ref[:, :, lanes].astype(F32)
        inner = plane_product(grad_ref[...].reshape(2 * ROWS, PLANE), weights, t).reshape(2, ROWS, TILE)
        outer = plane_product(edge_ref[...].reshape(2 * ROWS, PLANE), weights, t).reshape(2, ROWS, TILE)
        for i in range(2):
            value = (inner[i] + (edge[i] + mid[1 - i])) * (1.0 / 32.0)
            done_ref[i, :, lanes] = value.astype(BF16) * mask_ref[i, :, lanes]
            part_ref[i, :, lanes] = outer[i] + mid[i]
    copies = []
    for i in range(2):
        start = PLANE * (1 + i)
        copies.append(
            pltpu.make_async_copy(done_ref.at[i], out_ref.at[:, start : start + PLANE], sems.at[i])
        )
        copies[i].start()
    for copy in copies:
        copy.wait()


def finish_kernel(across_ref, mate_ref, part_ref, mask_ref, inner_ref, out_ref, done_ref, sems):
    copies = []
    for i, side in enumerate(sides(mate_ref, across_ref)):
        tiles = unfold(side)
        rest = slice(2 * ORB, ROWS) if i == 0 else slice(0, ORB)
        for t in range(PLANE // 128):
            lanes = slice(128 * t, 128 * t + 128)
            value = (part_ref[i, halo_rows(i), lanes] + tiles[t % 4]) * (1.0 / 32.0)
            done_ref[i, halo_rows(i), lanes] = value.astype(BF16) * mask_ref[i, halo_rows(i), lanes]
            value = part_ref[i, rest, lanes] * (1.0 / 32.0)
            done_ref[i, rest, lanes] = value.astype(BF16) * mask_ref[i, rest, lanes]
        start = PLANE * (CX - 1) * i
        copies.append(
            pltpu.make_async_copy(done_ref.at[i], out_ref.at[:, start : start + PLANE], sems.at[i])
        )
        copies[i].start()
    for copy in copies:
        copy.wait()


def shape(*dims, dtype=BF16):
    return jax.ShapeDtypeStruct(dims, dtype)


def cost(flops, moved):
    return pl.CostEstimate(flops=flops, bytes_accessed=moved, transcendentals=0)


PARAMS = pltpu.CompilerParams(vmem_limit_bytes=32 * 1024 * 1024)
WHOLE = pl.BlockSpec(memory_space=pltpu.VMEM)
FAR = pl.BlockSpec(memory_space=pltpu.HBM)


def far(value):
    return pltpu.with_memory_space_constraint(value, pltpu.HBM)


def per_device(pieces, potential, centers, pattern):
    count = lax.axis_size("sx")
    mates = [(i, i ^ 1) for i in range(count)]
    pairs = [[0, count - 1]] + [[i, i + 1] for i in range(1, count - 1, 2)]

    def to_mate(value):
        return lax.ppermute(value, "sx", mates)

    def across(value):
        both = lax.all_gather(value, "sx", axis_index_groups=pairs)
        first = (lax.axis_index("sx") % 2) == 1
        return jnp.where(first, both[1], both[0])

    table = centers.T
    pair = shape(2, ROWS, PLANE)

    edge, edge_mask, rows, for_mate, for_other = pl.pallas_call(
        edges_kernel,
        out_shape=(pair, pair, shape(ROWS, 16), shape(2 * ORB, HALF), shape(2 * ORB, HALF)),
        in_specs=[FAR, FAR],
        out_specs=(WHOLE,) * 5,
        scratch_shapes=[
            pltpu.VMEM((4, 4 * ORB), jnp.int32),
            pltpu.VMEM((2, ROWS, PLANE), BF16),
            pltpu.SemaphoreType.DMA((3,)),
        ],
        compiler_params=PARAMS,
        cost_estimate=cost(10**8, 10**6),
        name="edges",
    )(far(table), far(pieces))
    other_side = across(for_other)
    mate_side = to_mate(for_mate)

    mid, mid_mask, mid_energy, part, corr, ham = pl.pallas_call(
        energy_kernel,
        out_shape=(
            pair, pair, pair, shape(2, ROWS, PLANE, dtype=F32),
            shape(ROWS, ROWS, dtype=F32), shape(ROWS, ROWS, dtype=F32),
        ),
        in_specs=[WHOLE] * 4,
        out_specs=(WHOLE,) * 6,
        compiler_params=PARAMS,
        cost_estimate=cost(4 * 10**9, 10**7),
        name="energy",
    )(rows, pieces, potential, edge)

    edge_energy, own, for_mate = pl.pallas_call(
        bands_kernel,
        out_shape=(pair, shape(2, ROWS, TILE, dtype=F32), shape(3, 2 * ORB, 128)),
        in_specs=[WHOLE] * 7,
        out_specs=(WHOLE,) * 3,
        compiler_params=PARAMS,
        cost_estimate=cost(10**9, 10**7),
        name="bands",
    )(other_side, mate_side, part, edge_mask, edge, corr, ham)
    mate_rows = to_mate(for_mate)
    for_other = pl.pallas_call(
        relay_kernel,
        out_shape=shape(2, 2 * ORB, TILE),
        in_specs=[WHOLE] * 2,
        out_specs=WHOLE,
        compiler_params=PARAMS,
        cost_estimate=cost(10**6, 10**6),
        name="relay",
    )(own, mate_rows)
    other_rows = across(for_other)
    relayed = to_mate(other_rows)

    edge_grad, theta, for_mate, for_other = pl.pallas_call(
        gradient_kernel,
        out_shape=(pair, shape(ROWS, ROWS), shape(2 * ORB, HALF), shape(2 * ORB, HALF)),
        in_specs=[pl.BlockSpec(memory_space=pltpu.SMEM)] + [WHOLE] * 7,
        out_specs=(WHOLE,) * 4,
        scratch_shapes=[pltpu.VMEM((ROWS, 512), F32), pltpu.VMEM((ROWS, 512), F32)],
        compiler_params=PARAMS,
        cost_estimate=cost(10**9, 10**7),
        name="gradient",
    )(pattern.T, own, mate_rows, other_rows, relayed, edge, edge_energy, edge_mask)
    other_side = across(for_other)
    mate_side = to_mate(for_mate)

    inner, part = pl.pallas_call(
        smooth_kernel,
        out_shape=(pltpu.HBM((ROWS, CX * PLANE), BF16), shape(2, ROWS, PLANE, dtype=F32)),
        in_specs=[WHOLE] * 5,
        out_specs=(FAR, WHOLE),
        scratch_shapes=[
            pltpu.VMEM((2, ROWS, PLANE), BF16),
            pltpu.VMEM((2, ROWS, PLANE), BF16),
            pltpu.SemaphoreType.DMA((2,)),
        ],
        compiler_params=PARAMS,
        cost_estimate=cost(2 * 10**9, 10**7),
        name="smooth",
    )(theta, mid, mid_energy, edge_grad, mid_mask)

    return pl.pallas_call(
        finish_kernel,
        out_shape=pltpu.HBM((ROWS, CX * PLANE), BF16),
        in_specs=[WHOLE] * 4 + [FAR],
        out_specs=FAR,
        scratch_shapes=[pltpu.VMEM((2, ROWS, PLANE), BF16), pltpu.SemaphoreType.DMA((2,))],
        input_output_aliases={4: 0},
        compiler_params=PARAMS,
        cost_estimate=cost(10**7, 10**7),
        name="finish",
    )(other_side, mate_side, part, edge_mask, inner)


def solution(mesh):
    return jax.shard_map(
        per_device,
        mesh=mesh,
        in_specs=(P(("grp", "sx"), None), P(("grp", "sx"), None), P("grp", None), P("grp", None)),
        out_specs=P(("grp", "sx"), None),
        check_vma=False,
    )
```

```python
import functools

import jax
import jax.numpy as jnp
from jax import lax
from jax.experimental import pallas as pl
from jax.experimental.pallas import tpu as pltpu
from jax.sharding import PartitionSpec as P

ORB = 64
CX = 4
NY = 32
NZ = 32
ROWS = 3 * ORB
PLANE = NY * NZ
TILE = 256
HALF = PLANE // 4
F32 = jnp.float32
BF16 = jnp.bfloat16


def iota(shape, dim):
    return lax.broadcasted_iota(jnp.int32, shape, dim)


def window_start(width):
    slab = lax.axis_index("sx")
    first = jnp.clip(slab * ORB - ORB, 0, width - 4 * ORB) // 128 * 128
    return pl.multiple_of(first, 128)


def row_features(window_ref, first):
    slab = lax.axis_index("sx")
    count = lax.axis_size("sx")
    window = window_ref[...]
    shift = slab * ORB - ORB - first
    window = pltpu.roll(jnp.concatenate([window, window], axis=0), lax.rem(4 * ORB - shift, 4 * ORB), 1)
    lane = iota((1, 4 * ORB), 1)
    block = slab - 1 + lane // ORB
    valid = (block >= 0) & (block < count)
    cx = window[0:1] - slab * CX
    cy = window[1:2]
    cz = window[2:3]
    r = window[3:4]
    const = cx * cx + cy * cy + cz * cz - r * r
    const = jnp.where(valid, const, 65535)
    cx = jnp.where(valid, cx, 0)
    cy = jnp.where(valid, cy, 0)
    cz = jnp.where(valid, cz, 0)
    k = iota((16, 4 * ORB), 0)
    feats = jnp.where(k == 0, 1, 0)
    feats = jnp.where(k == 1, 256, feats)
    feats = jnp.where(k == 2, cy, feats)
    feats = jnp.where(k == 3, cz, feats)
    feats = jnp.where(k == 4, const & 255, feats)
    feats = jnp.where(k == 5, const >> 8, feats)
    feats = jnp.where(k == 6, cx, feats)
    return jnp.transpose(feats.astype(F32))[:ROWS].astype(BF16)


def cell_features(plane):
    k = iota((16, PLANE), 0)
    cell = iota((16, PLANE), 1)
    y = cell >> 5
    z = cell & 31
    sq = y * y + z * z + plane * plane
    feats = jnp.where(k == 0, sq & 255, 0)
    feats = jnp.where(k == 1, sq >> 8, feats)
    feats = jnp.where(k == 2, -2 * y, feats)
    feats = jnp.where(k == 3, -2 * z, feats)
    feats = jnp.where(k == 4, 1, feats)
    feats = jnp.where(k == 5, 256, feats)
    feats = jnp.where(k == 6, -2 * plane, feats)
    return feats.astype(F32).astype(BF16)


def sphere(rows, plane):
    reach = jnp.dot(rows, cell_features(plane), preferred_element_type=F32)
    return jnp.where(reach <= 0.0, 1.0, 0.0).astype(BF16)


def in_plane(center, beside):
    k = iota((2 * TILE, TILE), 0) - 128
    n = iota((2 * TILE, TILE), 1)
    diff = k - n
    near_y = (diff == NZ) | (diff == -NZ)
    near_z = ((diff == 1) | (diff == -1)) & ((k >> 5) == (n >> 5))
    w = jnp.where(near_y | near_z, float(beside), 0.0)
    return jnp.where(diff == 0, float(center), w).astype(BF16)


def plane_product(values, weights, t):
    low = max(0, TILE * t - 128)
    high = min(PLANE, TILE * t + TILE + 128)
    shift = 128 - TILE * t
    return jnp.dot(
        values[:, low:high], weights[low + shift : high + shift], preferred_element_type=F32
    )


def fold(values):
    half = values[:, : PLANE // 2] + values[:, PLANE // 2 :]
    low_z = (iota((1, 128), 1) & 31) < 16
    out = []
    for i in range(2):
        a = half[:, 256 * i : 256 * i + 128]
        b = half[:, 256 * i + 128 : 256 * i + 256]
        out.append(jnp.where(low_z, a + pltpu.roll(a, 112, 1), b + pltpu.roll(b, 16, 1)))
    return out


def unfold(packed):
    low_z = (iota((1, 128), 1) & 31) < 16
    tiles = []
    for i in range(2):
        p = packed[:, 128 * i : 128 * i + 128]
        tiles.append(jnp.where(low_z, p, pltpu.roll(p, 16, 1)))
        tiles.append(jnp.where(low_z, pltpu.roll(p, 112, 1), p))
    return tiles


def is_even():
    return lax.rem(lax.axis_index("sx"), 2) == 0


def at_end():
    slab = lax.axis_index("sx")
    return (slab == 0) | (slab == lax.axis_size("sx") - 1)


def put_messages(planes, mate_ref, across_ref):
    down = fold(planes[0, : 2 * ORB].astype(F32))
    up = fold(planes[1, ORB:].astype(F32))
    even = is_even()
    for i in range(2):
        lanes = slice(128 * i, 128 * i + 128)
        mate_ref[:, lanes] = jnp.where(even, up[i], down[i]).astype(BF16)
        value = jnp.where(even, down[i], up[i]).astype(BF16)
        across_ref[0, :, lanes] = value
        across_ref[1, :, lanes] = value


def sides(mate_ref, across_ref):
    mate = mate_ref[...].astype(F32)
    even = is_even()
    across = jnp.where(even, across_ref[0].astype(F32), across_ref[1].astype(F32))
    across = jnp.where(at_end(), 0.0, across)
    return (jnp.where(even, across, mate), jnp.where(even, mate, across))


def edges_kernel(
    table_ref, pieces_ref,
    phi_ref, mask_ref, rows_ref, mate_ref, across_ref,
    window_ref, raw_ref, sems,
):
    first = window_start(table_ref.shape[1])
    table_copy = pltpu.make_async_copy(table_ref.at[:, pl.ds(first, 4 * ORB)], window_ref, sems.at[2])
    table_copy.start()
    copies = []
    for i in range(2):
        start = (CX - 1) * PLANE * i
        copies.append(
            pltpu.make_async_copy(pieces_ref.at[:, start : start + PLANE], raw_ref.at[i], sems.at[i])
        )
        copies[i].start()
    table_copy.wait()
    rows = row_features(window_ref, first)
    rows_ref[...] = rows
    for i in range(2):
        mask_ref[i] = sphere(rows, (CX - 1) * i)
    for i in range(2):
        copies[i].wait()
        phi_ref[i] = raw_ref[i] * mask_ref[i]
    put_messages(phi_ref, mate_ref, across_ref)


def rows_product(a, b):
    return lax.dot_general(a, b, (((1,), (1,)), ((), ())), preferred_element_type=F32)


def energy_kernel(
    rows_ref, pieces_ref, pot_ref, edge_ref,
    phi_ref, mask_ref, energy_ref, part_ref, corr_ref, ham_ref,
):
    rows = rows_ref[...]
    for i in range(2):
        mask = sphere(rows, 1 + i)
        mask_ref[i] = mask
        phi_ref[i] = pieces_ref[:, PLANE * (1 + i) : PLANE * (2 + i)] * mask
    weights = in_plane(6, -1)
    for t in range(PLANE // TILE):
        lanes = slice(TILE * t, TILE * t + TILE)
        edge = edge_ref[:, :, lanes].astype(F32)
        mid = phi_ref[:, :, lanes].astype(F32)
        inner = plane_product(phi_ref[...].reshape(2 * ROWS, PLANE), weights, t).reshape(2, ROWS, TILE)
        outer = plane_product(edge_ref[...].reshape(2 * ROWS, PLANE), weights, t).reshape(2, ROWS, TILE)
        for i in range(2):
            value = 0.5 * (inner[i] - (edge[i] + mid[1 - i])) + pot_ref[1 + i : 2 + i, lanes] * mid[i]
            energy_ref[i, :, lanes] = value.astype(BF16) * mask_ref[i, :, lanes]
            plane = (CX - 1) * i
            part_ref[i, :, lanes] = 0.5 * (outer[i] - mid[i]) + pot_ref[plane : plane + 1, lanes] * edge[i]
    corr = jnp.zeros((ROWS, ROWS), F32)
    ham = jnp.zeros((ROWS, ROWS), F32)
    for i in range(2):
        corr = corr + rows_product(phi_ref[i], phi_ref[i]) + rows_product(edge_ref[i], edge_ref[i])
        ham = ham + rows_product(energy_ref[i], phi_ref[i])
    corr_ref[...] = corr
    ham_ref[...] = ham


def halo_rows(i):
    return slice(0, 2 * ORB) if i == 0 else slice(ORB, ROWS)


def bands_kernel(
    across_ref, mate_ref, part_ref, mask_ref, phi_ref, corr_ref, ham_ref,
    energy_ref, own_ref, rows_ref,
):
    volume = 1.0 / (4.0 * CX**3)
    ham = ham_ref[...]
    for i, side in enumerate(sides(mate_ref, across_ref)):
        tiles = unfold(side)
        rest = slice(2 * ORB, ROWS) if i == 0 else slice(0, ORB)
        for t in range(PLANE // 128):
            lanes = slice(128 * t, 128 * t + 128)
            value = part_ref[i, halo_rows(i), lanes] - 0.5 * tiles[t % 4]
            energy_ref[i, halo_rows(i), lanes] = value.astype(BF16) * mask_ref[i, halo_rows(i), lanes]
            energy_ref[i, rest, lanes] = part_ref[i, rest, lanes].astype(BF16) * mask_ref[i, rest, lanes]
        ham = ham + rows_product(energy_ref[i], phi_ref[i])
    own_ref[:, :, ROWS:] = jnp.zeros((2, ROWS, TILE - ROWS), F32)
    own_ref[0, :, :ROWS] = ham * volume
    own_ref[1, :, :ROWS] = corr_ref[...] * volume
    tail = jnp.where(low_half(), own_ref[0, :, 128:256], swapped(own_ref[1, :, 128:256]))
    even = is_even()
    for i, value in enumerate((own_ref[0, :, 0:128], own_ref[1, :, 0:128], tail)):
        rows_ref[i] = jnp.where(even, value[ORB:], value[: 2 * ORB]).astype(BF16)


def low_half():
    return iota((1, 128), 1) < 64


def swapped(value):
    return pltpu.roll(value, 64, 1)


def mate_blocks(rows_ref, which):
    tail = rows_ref[2].astype(F32)
    if which == 1:
        tail = swapped(tail)
    return rows_ref[which].astype(F32), jnp.where(low_half(), tail, 0.0)


def shifted(c01, c2x):
    low = low_half()
    turned = swapped(c01)
    return jnp.where(low, 0.0, turned), jnp.where(low, turned, swapped(c2x))


def picked(both_ref, even, which, rows, lanes):
    slab = lax.axis_index("sx")
    owner = jnp.where(even == is_even(), slab, slab + 1 - 2 * lax.rem(slab, 2))
    value = jnp.where(even, both_ref[0, which, rows, lanes].astype(F32), both_ref[1, which, rows, lanes].astype(F32))
    return jnp.where((owner == 0) | (owner == lax.axis_size("sx") - 1), 0.0, value)


def relay_kernel(own_ref, rows_ref, out_ref):
    even = is_even()
    for which in range(2):
        head, rest = shifted(own_ref[which, :, 0:128], own_ref[which, :, 128:256])
        c01, c2x = mate_blocks(rows_ref, which)
        c01 = jnp.where(even, c01[:ORB], c01[ORB:])
        c2x = jnp.where(even, c2x[:ORB], c2x[ORB:])
        own = slice(ORB, 2 * ORB)
        parts = (
            (head[own] + jnp.where(even, c2x, c01), rest[own] + jnp.where(even, c01, c2x)),
            (jnp.where(even, head[:ORB], head[2 * ORB :]), jnp.where(even, rest[:ORB], rest[2 * ORB :])),
        )
        for i in range(2):
            for q in range(2):
                value = parts[i][q].astype(BF16)
                out_ref[which, ORB * i : ORB * i + ORB, 128 * q : 128 * q + 128] = value


def put_gradient(theta, orbital_ref, energy_ref, mask_ref, out_ref):
    for i in range(2):
        for t in range(PLANE // TILE):
            lanes = slice(TILE * t, TILE * t + TILE)
            fix = jnp.dot(theta, orbital_ref[i, :, lanes], preferred_element_type=F32)
            value = energy_ref[i, :, lanes].astype(F32) - fix
            out_ref[i, :, lanes] = value.astype(BF16) * mask_ref[i, :, lanes]


def gradient_kernel(
    pattern_ref, own_ref, rows_ref, across_in_ref, relayed_ref,
    edge_ref, edge_energy_ref, edge_mask_ref,
    edge_grad_ref, theta_ref, mate_ref, across_ref,
    ham_ref, inv_ref,
):
    slab = lax.axis_index("sx")
    even = is_even()
    last = pattern_ref.shape[1] - 1
    low = low_half()
    zero = jnp.zeros((ORB, 128), F32)
    for which, band_ref in enumerate((ham_ref, inv_ref)):
        near, rest = shifted(*mate_blocks(rows_ref, which))
        ahead, beside = (
            picked(across_in_ref, even, which, slice(0, 2 * ORB), slice(128 * i, 128 * i + 128))
            for i in range(2)
        )
        front, turned = (
            swapped(picked(relayed_ref, ~even, which, slice(ORB, 2 * ORB), slice(128 * i, 128 * i + 128)))
            for i in range(2)
        )
        far0 = jnp.where(low, front, turned)
        far1 = jnp.where(low, turned, 0.0)
        got_even = (
            (ahead[:ORB], beside[:ORB], zero, zero),
            (ahead[ORB:], beside[ORB:] + near[:ORB], rest[:ORB], zero),
            (zero, near[ORB:], rest[ORB:] + far0, far1),
        )
        ahead_high = jnp.where(low, 0.0, ahead)
        ahead_low = jnp.where(low, ahead, 0.0)
        got_odd = (
            (near[:ORB] + far0, rest[:ORB] + far1, zero, zero),
            (near[ORB:], rest[ORB:] + ahead_high[ORB:], beside[ORB:], zero),
            (zero, ahead_high[:ORB], beside[:ORB], ahead_low[:ORB]),
        )
        for r in range(3):
            for q in range(4):
                kept = []
                for col in (2 * q, 2 * q + 1):
                    apart = abs(col - r - 2)
                    if apart == 0:
                        kept.append(1.0)
                    elif apart > 2:
                        kept.append(0.0)
                    else:
                        at = jnp.clip(slab - 3 + min(col, r + 2), 0, last)
                        kept.append(pattern_ref[apart - 1, at].astype(F32))
                value = jnp.where(even, got_even[r][q], got_odd[r][q])
                if q in (1, 2):
                    value = value + own_ref[which, ORB * r : ORB * r + ORB, 128 * q - 128 : 128 * q]
                value = value * jnp.where(low, kept[0], kept[1])
                if which == 1:
                    on = iota((ORB, 128), 0) + (ORB * (r + 2) - 128 * q) == iota((ORB, 128), 1)
                    value = jnp.where(on, 2.0, 0.0) - value
                band_ref[ORB * r : ORB * r + ORB, 128 * q : 128 * q + 128] = value
    theta = lax.dot_general(
        ham_ref[...], inv_ref[...], (((1,), (1,)), ((), ())),
        precision=lax.Precision.HIGHEST, preferred_element_type=F32,
    ).astype(BF16)
    theta_ref[...] = theta
    put_gradient(theta, edge_ref, edge_energy_ref, edge_mask_ref, edge_grad_ref)
    put_messages(edge_grad_ref, mate_ref, across_ref)


def smooth_kernel(
    theta_ref, phi_ref, energy_ref, edge_ref, mask_ref,
    out_ref, part_ref,
    grad_ref, done_ref, sems,
):
    put_gradient(theta_ref[...], phi_ref, energy_ref, mask_ref, grad_ref)
    weights = in_plane(8, 1)
    for t in range(PLANE // TILE):
        lanes = slice(TILE * t, TILE * t + TILE)
        edge = edge_ref[:, :, lanes].astype(F32)
        mid = grad_ref[:, :, lanes].astype(F32)
        inner = plane_product(grad_ref[...].reshape(2 * ROWS, PLANE), weights, t).reshape(2, ROWS, TILE)
        outer = plane_product(edge_ref[...].reshape(2 * ROWS, PLANE), weights, t).reshape(2, ROWS, TILE)
        for i in range(2):
            value = (inner[i] + (edge[i] + mid[1 - i])) * (1.0 / 32.0)
            done_ref[i, :, lanes] = value.astype(BF16) * mask_ref[i, :, lanes]
            part_ref[i, :, lanes] = outer[i] + mid[i]
    copies = []
    for i in range(2):
        start = PLANE * (1 + i)
        copies.append(
            pltpu.make_async_copy(done_ref.at[i], out_ref.at[:, start : start + PLANE], sems.at[i])
        )
        copies[i].start()
    for copy in copies:
        copy.wait()


def finish_kernel(across_ref, mate_ref, part_ref, mask_ref, inner_ref, out_ref, done_ref, sems):
    copies = []
    for i, side in enumerate(sides(mate_ref, across_ref)):
        tiles = unfold(side)
        rest = slice(2 * ORB, ROWS) if i == 0 else slice(0, ORB)
        for t in range(PLANE // 128):
            lanes = slice(128 * t, 128 * t + 128)
            value = (part_ref[i, halo_rows(i), lanes] + tiles[t % 4]) * (1.0 / 32.0)
            done_ref[i, halo_rows(i), lanes] = value.astype(BF16) * mask_ref[i, halo_rows(i), lanes]
            value = part_ref[i, rest, lanes] * (1.0 / 32.0)
            done_ref[i, rest, lanes] = value.astype(BF16) * mask_ref[i, rest, lanes]
        start = PLANE * (CX - 1) * i
        copies.append(
            pltpu.make_async_copy(done_ref.at[i], out_ref.at[:, start : start + PLANE], sems.at[i])
        )
        copies[i].start()
    for copy in copies:
        copy.wait()


def shape(*dims, dtype=BF16):
    return jax.ShapeDtypeStruct(dims, dtype)


def cost(flops, moved):
    return pl.CostEstimate(flops=flops, bytes_accessed=moved, transcendentals=0)


PARAMS = pltpu.CompilerParams(vmem_limit_bytes=32 * 1024 * 1024)
WHOLE = pl.BlockSpec(memory_space=pltpu.VMEM)
FAR = pl.BlockSpec(memory_space=pltpu.HBM)


def far(value):
    return pltpu.with_memory_space_constraint(value, pltpu.HBM)


def per_device(pieces, potential, centers, pattern):
    count = lax.axis_size("sx")
    mates = [(i, i ^ 1) for i in range(count)]
    groups = lax.axis_size("grp")
    pairs = []
    for g in range(0, groups, 2):
        for end in (0, count - 1):
            pairs.append([g * count + end, g * count + count + end])
    for g in range(groups):
        pairs += [[g * count + i, g * count + i + 1] for i in range(1, count - 1, 2)]

    def to_mate(value):
        return lax.ppermute(value, "sx", mates)

    def across(value):
        return lax.all_to_all(value, ("grp", "sx"), 0, 0, axis_index_groups=pairs)

    def gathered(value):
        return lax.all_gather(value, ("grp", "sx"), axis_index_groups=pairs)

    table = centers.T
    pair = shape(2, ROWS, PLANE)

    edge, edge_mask, rows, for_mate, for_other = pl.pallas_call(
        edges_kernel,
        out_shape=(pair, pair, shape(ROWS, 16), shape(2 * ORB, HALF), shape(2, 2 * ORB, HALF)),
        in_specs=[FAR, FAR],
        out_specs=(WHOLE,) * 5,
        scratch_shapes=[
            pltpu.VMEM((4, 4 * ORB), jnp.int32),
            pltpu.VMEM((2, ROWS, PLANE), BF16),
            pltpu.SemaphoreType.DMA((3,)),
        ],
        compiler_params=PARAMS,
        cost_estimate=cost(10**8, 10**6),
        name="edges",
    )(far(table), far(pieces))
    other_side = across(for_other)
    mate_side = to_mate(for_mate)

    mid, mid_mask, mid_energy, part, corr, ham = pl.pallas_call(
        energy_kernel,
        out_shape=(
            pair, pair, pair, shape(2, ROWS, PLANE, dtype=F32),
            shape(ROWS, ROWS, dtype=F32), shape(ROWS, ROWS, dtype=F32),
        ),
        in_specs=[WHOLE] * 4,
        out_specs=(WHOLE,) * 6,
        compiler_params=PARAMS,
        cost_estimate=cost(4 * 10**9, 10**7),
        name="energy",
    )(rows, pieces, potential, edge)

    edge_energy, own, for_mate = pl.pallas_call(
        bands_kernel,
        out_shape=(pair, shape(2, ROWS, TILE, dtype=F32), shape(3, 2 * ORB, 128)),
        in_specs=[WHOLE] * 7,
        out_specs=(WHOLE,) * 3,
        compiler_params=PARAMS,
        cost_estimate=cost(10**9, 10**7),
        name="bands",
    )(other_side, mate_side, part, edge_mask, edge, corr, ham)
    mate_rows = to_mate(for_mate)
    for_other = pl.pallas_call(
        relay_kernel,
        out_shape=shape(2, 2 * ORB, TILE),
        in_specs=[WHOLE] * 2,
        out_specs=WHOLE,
        compiler_params=PARAMS,
        cost_estimate=cost(10**6, 10**6),
        name="relay",
    )(own, mate_rows)
    both_rows = gathered(for_other)
    relayed = to_mate(both_rows)

    edge_grad, theta, for_mate, for_other = pl.pallas_call(
        gradient_kernel,
        out_shape=(pair, shape(ROWS, ROWS), shape(2 * ORB, HALF), shape(2, 2 * ORB, HALF)),
        in_specs=[pl.BlockSpec(memory_space=pltpu.SMEM)] + [WHOLE] * 7,
        out_specs=(WHOLE,) * 4,
        scratch_shapes=[pltpu.VMEM((ROWS, 512), F32), pltpu.VMEM((ROWS, 512), F32)],
        compiler_params=PARAMS,
        cost_estimate=cost(10**9, 10**7),
        name="gradient",
    )(pattern.T, own, mate_rows, both_rows, relayed, edge, edge_energy, edge_mask)
    other_side = across(for_other)
    mate_side = to_mate(for_mate)

    inner, part = pl.pallas_call(
        smooth_kernel,
        out_shape=(pltpu.HBM((ROWS, CX * PLANE), BF16), shape(2, ROWS, PLANE, dtype=F32)),
        in_specs=[WHOLE] * 5,
        out_specs=(FAR, WHOLE),
        scratch_shapes=[
            pltpu.VMEM((2, ROWS, PLANE), BF16),
            pltpu.VMEM((2, ROWS, PLANE), BF16),
            pltpu.SemaphoreType.DMA((2,)),
        ],
        compiler_params=PARAMS,
        cost_estimate=cost(2 * 10**9, 10**7),
        name="smooth",
    )(theta, mid, mid_energy, edge_grad, mid_mask)

    return pl.pallas_call(
        finish_kernel,
        out_shape=pltpu.HBM((ROWS, CX * PLANE), BF16),
        in_specs=[WHOLE] * 4 + [FAR],
        out_specs=FAR,
        scratch_shapes=[pltpu.VMEM((2, ROWS, PLANE), BF16), pltpu.SemaphoreType.DMA((2,))],
        input_output_aliases={4: 0},
        compiler_params=PARAMS,
        cost_estimate=cost(10**7, 10**7),
        name="finish",
    )(other_side, mate_side, part, edge_mask, inner)


def solution(mesh):
    return jax.shard_map(
        per_device,
        mesh=mesh,
        in_specs=(P(("grp", "sx"), None), P(("grp", "sx"), None), P("grp", None), P("grp", None)),
        out_specs=P(("grp", "sx"), None),
        check_vma=False,
    )
```

```python
import functools

import jax
import jax.numpy as jnp
from jax import lax
from jax.experimental import pallas as pl
from jax.experimental.pallas import tpu as pltpu
from jax.sharding import PartitionSpec as P

ORB = 64
CX = 4
NY = 32
NZ = 32
ROWS = 3 * ORB
PLANE = NY * NZ
TILE = 256
HALF = PLANE // 4
F32 = jnp.float32
BF16 = jnp.bfloat16


def iota(shape, dim):
    return lax.broadcasted_iota(jnp.int32, shape, dim)


def window_start(width):
    slab = lax.axis_index("sx")
    first = jnp.clip(slab * ORB - ORB, 0, width - 4 * ORB) // 128 * 128
    return pl.multiple_of(first, 128)


def row_features(window_ref, first):
    slab = lax.axis_index("sx")
    count = lax.axis_size("sx")
    window = window_ref[...]
    shift = slab * ORB - ORB - first
    window = pltpu.roll(jnp.concatenate([window, window], axis=0), lax.rem(4 * ORB - shift, 4 * ORB), 1)
    lane = iota((1, 4 * ORB), 1)
    block = slab - 1 + lane // ORB
    valid = (block >= 0) & (block < count)
    cx = window[0:1] - slab * CX
    cy = window[1:2]
    cz = window[2:3]
    r = window[3:4]
    const = cx * cx + cy * cy + cz * cz - r * r
    const = jnp.where(valid, const, 65535)
    cx = jnp.where(valid, cx, 0)
    cy = jnp.where(valid, cy, 0)
    cz = jnp.where(valid, cz, 0)
    k = iota((16, 4 * ORB), 0)
    feats = jnp.where(k == 0, 1, 0)
    feats = jnp.where(k == 1, 256, feats)
    feats = jnp.where(k == 2, cy, feats)
    feats = jnp.where(k == 3, cz, feats)
    feats = jnp.where(k == 4, const & 255, feats)
    feats = jnp.where(k == 5, const >> 8, feats)
    feats = jnp.where(k == 6, cx, feats)
    return jnp.transpose(feats.astype(F32))[:ROWS].astype(BF16)


def cell_features(plane):
    k = iota((16, PLANE), 0)
    cell = iota((16, PLANE), 1)
    y = cell >> 5
    z = cell & 31
    sq = y * y + z * z + plane * plane
    feats = jnp.where(k == 0, sq & 255, 0)
    feats = jnp.where(k == 1, sq >> 8, feats)
    feats = jnp.where(k == 2, -2 * y, feats)
    feats = jnp.where(k == 3, -2 * z, feats)
    feats = jnp.where(k == 4, 1, feats)
    feats = jnp.where(k == 5, 256, feats)
    feats = jnp.where(k == 6, -2 * plane, feats)
    return feats.astype(F32).astype(BF16)


def sphere(rows, plane):
    reach = jnp.dot(rows, cell_features(plane), preferred_element_type=F32)
    return jnp.where(reach <= 0.0, 1.0, 0.0).astype(BF16)


def in_plane(center, beside):
    k = iota((2 * TILE, TILE), 0) - 128
    n = iota((2 * TILE, TILE), 1)
    diff = k - n
    near_y = (diff == NZ) | (diff == -NZ)
    near_z = ((diff == 1) | (diff == -1)) & ((k >> 5) == (n >> 5))
    w = jnp.where(near_y | near_z, float(beside), 0.0)
    return jnp.where(diff == 0, float(center), w).astype(BF16)


def plane_product(values, weights, t):
    low = max(0, TILE * t - 128)
    high = min(PLANE, TILE * t + TILE + 128)
    shift = 128 - TILE * t
    return jnp.dot(
        values[:, low:high], weights[low + shift : high + shift], preferred_element_type=F32
    )


def fold(values):
    half = values[:, : PLANE // 2] + values[:, PLANE // 2 :]
    low_z = (iota((1, 128), 1) & 31) < 16
    out = []
    for i in range(2):
        a = half[:, 256 * i : 256 * i + 128]
        b = half[:, 256 * i + 128 : 256 * i + 256]
        out.append(jnp.where(low_z, a + pltpu.roll(a, 112, 1), b + pltpu.roll(b, 16, 1)))
    return out


def unfold(packed):
    low_z = (iota((1, 128), 1) & 31) < 16
    tiles = []
    for i in range(2):
        p = packed[:, 128 * i : 128 * i + 128]
        tiles.append(jnp.where(low_z, p, pltpu.roll(p, 16, 1)))
        tiles.append(jnp.where(low_z, pltpu.roll(p, 112, 1), p))
    return tiles


def is_even():
    return lax.rem(lax.axis_index("sx"), 2) == 0


def put_messages(planes, mate_ref, across_ref):
    down = fold(planes[0, : 2 * ORB].astype(F32))
    up = fold(planes[1, ORB:].astype(F32))
    even = is_even()
    for i in range(2):
        lanes = slice(128 * i, 128 * i + 128)
        mate_ref[:, lanes] = jnp.where(even, up[i], down[i]).astype(BF16)
        across_ref[:, lanes] = jnp.where(even, down[i], up[i]).astype(BF16)


def sides(mate_ref, across_ref):
    mate = mate_ref[...].astype(F32)
    across = across_ref[...].astype(F32)
    even = is_even()
    return (jnp.where(even, across, mate), jnp.where(even, mate, across))


def edges_kernel(
    table_ref, pieces_ref,
    phi_ref, mask_ref, rows_ref, mate_ref, across_ref,
    window_ref, raw_ref, sems,
):
    first = window_start(table_ref.shape[1])
    table_copy = pltpu.make_async_copy(table_ref.at[:, pl.ds(first, 4 * ORB)], window_ref, sems.at[2])
    table_copy.start()
    copies = []
    for i in range(2):
        start = (CX - 1) * PLANE * i
        copies.append(
            pltpu.make_async_copy(pieces_ref.at[:, start : start + PLANE], raw_ref.at[i], sems.at[i])
        )
        copies[i].start()
    table_copy.wait()
    rows = row_features(window_ref, first)
    rows_ref[...] = rows
    for i in range(2):
        mask_ref[i] = sphere(rows, (CX - 1) * i)
    for i in range(2):
        copies[i].wait()
        phi_ref[i] = raw_ref[i] * mask_ref[i]
    put_messages(phi_ref, mate_ref, across_ref)


def rows_product(a, b):
    return lax.dot_general(a, b, (((1,), (1,)), ((), ())), preferred_element_type=F32)


def energy_kernel(
    rows_ref, pieces_ref, pot_ref, edge_ref,
    phi_ref, mask_ref, energy_ref, part_ref, corr_ref, ham_ref,
):
    rows = rows_ref[...]
    for i in range(2):
        mask = sphere(rows, 1 + i)
        mask_ref[i] = mask
        phi_ref[i] = pieces_ref[:, PLANE * (1 + i) : PLANE * (2 + i)] * mask
    weights = in_plane(6, -1)
    for t in range(PLANE // TILE):
        lanes = slice(TILE * t, TILE * t + TILE)
        edge = edge_ref[:, :, lanes].astype(F32)
        mid = phi_ref[:, :, lanes].astype(F32)
        inner = plane_product(phi_ref[...].reshape(2 * ROWS, PLANE), weights, t).reshape(2, ROWS, TILE)
        outer = plane_product(edge_ref[...].reshape(2 * ROWS, PLANE), weights, t).reshape(2, ROWS, TILE)
        for i in range(2):
            value = 0.5 * (inner[i] - (edge[i] + mid[1 - i])) + pot_ref[1 + i : 2 + i, lanes] * mid[i]
            energy_ref[i, :, lanes] = value.astype(BF16) * mask_ref[i, :, lanes]
            plane = (CX - 1) * i
            part_ref[i, :, lanes] = 0.5 * (outer[i] - mid[i]) + pot_ref[plane : plane + 1, lanes] * edge[i]
    corr = jnp.zeros((ROWS, ROWS), F32)
    ham = jnp.zeros((ROWS, ROWS), F32)
    for i in range(2):
        corr = corr + rows_product(phi_ref[i], phi_ref[i]) + rows_product(edge_ref[i], edge_ref[i])
        ham = ham + rows_product(energy_ref[i], phi_ref[i])
    corr_ref[...] = corr
    ham_ref[...] = ham


def halo_rows(i):
    return slice(0, 2 * ORB) if i == 0 else slice(ORB, ROWS)


def rest_rows(i):
    return slice(2 * ORB, ROWS) if i == 0 else slice(0, ORB)


def bands_kernel(
    across_ref, mate_ref, part_ref, mask_ref, phi_ref, corr_ref, ham_ref,
    energy_ref, own_ref, rows_ref,
):
    volume = 1.0 / (4.0 * CX**3)
    ham = ham_ref[...]
    for i, side in enumerate(sides(mate_ref, across_ref)):
        tiles = unfold(side)
        rest = rest_rows(i)
        for t in range(PLANE // 128):
            lanes = slice(128 * t, 128 * t + 128)
            value = part_ref[i, halo_rows(i), lanes] - 0.5 * tiles[t % 4]
            energy_ref[i, halo_rows(i), lanes] = value.astype(BF16) * mask_ref[i, halo_rows(i), lanes]
            energy_ref[i, rest, lanes] = part_ref[i, rest, lanes].astype(BF16) * mask_ref[i, rest, lanes]
        ham = ham + rows_product(energy_ref[i], phi_ref[i])
    own_ref[:, :, ROWS:] = jnp.zeros((2, ROWS, TILE - ROWS), F32)
    own_ref[0, :, :ROWS] = ham * volume
    own_ref[1, :, :ROWS] = corr_ref[...] * volume
    tail = jnp.where(low_half(), own_ref[0, :, 128:256], swapped(own_ref[1, :, 128:256]))
    even = is_even()
    for i, value in enumerate((own_ref[0, :, 0:128], own_ref[1, :, 0:128], tail)):
        rows_ref[i] = jnp.where(even, value[ORB:], value[: 2 * ORB]).astype(BF16)


def low_half():
    return iota((1, 128), 1) < 64


def swapped(value):
    return pltpu.roll(value, 64, 1)


def mate_blocks(rows_ref, which):
    tail = rows_ref[2].astype(F32)
    if which == 1:
        tail = swapped(tail)
    return rows_ref[which].astype(F32), jnp.where(low_half(), tail, 0.0)


def shifted(c01, c2x):
    low = low_half()
    turned = swapped(c01)
    return jnp.where(low, 0.0, turned), jnp.where(low, turned, swapped(c2x))


def relay_kernel(own_ref, rows_ref, out_ref):
    even = is_even()
    heads = []
    for which in range(2):
        head, rest = shifted(own_ref[which, :, 0:128], own_ref[which, :, 128:256])
        c01, c2x = mate_blocks(rows_ref, which)
        c01 = jnp.where(even, c01[:ORB], c01[ORB:])
        c2x = jnp.where(even, c2x[:ORB], c2x[ORB:])
        own = slice(ORB, 2 * ORB)
        out_ref[2 * which] = (head[own] + jnp.where(even, c2x, c01)).astype(BF16)
        out_ref[2 * which + 1] = (rest[own] + jnp.where(even, c01, c2x)).astype(BF16)
        out_ref[5 + which] = jnp.where(even, rest[:ORB], rest[2 * ORB :]).astype(BF16)
        heads.append(jnp.where(even, head[:ORB], head[2 * ORB :]))
    out_ref[4] = jnp.where(low_half(), swapped(heads[1]), heads[0]).astype(BF16)


def shared_head(tile, which):
    tile = tile.astype(F32)
    if which == 1:
        tile = swapped(tile)
    return jnp.where(low_half(), 0.0, tile)


def put_gradient(theta, orbital_ref, energy_ref, mask_ref, out_ref):
    for i in range(2):
        for t in range(PLANE // TILE):
            lanes = slice(TILE * t, TILE * t + TILE)
            fix = jnp.dot(theta, orbital_ref[i, :, lanes], preferred_element_type=F32)
            value = energy_ref[i, :, lanes].astype(F32) - fix
            out_ref[i, :, lanes] = value.astype(BF16) * mask_ref[i, :, lanes]


def kept(pattern_ref, r, q):
    slab = lax.axis_index("sx")
    last = pattern_ref.shape[1] - 1
    values = []
    for col in (2 * q, 2 * q + 1):
        apart = abs(col - r - 2)
        if apart == 0:
            values.append(1.0)
        elif apart > 2:
            values.append(0.0)
        else:
            at = jnp.clip(slab - 3 + min(col, r + 2), 0, last)
            values.append(pattern_ref[apart - 1, at].astype(F32))
    return jnp.where(low_half(), values[0], values[1])


def split(value):
    high = value.astype(BF16)
    return high, (value - high.astype(F32)).astype(BF16)


def fine_product(a, b):
    return rows_product(a[0], b[0]) + (rows_product(a[0], b[1]) + rows_product(a[1], b[0]))


def theta_kernel(pattern_ref, own_ref, rows_ref, other_ref, ham_ref, inv_ref, theta_ref):
    even = is_even()
    low = low_half()
    zero = jnp.zeros((ORB, 128), F32)
    for which, band_ref in enumerate((ham_ref, inv_ref)):
        near, rest = shifted(*mate_blocks(rows_ref, which))
        ahead = other_ref[2 * which].astype(F32)
        beside = other_ref[2 * which + 1].astype(F32)
        head = shared_head(other_ref[4], which)
        tail = other_ref[5 + which].astype(F32)
        got_even = (
            (ahead, beside, zero, zero),
            (head, tail + near[:ORB], rest[:ORB], zero),
            (zero, near[ORB:], rest[ORB:], zero),
        )
        got_odd = (
            (near[:ORB], rest[:ORB], zero, zero),
            (near[ORB:], rest[ORB:] + head, tail, zero),
            (zero, jnp.where(low, 0.0, ahead), beside, jnp.where(low, ahead, 0.0)),
        )
        for r in range(3):
            for q in range(4):
                value = jnp.where(even, got_even[r][q], got_odd[r][q])
                if q in (1, 2):
                    value = value + own_ref[which, ORB * r : ORB * r + ORB, 128 * q - 128 : 128 * q]
                value = value * kept(pattern_ref, r, q)
                if which == 1:
                    on = iota((ORB, 128), 0) + (ORB * (r + 2) - 128 * q) == iota((ORB, 128), 1)
                    value = jnp.where(on, 2.0, 0.0) - value
                band_ref[ORB * r : ORB * r + ORB, 128 * q : 128 * q + 128] = value
    theta_ref[...] = fine_product(split(ham_ref[...]), split(inv_ref[...]))


def gradient_kernel(
    pattern_ref, relayed_ref, ham_ref, inv_ref, base_ref,
    edge_ref, edge_energy_ref, edge_mask_ref,
    edge_grad_ref, theta_ref, mate_ref, across_ref,
    more_ref,
):
    even = is_even()
    low = low_half()
    for which in range(2):
        front = swapped(shared_head(relayed_ref[0], which))
        turned = swapped(relayed_ref[1 + which].astype(F32))
        for q, value in enumerate((jnp.where(low, front, turned), jnp.where(low, turned, 0.0))):
            value = value * jnp.where(even, kept(pattern_ref, 2, 2 + q), kept(pattern_ref, 0, q))
            if which == 1:
                value = -value
            lanes = slice(128 * q, 128 * q + 128)
            more_ref[which, :ORB, lanes] = jnp.where(even, 0.0, value)
            more_ref[which, ORB : 2 * ORB, lanes] = jnp.zeros((ORB, 128), F32)
            more_ref[which, 2 * ORB :, lanes] = jnp.where(even, value, 0.0)
    ham = jnp.where(even, ham_ref[:, 256:512], ham_ref[:, 0:256]) + more_ref[0]
    inv = jnp.where(even, inv_ref[:, 256:512], inv_ref[:, 0:256])
    theta = base_ref[...] + fine_product(split(ham), split(more_ref[1]))
    theta = theta + fine_product(split(more_ref[0]), split(inv))
    theta = theta.astype(BF16)
    theta_ref[...] = theta
    put_gradient(theta, edge_ref, edge_energy_ref, edge_mask_ref, edge_grad_ref)
    put_messages(edge_grad_ref, mate_ref, across_ref)


def smooth_kernel(
    theta_ref, phi_ref, energy_ref, edge_ref, mask_ref, edge_mask_ref,
    out_ref, part_ref,
    grad_ref, done_ref, rest_ref, sems,
):
    put_gradient(theta_ref[...], phi_ref, energy_ref, mask_ref, grad_ref)
    weights = in_plane(8, 1)
    for t in range(PLANE // TILE):
        lanes = slice(TILE * t, TILE * t + TILE)
        edge = edge_ref[:, :, lanes].astype(F32)
        mid = grad_ref[:, :, lanes].astype(F32)
        inner = plane_product(grad_ref[...].reshape(2 * ROWS, PLANE), weights, t).reshape(2, ROWS, TILE)
        outer = plane_product(edge_ref[...].reshape(2 * ROWS, PLANE), weights, t).reshape(2, ROWS, TILE)
        for i in range(2):
            value = (inner[i] + (edge[i] + mid[1 - i])) * (1.0 / 32.0)
            done_ref[i, :, lanes] = value.astype(BF16) * mask_ref[i, :, lanes]
            part_ref[i, :, lanes] = outer[i] + mid[i]
        for i in range(2):
            rows = rest_rows(i)
            value = part_ref[i, rows, lanes] * (1.0 / 32.0)
            rest_ref[i, :, lanes] = value.astype(BF16) * edge_mask_ref[i, rows, lanes]
    copies = []
    for i in range(2):
        start = PLANE * (1 + i)
        copies.append(
            pltpu.make_async_copy(done_ref.at[i], out_ref.at[:, start : start + PLANE], sems.at[i])
        )
        start = PLANE * (CX - 1) * i
        copies.append(
            pltpu.make_async_copy(
                rest_ref.at[i], out_ref.at[rest_rows(i), start : start + PLANE], sems.at[2 + i]
            )
        )
    for copy in copies:
        copy.start()
    for copy in copies:
        copy.wait()


def finish_kernel(across_ref, mate_ref, part_ref, mask_ref, inner_ref, out_ref, done_ref, sems):
    copies = []
    for i, side in enumerate(sides(mate_ref, across_ref)):
        tiles = unfold(side)
        for half in range(2):
            rows = slice(ORB * (half + i), ORB * (half + i) + ORB)
            got = slice(ORB * half, ORB * half + ORB)
            for t in range(PLANE // 128):
                lanes = slice(128 * t, 128 * t + 128)
                value = (part_ref[i, rows, lanes] + tiles[t % 4][got]) * (1.0 / 32.0)
                done_ref[2 * i + half, :, lanes] = value.astype(BF16) * mask_ref[i, rows, lanes]
            start = PLANE * (CX - 1) * i
            copies.append(
                pltpu.make_async_copy(
                    done_ref.at[2 * i + half], out_ref.at[rows, start : start + PLANE], sems.at[2 * i + half]
                )
            )
            copies[-1].start()
    for copy in copies:
        copy.wait()


def shape(*dims, dtype=BF16):
    return jax.ShapeDtypeStruct(dims, dtype)


def cost(flops, moved):
    return pl.CostEstimate(flops=flops, bytes_accessed=moved, transcendentals=0)


PARAMS = pltpu.CompilerParams(vmem_limit_bytes=32 * 1024 * 1024)
WHOLE = pl.BlockSpec(memory_space=pltpu.VMEM)
FAR = pl.BlockSpec(memory_space=pltpu.HBM)


def far(value):
    return pltpu.with_memory_space_constraint(value, pltpu.HBM)


def per_device(pieces, potential, centers, pattern):
    count = lax.axis_size("sx")
    mates = [(i, i ^ 1) for i in range(count)]
    others = [(i, i + 1 if i % 2 else i - 1) for i in range(1, count - 1)]
    groups = lax.axis_size("grp")
    pairs = [[g * count + i, g * count + i + 1] for g in range(groups) for i in range(1, count - 1, 2)]
    ends = [g * count + end for g in range(groups) for end in (0, count - 1)]
    pairs += [[ends[i], ends[i + 2]] for i in range(len(ends)) if i % 4 < 2] if groups % 2 == 0 else [
        [ends[2 * i], ends[2 * i + 1]] for i in range(groups)
    ]
    slab = lax.axis_index("sx")

    def to_mate(value):
        return lax.ppermute(value, "sx", mates)

    def across(value):
        return lax.ppermute(value, "sx", others)

    def gathered(value):
        both = lax.all_gather(value, ("grp", "sx"), axis_index_groups=pairs)
        got = jnp.where(slab % 2 == 1, both[1], both[0])
        return jnp.where((slab == 0) | (slab == count - 1), jnp.zeros((), value.dtype), got)

    table = centers.T
    pair = shape(2, ROWS, PLANE)

    edge, edge_mask, rows, for_mate, for_other = pl.pallas_call(
        edges_kernel,
        out_shape=(pair, pair, shape(ROWS, 16), shape(2 * ORB, HALF), shape(2 * ORB, HALF)),
        in_specs=[FAR, FAR],
        out_specs=(WHOLE,) * 5,
        scratch_shapes=[
            pltpu.VMEM((4, 4 * ORB), jnp.int32),
            pltpu.VMEM((2, ROWS, PLANE), BF16),
            pltpu.SemaphoreType.DMA((3,)),
        ],
        compiler_params=PARAMS,
        cost_estimate=cost(10**8, 10**6),
        name="edges",
    )(far(table), far(pieces))
    other_side = across(for_other)
    mate_side = to_mate(for_mate)

    mid, mid_mask, mid_energy, part, corr, ham = pl.pallas_call(
        energy_kernel,
        out_shape=(
            pair, pair, pair, shape(2, ROWS, PLANE, dtype=F32),
            shape(ROWS, ROWS, dtype=F32), shape(ROWS, ROWS, dtype=F32),
        ),
        in_specs=[WHOLE] * 4,
        out_specs=(WHOLE,) * 6,
        compiler_params=PARAMS,
        cost_estimate=cost(4 * 10**9, 10**7),
        name="energy",
    )(rows, pieces, potential, edge)

    edge_energy, own, for_mate = pl.pallas_call(
        bands_kernel,
        out_shape=(pair, shape(2, ROWS, TILE, dtype=F32), shape(3, 2 * ORB, 128)),
        in_specs=[WHOLE] * 7,
        out_specs=(WHOLE,) * 3,
        compiler_params=PARAMS,
        cost_estimate=cost(10**9, 10**7),
        name="bands",
    )(other_side, mate_side, part, edge_mask, edge, corr, ham)
    mate_rows = to_mate(for_mate)
    for_other = pl.pallas_call(
        relay_kernel,
        out_shape=shape(7, ORB, 128),
        in_specs=[WHOLE] * 2,
        out_specs=WHOLE,
        compiler_params=PARAMS,
        cost_estimate=cost(10**6, 10**6),
        name="relay",
    )(own, mate_rows)
    other_rows = gathered(for_other)
    relayed = to_mate(other_rows[4:])

    patterns = pattern.T
    scalars = pl.BlockSpec(memory_space=pltpu.SMEM)
    band = shape(ROWS, 8 * ORB, dtype=F32)
    ham_band, inv_band, base = pl.pallas_call(
        theta_kernel,
        out_shape=(band, band, shape(ROWS, ROWS, dtype=F32)),
        in_specs=[scalars] + [WHOLE] * 3,
        out_specs=(WHOLE,) * 3,
        compiler_params=PARAMS,
        cost_estimate=cost(10**9, 4 * 10**6),
        name="theta",
    )(patterns, own, mate_rows, other_rows)
    edge_grad, theta, for_mate, for_other = pl.pallas_call(
        gradient_kernel,
        out_shape=(pair, shape(ROWS, ROWS), shape(2 * ORB, HALF), shape(2 * ORB, HALF)),
        in_specs=[scalars] + [WHOLE] * 7,
        out_specs=(WHOLE,) * 4,
        scratch_shapes=[pltpu.VMEM((2, ROWS, TILE), F32)],
        compiler_params=PARAMS,
        cost_estimate=cost(10**9, 10**7),
        name="gradient",
    )(patterns, relayed, ham_band, inv_band, base, edge, edge_energy, edge_mask)
    other_side = across(for_other)
    mate_side = to_mate(for_mate)

    inner, part = pl.pallas_call(
        smooth_kernel,
        out_shape=(pltpu.HBM((ROWS, CX * PLANE), BF16), shape(2, ROWS, PLANE, dtype=F32)),
        in_specs=[WHOLE] * 6,
        out_specs=(FAR, WHOLE),
        scratch_shapes=[
            pltpu.VMEM((2, ROWS, PLANE), BF16),
            pltpu.VMEM((2, ROWS, PLANE), BF16),
            pltpu.VMEM((2, ORB, PLANE), BF16),
            pltpu.SemaphoreType.DMA((4,)),
        ],
        compiler_params=PARAMS,
        cost_estimate=cost(2 * 10**9, 10**7),
        name="smooth",
    )(theta, mid, mid_energy, edge_grad, mid_mask, edge_mask)

    return pl.pallas_call(
        finish_kernel,
        out_shape=pltpu.HBM((ROWS, CX * PLANE), BF16),
        in_specs=[WHOLE] * 4 + [FAR],
        out_specs=FAR,
        scratch_shapes=[pltpu.VMEM((4, ORB, PLANE), BF16), pltpu.SemaphoreType.DMA((4,))],
        input_output_aliases={4: 0},
        compiler_params=PARAMS,
        cost_estimate=cost(10**7, 10**7),
        name="finish",
    )(other_side, mate_side, part, edge_mask, inner)


def solution(mesh):
    return jax.shard_map(
        per_device,
        mesh=mesh,
        in_specs=(P(("grp", "sx"), None), P(("grp", "sx"), None), P("grp", None), P("grp", None)),
        out_specs=P(("grp", "sx"), None),
        check_vma=False,
    )
```

```python
import functools

import jax
import jax.numpy as jnp
from jax import lax
from jax.experimental import pallas as pl
from jax.experimental.pallas import tpu as pltpu
from jax.sharding import PartitionSpec as P

ORB = 64
CX = 4
NY = 32
NZ = 32
ROWS = 3 * ORB
PLANE = NY * NZ
TILE = 256
F32 = jnp.float32
BF16 = jnp.bfloat16


def iota(shape, dim):
    return lax.broadcasted_iota(jnp.int32, shape, dim)


def window_start(width):
    slab = lax.axis_index("sx")
    first = jnp.clip(slab * ORB - ORB, 0, width - 4 * ORB) // 128 * 128
    return pl.multiple_of(first, 128)


def row_features(window_ref, first):
    slab = lax.axis_index("sx")
    count = lax.axis_size("sx")
    window = window_ref[...]
    shift = slab * ORB - ORB - first
    window = pltpu.roll(jnp.concatenate([window, window], axis=0), lax.rem(4 * ORB - shift, 4 * ORB), 1)
    lane = iota((1, 4 * ORB), 1)
    block = slab - 1 + lane // ORB
    valid = (block >= 0) & (block < count)
    cx = window[0:1] - slab * CX
    cy = window[1:2]
    cz = window[2:3]
    r = window[3:4]
    const = cx * cx + cy * cy + cz * cz - r * r
    const = jnp.where(valid, const, 65535)
    cx = jnp.where(valid, cx, 0)
    cy = jnp.where(valid, cy, 0)
    cz = jnp.where(valid, cz, 0)
    k = iota((16, 4 * ORB), 0)
    feats = jnp.where(k == 0, 1, 0)
    feats = jnp.where(k == 1, 256, feats)
    feats = jnp.where(k == 2, cy, feats)
    feats = jnp.where(k == 3, cz, feats)
    feats = jnp.where(k == 4, const & 255, feats)
    feats = jnp.where(k == 5, const >> 8, feats)
    feats = jnp.where(k == 6, cx, feats)
    return jnp.transpose(feats.astype(F32))[:ROWS].astype(BF16)


def cell_features(plane):
    k = iota((16, PLANE), 0)
    cell = iota((16, PLANE), 1)
    y = cell >> 5
    z = cell & 31
    sq = y * y + z * z + plane * plane
    feats = jnp.where(k == 0, sq & 255, 0)
    feats = jnp.where(k == 1, sq >> 8, feats)
    feats = jnp.where(k == 2, -2 * y, feats)
    feats = jnp.where(k == 3, -2 * z, feats)
    feats = jnp.where(k == 4, 1, feats)
    feats = jnp.where(k == 5, 256, feats)
    feats = jnp.where(k == 6, -2 * plane, feats)
    return feats.astype(F32).astype(BF16)


def sphere(rows, plane):
    reach = jnp.dot(rows, cell_features(plane), preferred_element_type=F32)
    return jnp.where(reach <= 0.0, 1.0, 0.0).astype(BF16)


def in_plane(center, beside):
    k = iota((2 * TILE, TILE), 0) - 128
    n = iota((2 * TILE, TILE), 1)
    diff = k - n
    near_y = (diff == NZ) | (diff == -NZ)
    near_z = ((diff == 1) | (diff == -1)) & ((k >> 5) == (n >> 5))
    w = jnp.where(near_y | near_z, float(beside), 0.0)
    return jnp.where(diff == 0, float(center), w).astype(BF16)


def plane_product(values, weights, t):
    low = max(0, TILE * t - 128)
    high = min(PLANE, TILE * t + TILE + 128)
    shift = 128 - TILE * t
    return jnp.dot(
        values[:, low:high], weights[low + shift : high + shift], preferred_element_type=F32
    )


def fold(values):
    tiles = [values[:, 128 * t : 128 * t + 128] for t in range(PLANE // 128)]
    a, b, c = (sum(tiles[t::3][1:], tiles[t]) for t in range(3))
    low_z = (iota((1, 128), 1) & 31) < 16
    top, bottom = c[:ORB], c[ORB:]
    return (
        jnp.where(low_z, a + pltpu.roll(a, 112, 1), b + pltpu.roll(b, 16, 1)),
        jnp.where(low_z, top + pltpu.roll(top, 112, 1), bottom + pltpu.roll(bottom, 16, 1)),
    )


def unfold(packed):
    low_z = (iota((1, 128), 1) & 31) < 16
    p, q = packed[: 2 * ORB], packed[2 * ORB :]
    return (
        jnp.where(low_z, p, pltpu.roll(p, 16, 1)),
        jnp.where(low_z, pltpu.roll(p, 112, 1), p),
        jnp.concatenate(
            [jnp.where(low_z, q, pltpu.roll(q, 16, 1)), jnp.where(low_z, pltpu.roll(q, 112, 1), q)], axis=0
        ),
    )


def is_even():
    return lax.rem(lax.axis_index("sx"), 2) == 0


def put_messages(planes, mate_ref, across_ref):
    down = fold(planes[0, : 2 * ORB].astype(F32))
    up = fold(planes[1, ORB:].astype(F32))
    even = is_even()
    for i, rows in enumerate((slice(0, 2 * ORB), slice(2 * ORB, ROWS))):
        mate_ref[rows] = jnp.where(even, up[i], down[i]).astype(BF16)
        across_ref[rows] = jnp.where(even, down[i], up[i]).astype(BF16)


def sides(mate_ref, across_ref):
    mate = mate_ref[...].astype(F32)
    across = across_ref[...].astype(F32)
    even = is_even()
    return (jnp.where(even, across, mate), jnp.where(even, mate, across))


def edges_kernel(
    table_ref, pieces_ref,
    phi_ref, mask_ref, rows_ref, mate_ref, across_ref,
    window_ref, raw_ref, sems,
):
    first = window_start(table_ref.shape[1])
    table_copy = pltpu.make_async_copy(table_ref.at[:, pl.ds(first, 4 * ORB)], window_ref, sems.at[2])
    table_copy.start()
    copies = []
    for i in range(2):
        start = (CX - 1) * PLANE * i
        copies.append(
            pltpu.make_async_copy(pieces_ref.at[:, start : start + PLANE], raw_ref.at[i], sems.at[i])
        )
        copies[i].start()
    table_copy.wait()
    rows = row_features(window_ref, first)
    rows_ref[...] = rows
    for i in range(2):
        mask_ref[i] = sphere(rows, (CX - 1) * i)
    for i in range(2):
        copies[i].wait()
        phi_ref[i] = raw_ref[i] * mask_ref[i]
    put_messages(phi_ref, mate_ref, across_ref)


def rows_product(a, b):
    return lax.dot_general(a, b, (((1,), (1,)), ((), ())), preferred_element_type=F32)


def energy_kernel(
    rows_ref, pieces_ref, pot_ref, edge_ref,
    edge_mask_ref,
    phi_ref, mask_ref, energy_ref, part_ref, edge_energy_ref, corr_ref, ham_ref,
):
    rows = rows_ref[...]
    for i in range(2):
        mask = sphere(rows, 1 + i)
        mask_ref[i] = mask
        phi_ref[i] = pieces_ref[:, PLANE * (1 + i) : PLANE * (2 + i)] * mask
    weights = in_plane(6, -1)
    for t in range(PLANE // TILE):
        lanes = slice(TILE * t, TILE * t + TILE)
        edge = edge_ref[:, :, lanes].astype(F32)
        mid = phi_ref[:, :, lanes].astype(F32)
        inner = plane_product(phi_ref[...].reshape(2 * ROWS, PLANE), weights, t).reshape(2, ROWS, TILE)
        outer = plane_product(edge_ref[...].reshape(2 * ROWS, PLANE), weights, t).reshape(2, ROWS, TILE)
        for i in range(2):
            value = 0.5 * (inner[i] - (edge[i] + mid[1 - i])) + pot_ref[1 + i : 2 + i, lanes] * mid[i]
            energy_ref[i, :, lanes] = value.astype(BF16) * mask_ref[i, :, lanes]
            plane = (CX - 1) * i
            value = 0.5 * (outer[i] - mid[i]) + pot_ref[plane : plane + 1, lanes] * edge[i]
            part_ref[i, :, lanes] = value
            rest = rest_rows(i)
            edge_energy_ref[i, rest, lanes] = value[rest].astype(BF16) * edge_mask_ref[i, rest, lanes]
    corr = jnp.zeros((ROWS, ROWS), F32)
    ham = jnp.zeros((ROWS, ROWS), F32)
    for i in range(2):
        corr = corr + rows_product(phi_ref[i], phi_ref[i]) + rows_product(edge_ref[i], edge_ref[i])
        ham = ham + rows_product(energy_ref[i], phi_ref[i])
    corr_ref[...] = corr
    ham_ref[...] = ham
    for i in range(2):
        rest = rest_rows(i)
        ham_ref[rest] += rows_product(edge_energy_ref[i, rest], edge_ref[i])


def halo_rows(i):
    return slice(0, 2 * ORB) if i == 0 else slice(ORB, ROWS)


def rest_rows(i):
    return slice(2 * ORB, ROWS) if i == 0 else slice(0, ORB)


def bands_kernel(
    across_ref, mate_ref, part_ref, mask_ref, phi_ref, corr_ref, ham_ref, rest_ref,
    energy_ref, own_ref, rows_ref,
):
    volume = 1.0 / (4.0 * CX**3)
    gram = []
    for i, side in enumerate(sides(mate_ref, across_ref)):
        tiles = unfold(side)
        for t in range(PLANE // 128):
            lanes = slice(128 * t, 128 * t + 128)
            value = part_ref[i, halo_rows(i), lanes] - 0.5 * tiles[t % 3]
            energy_ref[i, halo_rows(i), lanes] = value.astype(BF16) * mask_ref[i, halo_rows(i), lanes]
        gram.append(rows_product(energy_ref[i, halo_rows(i)], phi_ref[i]))
    own_ref[:, :, ROWS:] = jnp.zeros((2, ROWS, TILE - ROWS), F32)
    own_ref[0, :ORB, :ROWS] = (ham_ref[:ORB] + gram[0][:ORB]) * volume
    own_ref[0, ORB : 2 * ORB, :ROWS] = (ham_ref[ORB : 2 * ORB] + gram[0][ORB:] + gram[1][:ORB]) * volume
    own_ref[0, 2 * ORB :, :ROWS] = (ham_ref[2 * ORB :] + gram[1][ORB:]) * volume
    own_ref[1, :, :ROWS] = corr_ref[...] * volume
    tail = jnp.where(low_half(), own_ref[0, :, 128:256], swapped(own_ref[1, :, 128:256]))
    even = is_even()
    for i, value in enumerate((own_ref[0, :, 0:128], own_ref[1, :, 0:128], tail)):
        rows_ref[i] = jnp.where(even, value[ORB:], value[: 2 * ORB]).astype(BF16)


def low_half():
    return iota((1, 128), 1) < 64


def swapped(value):
    return pltpu.roll(value, 64, 1)


def mate_blocks(rows_ref, which):
    tail = rows_ref[2].astype(F32)
    if which == 1:
        tail = swapped(tail)
    return rows_ref[which].astype(F32), jnp.where(low_half(), tail, 0.0)


def shifted(c01, c2x):
    low = low_half()
    turned = swapped(c01)
    return jnp.where(low, 0.0, turned), jnp.where(low, turned, swapped(c2x))


def relay_kernel(own_ref, rows_ref, out_ref):
    even = is_even()
    heads = []
    for which in range(2):
        head, rest = shifted(own_ref[which, :, 0:128], own_ref[which, :, 128:256])
        c01, c2x = mate_blocks(rows_ref, which)
        c01 = jnp.where(even, c01[:ORB], c01[ORB:])
        c2x = jnp.where(even, c2x[:ORB], c2x[ORB:])
        own = slice(ORB, 2 * ORB)
        out_ref[2 * which] = (head[own] + jnp.where(even, c2x, c01)).astype(BF16)
        out_ref[2 * which + 1] = (rest[own] + jnp.where(even, c01, c2x)).astype(BF16)
        out_ref[5 + which] = jnp.where(even, rest[:ORB], rest[2 * ORB :]).astype(BF16)
        heads.append(jnp.where(even, head[:ORB], head[2 * ORB :]))
    out_ref[4] = jnp.where(low_half(), swapped(heads[1]), heads[0]).astype(BF16)


def shared_head(tile, which):
    tile = tile.astype(F32)
    if which == 1:
        tile = swapped(tile)
    return jnp.where(low_half(), 0.0, tile)


def pick_kernel(both_ref, other_ref, forward_ref):
    slab = lax.axis_index("sx")
    even = is_even()
    end = (slab == 0) | (slab == lax.axis_size("sx") - 1)
    for i in range(7):
        value = jnp.where(even, both_ref[0, i].astype(F32), both_ref[1, i].astype(F32))
        value = jnp.where(end, 0.0, value).astype(BF16)
        other_ref[i] = value
        if i >= 4:
            forward_ref[i - 4] = value


def put_gradient(theta, orbital_ref, energy_ref, mask_ref, out_ref):
    for i in range(2):
        for t in range(PLANE // TILE):
            lanes = slice(TILE * t, TILE * t + TILE)
            fix = jnp.dot(theta, orbital_ref[i, :, lanes], preferred_element_type=F32)
            value = energy_ref[i, :, lanes].astype(F32) - fix
            out_ref[i, :, lanes] = value.astype(BF16) * mask_ref[i, :, lanes]


def kept(pattern_ref, r, q):
    slab = lax.axis_index("sx")
    last = pattern_ref.shape[1] - 1
    values = []
    for col in (2 * q, 2 * q + 1):
        apart = abs(col - r - 2)
        if apart == 0:
            values.append(1.0)
        elif apart > 2:
            values.append(0.0)
        else:
            at = jnp.clip(slab - 3 + min(col, r + 2), 0, last)
            values.append(pattern_ref[apart - 1, at].astype(F32))
    return jnp.where(low_half(), values[0], values[1])


def split(value):
    high = value.astype(BF16)
    return high, (value - high.astype(F32)).astype(BF16)


def fine_product(a, b):
    return rows_product(a[0], b[0]) + (rows_product(a[0], b[1]) + rows_product(a[1], b[0]))


def theta_kernel(pattern_ref, own_ref, rows_ref, other_ref, ham_ref, inv_ref, theta_ref):
    even = is_even()
    low = low_half()
    zero = jnp.zeros((ORB, 128), F32)
    for which, band_ref in enumerate((ham_ref, inv_ref)):
        near, rest = shifted(*mate_blocks(rows_ref, which))
        ahead = other_ref[2 * which].astype(F32)
        beside = other_ref[2 * which + 1].astype(F32)
        head = shared_head(other_ref[4], which)
        tail = other_ref[5 + which].astype(F32)
        got_even = (
            (ahead, beside, zero, zero),
            (head, tail + near[:ORB], rest[:ORB], zero),
            (zero, near[ORB:], rest[ORB:], zero),
        )
        got_odd = (
            (near[:ORB], rest[:ORB], zero, zero),
            (near[ORB:], rest[ORB:] + head, tail, zero),
            (zero, jnp.where(low, 0.0, ahead), beside, jnp.where(low, ahead, 0.0)),
        )
        for r in range(3):
            for q in range(4):
                value = jnp.where(even, got_even[r][q], got_odd[r][q])
                if q in (1, 2):
                    value = value + own_ref[which, ORB * r : ORB * r + ORB, 128 * q - 128 : 128 * q]
                value = value * kept(pattern_ref, r, q)
                if which == 1:
                    on = iota((ORB, 128), 0) + (ORB * (r + 2) - 128 * q) == iota((ORB, 128), 1)
                    value = jnp.where(on, 2.0, 0.0) - value
                band_ref[ORB * r : ORB * r + ORB, 128 * q : 128 * q + 128] = value
    theta_ref[...] = fine_product(split(ham_ref[...]), split(inv_ref[...]))


def gradient_kernel(
    pattern_ref, relayed_ref, ham_ref, inv_ref, base_ref,
    edge_ref, edge_energy_ref, edge_mask_ref,
    edge_grad_ref, theta_ref, mate_ref, across_ref,
    window_ref, total_ref,
):
    even = is_even()
    low = low_half()
    more = []
    for which in range(2):
        front = swapped(shared_head(relayed_ref[0], which))
        turned = swapped(relayed_ref[1 + which].astype(F32))
        tiles = []
        for q, value in enumerate((jnp.where(low, front, turned), jnp.where(low, turned, 0.0))):
            tiles.append(value * jnp.where(even, kept(pattern_ref, 2, 2 + q), kept(pattern_ref, 0, q)))
        more.append(jnp.concatenate(tiles, axis=1))
    first, third = slice(0, ORB), slice(2 * ORB, ROWS)
    window_ref[...] = jnp.where(even, ham_ref[:, 256:512], ham_ref[:, 0:256])
    window_ref[first] += jnp.where(even, 0.0, more[0])
    window_ref[third] += jnp.where(even, more[0], 0.0)
    ham = jnp.concatenate(split(window_ref[...]), axis=1)
    inv = jnp.concatenate(split(jnp.where(even, inv_ref[:, 256:512], inv_ref[:, 0:256])), axis=1)
    more = [jnp.concatenate([value.astype(BF16)] * 2, axis=1) for value in more]
    column = rows_product(ham, more[1])
    row = rows_product(more[0], inv)
    total_ref[...] = base_ref[...]
    total_ref[first] += jnp.where(even, 0.0, row)
    total_ref[third] += jnp.where(even, row, 0.0)
    total_ref[:, first] -= jnp.where(even, 0.0, column)
    total_ref[:, third] -= jnp.where(even, column, 0.0)
    theta = total_ref[...].astype(BF16)
    theta_ref[...] = theta
    put_gradient(theta, edge_ref, edge_energy_ref, edge_mask_ref, edge_grad_ref)
    put_messages(edge_grad_ref, mate_ref, across_ref)


def smooth_kernel(
    theta_ref, phi_ref, energy_ref, edge_ref, mask_ref, edge_mask_ref,
    out_ref, part_ref,
    grad_ref, done_ref, rest_ref, sems,
):
    put_gradient(theta_ref[...], phi_ref, energy_ref, mask_ref, grad_ref)
    weights = in_plane(8, 1)
    for t in range(PLANE // TILE):
        lanes = slice(TILE * t, TILE * t + TILE)
        edge = edge_ref[:, :, lanes].astype(F32)
        mid = grad_ref[:, :, lanes].astype(F32)
        inner = plane_product(grad_ref[...].reshape(2 * ROWS, PLANE), weights, t).reshape(2, ROWS, TILE)
        outer = plane_product(edge_ref[...].reshape(2 * ROWS, PLANE), weights, t).reshape(2, ROWS, TILE)
        for i in range(2):
            value = (inner[i] + (edge[i] + mid[1 - i])) * (1.0 / 32.0)
            done_ref[i, :, lanes] = value.astype(BF16) * mask_ref[i, :, lanes]
            part_ref[i, :, lanes] = outer[i] + mid[i]
        for i in range(2):
            rows = rest_rows(i)
            value = part_ref[i, rows, lanes] * (1.0 / 32.0)
            rest_ref[i, :, lanes] = value.astype(BF16) * edge_mask_ref[i, rows, lanes]
    copies = []
    for i in range(2):
        start = PLANE * (1 + i)
        copies.append(
            pltpu.make_async_copy(done_ref.at[i], out_ref.at[:, start : start + PLANE], sems.at[i])
        )
        start = PLANE * (CX - 1) * i
        copies.append(
            pltpu.make_async_copy(
                rest_ref.at[i], out_ref.at[rest_rows(i), start : start + PLANE], sems.at[2 + i]
            )
        )
    for copy in copies:
        copy.start()
    for copy in copies:
        copy.wait()


def finish_kernel(across_ref, mate_ref, part_ref, mask_ref, inner_ref, out_ref, done_ref, sems):
    copies = []
    for i, side in enumerate(sides(mate_ref, across_ref)):
        tiles = unfold(side)
        for half in range(2):
            rows = slice(ORB * (half + i), ORB * (half + i) + ORB)
            got = slice(ORB * half, ORB * half + ORB)
            for t in range(PLANE // 128):
                lanes = slice(128 * t, 128 * t + 128)
                value = (part_ref[i, rows, lanes] + tiles[t % 3][got]) * (1.0 / 32.0)
                done_ref[2 * i + half, :, lanes] = value.astype(BF16) * mask_ref[i, rows, lanes]
            start = PLANE * (CX - 1) * i
            copies.append(
                pltpu.make_async_copy(
                    done_ref.at[2 * i + half], out_ref.at[rows, start : start + PLANE], sems.at[2 * i + half]
                )
            )
            copies[-1].start()
    for copy in copies:
        copy.wait()


def shape(*dims, dtype=BF16):
    return jax.ShapeDtypeStruct(dims, dtype)


def cost(flops, moved):
    return pl.CostEstimate(flops=flops, bytes_accessed=moved, transcendentals=0)


PARAMS = pltpu.CompilerParams(vmem_limit_bytes=32 * 1024 * 1024)
WHOLE = pl.BlockSpec(memory_space=pltpu.VMEM)
FAR = pl.BlockSpec(memory_space=pltpu.HBM)


def far(value):
    return pltpu.with_memory_space_constraint(value, pltpu.HBM)


def per_device(pieces, potential, centers, pattern):
    count = lax.axis_size("sx")
    mates = [(i, i ^ 1) for i in range(count)]
    others = [(i, i + 1 if i % 2 else i - 1) for i in range(1, count - 1)]
    groups = lax.axis_size("grp")
    pairs = [[g * count + i, g * count + i + 1] for g in range(groups) for i in range(1, count - 1, 2)]
    ends = [g * count + end for g in range(groups) for end in (0, count - 1)]
    pairs += [[ends[i], ends[i + 2]] for i in range(len(ends)) if i % 4 < 2] if groups % 2 == 0 else [
        [ends[2 * i], ends[2 * i + 1]] for i in range(groups)
    ]

    def to_mate(value):
        return lax.ppermute(value, "sx", mates)

    def across(value):
        return lax.ppermute(value, "sx", others)

    def gathered(value):
        return lax.all_gather(value, ("grp", "sx"), axis_index_groups=pairs)

    table = centers.T
    pair = shape(2, ROWS, PLANE)

    edge, edge_mask, rows, for_mate, for_other = pl.pallas_call(
        edges_kernel,
        out_shape=(pair, pair, shape(ROWS, 16), shape(ROWS, 128), shape(ROWS, 128)),
        in_specs=[FAR, FAR],
        out_specs=(WHOLE,) * 5,
        scratch_shapes=[
            pltpu.VMEM((4, 4 * ORB), jnp.int32),
            pltpu.VMEM((2, ROWS, PLANE), BF16),
            pltpu.SemaphoreType.DMA((3,)),
        ],
        compiler_params=PARAMS,
        cost_estimate=cost(10**8, 10**6),
        name="edges",
    )(far(table), far(pieces))
    other_side = across(for_other)
    mate_side = to_mate(for_mate)

    mid, mid_mask, mid_energy, part, rest_energy, corr, ham = pl.pallas_call(
        energy_kernel,
        out_shape=(
            pair, pair, pair, shape(2, ROWS, PLANE, dtype=F32), pair,
            shape(ROWS, ROWS, dtype=F32), shape(ROWS, ROWS, dtype=F32),
        ),
        in_specs=[WHOLE] * 5,
        out_specs=(WHOLE,) * 7,
        compiler_params=PARAMS,
        cost_estimate=cost(4 * 10**9, 10**7),
        name="energy",
    )(rows, pieces, potential, edge, edge_mask)

    edge_energy, own, for_mate = pl.pallas_call(
        bands_kernel,
        out_shape=(pair, shape(2, ROWS, TILE, dtype=F32), shape(3, 2 * ORB, 128)),
        in_specs=[WHOLE] * 8,
        out_specs=(WHOLE,) * 3,
        input_output_aliases={7: 0},
        compiler_params=PARAMS,
        cost_estimate=cost(10**9, 10**7),
        name="bands",
    )(other_side, mate_side, part, edge_mask, edge, corr, ham, rest_energy)
    mate_rows = to_mate(for_mate)
    for_other = pl.pallas_call(
        relay_kernel,
        out_shape=shape(7, ORB, 128),
        in_specs=[WHOLE] * 2,
        out_specs=WHOLE,
        compiler_params=PARAMS,
        cost_estimate=cost(10**6, 10**6),
        name="relay",
    )(own, mate_rows)
    other_rows, forward = pl.pallas_call(
        pick_kernel,
        out_shape=(shape(7, ORB, 128), shape(3, ORB, 128)),
        in_specs=[WHOLE],
        out_specs=(WHOLE,) * 2,
        compiler_params=PARAMS,
        cost_estimate=cost(10**6, 10**6),
        name="pick",
    )(gathered(for_other))
    relayed = to_mate(forward)

    patterns = pattern.T
    scalars = pl.BlockSpec(memory_space=pltpu.SMEM)
    band = shape(ROWS, 8 * ORB, dtype=F32)
    ham_band, inv_band, base = pl.pallas_call(
        theta_kernel,
        out_shape=(band, band, shape(ROWS, ROWS, dtype=F32)),
        in_specs=[scalars] + [WHOLE] * 3,
        out_specs=(WHOLE,) * 3,
        compiler_params=PARAMS,
        cost_estimate=cost(10**9, 4 * 10**6),
        name="theta",
    )(patterns, own, mate_rows, other_rows)
    edge_grad, theta, for_mate, for_other = pl.pallas_call(
        gradient_kernel,
        out_shape=(pair, shape(ROWS, ROWS), shape(ROWS, 128), shape(ROWS, 128)),
        in_specs=[scalars] + [WHOLE] * 7,
        out_specs=(WHOLE,) * 4,
        scratch_shapes=[pltpu.VMEM((ROWS, TILE), F32), pltpu.VMEM((ROWS, ROWS), F32)],
        compiler_params=PARAMS,
        cost_estimate=cost(10**9, 10**7),
        name="gradient",
    )(patterns, relayed, ham_band, inv_band, base, edge, edge_energy, edge_mask)
    other_side = across(for_other)
    mate_side = to_mate(for_mate)

    inner, part = pl.pallas_call(
        smooth_kernel,
        out_shape=(pltpu.HBM((ROWS, CX * PLANE), BF16), shape(2, ROWS, PLANE, dtype=F32)),
        in_specs=[WHOLE] * 6,
        out_specs=(FAR, WHOLE),
        scratch_shapes=[
            pltpu.VMEM((2, ROWS, PLANE), BF16),
            pltpu.VMEM((2, ROWS, PLANE), BF16),
            pltpu.VMEM((2, ORB, PLANE), BF16),
            pltpu.SemaphoreType.DMA((4,)),
        ],
        compiler_params=PARAMS,
        cost_estimate=cost(2 * 10**9, 10**7),
        name="smooth",
    )(theta, mid, mid_energy, edge_grad, mid_mask, edge_mask)

    return pl.pallas_call(
        finish_kernel,
        out_shape=pltpu.HBM((ROWS, CX * PLANE), BF16),
        in_specs=[WHOLE] * 4 + [FAR],
        out_specs=FAR,
        scratch_shapes=[pltpu.VMEM((4, ORB, PLANE), BF16), pltpu.SemaphoreType.DMA((4,))],
        input_output_aliases={4: 0},
        compiler_params=PARAMS,
        cost_estimate=cost(10**7, 10**7),
        name="finish",
    )(other_side, mate_side, part, edge_mask, inner)


def solution(mesh):
    return jax.shard_map(
        per_device,
        mesh=mesh,
        in_specs=(P(("grp", "sx"), None), P(("grp", "sx"), None), P("grp", None), P("grp", None)),
        out_specs=P(("grp", "sx"), None),
        check_vma=False,
    )
```

```python
import functools

import jax
import jax.numpy as jnp
from jax import lax
from jax.experimental import pallas as pl
from jax.experimental.pallas import tpu as pltpu
from jax.sharding import PartitionSpec as P

ORB = 64
CX = 4
NY = 32
NZ = 32
ROWS = 3 * ORB
PLANE = NY * NZ
TILE = 256
F32 = jnp.float32
BF16 = jnp.bfloat16


def iota(shape, dim):
    return lax.broadcasted_iota(jnp.int32, shape, dim)


def window_start(width):
    slab = lax.axis_index("sx")
    first = jnp.clip(slab * ORB - ORB, 0, width - 4 * ORB) // 128 * 128
    return pl.multiple_of(first, 128)


def row_features(window_ref, first):
    slab = lax.axis_index("sx")
    count = lax.axis_size("sx")
    window = window_ref[...]
    shift = slab * ORB - ORB - first
    window = pltpu.roll(jnp.concatenate([window, window], axis=0), lax.rem(4 * ORB - shift, 4 * ORB), 1)
    lane = iota((1, 4 * ORB), 1)
    block = slab - 1 + lane // ORB
    valid = (block >= 0) & (block < count)
    cx = window[0:1] - slab * CX
    cy = window[1:2]
    cz = window[2:3]
    r = window[3:4]
    const = cx * cx + cy * cy + cz * cz - r * r
    const = jnp.where(valid, const, 65535)
    cx = jnp.where(valid, cx, 0)
    cy = jnp.where(valid, cy, 0)
    cz = jnp.where(valid, cz, 0)
    k = iota((16, 4 * ORB), 0)
    feats = jnp.where(k == 0, 1, 0)
    feats = jnp.where(k == 1, 256, feats)
    feats = jnp.where(k == 2, cy, feats)
    feats = jnp.where(k == 3, cz, feats)
    feats = jnp.where(k == 4, const & 255, feats)
    feats = jnp.where(k == 5, const >> 8, feats)
    feats = jnp.where(k == 6, cx, feats)
    return jnp.transpose(feats.astype(F32))[:ROWS].astype(BF16)


def cell_features():
    k = iota((16, PLANE), 0)
    cell = iota((16, PLANE), 1)
    y = cell >> 5
    z = cell & 31
    sq = y * y + z * z
    feats = jnp.where(k == 0, sq & 255, 0)
    feats = jnp.where(k == 1, sq >> 8, feats)
    feats = jnp.where(k == 2, -2 * y, feats)
    feats = jnp.where(k == 3, -2 * z, feats)
    feats = jnp.where(k == 4, 1, feats)
    feats = jnp.where(k == 5, 256, feats)
    return feats.astype(F32).astype(BF16)


def sphere(reach, rows, plane):
    bound = rows[:, 6:7].astype(F32) * (2.0 * plane) - float(plane * plane)
    return jnp.where(reach <= bound, 1.0, 0.0).astype(BF16)


def in_plane(center, beside):
    k = iota((TILE, TILE), 0)
    n = iota((TILE, TILE), 1)
    diff = k - n
    near_y = (diff == NZ) | (diff == -NZ)
    near_z = ((diff == 1) | (diff == -1)) & ((k >> 5) == (n >> 5))
    w = jnp.where(near_y | near_z, float(beside), 0.0)
    return jnp.where(diff == 0, float(center), w).astype(BF16)


def plane_product(ref, weights, beside, t):
    start = TILE * t
    values = ref[:, :, start : start + TILE].reshape(2 * ROWS, TILE)
    out = jnp.dot(values, weights, preferred_element_type=F32).reshape(2, ROWS, TILE)
    lane = iota((1, 1, 128), 2)
    first, last = out[:, :, :128], out[:, :, 128:]
    if t > 0:
        turned = pltpu.roll(ref[:, :, start - 128 : start].astype(F32), NZ, 2)
        first = first + jnp.where(lane < NZ, turned * beside, 0.0)
    if start + TILE < PLANE:
        turned = pltpu.roll(ref[:, :, start + TILE : start + TILE + 128].astype(F32), 128 - NZ, 2)
        last = last + jnp.where(lane >= 128 - NZ, turned * beside, 0.0)
    return jnp.concatenate([first, last], axis=2)


def fold(values):
    tiles = [values[:, 128 * t : 128 * t + 128] for t in range(PLANE // 128)]
    a, b, c = (sum(tiles[t::3][1:], tiles[t]) for t in range(3))
    low_z = (iota((1, 128), 1) & 31) < 16
    top, bottom = c[:ORB], c[ORB:]
    return (
        jnp.where(low_z, a + pltpu.roll(a, 112, 1), b + pltpu.roll(b, 16, 1)),
        jnp.where(low_z, top + pltpu.roll(top, 112, 1), bottom + pltpu.roll(bottom, 16, 1)),
    )


def unfold(packed):
    low_z = (iota((1, 128), 1) & 31) < 16
    p, q = packed[: 2 * ORB], packed[2 * ORB :]
    return (
        jnp.where(low_z, p, pltpu.roll(p, 16, 1)),
        jnp.where(low_z, pltpu.roll(p, 112, 1), p),
        jnp.concatenate(
            [jnp.where(low_z, q, pltpu.roll(q, 16, 1)), jnp.where(low_z, pltpu.roll(q, 112, 1), q)], axis=0
        ),
    )


def is_even():
    return lax.rem(lax.axis_index("sx"), 2) == 0


def put_messages(planes, mate_ref, across_ref):
    down = fold(planes[0, : 2 * ORB].astype(F32))
    up = fold(planes[1, ORB:].astype(F32))
    even = is_even()
    for i, rows in enumerate((slice(0, 2 * ORB), slice(2 * ORB, ROWS))):
        mate_ref[rows] = jnp.where(even, up[i], down[i]).astype(BF16)
        across_ref[rows] = jnp.where(even, down[i], up[i]).astype(BF16)


def sides(mate, across):
    even = is_even()
    return (jnp.where(even, across, mate), jnp.where(even, mate, across))


def at_end():
    slab = lax.axis_index("sx")
    return (slab == 0) | (slab == lax.axis_size("sx") - 1)


def edges_kernel(
    table_ref, pieces_ref,
    phi_ref, mask_ref, rows_ref, reach_ref, mate_ref, across_ref,
    window_ref, raw_ref, sems,
):
    first = window_start(table_ref.shape[1])
    table_copy = pltpu.make_async_copy(table_ref.at[:, pl.ds(first, 4 * ORB)], window_ref, sems.at[2])
    table_copy.start()
    copies = []
    for i in range(2):
        start = (CX - 1) * PLANE * i
        copies.append(
            pltpu.make_async_copy(pieces_ref.at[:, start : start + PLANE], raw_ref.at[i], sems.at[i])
        )
        copies[i].start()
    table_copy.wait()
    rows = row_features(window_ref, first)
    rows_ref[...] = rows
    reach = jnp.dot(rows, cell_features(), preferred_element_type=F32)
    reach_ref[...] = reach
    for i in range(2):
        mask_ref[i] = sphere(reach, rows, (CX - 1) * i)
    for i in range(2):
        copies[i].wait()
        phi_ref[i] = raw_ref[i] * mask_ref[i]
    put_messages(phi_ref, mate_ref, across_ref)


def rows_product(a, b):
    return lax.dot_general(a, b, (((1,), (1,)), ((), ())), preferred_element_type=F32)


def energy_kernel(
    rows_ref, reach_ref, pieces_ref, pot_ref, edge_ref, edge_mask_ref,
    phi_ref, mask_ref, energy_ref, part_ref, edge_energy_ref, corr_ref, ham_ref,
):
    rows = rows_ref[...]
    for i in range(2):
        mask = sphere(reach_ref[...], rows, 1 + i)
        mask_ref[i] = mask
        phi_ref[i] = pieces_ref[:, PLANE * (1 + i) : PLANE * (2 + i)] * mask
    weights = in_plane(6, -1)
    for t in range(PLANE // TILE):
        lanes = slice(TILE * t, TILE * t + TILE)
        edge = edge_ref[:, :, lanes].astype(F32)
        mid = phi_ref[:, :, lanes].astype(F32)
        inner = plane_product(phi_ref, weights, -1.0, t)
        outer = plane_product(edge_ref, weights, -1.0, t)
        for i in range(2):
            value = 0.5 * (inner[i] - (edge[i] + mid[1 - i])) + pot_ref[1 + i : 2 + i, lanes] * mid[i]
            energy_ref[i, :, lanes] = value.astype(BF16) * mask_ref[i, :, lanes]
            plane = (CX - 1) * i
            value = 0.5 * (outer[i] - mid[i]) + pot_ref[plane : plane + 1, lanes] * edge[i]
            part_ref[i, :, lanes] = value
            rest = rest_rows(i)
            edge_energy_ref[i, rest, lanes] = value[rest].astype(BF16) * edge_mask_ref[i, rest, lanes]
    mid = jnp.concatenate([phi_ref[0], phi_ref[1]], axis=1)
    both = jnp.concatenate([energy_ref[0], energy_ref[1]], axis=1)
    gram = rows_product(jnp.concatenate([mid, both], axis=0), mid)
    corr = gram[:ROWS]
    ham_ref[...] = gram[ROWS:]
    for i in range(2):
        rest = rest_rows(i)
        gram = rows_product(jnp.concatenate([edge_ref[i], edge_energy_ref[i, rest]], axis=0), edge_ref[i])
        corr = corr + gram[:ROWS]
        ham_ref[rest] += gram[ROWS:]
    corr_ref[...] = corr


def halo_rows(i):
    return slice(0, 2 * ORB) if i == 0 else slice(ORB, ROWS)


def rest_rows(i):
    return slice(2 * ORB, ROWS) if i == 0 else slice(0, ORB)


def bands_kernel(
    across_ref, mate_ref, part_ref, mask_ref, phi_ref, corr_ref, ham_ref, rest_ref,
    energy_ref, own_ref, rows_ref,
):
    volume = 1.0 / (4.0 * CX**3)
    gram = []
    for i, side in enumerate(sides(mate_ref[...].astype(F32), across_ref[...].astype(F32))):
        tiles = unfold(side)
        for t in range(PLANE // 128):
            lanes = slice(128 * t, 128 * t + 128)
            value = part_ref[i, halo_rows(i), lanes] - 0.5 * tiles[t % 3]
            energy_ref[i, halo_rows(i), lanes] = value.astype(BF16) * mask_ref[i, halo_rows(i), lanes]
        gram.append(rows_product(energy_ref[i, halo_rows(i)], phi_ref[i]))
    own_ref[:, :, ROWS:] = jnp.zeros((2, ROWS, TILE - ROWS), F32)
    own_ref[0, :ORB, :ROWS] = (ham_ref[:ORB] + gram[0][:ORB]) * volume
    own_ref[0, ORB : 2 * ORB, :ROWS] = (ham_ref[ORB : 2 * ORB] + gram[0][ORB:] + gram[1][:ORB]) * volume
    own_ref[0, 2 * ORB :, :ROWS] = (ham_ref[2 * ORB :] + gram[1][ORB:]) * volume
    own_ref[1, :, :ROWS] = corr_ref[...] * volume
    tail = jnp.where(low_half(), own_ref[0, :, 128:256], swapped(own_ref[1, :, 128:256]))
    even = is_even()
    for i, value in enumerate((own_ref[0, :, 0:128], own_ref[1, :, 0:128], tail)):
        rows_ref[i] = jnp.where(even, value[ORB:], value[: 2 * ORB]).astype(BF16)


def low_half():
    return iota((1, 128), 1) < 64


def swapped(value):
    return pltpu.roll(value, 64, 1)


def mate_blocks(rows_ref, which):
    tail = rows_ref[2].astype(F32)
    if which == 1:
        tail = swapped(tail)
    return rows_ref[which].astype(F32), jnp.where(low_half(), tail, 0.0)


def shifted(c01, c2x):
    low = low_half()
    turned = swapped(c01)
    return jnp.where(low, 0.0, turned), jnp.where(low, turned, swapped(c2x))


def relay_kernel(own_ref, rows_ref, out_ref):
    even = is_even()
    heads = []
    for which in range(2):
        head, rest = shifted(own_ref[which, :, 0:128], own_ref[which, :, 128:256])
        c01, c2x = mate_blocks(rows_ref, which)
        c01 = jnp.where(even, c01[:ORB], c01[ORB:])
        c2x = jnp.where(even, c2x[:ORB], c2x[ORB:])
        own = slice(ORB, 2 * ORB)
        out_ref[2 * which] = (head[own] + jnp.where(even, c2x, c01)).astype(BF16)
        out_ref[2 * which + 1] = (rest[own] + jnp.where(even, c01, c2x)).astype(BF16)
        out_ref[5 + which] = jnp.where(even, rest[:ORB], rest[2 * ORB :]).astype(BF16)
        heads.append(jnp.where(even, head[:ORB], head[2 * ORB :]))
    out_ref[4] = jnp.where(low_half(), swapped(heads[1]), heads[0]).astype(BF16)


def shared_head(tile, which):
    tile = tile.astype(F32)
    if which == 1:
        tile = swapped(tile)
    return jnp.where(low_half(), 0.0, tile)


def pick_kernel(both_ref, other_ref, forward_ref):
    even = is_even()
    for i in range(7):
        value = jnp.where(even, both_ref[0, i].astype(F32), both_ref[1, i].astype(F32))
        value = jnp.where(at_end(), 0.0, value).astype(BF16)
        other_ref[i] = value
        if i >= 4:
            forward_ref[i - 4] = value


def put_gradient(theta, orbital_ref, energy_ref, mask_ref, out_ref):
    for i in range(2):
        for t in range(PLANE // TILE):
            lanes = slice(TILE * t, TILE * t + TILE)
            fix = jnp.dot(theta, orbital_ref[i, :, lanes], preferred_element_type=F32)
            value = energy_ref[i, :, lanes].astype(F32) - fix
            out_ref[i, :, lanes] = value.astype(BF16) * mask_ref[i, :, lanes]


def kept(pattern_ref, r, q):
    slab = lax.axis_index("sx")
    last = pattern_ref.shape[1] - 1
    values = []
    for col in (2 * q, 2 * q + 1):
        apart = abs(col - r - 2)
        if apart == 0:
            values.append(1.0)
        elif apart > 2:
            values.append(0.0)
        else:
            at = jnp.clip(slab - 3 + min(col, r + 2), 0, last)
            values.append(pattern_ref[apart - 1, at].astype(F32))
    return jnp.where(low_half(), values[0], values[1])


def split(value):
    high = value.astype(BF16)
    return high, (value - high.astype(F32)).astype(BF16)


def fine_product(a, b):
    return rows_product(a[0], b[0]) + (rows_product(a[0], b[1]) + rows_product(a[1], b[0]))


def theta_kernel(pattern_ref, own_ref, rows_ref, other_ref, ham_ref, inv_ref, theta_ref):
    even = is_even()
    low = low_half()
    zero = jnp.zeros((ORB, 128), F32)
    for which, band_ref in enumerate((ham_ref, inv_ref)):
        near, rest = shifted(*mate_blocks(rows_ref, which))
        ahead = other_ref[2 * which].astype(F32)
        beside = other_ref[2 * which + 1].astype(F32)
        head = shared_head(other_ref[4], which)
        tail = other_ref[5 + which].astype(F32)
        got_even = (
            (ahead, beside, zero, zero),
            (head, tail + near[:ORB], rest[:ORB], zero),
            (zero, near[ORB:], rest[ORB:], zero),
        )
        got_odd = (
            (near[:ORB], rest[:ORB], zero, zero),
            (near[ORB:], rest[ORB:] + head, tail, zero),
            (zero, jnp.where(low, 0.0, ahead), beside, jnp.where(low, ahead, 0.0)),
        )
        for r in range(3):
            for q in range(4):
                value = jnp.where(even, got_even[r][q], got_odd[r][q])
                if q in (1, 2):
                    value = value + own_ref[which, ORB * r : ORB * r + ORB, 128 * q - 128 : 128 * q]
                value = value * kept(pattern_ref, r, q)
                if which == 1:
                    on = iota((ORB, 128), 0) + (ORB * (r + 2) - 128 * q) == iota((ORB, 128), 1)
                    value = jnp.where(on, 2.0, 0.0) - value
                band_ref[ORB * r : ORB * r + ORB, 128 * q : 128 * q + 128] = value
    theta_ref[...] = fine_product(split(ham_ref[...]), split(inv_ref[...]))


def gradient_kernel(
    pattern_ref, relayed_ref, ham_ref, inv_ref, base_ref,
    edge_ref, edge_energy_ref, edge_mask_ref,
    edge_grad_ref, theta_ref, mate_ref, across_ref,
    window_ref, total_ref,
):
    even = is_even()
    low = low_half()
    more = []
    for which in range(2):
        front = swapped(shared_head(relayed_ref[0], which))
        turned = swapped(relayed_ref[1 + which].astype(F32))
        tiles = []
        for q, value in enumerate((jnp.where(low, front, turned), jnp.where(low, turned, 0.0))):
            tiles.append(value * jnp.where(even, kept(pattern_ref, 2, 2 + q), kept(pattern_ref, 0, q)))
        more.append(jnp.concatenate(tiles, axis=1))
    first, third = slice(0, ORB), slice(2 * ORB, ROWS)
    window_ref[...] = jnp.where(even, ham_ref[:, 256:512], ham_ref[:, 0:256])
    window_ref[first] += jnp.where(even, 0.0, more[0])
    window_ref[third] += jnp.where(even, more[0], 0.0)
    ham = jnp.concatenate(split(window_ref[...]), axis=1)
    inv = jnp.concatenate(split(jnp.where(even, inv_ref[:, 256:512], inv_ref[:, 0:256])), axis=1)
    more = [jnp.concatenate([value.astype(BF16)] * 2, axis=1) for value in more]
    column = rows_product(ham, more[1])
    row = rows_product(more[0], inv)
    total_ref[...] = base_ref[...]
    total_ref[first] += jnp.where(even, 0.0, row)
    total_ref[third] += jnp.where(even, row, 0.0)
    total_ref[:, first] -= jnp.where(even, 0.0, column)
    total_ref[:, third] -= jnp.where(even, column, 0.0)
    theta = total_ref[...].astype(BF16)
    theta_ref[...] = theta
    put_gradient(theta, edge_ref, edge_energy_ref, edge_mask_ref, edge_grad_ref)
    put_messages(edge_grad_ref, mate_ref, across_ref)


def final_kernel(
    both_ref, mate_ref, theta_ref, phi_ref, energy_ref, edge_ref, mask_ref, edge_mask_ref,
    out_ref,
    grad_ref, done_ref, sems,
):
    put_gradient(theta_ref[...], phi_ref, energy_ref, mask_ref, grad_ref)
    weights = in_plane(8, 1)
    across = jnp.where(is_even(), both_ref[0].astype(F32), both_ref[1].astype(F32))
    halos = [unfold(side) for side in sides(mate_ref[...].astype(F32), jnp.where(at_end(), 0.0, across))]
    copies = []
    for t in range(PLANE // TILE):
        lanes = slice(TILE * t, TILE * t + TILE)
        edge = edge_ref[:, :, lanes].astype(F32)
        mid = grad_ref[:, :, lanes].astype(F32)
        inner = plane_product(grad_ref, weights, 1.0, t)
        outer = plane_product(edge_ref, weights, 1.0, t)
        for i in range(2):
            value = (inner[i] + (edge[i] + mid[1 - i])) * (1.0 / 32.0)
            done_ref[1 + i, :, lanes] = value.astype(BF16) * mask_ref[i, :, lanes]
            plane = (CX - 1) * i
            halo = jnp.concatenate([halos[i][2 * t % 3], halos[i][(2 * t + 1) % 3]], axis=1)
            base = outer[i] + mid[i]
            value = (base[halo_rows(i)] + halo) * (1.0 / 32.0)
            done_ref[plane, halo_rows(i), lanes] = value.astype(BF16) * edge_mask_ref[i, halo_rows(i), lanes]
            value = base[rest_rows(i)] * (1.0 / 32.0)
            done_ref[plane, rest_rows(i), lanes] = value.astype(BF16) * edge_mask_ref[i, rest_rows(i), lanes]
        for plane in range(CX):
            start = PLANE * plane + TILE * t
            copies.append(
                pltpu.make_async_copy(
                    done_ref.at[plane, :, lanes], out_ref.at[:, start : start + TILE], sems.at[t, plane]
                )
            )
            copies[-1].start()
    for copy in copies:
        copy.wait()


def shape(*dims, dtype=BF16):
    return jax.ShapeDtypeStruct(dims, dtype)


def cost(flops, moved):
    return pl.CostEstimate(flops=flops, bytes_accessed=moved, transcendentals=0)


PARAMS = pltpu.CompilerParams(vmem_limit_bytes=32 * 1024 * 1024)
WHOLE = pl.BlockSpec(memory_space=pltpu.VMEM)
FAR = pl.BlockSpec(memory_space=pltpu.HBM)


def far(value):
    return pltpu.with_memory_space_constraint(value, pltpu.HBM)


def per_device(pieces, potential, centers, pattern):
    count = lax.axis_size("sx")
    mates = [(i, i ^ 1) for i in range(count)]
    others = [(i, i + 1 if i % 2 else i - 1) for i in range(1, count - 1)]
    groups = lax.axis_size("grp")
    pairs = [[g * count + i, g * count + i + 1] for g in range(groups) for i in range(1, count - 1, 2)]
    ends = [g * count + end for g in range(groups) for end in (0, count - 1)]
    pairs += [[ends[i], ends[i + 2]] for i in range(len(ends)) if i % 4 < 2] if groups % 2 == 0 else [
        [ends[2 * i], ends[2 * i + 1]] for i in range(groups)
    ]

    def to_mate(value):
        return lax.ppermute(value, "sx", mates)

    def across(value):
        return lax.ppermute(value, "sx", others)

    def gathered(value):
        return lax.all_gather(value, ("grp", "sx"), axis_index_groups=pairs)

    table = centers.T
    pair = shape(2, ROWS, PLANE)

    edge, edge_mask, rows, reach, for_mate, for_other = pl.pallas_call(
        edges_kernel,
        out_shape=(
            pair, pair, shape(ROWS, 16), shape(ROWS, PLANE, dtype=F32), shape(ROWS, 128), shape(ROWS, 128),
        ),
        in_specs=[FAR, FAR],
        out_specs=(WHOLE,) * 6,
        scratch_shapes=[
            pltpu.VMEM((4, 4 * ORB), jnp.int32),
            pltpu.VMEM((2, ROWS, PLANE), BF16),
            pltpu.SemaphoreType.DMA((3,)),
        ],
        compiler_params=PARAMS,
        cost_estimate=cost(10**8, 10**6),
        name="edges",
    )(far(table), far(pieces))
    other_side = across(for_other)
    mate_side = to_mate(for_mate)

    mid, mid_mask, mid_energy, part, rest_energy, corr, ham = pl.pallas_call(
        energy_kernel,
        out_shape=(
            pair, pair, pair, shape(2, ROWS, PLANE, dtype=F32), pair,
            shape(ROWS, ROWS, dtype=F32), shape(ROWS, ROWS, dtype=F32),
        ),
        in_specs=[WHOLE] * 6,
        out_specs=(WHOLE,) * 7,
        compiler_params=PARAMS,
        cost_estimate=cost(4 * 10**9, 10**7),
        name="energy",
    )(rows, reach, pieces, potential, edge, edge_mask)

    edge_energy, own, for_mate = pl.pallas_call(
        bands_kernel,
        out_shape=(pair, shape(2, ROWS, TILE, dtype=F32), shape(3, 2 * ORB, 128)),
        in_specs=[WHOLE] * 8,
        out_specs=(WHOLE,) * 3,
        input_output_aliases={7: 0},
        compiler_params=PARAMS,
        cost_estimate=cost(10**9, 10**7),
        name="bands",
    )(other_side, mate_side, part, edge_mask, edge, corr, ham, rest_energy)
    mate_rows = to_mate(for_mate)
    for_other = pl.pallas_call(
        relay_kernel,
        out_shape=shape(7, ORB, 128),
        in_specs=[WHOLE] * 2,
        out_specs=WHOLE,
        compiler_params=PARAMS,
        cost_estimate=cost(10**6, 10**6),
        name="relay",
    )(own, mate_rows)
    other_rows, forward = pl.pallas_call(
        pick_kernel,
        out_shape=(shape(7, ORB, 128), shape(3, ORB, 128)),
        in_specs=[WHOLE],
        out_specs=(WHOLE,) * 2,
        compiler_params=PARAMS,
        cost_estimate=cost(10**6, 10**6),
        name="pick",
    )(gathered(for_other))
    relayed = to_mate(forward)

    patterns = pattern.T
    scalars = pl.BlockSpec(memory_space=pltpu.SMEM)
    band = shape(ROWS, 8 * ORB, dtype=F32)
    ham_band, inv_band, base = pl.pallas_call(
        theta_kernel,
        out_shape=(band, band, shape(ROWS, ROWS, dtype=F32)),
        in_specs=[scalars] + [WHOLE] * 3,
        out_specs=(WHOLE,) * 3,
        compiler_params=PARAMS,
        cost_estimate=cost(10**9, 4 * 10**6),
        name="theta",
    )(patterns, own, mate_rows, other_rows)
    edge_grad, theta, for_mate, for_other = pl.pallas_call(
        gradient_kernel,
        out_shape=(pair, shape(ROWS, ROWS), shape(ROWS, 128), shape(ROWS, 128)),
        in_specs=[scalars] + [WHOLE] * 7,
        out_specs=(WHOLE,) * 4,
        scratch_shapes=[pltpu.VMEM((ROWS, TILE), F32), pltpu.VMEM((ROWS, ROWS), F32)],
        compiler_params=PARAMS,
        cost_estimate=cost(10**9, 10**7),
        name="gradient",
    )(patterns, relayed, ham_band, inv_band, base, edge, edge_energy, edge_mask)
    mate_side = to_mate(for_mate)
    both_sides = gathered(for_other)

    return pl.pallas_call(
        final_kernel,
        out_shape=pltpu.HBM((ROWS, CX * PLANE), BF16),
        in_specs=[WHOLE] * 8,
        out_specs=FAR,
        scratch_shapes=[
            pltpu.VMEM((2, ROWS, PLANE), BF16),
            pltpu.VMEM((CX, ROWS, PLANE), BF16),
            pltpu.SemaphoreType.DMA((PLANE // TILE, CX)),
        ],
        compiler_params=PARAMS,
        cost_estimate=cost(2 * 10**9, 10**7),
        name="final",
    )(both_sides, mate_side, theta, mid, mid_energy, edge_grad, mid_mask, edge_mask)


def solution(mesh):
    return jax.shard_map(
        per_device,
        mesh=mesh,
        in_specs=(P(("grp", "sx"), None), P(("grp", "sx"), None), P("grp", None), P("grp", None)),
        out_specs=P(("grp", "sx"), None),
        check_vma=False,
    )
```

```python
import functools

import jax
import jax.numpy as jnp
from jax import lax
from jax.experimental import pallas as pl
from jax.experimental.pallas import tpu as pltpu
from jax.sharding import PartitionSpec as P

ORB = 64
CX = 4
NY = 32
NZ = 32
ROWS = 3 * ORB
PLANE = NY * NZ
TILE = 256
F32 = jnp.float32
BF16 = jnp.bfloat16


def iota(shape, dim):
    return lax.broadcasted_iota(jnp.int32, shape, dim)


def window_start(width):
    slab = lax.axis_index("sx")
    first = jnp.clip(slab * ORB - ORB, 0, width - 4 * ORB) // 128 * 128
    return pl.multiple_of(first, 128)


def row_features(window_ref, first):
    slab = lax.axis_index("sx")
    count = lax.axis_size("sx")
    window = window_ref[...]
    shift = slab * ORB - ORB - first
    window = pltpu.roll(jnp.concatenate([window, window], axis=0), lax.rem(4 * ORB - shift, 4 * ORB), 1)
    lane = iota((1, 4 * ORB), 1)
    block = slab - 1 + lane // ORB
    valid = (block >= 0) & (block < count)
    cx = window[0:1] - slab * CX
    cy = window[1:2]
    cz = window[2:3]
    r = window[3:4]
    const = cx * cx + cy * cy + cz * cz - r * r
    const = jnp.where(valid, const, 65535)
    cx = jnp.where(valid, cx, 0)
    cy = jnp.where(valid, cy, 0)
    cz = jnp.where(valid, cz, 0)
    k = iota((16, 4 * ORB), 0)
    feats = jnp.where(k == 0, 1, 0)
    feats = jnp.where(k == 1, 256, feats)
    feats = jnp.where(k == 2, cy, feats)
    feats = jnp.where(k == 3, cz, feats)
    feats = jnp.where(k == 4, const & 255, feats)
    feats = jnp.where(k == 5, const >> 8, feats)
    feats = jnp.where(k == 6, cx, feats)
    return jnp.transpose(feats.astype(F32))[:ROWS].astype(BF16)


def cell_features():
    k = iota((16, PLANE), 0)
    cell = iota((16, PLANE), 1)
    y = cell >> 5
    z = cell & 31
    sq = y * y + z * z
    feats = jnp.where(k == 0, sq & 255, 0)
    feats = jnp.where(k == 1, sq >> 8, feats)
    feats = jnp.where(k == 2, -2 * y, feats)
    feats = jnp.where(k == 3, -2 * z, feats)
    feats = jnp.where(k == 4, 1, feats)
    feats = jnp.where(k == 5, 256, feats)
    return feats.astype(F32).astype(BF16)


def sphere(reach, rows, plane):
    bound = rows[:, 6:7].astype(F32) * (2.0 * plane) - float(plane * plane)
    return jnp.where(reach <= bound, 1.0, 0.0).astype(BF16)


def in_plane(center, beside):
    k = iota((TILE, TILE), 0)
    n = iota((TILE, TILE), 1)
    diff = k - n
    near_y = (diff == NZ) | (diff == -NZ)
    near_z = ((diff == 1) | (diff == -1)) & ((k >> 5) == (n >> 5))
    w = jnp.where(near_y | near_z, float(beside), 0.0)
    return jnp.where(diff == 0, float(center), w).astype(BF16)


def plane_product(ref, weights, beside, t):
    start = TILE * t
    values = ref[:, :, start : start + TILE].reshape(2 * ROWS, TILE)
    out = jnp.dot(values, weights, preferred_element_type=F32).reshape(2, ROWS, TILE)
    lane = iota((1, 1, 128), 2)
    first, last = out[:, :, :128], out[:, :, 128:]
    if t > 0:
        turned = pltpu.roll(ref[:, :, start - 128 : start].astype(F32), NZ, 2)
        turned = jnp.where(lane < NZ, turned, 0.0)
        first = first + turned if beside > 0 else first - turned
    if start + TILE < PLANE:
        turned = pltpu.roll(ref[:, :, start + TILE : start + TILE + 128].astype(F32), 128 - NZ, 2)
        turned = jnp.where(lane >= 128 - NZ, turned, 0.0)
        last = last + turned if beside > 0 else last - turned
    return jnp.concatenate([first, last], axis=2)


def fold(values):
    tiles = [values[:, 128 * t : 128 * t + 128] for t in range(PLANE // 128)]
    a, b, c = (sum(tiles[t::3][1:], tiles[t]) for t in range(3))
    low_z = (iota((1, 128), 1) & 31) < 16
    top, bottom = c[:ORB], c[ORB:]
    return (
        jnp.where(low_z, a + pltpu.roll(a, 112, 1), b + pltpu.roll(b, 16, 1)),
        jnp.where(low_z, top + pltpu.roll(top, 112, 1), bottom + pltpu.roll(bottom, 16, 1)),
    )


def unfold(packed):
    low_z = (iota((1, 128), 1) & 31) < 16
    p, q = packed[: 2 * ORB], packed[2 * ORB :]
    return (
        jnp.where(low_z, p, pltpu.roll(p, 16, 1)),
        jnp.where(low_z, pltpu.roll(p, 112, 1), p),
        jnp.concatenate(
            [jnp.where(low_z, q, pltpu.roll(q, 16, 1)), jnp.where(low_z, pltpu.roll(q, 112, 1), q)], axis=0
        ),
    )


def is_even():
    return lax.rem(lax.axis_index("sx"), 2) == 0


def put_messages(planes, mate_ref, across_ref):
    down = fold(planes[0, : 2 * ORB].astype(F32))
    up = fold(planes[1, ORB:].astype(F32))
    even = is_even()
    for i, rows in enumerate((slice(0, 2 * ORB), slice(2 * ORB, ROWS))):
        mate_ref[rows] = jnp.where(even, up[i], down[i]).astype(BF16)
        across_ref[rows] = jnp.where(even, down[i], up[i]).astype(BF16)


def sides(mate, across):
    even = is_even()
    return (jnp.where(even, across, mate), jnp.where(even, mate, across))


def at_end():
    slab = lax.axis_index("sx")
    return (slab == 0) | (slab == lax.axis_size("sx") - 1)


def edges_kernel(
    table_ref, pieces_ref,
    phi_ref, mask_ref, rows_ref, reach_ref, mate_ref, across_ref,
    window_ref, raw_ref, sems,
):
    first = window_start(table_ref.shape[1])
    table_copy = pltpu.make_async_copy(table_ref.at[:, pl.ds(first, 4 * ORB)], window_ref, sems.at[2])
    table_copy.start()
    copies = []
    for i in range(2):
        start = (CX - 1) * PLANE * i
        copies.append(
            pltpu.make_async_copy(pieces_ref.at[:, start : start + PLANE], raw_ref.at[i], sems.at[i])
        )
        copies[i].start()
    cells = cell_features()
    table_copy.wait()
    rows = row_features(window_ref, first)
    rows_ref[...] = rows
    reach = jnp.dot(rows, cells, preferred_element_type=F32)
    reach_ref[...] = reach
    for i in range(2):
        mask_ref[i] = sphere(reach, rows, (CX - 1) * i)
    for i in range(2):
        copies[i].wait()
        phi_ref[i] = raw_ref[i] * mask_ref[i]
    put_messages(phi_ref, mate_ref, across_ref)


def rows_product(a, b):
    return lax.dot_general(a, b, (((1,), (1,)), ((), ())), preferred_element_type=F32)


def energy_kernel(
    rows_ref, reach_ref, pieces_ref, pot_ref, edge_ref, edge_mask_ref,
    phi_ref, mask_ref, energy_ref, part_ref, edge_energy_ref, corr_ref, ham_ref,
):
    rows = rows_ref[...]
    for i in range(2):
        mask = sphere(reach_ref[...], rows, 1 + i)
        mask_ref[i] = mask
        phi_ref[i] = pieces_ref[:, PLANE * (1 + i) : PLANE * (2 + i)] * mask
    weights = in_plane(6, -1)
    for t in range(PLANE // TILE):
        lanes = slice(TILE * t, TILE * t + TILE)
        edge = edge_ref[:, :, lanes].astype(F32)
        mid = phi_ref[:, :, lanes].astype(F32)
        inner = plane_product(phi_ref, weights, -1.0, t)
        outer = plane_product(edge_ref, weights, -1.0, t)
        for i in range(2):
            value = 0.5 * (inner[i] - (edge[i] + mid[1 - i])) + pot_ref[1 + i : 2 + i, lanes] * mid[i]
            energy_ref[i, :, lanes] = value.astype(BF16) * mask_ref[i, :, lanes]
            plane = (CX - 1) * i
            value = 0.5 * (outer[i] - mid[i]) + pot_ref[plane : plane + 1, lanes] * edge[i]
            part_ref[i, :, lanes] = value
            rest = rest_rows(i)
            edge_energy_ref[i, rest, lanes] = value[rest].astype(BF16) * edge_mask_ref[i, rest, lanes]
    mid = jnp.concatenate([phi_ref[0], phi_ref[1]], axis=1)
    both = jnp.concatenate([energy_ref[0], energy_ref[1]], axis=1)
    gram = rows_product(jnp.concatenate([mid, both], axis=0), mid)
    corr = gram[:ROWS]
    ham_ref[...] = gram[ROWS:]
    for i in range(2):
        rest = rest_rows(i)
        gram = rows_product(jnp.concatenate([edge_ref[i], edge_energy_ref[i, rest]], axis=0), edge_ref[i])
        corr = corr + gram[:ROWS]
        ham_ref[rest] += gram[ROWS:]
    corr_ref[...] = corr


def halo_rows(i):
    return slice(0, 2 * ORB) if i == 0 else slice(ORB, ROWS)


def rest_rows(i):
    return slice(2 * ORB, ROWS) if i == 0 else slice(0, ORB)


def bands_kernel(
    across_ref, mate_ref, part_ref, mask_ref, phi_ref, corr_ref, ham_ref, rest_ref,
    energy_ref, own_ref, rows_ref,
):
    volume = 1.0 / (4.0 * CX**3)
    gram = []
    for i, side in enumerate(sides(mate_ref[...].astype(F32), across_ref[...].astype(F32))):
        tiles = unfold(side)
        for t in range(PLANE // 128):
            lanes = slice(128 * t, 128 * t + 128)
            value = part_ref[i, halo_rows(i), lanes] - 0.5 * tiles[t % 3]
            energy_ref[i, halo_rows(i), lanes] = value.astype(BF16) * mask_ref[i, halo_rows(i), lanes]
        gram.append(rows_product(energy_ref[i, halo_rows(i)], phi_ref[i]))
    own_ref[:, :, ROWS:] = jnp.zeros((2, ROWS, TILE - ROWS), F32)
    own_ref[0, :ORB, :ROWS] = (ham_ref[:ORB] + gram[0][:ORB]) * volume
    own_ref[0, ORB : 2 * ORB, :ROWS] = (ham_ref[ORB : 2 * ORB] + gram[0][ORB:] + gram[1][:ORB]) * volume
    own_ref[0, 2 * ORB :, :ROWS] = (ham_ref[2 * ORB :] + gram[1][ORB:]) * volume
    own_ref[1, :, :ROWS] = corr_ref[...] * volume
    tail = jnp.where(low_half(), own_ref[0, :, 128:256], swapped(own_ref[1, :, 128:256]))
    even = is_even()
    for i, value in enumerate((own_ref[0, :, 0:128], own_ref[1, :, 0:128], tail)):
        rows_ref[i] = jnp.where(even, value[ORB:], value[: 2 * ORB]).astype(BF16)


def low_half():
    return iota((1, 128), 1) < 64


def swapped(value):
    return pltpu.roll(value, 64, 1)


def mate_blocks(rows_ref, which):
    tail = rows_ref[2].astype(F32)
    if which == 1:
        tail = swapped(tail)
    return rows_ref[which].astype(F32), jnp.where(low_half(), tail, 0.0)


def shifted(c01, c2x):
    low = low_half()
    turned = swapped(c01)
    return jnp.where(low, 0.0, turned), jnp.where(low, turned, swapped(c2x))


def relay_kernel(own_ref, rows_ref, out_ref):
    even = is_even()
    heads = []
    for which in range(2):
        head, rest = shifted(own_ref[which, :, 0:128], own_ref[which, :, 128:256])
        c01, c2x = mate_blocks(rows_ref, which)
        c01 = jnp.where(even, c01[:ORB], c01[ORB:])
        c2x = jnp.where(even, c2x[:ORB], c2x[ORB:])
        own = slice(ORB, 2 * ORB)
        out_ref[2 * which] = (head[own] + jnp.where(even, c2x, c01)).astype(BF16)
        out_ref[2 * which + 1] = (rest[own] + jnp.where(even, c01, c2x)).astype(BF16)
        out_ref[5 + which] = jnp.where(even, rest[:ORB], rest[2 * ORB :]).astype(BF16)
        heads.append(jnp.where(even, head[:ORB], head[2 * ORB :]))
    out_ref[4] = jnp.where(low_half(), swapped(heads[1]), heads[0]).astype(BF16)


def shared_head(tile, which):
    tile = tile.astype(F32)
    if which == 1:
        tile = swapped(tile)
    return jnp.where(low_half(), 0.0, tile)


def pick_kernel(both_ref, other_ref, forward_ref):
    even = is_even()
    for i in range(7):
        value = jnp.where(even, both_ref[0, i].astype(F32), both_ref[1, i].astype(F32))
        value = jnp.where(at_end(), 0.0, value).astype(BF16)
        other_ref[i] = value
        if i >= 4:
            forward_ref[i - 4] = value


def put_gradient(theta, orbital_ref, energy_ref, mask_ref, out_ref):
    for i in range(2):
        for t in range(PLANE // TILE):
            lanes = slice(TILE * t, TILE * t + TILE)
            fix = jnp.dot(theta, orbital_ref[i, :, lanes], preferred_element_type=F32)
            value = energy_ref[i, :, lanes].astype(F32) - fix
            out_ref[i, :, lanes] = value.astype(BF16) * mask_ref[i, :, lanes]


def kept(pattern_ref, r, q):
    slab = lax.axis_index("sx")
    last = pattern_ref.shape[1] - 1
    values = []
    for col in (2 * q, 2 * q + 1):
        apart = abs(col - r - 2)
        if apart == 0:
            values.append(1.0)
        elif apart > 2:
            values.append(0.0)
        else:
            at = jnp.clip(slab - 3 + min(col, r + 2), 0, last)
            values.append(pattern_ref[apart - 1, at].astype(F32))
    return jnp.where(low_half(), values[0], values[1])


def split(value):
    high = value.astype(BF16)
    return high, (value - high.astype(F32)).astype(BF16)


def fine_product(a, b):
    return rows_product(a[0], b[0]) + (rows_product(a[0], b[1]) + rows_product(a[1], b[0]))


def theta_kernel(
    pattern_ref, own_ref, rows_ref, other_ref,
    window_ref, theta_ref,
    ham_ref, inv_ref,
):
    even = is_even()
    low = low_half()
    zero = jnp.zeros((ORB, 128), F32)
    for which, band_ref in enumerate((ham_ref, inv_ref)):
        near, rest = shifted(*mate_blocks(rows_ref, which))
        ahead = other_ref[2 * which].astype(F32)
        beside = other_ref[2 * which + 1].astype(F32)
        head = shared_head(other_ref[4], which)
        tail = other_ref[5 + which].astype(F32)
        got_even = (
            (ahead, beside, zero, zero),
            (head, tail + near[:ORB], rest[:ORB], zero),
            (zero, near[ORB:], rest[ORB:], zero),
        )
        got_odd = (
            (near[:ORB], rest[:ORB], zero, zero),
            (near[ORB:], rest[ORB:] + head, tail, zero),
            (zero, jnp.where(low, 0.0, ahead), beside, jnp.where(low, ahead, 0.0)),
        )
        for r in range(3):
            for q in range(4):
                value = jnp.where(even, got_even[r][q], got_odd[r][q])
                if q in (1, 2):
                    value = value + own_ref[which, ORB * r : ORB * r + ORB, 128 * q - 128 : 128 * q]
                value = value * kept(pattern_ref, r, q)
                if which == 1:
                    on = iota((ORB, 128), 0) + (ORB * (r + 2) - 128 * q) == iota((ORB, 128), 1)
                    value = jnp.where(on, 2.0, 0.0) - value
                band_ref[ORB * r : ORB * r + ORB, 128 * q : 128 * q + 128] = value
    ham, inv = split(ham_ref[...]), split(inv_ref[...])
    theta_ref[...] = fine_product(ham, inv)
    for which, (high, _) in enumerate((ham, inv)):
        window_ref[which] = jnp.where(even, high[:, 256:512].astype(F32), high[:, 0:256].astype(F32)).astype(BF16)


def gradient_kernel(
    pattern_ref, relayed_ref, bands_ref, base_ref,
    edge_ref, edge_energy_ref, edge_mask_ref,
    edge_grad_ref, theta_ref, mate_ref, across_ref,
    window_ref, total_ref,
):
    even = is_even()
    low = low_half()
    more = []
    for which in range(2):
        front = swapped(shared_head(relayed_ref[0], which))
        turned = swapped(relayed_ref[1 + which].astype(F32))
        tiles = []
        for q, value in enumerate((jnp.where(low, front, turned), jnp.where(low, turned, 0.0))):
            tiles.append(value * jnp.where(even, kept(pattern_ref, 2, 2 + q), kept(pattern_ref, 0, q)))
        more.append(jnp.concatenate(tiles, axis=1))
    first, third = slice(0, ORB), slice(2 * ORB, ROWS)
    window_ref[...] = bands_ref[0]
    window_ref[first] = (bands_ref[0, first].astype(F32) + jnp.where(even, 0.0, more[0])).astype(BF16)
    window_ref[third] = (bands_ref[0, third].astype(F32) + jnp.where(even, more[0], 0.0)).astype(BF16)
    more = [value.astype(BF16) for value in more]
    column = rows_product(window_ref[...], more[1])
    row = rows_product(more[0], bands_ref[1])
    total_ref[...] = base_ref[...]
    total_ref[first] += jnp.where(even, 0.0, row)
    total_ref[third] += jnp.where(even, row, 0.0)
    total_ref[:, first] -= jnp.where(even, 0.0, column)
    total_ref[:, third] -= jnp.where(even, column, 0.0)
    theta = total_ref[...].astype(BF16)
    theta_ref[...] = theta
    put_gradient(theta, edge_ref, edge_energy_ref, edge_mask_ref, edge_grad_ref)
    put_messages(edge_grad_ref, mate_ref, across_ref)


def smooth_kernel(
    theta_ref, phi_ref, energy_ref, edge_ref, mask_ref, edge_mask_ref,
    out_ref, part_ref,
    grad_ref, done_ref, rest_ref, sems,
):
    put_gradient(theta_ref[...], phi_ref, energy_ref, mask_ref, grad_ref)
    weights = in_plane(8, 1)
    copies = []

    def send(source, rows, start, sem):
        copies.append(pltpu.make_async_copy(source, out_ref.at[rows, start : start + TILE], sem))
        copies[-1].start()

    for t in range(PLANE // TILE):
        lanes = slice(TILE * t, TILE * t + TILE)
        edge = edge_ref[:, :, lanes].astype(F32)
        mid = grad_ref[:, :, lanes].astype(F32)
        inner = plane_product(grad_ref, weights, 1.0, t)
        outer = plane_product(edge_ref, weights, 1.0, t)
        for i in range(2):
            value = (inner[i] + (edge[i] + mid[1 - i])) * (1.0 / 32.0)
            done_ref[i, :, lanes] = value.astype(BF16) * mask_ref[i, :, lanes]
            value = outer[i] + mid[i]
            part_ref[i, :, lanes] = value
            rest = rest_rows(i)
            value = value[rest] * (1.0 / 32.0)
            rest_ref[i, :, lanes] = value.astype(BF16) * edge_mask_ref[i, rest, lanes]
        for i in range(2):
            send(done_ref.at[i, :, lanes], slice(0, ROWS), PLANE * (1 + i) + TILE * t, sems.at[t, i])
            send(rest_ref.at[i, :, lanes], rest_rows(i), PLANE * (CX - 1) * i + TILE * t, sems.at[t, 2 + i])
    for copy in copies:
        copy.wait()


def finish_kernel(across_ref, mate_ref, part_ref, mask_ref, inner_ref, out_ref, done_ref, sems):
    halos = [unfold(side) for side in sides(mate_ref[...].astype(F32), across_ref[...].astype(F32))]
    copies = []
    for h in range(4):
        for i in range(2):
            for t in (2 * h, 2 * h + 1):
                lanes = slice(128 * t, 128 * t + 128)
                value = (part_ref[i, halo_rows(i), lanes] + halos[i][t % 3]) * (1.0 / 32.0)
                done_ref[i, :, lanes] = value.astype(BF16) * mask_ref[i, halo_rows(i), lanes]
            start = PLANE * (CX - 1) * i + TILE * h
            copies.append(
                pltpu.make_async_copy(
                    done_ref.at[i, :, TILE * h : TILE * h + TILE],
                    out_ref.at[halo_rows(i), start : start + TILE],
                    sems.at[i, h],
                )
            )
            copies[-1].start()
    for copy in copies:
        copy.wait()


def shape(*dims, dtype=BF16):
    return jax.ShapeDtypeStruct(dims, dtype)


def cost(flops, moved):
    return pl.CostEstimate(flops=flops, bytes_accessed=moved, transcendentals=0)


PARAMS = pltpu.CompilerParams(vmem_limit_bytes=32 * 1024 * 1024)
WHOLE = pl.BlockSpec(memory_space=pltpu.VMEM)
FAR = pl.BlockSpec(memory_space=pltpu.HBM)


def far(value):
    return pltpu.with_memory_space_constraint(value, pltpu.HBM)


def per_device(pieces, potential, centers, pattern):
    count = lax.axis_size("sx")
    mates = [(i, i ^ 1) for i in range(count)]
    others = [(i, i + 1 if i % 2 else i - 1) for i in range(1, count - 1)]
    groups = lax.axis_size("grp")
    pairs = [[g * count + i, g * count + i + 1] for g in range(groups) for i in range(1, count - 1, 2)]
    ends = [g * count + end for g in range(groups) for end in (0, count - 1)]
    pairs += [[ends[i], ends[i + 2]] for i in range(len(ends)) if i % 4 < 2] if groups % 2 == 0 else [
        [ends[2 * i], ends[2 * i + 1]] for i in range(groups)
    ]

    def to_mate(value):
        return lax.ppermute(value, "sx", mates)

    def across(value):
        return lax.ppermute(value, "sx", others)

    def gathered(value):
        return lax.all_gather(value, ("grp", "sx"), axis_index_groups=pairs)

    table = centers.T
    pair = shape(2, ROWS, PLANE)

    edge, edge_mask, rows, reach, for_mate, for_other = pl.pallas_call(
        edges_kernel,
        out_shape=(
            pair, pair, shape(ROWS, 16), shape(ROWS, PLANE, dtype=F32), shape(ROWS, 128), shape(ROWS, 128),
        ),
        in_specs=[FAR, FAR],
        out_specs=(WHOLE,) * 6,
        scratch_shapes=[
            pltpu.VMEM((4, 4 * ORB), jnp.int32),
            pltpu.VMEM((2, ROWS, PLANE), BF16),
            pltpu.SemaphoreType.DMA((3,)),
        ],
        compiler_params=PARAMS,
        cost_estimate=cost(10**8, 10**6),
        name="edges",
    )(far(table), far(pieces))
    other_side = across(for_other)
    mate_side = to_mate(for_mate)

    mid, mid_mask, mid_energy, part, rest_energy, corr, ham = pl.pallas_call(
        energy_kernel,
        out_shape=(
            pair, pair, pair, shape(2, ROWS, PLANE, dtype=F32), pair,
            shape(ROWS, ROWS, dtype=F32), shape(ROWS, ROWS, dtype=F32),
        ),
        in_specs=[WHOLE] * 6,
        out_specs=(WHOLE,) * 7,
        compiler_params=PARAMS,
        cost_estimate=cost(4 * 10**9, 10**7),
        name="energy",
    )(rows, reach, pieces, potential, edge, edge_mask)

    edge_energy, own, for_mate = pl.pallas_call(
        bands_kernel,
        out_shape=(pair, shape(2, ROWS, TILE, dtype=F32), shape(3, 2 * ORB, 128)),
        in_specs=[WHOLE] * 8,
        out_specs=(WHOLE,) * 3,
        input_output_aliases={7: 0},
        compiler_params=PARAMS,
        cost_estimate=cost(10**9, 10**7),
        name="bands",
    )(other_side, mate_side, part, edge_mask, edge, corr, ham, rest_energy)
    mate_rows = to_mate(for_mate)
    for_other = pl.pallas_call(
        relay_kernel,
        out_shape=shape(7, ORB, 128),
        in_specs=[WHOLE] * 2,
        out_specs=WHOLE,
        compiler_params=PARAMS,
        cost_estimate=cost(10**6, 10**6),
        name="relay",
    )(own, mate_rows)
    other_rows, forward = pl.pallas_call(
        pick_kernel,
        out_shape=(shape(7, ORB, 128), shape(3, ORB, 128)),
        in_specs=[WHOLE],
        out_specs=(WHOLE,) * 2,
        compiler_params=PARAMS,
        cost_estimate=cost(10**6, 10**6),
        name="pick",
    )(gathered(for_other))
    relayed = to_mate(forward)

    patterns = pattern.T
    scalars = pl.BlockSpec(memory_space=pltpu.SMEM)
    bands, base = pl.pallas_call(
        theta_kernel,
        out_shape=(shape(2, ROWS, TILE), shape(ROWS, ROWS, dtype=F32)),
        in_specs=[scalars] + [WHOLE] * 3,
        out_specs=(WHOLE,) * 2,
        scratch_shapes=[pltpu.VMEM((ROWS, 8 * ORB), F32), pltpu.VMEM((ROWS, 8 * ORB), F32)],
        compiler_params=PARAMS,
        cost_estimate=cost(10**9, 4 * 10**6),
        name="theta",
    )(patterns, own, mate_rows, other_rows)
    edge_grad, theta, for_mate, for_other = pl.pallas_call(
        gradient_kernel,
        out_shape=(pair, shape(ROWS, ROWS), shape(ROWS, 128), shape(ROWS, 128)),
        in_specs=[scalars] + [WHOLE] * 6,
        out_specs=(WHOLE,) * 4,
        scratch_shapes=[pltpu.VMEM((ROWS, TILE), BF16), pltpu.VMEM((ROWS, ROWS), F32)],
        compiler_params=PARAMS,
        cost_estimate=cost(10**9, 10**7),
        name="gradient",
    )(patterns, relayed, bands, base, edge, edge_energy, edge_mask)
    other_side = across(for_other)
    mate_side = to_mate(for_mate)

    inner, part = pl.pallas_call(
        smooth_kernel,
        out_shape=(pltpu.HBM((ROWS, CX * PLANE), BF16), shape(2, ROWS, PLANE, dtype=F32)),
        in_specs=[WHOLE] * 6,
        out_specs=(FAR, WHOLE),
        scratch_shapes=[
            pltpu.VMEM((2, ROWS, PLANE), BF16),
            pltpu.VMEM((2, ROWS, PLANE), BF16),
            pltpu.VMEM((2, ORB, PLANE), BF16),
            pltpu.SemaphoreType.DMA((PLANE // TILE, 4)),
        ],
        compiler_params=PARAMS,
        cost_estimate=cost(2 * 10**9, 10**7),
        name="smooth",
    )(theta, mid, mid_energy, edge_grad, mid_mask, edge_mask)

    return pl.pallas_call(
        finish_kernel,
        out_shape=pltpu.HBM((ROWS, CX * PLANE), BF16),
        in_specs=[WHOLE] * 4 + [FAR],
        out_specs=FAR,
        scratch_shapes=[pltpu.VMEM((2, 2 * ORB, PLANE), BF16), pltpu.SemaphoreType.DMA((2, PLANE // TILE))],
        input_output_aliases={4: 0},
        compiler_params=PARAMS,
        cost_estimate=cost(10**7, 10**7),
        name="finish",
    )(other_side, mate_side, part, edge_mask, inner)


def solution(mesh):
    return jax.shard_map(
        per_device,
        mesh=mesh,
        in_specs=(P(("grp", "sx"), None), P(("grp", "sx"), None), P("grp", None), P("grp", None)),
        out_specs=P(("grp", "sx"), None),
        check_vma=False,
    )
```

```python
import functools

import jax
import jax.numpy as jnp
from jax import lax
from jax.experimental import pallas as pl
from jax.experimental.pallas import tpu as pltpu
from jax.sharding import PartitionSpec as P

ORB = 64
CX = 4
NY = 32
NZ = 32
ROWS = 3 * ORB
PLANE = NY * NZ
TILE = 256
F32 = jnp.float32
BF16 = jnp.bfloat16


def iota(shape, dim):
    return lax.broadcasted_iota(jnp.int32, shape, dim)


def window_start(width):
    slab = lax.axis_index("sx")
    first = jnp.clip(slab * ORB - ORB, 0, width - 4 * ORB) // 128 * 128
    return pl.multiple_of(first, 128)


def row_features(window_ref, first):
    slab = lax.axis_index("sx")
    count = lax.axis_size("sx")
    window = window_ref[...]
    shift = slab * ORB - ORB - first
    window = pltpu.roll(jnp.concatenate([window, window], axis=0), lax.rem(4 * ORB - shift, 4 * ORB), 1)
    lane = iota((1, 4 * ORB), 1)
    block = slab - 1 + lane // ORB
    valid = (block >= 0) & (block < count)
    cx = window[0:1] - slab * CX
    cy = window[1:2]
    cz = window[2:3]
    r = window[3:4]
    const = cx * cx + cy * cy + cz * cz - r * r
    const = jnp.where(valid, const, 65535)
    cx = jnp.where(valid, cx, 0)
    cy = jnp.where(valid, cy, 0)
    cz = jnp.where(valid, cz, 0)
    k = iota((16, 4 * ORB), 0)
    feats = jnp.where(k == 0, 1, 0)
    feats = jnp.where(k == 1, 256, feats)
    feats = jnp.where(k == 2, cy, feats)
    feats = jnp.where(k == 3, cz, feats)
    feats = jnp.where(k == 4, const & 255, feats)
    feats = jnp.where(k == 5, const >> 8, feats)
    feats = jnp.where(k == 6, cx, feats)
    return jnp.transpose(feats.astype(F32))[:ROWS].astype(BF16)


def cell_features():
    k = iota((16, PLANE), 0)
    cell = iota((16, PLANE), 1)
    y = cell >> 5
    z = cell & 31
    sq = y * y + z * z
    feats = jnp.where(k == 0, sq & 255, 0)
    feats = jnp.where(k == 1, sq >> 8, feats)
    feats = jnp.where(k == 2, -2 * y, feats)
    feats = jnp.where(k == 3, -2 * z, feats)
    feats = jnp.where(k == 4, 1, feats)
    feats = jnp.where(k == 5, 256, feats)
    return feats.astype(F32).astype(BF16)


def sphere(reach, rows, plane):
    bound = rows[:, 6:7].astype(F32) * (2.0 * plane) - float(plane * plane)
    return jnp.where(reach <= bound, 1.0, 0.0).astype(BF16)


def in_plane(center, beside):
    k = iota((TILE, TILE), 0)
    n = iota((TILE, TILE), 1)
    diff = k - n
    near_y = (diff == NZ) | (diff == -NZ)
    near_z = ((diff == 1) | (diff == -1)) & ((k >> 5) == (n >> 5))
    w = jnp.where(near_y | near_z, float(beside), 0.0)
    return jnp.where(diff == 0, float(center), w).astype(BF16)


def plane_product(ref, weights, beside, t):
    start = TILE * t
    values = ref[:, :, start : start + TILE].reshape(2 * ROWS, TILE)
    out = jnp.dot(values, weights, preferred_element_type=F32).reshape(2, ROWS, TILE)
    lane = iota((1, 1, 128), 2)
    first, last = out[:, :, :128], out[:, :, 128:]
    if t > 0:
        turned = pltpu.roll(ref[:, :, start - 128 : start].astype(F32), NZ, 2)
        turned = jnp.where(lane < NZ, turned, 0.0)
        first = first + turned if beside > 0 else first - turned
    if start + TILE < PLANE:
        turned = pltpu.roll(ref[:, :, start + TILE : start + TILE + 128].astype(F32), 128 - NZ, 2)
        turned = jnp.where(lane >= 128 - NZ, turned, 0.0)
        last = last + turned if beside > 0 else last - turned
    return jnp.concatenate([first, last], axis=2)


def fold(values):
    tiles = [values[:, 128 * t : 128 * t + 128] for t in range(PLANE // 128)]
    a, b, c = (sum(tiles[t::3][1:], tiles[t]) for t in range(3))
    low_z = (iota((1, 128), 1) & 31) < 16
    top, bottom = c[:ORB], c[ORB:]
    return (
        jnp.where(low_z, a + pltpu.roll(a, 112, 1), b + pltpu.roll(b, 16, 1)),
        jnp.where(low_z, top + pltpu.roll(top, 112, 1), bottom + pltpu.roll(bottom, 16, 1)),
    )


def unfold(packed):
    low_z = (iota((1, 128), 1) & 31) < 16
    p, q = packed[: 2 * ORB], packed[2 * ORB :]
    return (
        jnp.where(low_z, p, pltpu.roll(p, 16, 1)),
        jnp.where(low_z, pltpu.roll(p, 112, 1), p),
        jnp.concatenate(
            [jnp.where(low_z, q, pltpu.roll(q, 16, 1)), jnp.where(low_z, pltpu.roll(q, 112, 1), q)], axis=0
        ),
    )


def is_even():
    return lax.rem(lax.axis_index("sx"), 2) == 0


def put_messages(planes, mate_ref, across_ref):
    down = fold(planes[0, : 2 * ORB].astype(F32))
    up = fold(planes[1, ORB:].astype(F32))
    even = is_even()
    for i, rows in enumerate((slice(0, 2 * ORB), slice(2 * ORB, ROWS))):
        mate_ref[rows] = jnp.where(even, up[i], down[i]).astype(BF16)
        across_ref[rows] = jnp.where(even, down[i], up[i]).astype(BF16)


def sides(mate, across):
    even = is_even()
    return (jnp.where(even, across, mate), jnp.where(even, mate, across))


def at_end():
    slab = lax.axis_index("sx")
    return (slab == 0) | (slab == lax.axis_size("sx") - 1)


def kept(pattern_ref, r, q):
    slab = lax.axis_index("sx")
    last = pattern_ref.shape[1] - 1
    values = []
    for col in (2 * q, 2 * q + 1):
        apart = abs(col - r - 2)
        if apart == 0:
            values.append(1.0)
        elif apart > 2:
            values.append(0.0)
        else:
            at = jnp.clip(slab - 3 + min(col, r + 2), 0, last)
            values.append(pattern_ref[apart - 1, at].astype(F32))
    return jnp.where(low_half(), values[0], values[1])


def edges_kernel(
    table_ref, pattern_ref, pieces_ref,
    phi_ref, mask_ref, rows_ref, reach_ref, keep_ref, mate_ref, across_ref,
    window_ref, raw_ref, scalar_ref, sems,
):
    first = window_start(table_ref.shape[1])
    table_copy = pltpu.make_async_copy(table_ref.at[:, pl.ds(first, 4 * ORB)], window_ref, sems.at[2])
    table_copy.start()
    pattern_copy = pltpu.make_async_copy(pattern_ref, scalar_ref, sems.at[3])
    pattern_copy.start()
    copies = []
    for i in range(2):
        start = (CX - 1) * PLANE * i
        copies.append(
            pltpu.make_async_copy(pieces_ref.at[:, start : start + PLANE], raw_ref.at[i], sems.at[i])
        )
        copies[i].start()
    cells = cell_features()
    table_copy.wait()
    rows = row_features(window_ref, first)
    rows_ref[...] = rows
    reach = jnp.dot(rows, cells, preferred_element_type=F32)
    reach_ref[...] = reach
    for i in range(2):
        mask_ref[i] = sphere(reach, rows, (CX - 1) * i)
    pattern_copy.wait()
    for r in range(3):
        for q in range(4):
            keep_ref[r : r + 1, 128 * q : 128 * q + 128] = kept(scalar_ref, r, q)
    for i in range(2):
        copies[i].wait()
        phi_ref[i] = raw_ref[i] * mask_ref[i]
    put_messages(phi_ref, mate_ref, across_ref)


def rows_product(a, b):
    return lax.dot_general(a, b, (((1,), (1,)), ((), ())), preferred_element_type=F32)


def energy_kernel(
    rows_ref, reach_ref, pieces_ref, pot_ref, edge_ref, edge_mask_ref,
    phi_ref, mask_ref, energy_ref, part_ref, edge_energy_ref, corr_ref, ham_ref,
):
    rows = rows_ref[...]
    for i in range(2):
        mask = sphere(reach_ref[...], rows, 1 + i)
        mask_ref[i] = mask
        phi_ref[i] = pieces_ref[:, PLANE * (1 + i) : PLANE * (2 + i)] * mask
    weights = in_plane(6, -1)
    for t in range(PLANE // TILE):
        lanes = slice(TILE * t, TILE * t + TILE)
        edge = edge_ref[:, :, lanes].astype(F32)
        mid = phi_ref[:, :, lanes].astype(F32)
        inner = plane_product(phi_ref, weights, -1.0, t)
        outer = plane_product(edge_ref, weights, -1.0, t)
        for i in range(2):
            value = 0.5 * (inner[i] - (edge[i] + mid[1 - i])) + pot_ref[1 + i : 2 + i, lanes] * mid[i]
            energy_ref[i, :, lanes] = value.astype(BF16) * mask_ref[i, :, lanes]
            plane = (CX - 1) * i
            value = 0.5 * (outer[i] - mid[i]) + pot_ref[plane : plane + 1, lanes] * edge[i]
            part_ref[i, :, lanes] = value
            rest = rest_rows(i)
            edge_energy_ref[i, rest, lanes] = value[rest].astype(BF16) * edge_mask_ref[i, rest, lanes]
    mid = jnp.concatenate([phi_ref[0], phi_ref[1]], axis=1)
    both = jnp.concatenate([energy_ref[0], energy_ref[1]], axis=1)
    gram = rows_product(jnp.concatenate([mid, both], axis=0), mid)
    corr = gram[:ROWS]
    ham_ref[...] = gram[ROWS:]
    for i in range(2):
        rest = rest_rows(i)
        gram = rows_product(jnp.concatenate([edge_ref[i], edge_energy_ref[i, rest]], axis=0), edge_ref[i])
        corr = corr + gram[:ROWS]
        ham_ref[rest] += gram[ROWS:]
    corr_ref[...] = corr


def halo_rows(i):
    return slice(0, 2 * ORB) if i == 0 else slice(ORB, ROWS)


def rest_rows(i):
    return slice(2 * ORB, ROWS) if i == 0 else slice(0, ORB)


def bands_kernel(
    across_ref, mate_ref, part_ref, mask_ref, phi_ref, corr_ref, ham_ref, rest_ref,
    energy_ref, own_ref, rows_ref,
):
    volume = 1.0 / (4.0 * CX**3)
    gram = []
    for i, side in enumerate(sides(mate_ref[...].astype(F32), across_ref[...].astype(F32))):
        tiles = unfold(side)
        for t in range(PLANE // 128):
            lanes = slice(128 * t, 128 * t + 128)
            value = part_ref[i, halo_rows(i), lanes] - 0.5 * tiles[t % 3]
            energy_ref[i, halo_rows(i), lanes] = value.astype(BF16) * mask_ref[i, halo_rows(i), lanes]
        gram.append(rows_product(energy_ref[i, halo_rows(i)], phi_ref[i]))
    own_ref[:, :, ROWS:] = jnp.zeros((2, ROWS, TILE - ROWS), F32)
    own_ref[0, :ORB, :ROWS] = (ham_ref[:ORB] + gram[0][:ORB]) * volume
    own_ref[0, ORB : 2 * ORB, :ROWS] = (ham_ref[ORB : 2 * ORB] + gram[0][ORB:] + gram[1][:ORB]) * volume
    own_ref[0, 2 * ORB :, :ROWS] = (ham_ref[2 * ORB :] + gram[1][ORB:]) * volume
    own_ref[1, :, :ROWS] = corr_ref[...] * volume
    tail = jnp.where(low_half(), own_ref[0, :, 128:256], swapped(own_ref[1, :, 128:256]))
    even = is_even()
    for i, value in enumerate((own_ref[0, :, 0:128], own_ref[1, :, 0:128], tail)):
        rows_ref[i] = jnp.where(even, value[ORB:], value[: 2 * ORB]).astype(BF16)


def low_half():
    return iota((1, 128), 1) < 64


def swapped(value):
    return pltpu.roll(value, 64, 1)


def mate_blocks(rows_ref, which):
    tail = rows_ref[2].astype(F32)
    if which == 1:
        tail = swapped(tail)
    return rows_ref[which].astype(F32), jnp.where(low_half(), tail, 0.0)


def shifted(c01, c2x):
    low = low_half()
    turned = swapped(c01)
    return jnp.where(low, 0.0, turned), jnp.where(low, turned, swapped(c2x))


def relay_kernel(own_ref, rows_ref, out_ref):
    even = is_even()
    heads = []
    for which in range(2):
        head, rest = shifted(own_ref[which, :, 0:128], own_ref[which, :, 128:256])
        c01, c2x = mate_blocks(rows_ref, which)
        c01 = jnp.where(even, c01[:ORB], c01[ORB:])
        c2x = jnp.where(even, c2x[:ORB], c2x[ORB:])
        own = slice(ORB, 2 * ORB)
        out_ref[2 * which] = (head[own] + jnp.where(even, c2x, c01)).astype(BF16)
        out_ref[2 * which + 1] = (rest[own] + jnp.where(even, c01, c2x)).astype(BF16)
        out_ref[5 + which] = jnp.where(even, rest[:ORB], rest[2 * ORB :]).astype(BF16)
        heads.append(jnp.where(even, head[:ORB], head[2 * ORB :]))
    out_ref[4] = jnp.where(low_half(), swapped(heads[1]), heads[0]).astype(BF16)


def shared_head(tile, which):
    tile = tile.astype(F32)
    if which == 1:
        tile = swapped(tile)
    return jnp.where(low_half(), 0.0, tile)


def pick_kernel(both_ref, other_ref, forward_ref):
    even = is_even()
    for i in range(7):
        value = jnp.where(even, both_ref[0, i].astype(F32), both_ref[1, i].astype(F32))
        value = jnp.where(at_end(), 0.0, value).astype(BF16)
        other_ref[i] = value
        if i >= 4:
            forward_ref[i - 4] = value


def put_gradient(theta, orbital_ref, energy_ref, mask_ref, out_ref):
    for i in range(2):
        for t in range(PLANE // TILE):
            lanes = slice(TILE * t, TILE * t + TILE)
            fix = jnp.dot(theta, orbital_ref[i, :, lanes], preferred_element_type=F32)
            value = energy_ref[i, :, lanes].astype(F32) - fix
            out_ref[i, :, lanes] = value.astype(BF16) * mask_ref[i, :, lanes]


def split(value):
    high = value.astype(BF16)
    return high, (value - high.astype(F32)).astype(BF16)


def fine_product(a, b):
    return rows_product(a[0], b[0]) + (rows_product(a[0], b[1]) + rows_product(a[1], b[0]))


def theta_kernel(
    keep_ref, own_ref, rows_ref, other_ref,
    window_ref, theta_ref,
    ham_ref, inv_ref,
):
    even = is_even()
    low = low_half()
    zero = jnp.zeros((ORB, 128), F32)
    for which, band_ref in enumerate((ham_ref, inv_ref)):
        near, rest = shifted(*mate_blocks(rows_ref, which))
        ahead = other_ref[2 * which].astype(F32)
        beside = other_ref[2 * which + 1].astype(F32)
        head = shared_head(other_ref[4], which)
        tail = other_ref[5 + which].astype(F32)
        got_even = (
            (ahead, beside, zero, zero),
            (head, tail + near[:ORB], rest[:ORB], zero),
            (zero, near[ORB:], rest[ORB:], zero),
        )
        got_odd = (
            (near[:ORB], rest[:ORB], zero, zero),
            (near[ORB:], rest[ORB:] + head, tail, zero),
            (zero, jnp.where(low, 0.0, ahead), beside, jnp.where(low, ahead, 0.0)),
        )
        for r in range(3):
            for q in range(4):
                value = jnp.where(even, got_even[r][q], got_odd[r][q])
                if q in (1, 2):
                    value = value + own_ref[which, ORB * r : ORB * r + ORB, 128 * q - 128 : 128 * q]
                value = value * keep_ref[r : r + 1, 128 * q : 128 * q + 128]
                if which == 1:
                    on = iota((ORB, 128), 0) + (ORB * (r + 2) - 128 * q) == iota((ORB, 128), 1)
                    value = jnp.where(on, 2.0, 0.0) - value
                band_ref[ORB * r : ORB * r + ORB, 128 * q : 128 * q + 128] = value
    ham, inv = split(ham_ref[...]), split(inv_ref[...])
    theta_ref[...] = fine_product(ham, inv)
    for which, (high, _) in enumerate((ham, inv)):
        window_ref[which] = jnp.where(even, high[:, 256:512].astype(F32), high[:, 0:256].astype(F32)).astype(BF16)


def gradient_kernel(
    keep_ref, relayed_ref, bands_ref, base_ref,
    edge_ref, edge_energy_ref, edge_mask_ref,
    edge_grad_ref, theta_ref, mate_ref, across_ref,
    window_ref, total_ref,
):
    even = is_even()
    low = low_half()
    more = []
    for which in range(2):
        front = swapped(shared_head(relayed_ref[0], which))
        turned = swapped(relayed_ref[1 + which].astype(F32))
        tiles = []
        for q, value in enumerate((jnp.where(low, front, turned), jnp.where(low, turned, 0.0))):
            at_even = keep_ref[2:3, 128 * q + 256 : 128 * q + 384]
            tiles.append(value * jnp.where(even, at_even, keep_ref[0:1, 128 * q : 128 * q + 128]))
        more.append(jnp.concatenate(tiles, axis=1))
    first, third = slice(0, ORB), slice(2 * ORB, ROWS)
    window_ref[...] = bands_ref[0]
    window_ref[first] = (bands_ref[0, first].astype(F32) + jnp.where(even, 0.0, more[0])).astype(BF16)
    window_ref[third] = (bands_ref[0, third].astype(F32) + jnp.where(even, more[0], 0.0)).astype(BF16)
    more = [value.astype(BF16) for value in more]
    column = rows_product(window_ref[...], more[1])
    row = rows_product(more[0], bands_ref[1])
    total_ref[...] = base_ref[...]
    total_ref[first] += jnp.where(even, 0.0, row)
    total_ref[third] += jnp.where(even, row, 0.0)
    total_ref[:, first] -= jnp.where(even, 0.0, column)
    total_ref[:, third] -= jnp.where(even, column, 0.0)
    theta = total_ref[...].astype(BF16)
    theta_ref[...] = theta
    put_gradient(theta, edge_ref, edge_energy_ref, edge_mask_ref, edge_grad_ref)
    put_messages(edge_grad_ref, mate_ref, across_ref)


def smooth_kernel(
    theta_ref, phi_ref, energy_ref, edge_ref, mask_ref, edge_mask_ref,
    out_ref, part_ref,
    grad_ref, done_ref, rest_ref, sems,
):
    put_gradient(theta_ref[...], phi_ref, energy_ref, mask_ref, grad_ref)
    weights = in_plane(8, 1)
    copies = []

    def send(source, rows, start, sem):
        copies.append(pltpu.make_async_copy(source, out_ref.at[rows, start : start + TILE], sem))
        copies[-1].start()

    for t in range(PLANE // TILE):
        lanes = slice(TILE * t, TILE * t + TILE)
        edge = edge_ref[:, :, lanes].astype(F32)
        mid = grad_ref[:, :, lanes].astype(F32)
        inner = plane_product(grad_ref, weights, 1.0, t)
        outer = plane_product(edge_ref, weights, 1.0, t)
        for i in range(2):
            value = (inner[i] + (edge[i] + mid[1 - i])) * (1.0 / 32.0)
            done_ref[i, :, lanes] = value.astype(BF16) * mask_ref[i, :, lanes]
            value = outer[i] + mid[i]
            part_ref[i, :, lanes] = value
            rest = rest_rows(i)
            value = value[rest] * (1.0 / 32.0)
            rest_ref[i, :, lanes] = value.astype(BF16) * edge_mask_ref[i, rest, lanes]
        for i in range(2):
            send(done_ref.at[i, :, lanes], slice(0, ROWS), PLANE * (1 + i) + TILE * t, sems.at[t, i])
            send(rest_ref.at[i, :, lanes], rest_rows(i), PLANE * (CX - 1) * i + TILE * t, sems.at[t, 2 + i])
    for copy in copies:
        copy.wait()


def finish_kernel(across_ref, mate_ref, part_ref, mask_ref, inner_ref, out_ref, done_ref, sems):
    halos = [unfold(side) for side in sides(mate_ref[...].astype(F32), across_ref[...].astype(F32))]
    copies = []
    for i in range(2):
        start = PLANE * (CX - 1) * i
        for half in range(2):
            rows = slice(ORB * (half + i), ORB * (half + i) + ORB)
            got = slice(ORB * half, ORB * half + ORB)
            for t in range(PLANE // 128):
                lanes = slice(128 * t, 128 * t + 128)
                value = (part_ref[i, rows, lanes] + halos[i][t % 3][got]) * (1.0 / 32.0)
                done_ref[i, got, lanes] = value.astype(BF16) * mask_ref[i, rows, lanes]
            copies.append(
                pltpu.make_async_copy(
                    done_ref.at[i, got], out_ref.at[rows, start : start + PLANE], sems.at[i, half]
                )
            )
            copies[-1].start()
    for copy in copies:
        copy.wait()


def shape(*dims, dtype=BF16):
    return jax.ShapeDtypeStruct(dims, dtype)


def cost(flops, moved):
    return pl.CostEstimate(flops=flops, bytes_accessed=moved, transcendentals=0)


PARAMS = pltpu.CompilerParams(vmem_limit_bytes=32 * 1024 * 1024)
WHOLE = pl.BlockSpec(memory_space=pltpu.VMEM)
FAR = pl.BlockSpec(memory_space=pltpu.HBM)


def far(value):
    return pltpu.with_memory_space_constraint(value, pltpu.HBM)


def per_device(pieces, potential, centers, pattern):
    count = lax.axis_size("sx")
    mates = [(i, i ^ 1) for i in range(count)]
    others = [(i, i + 1 if i % 2 else i - 1) for i in range(1, count - 1)]
    groups = lax.axis_size("grp")
    pairs = [[g * count + i, g * count + i + 1] for g in range(groups) for i in range(1, count - 1, 2)]
    ends = [g * count + end for g in range(groups) for end in (0, count - 1)]
    pairs += [[ends[i], ends[i + 2]] for i in range(len(ends)) if i % 4 < 2] if groups % 2 == 0 else [
        [ends[2 * i], ends[2 * i + 1]] for i in range(groups)
    ]

    def to_mate(value):
        return lax.ppermute(value, "sx", mates)

    def across(value):
        return lax.ppermute(value, "sx", others)

    def gathered(value):
        return lax.all_gather(value, ("grp", "sx"), axis_index_groups=pairs)

    table = centers.T
    patterns = pattern.T
    pair = shape(2, ROWS, PLANE)

    edge, edge_mask, rows, reach, keep, for_mate, for_other = pl.pallas_call(
        edges_kernel,
        out_shape=(
            pair, pair, shape(ROWS, 16), shape(ROWS, PLANE, dtype=F32), shape(3, 8 * ORB, dtype=F32),
            shape(ROWS, 128), shape(ROWS, 128),
        ),
        in_specs=[FAR, FAR, FAR],
        out_specs=(WHOLE,) * 7,
        scratch_shapes=[
            pltpu.VMEM((4, 4 * ORB), jnp.int32),
            pltpu.VMEM((2, ROWS, PLANE), BF16),
            pltpu.SMEM(patterns.shape, jnp.int32),
            pltpu.SemaphoreType.DMA((4,)),
        ],
        compiler_params=PARAMS,
        cost_estimate=cost(10**8, 10**6),
        name="edges",
    )(far(table), far(patterns), far(pieces))
    other_side = across(for_other)
    mate_side = to_mate(for_mate)

    mid, mid_mask, mid_energy, part, rest_energy, corr, ham = pl.pallas_call(
        energy_kernel,
        out_shape=(
            pair, pair, pair, shape(2, ROWS, PLANE, dtype=F32), pair,
            shape(ROWS, ROWS, dtype=F32), shape(ROWS, ROWS, dtype=F32),
        ),
        in_specs=[WHOLE] * 6,
        out_specs=(WHOLE,) * 7,
        compiler_params=PARAMS,
        cost_estimate=cost(4 * 10**9, 10**7),
        name="energy",
    )(rows, reach, pieces, potential, edge, edge_mask)

    edge_energy, own, for_mate = pl.pallas_call(
        bands_kernel,
        out_shape=(pair, shape(2, ROWS, TILE, dtype=F32), shape(3, 2 * ORB, 128)),
        in_specs=[WHOLE] * 8,
        out_specs=(WHOLE,) * 3,
        input_output_aliases={7: 0},
        compiler_params=PARAMS,
        cost_estimate=cost(10**9, 10**7),
        name="bands",
    )(other_side, mate_side, part, edge_mask, edge, corr, ham, rest_energy)
    mate_rows = to_mate(for_mate)
    for_other = pl.pallas_call(
        relay_kernel,
        out_shape=shape(7, ORB, 128),
        in_specs=[WHOLE] * 2,
        out_specs=WHOLE,
        compiler_params=PARAMS,
        cost_estimate=cost(10**6, 10**6),
        name="relay",
    )(own, mate_rows)
    other_rows, forward = pl.pallas_call(
        pick_kernel,
        out_shape=(shape(7, ORB, 128), shape(3, ORB, 128)),
        in_specs=[WHOLE],
        out_specs=(WHOLE,) * 2,
        compiler_params=PARAMS,
        cost_estimate=cost(10**6, 10**6),
        name="pick",
    )(gathered(for_other))
    relayed = to_mate(forward)

    bands, base = pl.pallas_call(
        theta_kernel,
        out_shape=(shape(2, ROWS, TILE), shape(ROWS, ROWS, dtype=F32)),
        in_specs=[WHOLE] * 4,
        out_specs=(WHOLE,) * 2,
        scratch_shapes=[pltpu.VMEM((ROWS, 8 * ORB), F32), pltpu.VMEM((ROWS, 8 * ORB), F32)],
        compiler_params=PARAMS,
        cost_estimate=cost(10**9, 4 * 10**6),
        name="theta",
    )(keep, own, mate_rows, other_rows)
    edge_grad, theta, for_mate, for_other = pl.pallas_call(
        gradient_kernel,
        out_shape=(pair, shape(ROWS, ROWS), shape(ROWS, 128), shape(ROWS, 128)),
        in_specs=[WHOLE] * 7,
        out_specs=(WHOLE,) * 4,
        scratch_shapes=[pltpu.VMEM((ROWS, TILE), BF16), pltpu.VMEM((ROWS, ROWS), F32)],
        compiler_params=PARAMS,
        cost_estimate=cost(10**9, 10**7),
        name="gradient",
    )(keep, relayed, bands, base, edge, edge_energy, edge_mask)
    other_side = across(for_other)
    mate_side = to_mate(for_mate)

    inner, part = pl.pallas_call(
        smooth_kernel,
        out_shape=(pltpu.HBM((ROWS, CX * PLANE), BF16), shape(2, ROWS, PLANE, dtype=F32)),
        in_specs=[WHOLE] * 6,
        out_specs=(FAR, WHOLE),
        scratch_shapes=[
            pltpu.VMEM((2, ROWS, PLANE), BF16),
            pltpu.VMEM((2, ROWS, PLANE), BF16),
            pltpu.VMEM((2, ORB, PLANE), BF16),
            pltpu.SemaphoreType.DMA((PLANE // TILE, 4)),
        ],
        compiler_params=PARAMS,
        cost_estimate=cost(2 * 10**9, 10**7),
        name="smooth",
    )(theta, mid, mid_energy, edge_grad, mid_mask, edge_mask)

    return pl.pallas_call(
        finish_kernel,
        out_shape=pltpu.HBM((ROWS, CX * PLANE), BF16),
        in_specs=[WHOLE] * 4 + [FAR],
        out_specs=FAR,
        scratch_shapes=[pltpu.VMEM((2, 2 * ORB, PLANE), BF16), pltpu.SemaphoreType.DMA((2, 2))],
        input_output_aliases={4: 0},
        compiler_params=PARAMS,
        cost_estimate=cost(10**7, 10**7),
        name="finish",
    )(other_side, mate_side, part, edge_mask, inner)


def solution(mesh):
    return jax.shard_map(
        per_device,
        mesh=mesh,
        in_specs=(P(("grp", "sx"), None), P(("grp", "sx"), None), P("grp", None), P("grp", None)),
        out_specs=P(("grp", "sx"), None),
        check_vma=False,
    )
```

```python
import functools

import jax
import jax.numpy as jnp
from jax import lax
from jax.experimental import pallas as pl
from jax.experimental.pallas import tpu as pltpu
from jax.sharding import PartitionSpec as P

ORB = 64
CX = 4
NY = 32
NZ = 32
ROWS = 3 * ORB
PLANE = NY * NZ
TILE = 256
WINDOW = 6 * ORB
FACE = ROWS + ROWS // 2
F32 = jnp.float32
BF16 = jnp.bfloat16


def iota(shape, dim):
    return lax.broadcasted_iota(jnp.int32, shape, dim)


def window_start(width):
    slab = lax.axis_index("sx")
    first = jnp.clip(slab * ORB - 2 * ORB, 0, width - WINDOW) // 128 * 128
    return pl.multiple_of(first, 128)


def row_features(window_ref, first):
    slab = lax.axis_index("sx")
    count = lax.axis_size("sx")
    window = window_ref[...]
    shift = slab * ORB - 2 * ORB - first
    window = pltpu.roll(jnp.concatenate([window, window], axis=0), lax.rem(WINDOW - shift, WINDOW), 1)
    lane = iota((1, WINDOW), 1)
    block = slab - 2 + lane // ORB
    valid = (block >= 0) & (block < count)
    cx = window[0:1] - slab * CX
    cy = window[1:2]
    cz = window[2:3]
    r = window[3:4]
    const = cx * cx + cy * cy + cz * cz - r * r
    const = jnp.where(valid, const, 65535)
    cx = jnp.where(valid, cx, 0)
    cy = jnp.where(valid, cy, 0)
    cz = jnp.where(valid, cz, 0)
    k = iota((16, WINDOW), 0)
    feats = jnp.where(k == 0, 1, 0)
    feats = jnp.where(k == 1, 256, feats)
    feats = jnp.where(k == 2, cy, feats)
    feats = jnp.where(k == 3, cz, feats)
    feats = jnp.where(k == 4, const & 255, feats)
    feats = jnp.where(k == 5, const >> 8, feats)
    feats = jnp.where(k == 6, cx, feats)
    return jnp.transpose(feats.astype(F32))[: 5 * ORB].astype(BF16)


def cell_features():
    k = iota((16, PLANE), 0)
    cell = iota((16, PLANE), 1)
    y = cell >> 5
    z = cell & 31
    sq = y * y + z * z
    feats = jnp.where(k == 0, sq & 255, 0)
    feats = jnp.where(k == 1, sq >> 8, feats)
    feats = jnp.where(k == 2, -2 * y, feats)
    feats = jnp.where(k == 3, -2 * z, feats)
    feats = jnp.where(k == 4, 1, feats)
    feats = jnp.where(k == 5, 256, feats)
    return feats.astype(F32).astype(BF16)


def sphere(reach, rows, plane):
    bound = rows[:, 6:7].astype(F32) * (2.0 * plane) - float(plane * plane)
    return jnp.where(reach <= bound, 1.0, 0.0).astype(BF16)


def in_plane(center, beside):
    k = iota((TILE, TILE), 0)
    n = iota((TILE, TILE), 1)
    diff = k - n
    near_y = (diff == NZ) | (diff == -NZ)
    near_z = ((diff == 1) | (diff == -1)) & ((k >> 5) == (n >> 5))
    w = jnp.where(near_y | near_z, float(beside), 0.0)
    return jnp.where(diff == 0, float(center), w).astype(BF16)


def plane_product(ref, weights, beside, t):
    start = TILE * t
    values = ref[:, :, start : start + TILE].reshape(2 * ROWS, TILE)
    out = jnp.dot(values, weights, preferred_element_type=F32).reshape(2, ROWS, TILE)
    lane = iota((1, 1, 128), 2)
    first, last = out[:, :, :128], out[:, :, 128:]
    if t > 0:
        turned = pltpu.roll(ref[:, :, start - 128 : start].astype(F32), NZ, 2)
        turned = jnp.where(lane < NZ, turned, 0.0)
        first = first + turned if beside > 0 else first - turned
    if start + TILE < PLANE:
        turned = pltpu.roll(ref[:, :, start + TILE : start + TILE + 128].astype(F32), 128 - NZ, 2)
        turned = jnp.where(lane >= 128 - NZ, turned, 0.0)
        last = last + turned if beside > 0 else last - turned
    return jnp.concatenate([first, last], axis=2)


def fold(values):
    tiles = [values[:, 128 * t : 128 * t + 128] for t in range(PLANE // 128)]
    a, b, c = (sum(tiles[t::3][1:], tiles[t]) for t in range(3))
    low_z = (iota((1, 128), 1) & 31) < 16
    half = values.shape[0] // 2
    top, bottom = c[:half], c[half:]
    return (
        jnp.where(low_z, a + pltpu.roll(a, 112, 1), b + pltpu.roll(b, 16, 1)),
        jnp.where(low_z, top + pltpu.roll(top, 112, 1), bottom + pltpu.roll(bottom, 16, 1)),
    )


def unfold(packed):
    low_z = (iota((1, 128), 1) & 31) < 16
    count = packed.shape[0] // 3 * 2
    p, q = packed[:count], packed[count:]
    return (
        jnp.where(low_z, p, pltpu.roll(p, 16, 1)),
        jnp.where(low_z, pltpu.roll(p, 112, 1), p),
        jnp.concatenate(
            [jnp.where(low_z, q, pltpu.roll(q, 16, 1)), jnp.where(low_z, pltpu.roll(q, 112, 1), q)], axis=0
        ),
    )


def is_even():
    return lax.rem(lax.axis_index("sx"), 2) == 0


def put_messages(planes, mate_ref, across_ref):
    down = fold(planes[0, : 2 * ORB].astype(F32))
    up = fold(planes[1, ORB:].astype(F32))
    even = is_even()
    for i, rows in enumerate((slice(0, 2 * ORB), slice(2 * ORB, ROWS))):
        mate_ref[rows] = jnp.where(even, up[i], down[i]).astype(BF16)
        across_ref[rows] = jnp.where(even, down[i], up[i]).astype(BF16)


def sides(mate, across):
    even = is_even()
    return (jnp.where(even, across, mate), jnp.where(even, mate, across))


def at_end():
    slab = lax.axis_index("sx")
    return (slab == 0) | (slab == lax.axis_size("sx") - 1)


def kept(pattern_ref, r, q):
    slab = lax.axis_index("sx")
    last = pattern_ref.shape[1] - 1
    values = []
    for col in (2 * q, 2 * q + 1):
        apart = abs(col - r - 2)
        if apart == 0:
            values.append(1.0)
        elif apart > 2:
            values.append(0.0)
        else:
            at = jnp.clip(slab - 3 + min(col, r + 2), 0, last)
            values.append(pattern_ref[apart - 1, at].astype(F32))
    return jnp.where(low_half(), values[0], values[1])


def edges_kernel(
    table_ref, pattern_ref, pieces_ref,
    phi_ref, mask_ref, rows_ref, reach_ref, keep_ref, mate_ref, across_ref,
    window_ref, raw_ref, scalar_ref, sems,
):
    first = window_start(table_ref.shape[1])
    table_copy = pltpu.make_async_copy(table_ref.at[:, pl.ds(first, WINDOW)], window_ref, sems.at[2])
    table_copy.start()
    pattern_copy = pltpu.make_async_copy(pattern_ref, scalar_ref, sems.at[3])
    pattern_copy.start()
    copies = []
    for i in range(2):
        start = (CX - 1) * PLANE * i
        copies.append(
            pltpu.make_async_copy(pieces_ref.at[:, start : start + PLANE], raw_ref.at[i], sems.at[i])
        )
        copies[i].start()
    cells = cell_features()
    table_copy.wait()
    blocks = row_features(window_ref, first)
    rows_ref[...] = blocks
    rows = blocks[ORB : 4 * ORB]
    reach = jnp.dot(rows, cells, preferred_element_type=F32)
    reach_ref[...] = reach
    for i in range(2):
        mask_ref[i] = sphere(reach, rows, (CX - 1) * i)
    pattern_copy.wait()
    for r in range(3):
        for q in range(4):
            keep_ref[r : r + 1, 128 * q : 128 * q + 128] = kept(scalar_ref, r, q)
    for i in range(2):
        copies[i].wait()
        phi_ref[i] = raw_ref[i] * mask_ref[i]
    even = is_even()
    face = jnp.where(even, phi_ref[1, ORB:].astype(F32), phi_ref[0, : 2 * ORB].astype(F32))
    mate_ref[: 2 * ORB], mate_ref[2 * ORB :] = (value.astype(BF16) for value in fold(face))
    face = jnp.where(even, phi_ref[0].astype(F32), phi_ref[1].astype(F32))
    across_ref[:ROWS], across_ref[ROWS:] = (value.astype(BF16) for value in fold(face))


def rows_product(a, b):
    return lax.dot_general(a, b, (((1,), (1,)), ((), ())), preferred_element_type=F32)


def energy_kernel(
    rows_ref, reach_ref, pieces_ref, pot_ref, edge_ref, edge_mask_ref,
    phi_ref, mask_ref, energy_ref, part_ref, edge_energy_ref, corr_ref, ham_ref,
):
    rows = rows_ref[ORB : 4 * ORB]
    for i in range(2):
        mask = sphere(reach_ref[...], rows, 1 + i)
        mask_ref[i] = mask
        phi_ref[i] = pieces_ref[:, PLANE * (1 + i) : PLANE * (2 + i)] * mask
    weights = in_plane(6, -1)
    for t in range(PLANE // TILE):
        lanes = slice(TILE * t, TILE * t + TILE)
        edge = edge_ref[:, :, lanes].astype(F32)
        mid = phi_ref[:, :, lanes].astype(F32)
        inner = plane_product(phi_ref, weights, -1.0, t)
        outer = plane_product(edge_ref, weights, -1.0, t)
        for i in range(2):
            value = 0.5 * (inner[i] - (edge[i] + mid[1 - i])) + pot_ref[1 + i : 2 + i, lanes] * mid[i]
            energy_ref[i, :, lanes] = value.astype(BF16) * mask_ref[i, :, lanes]
            plane = (CX - 1) * i
            value = 0.5 * (outer[i] - mid[i]) + pot_ref[plane : plane + 1, lanes] * edge[i]
            part_ref[i, :, lanes] = value
            rest = rest_rows(i)
            edge_energy_ref[i, rest, lanes] = value[rest].astype(BF16) * edge_mask_ref[i, rest, lanes]
    mid = jnp.concatenate([phi_ref[0], phi_ref[1]], axis=1)
    both = jnp.concatenate([energy_ref[0], energy_ref[1]], axis=1)
    gram = rows_product(jnp.concatenate([mid, both], axis=0), mid)
    corr = gram[:ROWS]
    ham_ref[...] = gram[ROWS:]
    for i in range(2):
        rest = rest_rows(i)
        gram = rows_product(jnp.concatenate([edge_ref[i], edge_energy_ref[i, rest]], axis=0), edge_ref[i])
        corr = corr + gram[:ROWS]
        ham_ref[rest] += gram[ROWS:]
    corr_ref[...] = corr


def halo_rows(i):
    return slice(0, 2 * ORB) if i == 0 else slice(ORB, ROWS)


def rest_rows(i):
    return slice(2 * ORB, ROWS) if i == 0 else slice(0, ORB)


def bands_kernel(
    mate_ref, part_ref, mask_ref, phi_ref, corr_ref, ham_ref, rest_ref,
    energy_ref, own_ref, rows_ref,
):
    volume = 1.0 / (4.0 * CX**3)
    gram = []
    mate = mate_ref[...].astype(F32)
    for i, side in enumerate(sides(mate, jnp.zeros_like(mate))):
        tiles = unfold(side)
        for t in range(PLANE // 128):
            lanes = slice(128 * t, 128 * t + 128)
            value = part_ref[i, halo_rows(i), lanes] - 0.5 * tiles[t % 3]
            energy_ref[i, halo_rows(i), lanes] = value.astype(BF16) * mask_ref[i, halo_rows(i), lanes]
        gram.append(rows_product(energy_ref[i, halo_rows(i)], phi_ref[i]))
    own_ref[:, :, ROWS:] = jnp.zeros((2, ROWS, TILE - ROWS), F32)
    own_ref[0, :ORB, :ROWS] = (ham_ref[:ORB] + gram[0][:ORB]) * volume
    own_ref[0, ORB : 2 * ORB, :ROWS] = (ham_ref[ORB : 2 * ORB] + gram[0][ORB:] + gram[1][:ORB]) * volume
    own_ref[0, 2 * ORB :, :ROWS] = (ham_ref[2 * ORB :] + gram[1][ORB:]) * volume
    own_ref[1, :, :ROWS] = corr_ref[...] * volume
    tail = jnp.where(low_half(), own_ref[0, :, 128:256], swapped(own_ref[1, :, 128:256]))
    even = is_even()
    for i, value in enumerate((own_ref[0, :, 0:128], own_ref[1, :, 0:128], tail)):
        rows_ref[i] = jnp.where(even, value[ORB:], value[: 2 * ORB]).astype(BF16)


def low_half():
    return iota((1, 128), 1) < 64


def swapped(value):
    return pltpu.roll(value, 64, 1)


def mate_blocks(rows_ref, which):
    tail = rows_ref[2].astype(F32)
    if which == 1:
        tail = swapped(tail)
    return rows_ref[which].astype(F32), jnp.where(low_half(), tail, 0.0)


def shifted(c01, c2x):
    low = low_half()
    turned = swapped(c01)
    return jnp.where(low, 0.0, turned), jnp.where(low, turned, swapped(c2x))


def relay_kernel(own_ref, rows_ref, face_ref, out_ref):
    even = is_even()
    heads = []

    def put(i, value):
        out_ref[ORB * i : ORB * i + ORB] = value.astype(BF16)

    for which in range(2):
        head, rest = shifted(own_ref[which, :, 0:128], own_ref[which, :, 128:256])
        c01, c2x = mate_blocks(rows_ref, which)
        c01 = jnp.where(even, c01[:ORB], c01[ORB:])
        c2x = jnp.where(even, c2x[:ORB], c2x[ORB:])
        own = slice(ORB, 2 * ORB)
        put(2 * which, head[own] + jnp.where(even, c2x, c01))
        put(2 * which + 1, rest[own] + jnp.where(even, c01, c2x))
        put(5 + which, jnp.where(even, rest[:ORB], rest[2 * ORB :]))
        heads.append(jnp.where(even, head[:ORB], head[2 * ORB :]))
    put(4, jnp.where(low_half(), swapped(heads[1]), heads[0]))
    out_ref[7 * ORB :] = face_ref[...]


def around_kernel(rows_ref, mask_ref):
    even = is_even()
    rows = jnp.where(even, rows_ref[:ROWS].astype(F32), rows_ref[2 * ORB :].astype(F32))
    reach = jnp.dot(rows.astype(BF16), cell_features(), preferred_element_type=F32)
    plane = jnp.where(even, -1.0, float(CX))
    bound = rows[:, 6:7] * (2.0 * plane) - plane * plane
    mask_ref[...] = jnp.where(reach <= bound, 1.0, 0.0).astype(BF16)


def shared_head(tile, which):
    tile = tile.astype(F32)
    if which == 1:
        tile = swapped(tile)
    return jnp.where(low_half(), 0.0, tile)


def face_kernel(
    both_ref, around_ref, phi_ref, mask_ref, part_ref, energy_in_ref,
    energy_ref, other_ref, extra_ref, forward_ref,
    beyond_ref, halo_ref, back_ref, work_ref,
):
    even = is_even()
    low = low_half()
    scale = -0.5 / (4.0 * CX**3)

    def got(start, size):
        rows = slice(start, start + size)
        value = jnp.where(even, both_ref[0, rows].astype(F32), both_ref[1, rows].astype(F32))
        return jnp.where(at_end(), 0.0, value)

    tiles = [got(ORB * i, ORB) for i in range(7)]
    for i in range(7):
        other_ref[i] = tiles[i].astype(BF16)
    spread = unfold(got(7 * ORB, FACE))
    for t in range(PLANE // 128):
        lanes = slice(128 * t, 128 * t + 128)
        beyond_ref[:, lanes] = spread[t % 3].astype(BF16) * around_ref[:, lanes]
    extra_ref[...] = jnp.zeros((ROWS, 8 * ORB), F32)
    work_ref[:, :, ROWS:] = jnp.zeros((2, 2 * ORB, TILE - ROWS), F32)
    head, tail = shared_head(tiles[4], 1), tiles[6]
    forward_ref[2] = jnp.where(low, swapped(head), swapped(tail)).astype(BF16)
    forward_ref[3] = jnp.where(low, swapped(tail), 0.0).astype(BF16)

    def add_face(i):
        here = halo_rows(i)
        there = slice(ORB, ROWS) if i == 0 else slice(0, 2 * ORB)
        for t in range(PLANE // 128):
            lanes = slice(128 * t, 128 * t + 128)
            value = spread[t % 3][there]
            mask = mask_ref[i, here, lanes]
            halo_ref[:, lanes] = value.astype(BF16) * mask
            energy_ref[i, here, lanes] = (part_ref[i, here, lanes] - 0.5 * value).astype(BF16) * mask
            back_ref[:, lanes] = phi_ref[i, here, lanes] * around_ref[there, lanes]
        work_ref[0, :, :ROWS] = rows_product(halo_ref[...], phi_ref[i]) * scale
        work_ref[1, :, :ROWS] = rows_product(back_ref[...], beyond_ref[...]) * scale
        x, y = work_ref[0, :, 0:128], work_ref[0, :, 128:256]
        a, b = shifted(work_ref[1, :, 0:128], work_ref[1, :, 128:256])
        if i == 0:
            extra_ref[here, 0:128] = a
            extra_ref[here, 128:256] = b + x
            extra_ref[here, 256:384] = y
            own = slice(ORB, 2 * ORB)
        else:
            extra_ref[here, 128:256] = a + x
            extra_ref[here, 256:384] = b + y
            own = slice(0, ORB)
        a = swapped(shared_head(tiles[4], 0) + a[own])
        b = swapped(tiles[5] + b[own])
        x, y = swapped(x[own]), swapped(y[own])
        if i == 0:
            forward_ref[0] = jnp.where(low, a, b + x).astype(BF16)
            forward_ref[1] = jnp.where(low, b + x, y).astype(BF16)
        else:
            forward_ref[0] = jnp.where(low, a + x, b + y).astype(BF16)
            forward_ref[1] = jnp.where(low, b, x).astype(BF16)

    pl.when(even)(lambda: add_face(0))
    pl.when(jnp.logical_not(even))(lambda: add_face(1))


def put_gradient(theta, orbital_ref, energy_ref, mask_ref, out_ref):
    for i in range(2):
        for t in range(PLANE // TILE):
            lanes = slice(TILE * t, TILE * t + TILE)
            fix = jnp.dot(theta, orbital_ref[i, :, lanes], preferred_element_type=F32)
            value = energy_ref[i, :, lanes].astype(F32) - fix
            out_ref[i, :, lanes] = value.astype(BF16) * mask_ref[i, :, lanes]


def split(value):
    high = value.astype(BF16)
    return high, (value - high.astype(F32)).astype(BF16)


def fine_product(a, b):
    return rows_product(a[0], b[0]) + (rows_product(a[0], b[1]) + rows_product(a[1], b[0]))


def theta_kernel(
    keep_ref, own_ref, rows_ref, other_ref, extra_ref,
    window_ref, theta_ref,
    ham_ref, inv_ref,
):
    even = is_even()
    low = low_half()
    zero = jnp.zeros((ORB, 128), F32)
    for which, band_ref in enumerate((ham_ref, inv_ref)):
        near, rest = shifted(*mate_blocks(rows_ref, which))
        ahead = other_ref[2 * which].astype(F32)
        beside = other_ref[2 * which + 1].astype(F32)
        head = shared_head(other_ref[4], which)
        tail = other_ref[5 + which].astype(F32)
        got_even = (
            (ahead, beside, zero, zero),
            (head, tail + near[:ORB], rest[:ORB], zero),
            (zero, near[ORB:], rest[ORB:], zero),
        )
        got_odd = (
            (near[:ORB], rest[:ORB], zero, zero),
            (near[ORB:], rest[ORB:] + head, tail, zero),
            (zero, jnp.where(low, 0.0, ahead), beside, jnp.where(low, ahead, 0.0)),
        )
        for r in range(3):
            for q in range(4):
                value = jnp.where(even, got_even[r][q], got_odd[r][q])
                if q in (1, 2):
                    value = value + own_ref[which, ORB * r : ORB * r + ORB, 128 * q - 128 : 128 * q]
                if which == 0:
                    value = value + extra_ref[ORB * r : ORB * r + ORB, 128 * q : 128 * q + 128]
                value = value * keep_ref[r : r + 1, 128 * q : 128 * q + 128]
                if which == 1:
                    on = iota((ORB, 128), 0) + (ORB * (r + 2) - 128 * q) == iota((ORB, 128), 1)
                    value = jnp.where(on, 2.0, 0.0) - value
                band_ref[ORB * r : ORB * r + ORB, 128 * q : 128 * q + 128] = value
    ham, inv = split(ham_ref[...]), split(inv_ref[...])
    theta_ref[...] = fine_product(ham, inv)
    for which, (high, _) in enumerate((ham, inv)):
        quarter = [high[:, 128 * q : 128 * q + 128].astype(F32) for q in range(4)]
        window_ref[which, :, 0:128] = jnp.where(even, quarter[2], quarter[0]).astype(BF16)
        last = jnp.where(even, jnp.where(low, quarter[3], quarter[1]), quarter[1])
        window_ref[which, :, 128:256] = last.astype(BF16)


def gradient_kernel(
    keep_ref, relayed_ref, bands_ref, base_ref,
    edge_ref, edge_energy_ref, edge_mask_ref,
    edge_grad_ref, theta_ref, mate_ref, across_ref,
    window_ref, total_ref,
):
    even = is_even()
    low = low_half()
    more = []
    kept_even = (keep_ref[2:3, 256:384], jnp.where(low, keep_ref[2:3, 384:512], keep_ref[2:3, 128:256]))
    kept_odd = (keep_ref[0:1, 0:128], keep_ref[0:1, 128:256])
    for which in range(2):
        tiles = []
        for q in range(2):
            value = relayed_ref[2 * which + q].astype(F32)
            tiles.append(value * jnp.where(even, kept_even[q], kept_odd[q]))
        more.append(jnp.concatenate(tiles, axis=1))
    first, third = slice(0, ORB), slice(2 * ORB, ROWS)
    window_ref[...] = bands_ref[0]
    window_ref[first] = (bands_ref[0, first].astype(F32) + jnp.where(even, 0.0, more[0])).astype(BF16)
    window_ref[third] = (bands_ref[0, third].astype(F32) + jnp.where(even, more[0], 0.0)).astype(BF16)
    more = [value.astype(BF16) for value in more]
    column = rows_product(window_ref[...], more[1])
    row = rows_product(more[0], bands_ref[1])
    total_ref[...] = base_ref[...]
    total_ref[first] += jnp.where(even, 0.0, row)
    total_ref[third] += jnp.where(even, row, 0.0)
    total_ref[:, first] -= jnp.where(even, 0.0, column)
    total_ref[:, third] -= jnp.where(even, column, 0.0)
    theta = total_ref[...].astype(BF16)
    theta_ref[...] = theta
    put_gradient(theta, edge_ref, edge_energy_ref, edge_mask_ref, edge_grad_ref)
    put_messages(edge_grad_ref, mate_ref, across_ref)


def smooth_kernel(
    theta_ref, phi_ref, energy_ref, edge_ref, mask_ref, edge_mask_ref,
    out_ref, part_ref,
    grad_ref, done_ref, rest_ref, sems,
):
    put_gradient(theta_ref[...], phi_ref, energy_ref, mask_ref, grad_ref)
    weights = in_plane(8, 1)
    copies = []

    def send(source, rows, start, sem):
        copies.append(pltpu.make_async_copy(source, out_ref.at[rows, start : start + TILE], sem))
        copies[-1].start()

    for t in range(PLANE // TILE):
        lanes = slice(TILE * t, TILE * t + TILE)
        edge = edge_ref[:, :, lanes].astype(F32)
        mid = grad_ref[:, :, lanes].astype(F32)
        inner = plane_product(grad_ref, weights, 1.0, t)
        outer = plane_product(edge_ref, weights, 1.0, t)
        for i in range(2):
            value = (inner[i] + (edge[i] + mid[1 - i])) * (1.0 / 32.0)
            done_ref[i, :, lanes] = value.astype(BF16) * mask_ref[i, :, lanes]
            value = outer[i] + mid[i]
            part_ref[i, :, lanes] = value
            rest = rest_rows(i)
            value = value[rest] * (1.0 / 32.0)
            rest_ref[i, :, lanes] = value.astype(BF16) * edge_mask_ref[i, rest, lanes]
        for i in range(2):
            send(done_ref.at[i, :, lanes], slice(0, ROWS), PLANE * (1 + i) + TILE * t, sems.at[t, i])
            send(rest_ref.at[i, :, lanes], rest_rows(i), PLANE * (CX - 1) * i + TILE * t, sems.at[t, 2 + i])
    for copy in copies:
        copy.wait()


def finish_kernel(across_ref, mate_ref, part_ref, mask_ref, inner_ref, out_ref, done_ref, sems):
    halos = [unfold(side) for side in sides(mate_ref[...].astype(F32), across_ref[...].astype(F32))]
    copies = []
    for i in range(2):
        start = PLANE * (CX - 1) * i
        for half in range(2):
            rows = slice(ORB * (half + i), ORB * (half + i) + ORB)
            got = slice(ORB * half, ORB * half + ORB)
            for t in range(PLANE // 128):
                lanes = slice(128 * t, 128 * t + 128)
                value = (part_ref[i, rows, lanes] + halos[i][t % 3][got]) * (1.0 / 32.0)
                done_ref[i, got, lanes] = value.astype(BF16) * mask_ref[i, rows, lanes]
            copies.append(
                pltpu.make_async_copy(
                    done_ref.at[i, got], out_ref.at[rows, start : start + PLANE], sems.at[i, half]
                )
            )
            copies[-1].start()
    for copy in copies:
        copy.wait()


def shape(*dims, dtype=BF16):
    return jax.ShapeDtypeStruct(dims, dtype)


def cost(flops, moved):
    return pl.CostEstimate(flops=flops, bytes_accessed=moved, transcendentals=0)


PARAMS = pltpu.CompilerParams(vmem_limit_bytes=32 * 1024 * 1024)
WHOLE = pl.BlockSpec(memory_space=pltpu.VMEM)
FAR = pl.BlockSpec(memory_space=pltpu.HBM)


def far(value):
    return pltpu.with_memory_space_constraint(value, pltpu.HBM)


def per_device(pieces, potential, centers, pattern):
    count = lax.axis_size("sx")
    mates = [(i, i ^ 1) for i in range(count)]
    others = [(i, i + 1 if i % 2 else i - 1) for i in range(1, count - 1)]
    groups = lax.axis_size("grp")
    pairs = [[g * count + i, g * count + i + 1] for g in range(groups) for i in range(1, count - 1, 2)]
    ends = [g * count + end for g in range(groups) for end in (0, count - 1)]
    pairs += [[ends[i], ends[i + 2]] for i in range(len(ends)) if i % 4 < 2] if groups % 2 == 0 else [
        [ends[2 * i], ends[2 * i + 1]] for i in range(groups)
    ]

    def to_mate(value):
        return lax.ppermute(value, "sx", mates)

    def across(value):
        return lax.ppermute(value, "sx", others)

    def gathered(value):
        return lax.all_gather(value, ("grp", "sx"), axis_index_groups=pairs)

    table = centers.T
    patterns = pattern.T
    pair = shape(2, ROWS, PLANE)

    edge, edge_mask, rows, reach, keep, for_mate, face = pl.pallas_call(
        edges_kernel,
        out_shape=(
            pair, pair, shape(5 * ORB, 16), shape(ROWS, PLANE, dtype=F32), shape(3, 8 * ORB, dtype=F32),
            shape(ROWS, 128), shape(FACE, 128),
        ),
        in_specs=[FAR, FAR, FAR],
        out_specs=(WHOLE,) * 7,
        scratch_shapes=[
            pltpu.VMEM((4, WINDOW), jnp.int32),
            pltpu.VMEM((2, ROWS, PLANE), BF16),
            pltpu.SMEM(patterns.shape, jnp.int32),
            pltpu.SemaphoreType.DMA((4,)),
        ],
        compiler_params=PARAMS,
        cost_estimate=cost(10**8, 10**6),
        name="edges",
    )(far(table), far(patterns), far(pieces))
    mate_side = to_mate(for_mate)

    mid, mid_mask, mid_energy, part, rest_energy, corr, ham = pl.pallas_call(
        energy_kernel,
        out_shape=(
            pair, pair, pair, shape(2, ROWS, PLANE, dtype=F32), pair,
            shape(ROWS, ROWS, dtype=F32), shape(ROWS, ROWS, dtype=F32),
        ),
        in_specs=[WHOLE] * 6,
        out_specs=(WHOLE,) * 7,
        compiler_params=PARAMS,
        cost_estimate=cost(4 * 10**9, 10**7),
        name="energy",
    )(rows, reach, pieces, potential, edge, edge_mask)

    edge_energy, own, for_mate = pl.pallas_call(
        bands_kernel,
        out_shape=(pair, shape(2, ROWS, TILE, dtype=F32), shape(3, 2 * ORB, 128)),
        in_specs=[WHOLE] * 7,
        out_specs=(WHOLE,) * 3,
        input_output_aliases={6: 0},
        compiler_params=PARAMS,
        cost_estimate=cost(10**9, 10**7),
        name="bands",
    )(mate_side, part, edge_mask, edge, corr, ham, rest_energy)
    mate_rows = to_mate(for_mate)
    around = pl.pallas_call(
        around_kernel,
        out_shape=shape(ROWS, PLANE),
        in_specs=[WHOLE],
        out_specs=WHOLE,
        compiler_params=PARAMS,
        cost_estimate=cost(10**8, 10**6),
        name="around",
    )(rows)
    for_other = pl.pallas_call(
        relay_kernel,
        out_shape=shape(7 * ORB + FACE, 128),
        in_specs=[WHOLE] * 3,
        out_specs=WHOLE,
        compiler_params=PARAMS,
        cost_estimate=cost(10**6, 10**6),
        name="relay",
    )(own, mate_rows, face)
    edge_energy, other_rows, extra, forward = pl.pallas_call(
        face_kernel,
        out_shape=(pair, shape(7, ORB, 128), shape(ROWS, 8 * ORB, dtype=F32), shape(4, ORB, 128)),
        in_specs=[WHOLE] * 6,
        out_specs=(WHOLE,) * 4,
        scratch_shapes=[
            pltpu.VMEM((ROWS, PLANE), BF16),
            pltpu.VMEM((2 * ORB, PLANE), BF16),
            pltpu.VMEM((2 * ORB, PLANE), BF16),
            pltpu.VMEM((2, 2 * ORB, TILE), F32),
        ],
        input_output_aliases={5: 0},
        compiler_params=PARAMS,
        cost_estimate=cost(10**8, 10**6),
        name="face",
    )(gathered(for_other), around, edge, edge_mask, part, edge_energy)
    relayed = to_mate(forward)

    bands, base = pl.pallas_call(
        theta_kernel,
        out_shape=(shape(2, ROWS, TILE), shape(ROWS, ROWS, dtype=F32)),
        in_specs=[WHOLE] * 5,
        out_specs=(WHOLE,) * 2,
        scratch_shapes=[pltpu.VMEM((ROWS, 8 * ORB), F32), pltpu.VMEM((ROWS, 8 * ORB), F32)],
        compiler_params=PARAMS,
        cost_estimate=cost(10**9, 4 * 10**6),
        name="theta",
    )(keep, own, mate_rows, other_rows, extra)
    edge_grad, theta, for_mate, for_other = pl.pallas_call(
        gradient_kernel,
        out_shape=(pair, shape(ROWS, ROWS), shape(ROWS, 128), shape(ROWS, 128)),
        in_specs=[WHOLE] * 7,
        out_specs=(WHOLE,) * 4,
        scratch_shapes=[pltpu.VMEM((ROWS, TILE), BF16), pltpu.VMEM((ROWS, ROWS), F32)],
        compiler_params=PARAMS,
        cost_estimate=cost(10**9, 10**7),
        name="gradient",
    )(keep, relayed, bands, base, edge, edge_energy, edge_mask)
    other_side = across(for_other)
    mate_side = to_mate(for_mate)

    inner, part = pl.pallas_call(
        smooth_kernel,
        out_shape=(pltpu.HBM((ROWS, CX * PLANE), BF16), shape(2, ROWS, PLANE, dtype=F32)),
        in_specs=[WHOLE] * 6,
        out_specs=(FAR, WHOLE),
        scratch_shapes=[
            pltpu.VMEM((2, ROWS, PLANE), BF16),
            pltpu.VMEM((2, ROWS, PLANE), BF16),
            pltpu.VMEM((2, ORB, PLANE), BF16),
            pltpu.SemaphoreType.DMA((PLANE // TILE, 4)),
        ],
        compiler_params=PARAMS,
        cost_estimate=cost(2 * 10**9, 10**7),
        name="smooth",
    )(theta, mid, mid_energy, edge_grad, mid_mask, edge_mask)

    return pl.pallas_call(
        finish_kernel,
        out_shape=pltpu.HBM((ROWS, CX * PLANE), BF16),
        in_specs=[WHOLE] * 4 + [FAR],
        out_specs=FAR,
        scratch_shapes=[pltpu.VMEM((2, 2 * ORB, PLANE), BF16), pltpu.SemaphoreType.DMA((2, 2))],
        input_output_aliases={4: 0},
        compiler_params=PARAMS,
        cost_estimate=cost(10**7, 10**7),
        name="finish",
    )(other_side, mate_side, part, edge_mask, inner)


def solution(mesh):
    return jax.shard_map(
        per_device,
        mesh=mesh,
        in_specs=(P(("grp", "sx"), None), P(("grp", "sx"), None), P("grp", None), P("grp", None)),
        out_specs=P(("grp", "sx"), None),
        check_vma=False,
    )
```

```python
import functools

import jax
import jax.numpy as jnp
from jax import lax
from jax.experimental import pallas as pl
from jax.experimental.pallas import tpu as pltpu
from jax.sharding import PartitionSpec as P

ORB = 64
CX = 4
NY = 32
NZ = 32
ROWS = 3 * ORB
PLANE = NY * NZ
TILE = 256
WINDOW = 6 * ORB
FACE = 2 * ORB + ORB // 4
F32 = jnp.float32
BF16 = jnp.bfloat16


def iota(shape, dim):
    return lax.broadcasted_iota(jnp.int32, shape, dim)


def window_start(width):
    slab = lax.axis_index("sx")
    first = jnp.clip(slab * ORB - 2 * ORB, 0, width - WINDOW) // 128 * 128
    return pl.multiple_of(first, 128)


def row_features(window_ref, first):
    slab = lax.axis_index("sx")
    count = lax.axis_size("sx")
    window = window_ref[...]
    shift = slab * ORB - 2 * ORB - first
    window = pltpu.roll(jnp.concatenate([window, window], axis=0), lax.rem(WINDOW - shift, WINDOW), 1)
    lane = iota((1, WINDOW), 1)
    block = slab - 2 + lane // ORB
    valid = (block >= 0) & (block < count)
    cx = window[0:1] - slab * CX
    cy = window[1:2]
    cz = window[2:3]
    r = window[3:4]
    const = cx * cx + cy * cy + cz * cz - r * r
    const = jnp.where(valid, const, 65535)
    cx = jnp.where(valid, cx, 0)
    cy = jnp.where(valid, cy, 0)
    cz = jnp.where(valid, cz, 0)
    k = iota((16, WINDOW), 0)
    feats = jnp.where(k == 0, 1, 0)
    feats = jnp.where(k == 1, 256, feats)
    feats = jnp.where(k == 2, cy, feats)
    feats = jnp.where(k == 3, cz, feats)
    feats = jnp.where(k == 4, const & 255, feats)
    feats = jnp.where(k == 5, const >> 8, feats)
    feats = jnp.where(k == 6, cx, feats)
    return jnp.transpose(feats.astype(F32))[: 5 * ORB].astype(BF16)


def cell_features():
    k = iota((16, PLANE), 0)
    cell = iota((16, PLANE), 1)
    y = cell >> 5
    z = cell & 31
    sq = y * y + z * z
    feats = jnp.where(k == 0, sq & 255, 0)
    feats = jnp.where(k == 1, sq >> 8, feats)
    feats = jnp.where(k == 2, -2 * y, feats)
    feats = jnp.where(k == 3, -2 * z, feats)
    feats = jnp.where(k == 4, 1, feats)
    feats = jnp.where(k == 5, 256, feats)
    return feats.astype(F32).astype(BF16)


def sphere(reach, rows, plane):
    bound = rows[:, 6:7].astype(F32) * (2.0 * plane) - float(plane * plane)
    return jnp.where(reach <= bound, 1.0, 0.0).astype(BF16)


def in_plane(center, beside):
    k = iota((TILE, TILE), 0)
    n = iota((TILE, TILE), 1)
    diff = k - n
    near_y = (diff == NZ) | (diff == -NZ)
    near_z = ((diff == 1) | (diff == -1)) & ((k >> 5) == (n >> 5))
    w = jnp.where(near_y | near_z, float(beside), 0.0)
    return jnp.where(diff == 0, float(center), w).astype(BF16)


def plane_product(ref, weights, beside, t):
    start = TILE * t
    values = ref[:, :, start : start + TILE].reshape(2 * ROWS, TILE)
    out = jnp.dot(values, weights, preferred_element_type=F32).reshape(2, ROWS, TILE)
    lane = iota((1, 1, 128), 2)
    first, last = out[:, :, :128], out[:, :, 128:]
    if t > 0:
        turned = pltpu.roll(ref[:, :, start - 128 : start].astype(F32), NZ, 2)
        turned = jnp.where(lane < NZ, turned, 0.0)
        first = first + turned if beside > 0 else first - turned
    if start + TILE < PLANE:
        turned = pltpu.roll(ref[:, :, start + TILE : start + TILE + 128].astype(F32), 128 - NZ, 2)
        turned = jnp.where(lane >= 128 - NZ, turned, 0.0)
        last = last + turned if beside > 0 else last - turned
    return jnp.concatenate([first, last], axis=2)


def low_lanes(width):
    return (iota((1, 128), 1) & (2 * width - 1)) < width


def pack(first, second, width):
    return jnp.where(
        low_lanes(width),
        first + pltpu.roll(first, 128 - width, 1),
        second + pltpu.roll(second, width, 1),
    )


def unpack(packed, width):
    low = low_lanes(width)
    return (
        jnp.where(low, packed, pltpu.roll(packed, width, 1)),
        jnp.where(low, pltpu.roll(packed, 128 - width, 1), packed),
    )


def lane_tiles(values):
    return [values[:, 128 * t : 128 * t + 128] for t in range(PLANE // 128)]


def halves(values):
    half = values.shape[0] // 2
    return values[:half], values[half:]


def fold(full, side):
    tiles = lane_tiles(full)
    a, b, c = (sum(tiles[t::3][1:], tiles[t]) for t in range(3))
    tiles = lane_tiles(side)
    d, e = (sum(tiles[t::2][1:], tiles[t]) for t in range(2))
    return pack(a, b, 16), pack(*halves(c), 16), pack(*halves(pack(d, e, 16)), 8)


def unfold(packed):
    a, b = unpack(packed[:ORB], 16)
    c = jnp.concatenate(unpack(packed[ORB : ORB + ORB // 2], 16), axis=0)
    d, e = unpack(jnp.concatenate(unpack(packed[ORB + ORB // 2 : 2 * ORB], 8), axis=0), 16)
    return (a, b, c), (d, e)


def fold_far(values):
    tiles = lane_tiles(values)
    return pack(*halves(pack(*halves(sum(tiles[1:], tiles[0])), 16)), 8)


def unfold_far(packed):
    half = jnp.concatenate(unpack(packed, 8), axis=0)
    return jnp.concatenate(unpack(half, 16), axis=0)


def put_fold(ref, parts):
    start = 0
    for part in parts:
        ref[start : start + part.shape[0]] = part.astype(BF16)
        start += part.shape[0]


def side_by_side(unfolded, i):
    full, side = unfolded
    tiles = []
    for t in range(PLANE // 128):
        pair = [full[t % 3], side[t % 2]]
        tiles.append(jnp.concatenate(pair if i == 0 else pair[::-1], axis=0))
    return tiles


def is_even():
    return lax.rem(lax.axis_index("sx"), 2) == 0


def put_messages(planes, mate_ref, across_ref):
    own = slice(ORB, 2 * ORB)
    down = fold(planes[0, own].astype(F32), planes[0, :ORB].astype(F32))
    up = fold(planes[1, own].astype(F32), planes[1, 2 * ORB :].astype(F32))
    even = is_even()
    put_fold(mate_ref, [jnp.where(even, u, d) for u, d in zip(up, down)])
    put_fold(across_ref, [jnp.where(even, d, u) for u, d in zip(up, down)])


def sides(mate, across):
    even = is_even()
    return (jnp.where(even, across, mate), jnp.where(even, mate, across))


def at_end():
    slab = lax.axis_index("sx")
    return (slab == 0) | (slab == lax.axis_size("sx") - 1)


def kept(pattern_ref, r, q):
    slab = lax.axis_index("sx")
    last = pattern_ref.shape[1] - 1
    values = []
    for col in (2 * q, 2 * q + 1):
        apart = abs(col - r - 2)
        if apart == 0:
            values.append(1.0)
        elif apart > 2:
            values.append(0.0)
        else:
            at = jnp.clip(slab - 3 + min(col, r + 2), 0, last)
            values.append(pattern_ref[apart - 1, at].astype(F32))
    return jnp.where(low_half(), values[0], values[1])


def edges_kernel(
    table_ref, pattern_ref, pieces_ref,
    phi_ref, mask_ref, rows_ref, reach_ref, keep_ref, mate_ref, across_ref,
    window_ref, raw_ref, scalar_ref, sems,
):
    first = window_start(table_ref.shape[1])
    table_copy = pltpu.make_async_copy(table_ref.at[:, pl.ds(first, WINDOW)], window_ref, sems.at[2])
    table_copy.start()
    pattern_copy = pltpu.make_async_copy(pattern_ref, scalar_ref, sems.at[3])
    pattern_copy.start()
    copies = []
    for i in range(2):
        start = (CX - 1) * PLANE * i
        copies.append(
            pltpu.make_async_copy(pieces_ref.at[:, start : start + PLANE], raw_ref.at[i], sems.at[i])
        )
        copies[i].start()
    cells = cell_features()
    table_copy.wait()
    blocks = row_features(window_ref, first)
    rows_ref[...] = blocks
    rows = blocks[ORB : 4 * ORB]
    reach = jnp.dot(rows, cells, preferred_element_type=F32)
    reach_ref[...] = reach
    for i in range(2):
        mask_ref[i] = sphere(reach, rows, (CX - 1) * i)
    pattern_copy.wait()
    for r in range(3):
        for q in range(4):
            keep_ref[r : r + 1, 128 * q : 128 * q + 128] = kept(scalar_ref, r, q)
    for i in range(2):
        copies[i].wait()
        phi_ref[i] = raw_ref[i] * mask_ref[i]
    even = is_even()
    own = slice(ORB, 2 * ORB)
    lower, upper = phi_ref[0].astype(F32), phi_ref[1].astype(F32)
    put_fold(mate_ref, fold(jnp.where(even, upper[own], lower[own]), jnp.where(even, upper[2 * ORB :], lower[:ORB])))
    parts = fold(jnp.where(even, lower[own], upper[own]), jnp.where(even, lower[:ORB], upper[2 * ORB :]))
    put_fold(across_ref, parts + (fold_far(jnp.where(even, lower[2 * ORB :], upper[:ORB])),))


def rows_product(a, b):
    return lax.dot_general(a, b, (((1,), (1,)), ((), ())), preferred_element_type=F32)


def energy_kernel(
    rows_ref, reach_ref, pieces_ref, pot_ref, edge_ref, edge_mask_ref,
    phi_ref, mask_ref, energy_ref, part_ref, edge_energy_ref, corr_ref, ham_ref,
):
    rows = rows_ref[ORB : 4 * ORB]
    for i in range(2):
        mask = sphere(reach_ref[...], rows, 1 + i)
        mask_ref[i] = mask
        phi_ref[i] = pieces_ref[:, PLANE * (1 + i) : PLANE * (2 + i)] * mask
    weights = in_plane(6, -1)
    for t in range(PLANE // TILE):
        lanes = slice(TILE * t, TILE * t + TILE)
        edge = edge_ref[:, :, lanes].astype(F32)
        mid = phi_ref[:, :, lanes].astype(F32)
        inner = plane_product(phi_ref, weights, -1.0, t)
        outer = plane_product(edge_ref, weights, -1.0, t)
        for i in range(2):
            value = 0.5 * (inner[i] - (edge[i] + mid[1 - i])) + pot_ref[1 + i : 2 + i, lanes] * mid[i]
            energy_ref[i, :, lanes] = value.astype(BF16) * mask_ref[i, :, lanes]
            plane = (CX - 1) * i
            value = 0.5 * (outer[i] - mid[i]) + pot_ref[plane : plane + 1, lanes] * edge[i]
            part_ref[i, :, lanes] = value
            rest = rest_rows(i)
            edge_energy_ref[i, rest, lanes] = value[rest].astype(BF16) * edge_mask_ref[i, rest, lanes]
        orbitals = jnp.concatenate([phi_ref[0, :, lanes], phi_ref[1, :, lanes]], axis=1)
        energies = jnp.concatenate([energy_ref[0, :, lanes], energy_ref[1, :, lanes]], axis=1)
        grams = [rows_product(jnp.concatenate([orbitals, energies], axis=0), orbitals)]
        for i in range(2):
            orbitals = edge_ref[i, :, lanes]
            energies = edge_energy_ref[i, rest_rows(i), lanes]
            grams.append(rows_product(jnp.concatenate([orbitals, energies], axis=0), orbitals))
        total = grams if t == 0 else [a + b for a, b in zip(total, grams)]
    corr_ref[...] = total[0][:ROWS] + (total[1][:ROWS] + total[2][:ROWS])
    ham_ref[...] = total[0][ROWS:]
    for i in range(2):
        ham_ref[rest_rows(i)] += total[1 + i][ROWS:]


def halo_rows(i):
    return slice(0, 2 * ORB) if i == 0 else slice(ORB, ROWS)


def rest_rows(i):
    return slice(2 * ORB, ROWS) if i == 0 else slice(0, ORB)


def bands_kernel(
    mate_ref, part_ref, mask_ref, phi_ref, corr_ref, ham_ref, rest_ref,
    energy_ref, own_ref, rows_ref,
):
    volume = 1.0 / (4.0 * CX**3)
    gram = []
    mate = mate_ref[...].astype(F32)
    for i, side in enumerate(sides(mate, jnp.zeros_like(mate))):
        tiles = side_by_side(unfold(side), i)
        for t in range(PLANE // 128):
            lanes = slice(128 * t, 128 * t + 128)
            value = part_ref[i, halo_rows(i), lanes] - 0.5 * tiles[t]
            energy_ref[i, halo_rows(i), lanes] = value.astype(BF16) * mask_ref[i, halo_rows(i), lanes]
        gram.append(rows_product(energy_ref[i, halo_rows(i)], phi_ref[i]))
    own_ref[:, :, ROWS:] = jnp.zeros((2, ROWS, TILE - ROWS), F32)
    own_ref[0, :ORB, :ROWS] = (ham_ref[:ORB] + gram[0][:ORB]) * volume
    own_ref[0, ORB : 2 * ORB, :ROWS] = (ham_ref[ORB : 2 * ORB] + gram[0][ORB:] + gram[1][:ORB]) * volume
    own_ref[0, 2 * ORB :, :ROWS] = (ham_ref[2 * ORB :] + gram[1][ORB:]) * volume
    own_ref[1, :, :ROWS] = corr_ref[...] * volume
    tail = jnp.where(low_half(), own_ref[0, :, 128:256], swapped(own_ref[1, :, 128:256]))
    even = is_even()
    for i, value in enumerate((own_ref[0, :, 0:128], own_ref[1, :, 0:128], tail)):
        rows_ref[i] = jnp.where(even, value[ORB:], value[: 2 * ORB]).astype(BF16)


def low_half():
    return iota((1, 128), 1) < 64


def swapped(value):
    return pltpu.roll(value, 64, 1)


def mate_blocks(rows_ref, which):
    tail = rows_ref[2].astype(F32)
    if which == 1:
        tail = swapped(tail)
    return rows_ref[which].astype(F32), jnp.where(low_half(), tail, 0.0)


def shifted(c01, c2x):
    low = low_half()
    turned = swapped(c01)
    return jnp.where(low, 0.0, turned), jnp.where(low, turned, swapped(c2x))


def relay_kernel(own_ref, rows_ref, face_ref, out_ref):
    even = is_even()
    heads = []

    def put(i, value):
        out_ref[ORB * i : ORB * i + ORB] = value.astype(BF16)

    for which in range(2):
        head, rest = shifted(own_ref[which, :, 0:128], own_ref[which, :, 128:256])
        c01, c2x = mate_blocks(rows_ref, which)
        c01 = jnp.where(even, c01[:ORB], c01[ORB:])
        c2x = jnp.where(even, c2x[:ORB], c2x[ORB:])
        own = slice(ORB, 2 * ORB)
        put(2 * which, head[own] + jnp.where(even, c2x, c01))
        put(2 * which + 1, rest[own] + jnp.where(even, c01, c2x))
        put(5 + which, jnp.where(even, rest[:ORB], rest[2 * ORB :]))
        heads.append(jnp.where(even, head[:ORB], head[2 * ORB :]))
    put(4, jnp.where(low_half(), swapped(heads[1]), heads[0]))
    out_ref[7 * ORB :] = face_ref[...]


def around_kernel(rows_ref, mask_ref):
    even = is_even()
    rows = jnp.where(even, rows_ref[:ROWS].astype(F32), rows_ref[2 * ORB :].astype(F32))
    reach = jnp.dot(rows.astype(BF16), cell_features(), preferred_element_type=F32)
    plane = jnp.where(even, -1.0, float(CX))
    bound = rows[:, 6:7] * (2.0 * plane) - plane * plane
    mask_ref[...] = jnp.where(reach <= bound, 1.0, 0.0).astype(BF16)


def shared_head(tile, which):
    tile = tile.astype(F32)
    if which == 1:
        tile = swapped(tile)
    return jnp.where(low_half(), 0.0, tile)


def face_kernel(
    both_ref, around_ref, phi_ref, mask_ref, part_ref, energy_in_ref,
    energy_ref, other_ref, extra_ref, forward_ref,
    beyond_ref, halo_ref, back_ref, work_ref,
):
    even = is_even()
    low = low_half()
    scale = -0.5 / (4.0 * CX**3)

    def got(start, size):
        rows = slice(start, start + size)
        value = jnp.where(even, both_ref[0, rows].astype(F32), both_ref[1, rows].astype(F32))
        return jnp.where(at_end(), 0.0, value)

    tiles = [got(ORB * i, ORB) for i in range(7)]
    for i in range(7):
        other_ref[i] = tiles[i].astype(BF16)
    beside = unfold(got(7 * ORB, 2 * ORB))
    far_off = unfold_far(got(9 * ORB, ORB // 4)).astype(BF16)
    extra_ref[...] = jnp.zeros((ROWS, 8 * ORB), F32)
    work_ref[:, :, ROWS:] = jnp.zeros((2, 2 * ORB, TILE - ROWS), F32)
    head, tail = shared_head(tiles[4], 1), tiles[6]
    forward_ref[2] = jnp.where(low, swapped(head), swapped(tail)).astype(BF16)
    forward_ref[3] = jnp.where(low, swapped(tail), 0.0).astype(BF16)

    def add_face(i):
        here = halo_rows(i)
        there = slice(ORB, ROWS) if i == 0 else slice(0, 2 * ORB)
        outer = slice(0, ORB) if i == 0 else slice(2 * ORB, ROWS)
        for t, value in enumerate(side_by_side(beside, i)):
            lanes = slice(128 * t, 128 * t + 128)
            beyond_ref[there, lanes] = value.astype(BF16) * around_ref[there, lanes]
            beyond_ref[outer, lanes] = far_off * around_ref[outer, lanes]
            mask = mask_ref[i, here, lanes]
            halo_ref[:, lanes] = value.astype(BF16) * mask
            energy_ref[i, here, lanes] = (part_ref[i, here, lanes] - 0.5 * value).astype(BF16) * mask
            back_ref[:, lanes] = phi_ref[i, here, lanes] * around_ref[there, lanes]
        work_ref[0, :, :ROWS] = rows_product(halo_ref[...], phi_ref[i]) * scale
        work_ref[1, :, :ROWS] = rows_product(back_ref[...], beyond_ref[...]) * scale
        x, y = work_ref[0, :, 0:128], work_ref[0, :, 128:256]
        a, b = shifted(work_ref[1, :, 0:128], work_ref[1, :, 128:256])
        if i == 0:
            extra_ref[here, 0:128] = a
            extra_ref[here, 128:256] = b + x
            extra_ref[here, 256:384] = y
            own = slice(ORB, 2 * ORB)
        else:
            extra_ref[here, 128:256] = a + x
            extra_ref[here, 256:384] = b + y
            own = slice(0, ORB)
        a = swapped(shared_head(tiles[4], 0) + a[own])
        b = swapped(tiles[5] + b[own])
        x, y = swapped(x[own]), swapped(y[own])
        if i == 0:
            forward_ref[0] = jnp.where(low, a, b + x).astype(BF16)
            forward_ref[1] = jnp.where(low, b + x, y).astype(BF16)
        else:
            forward_ref[0] = jnp.where(low, a + x, b + y).astype(BF16)
            forward_ref[1] = jnp.where(low, b, x).astype(BF16)

    pl.when(even)(lambda: add_face(0))
    pl.when(jnp.logical_not(even))(lambda: add_face(1))


def put_gradient(theta, orbital_ref, energy_ref, mask_ref, out_ref):
    for i in range(2):
        for t in range(PLANE // TILE):
            lanes = slice(TILE * t, TILE * t + TILE)
            fix = jnp.dot(theta, orbital_ref[i, :, lanes], preferred_element_type=F32)
            value = energy_ref[i, :, lanes].astype(F32) - fix
            out_ref[i, :, lanes] = value.astype(BF16) * mask_ref[i, :, lanes]


def split(value):
    high = value.astype(BF16)
    return high, (value - high.astype(F32)).astype(BF16)


def fine_product(a, b):
    return rows_product(a[0], b[0]) + (rows_product(a[0], b[1]) + rows_product(a[1], b[0]))


def theta_kernel(
    keep_ref, own_ref, rows_ref, other_ref, extra_ref,
    window_ref, theta_ref,
    ham_ref, inv_ref,
):
    even = is_even()
    low = low_half()
    zero = jnp.zeros((ORB, 128), F32)
    for which, band_ref in enumerate((ham_ref, inv_ref)):
        near, rest = shifted(*mate_blocks(rows_ref, which))
        ahead = other_ref[2 * which].astype(F32)
        beside = other_ref[2 * which + 1].astype(F32)
        head = shared_head(other_ref[4], which)
        tail = other_ref[5 + which].astype(F32)
        got_even = (
            (ahead, beside, zero, zero),
            (head, tail + near[:ORB], rest[:ORB], zero),
            (zero, near[ORB:], rest[ORB:], zero),
        )
        got_odd = (
            (near[:ORB], rest[:ORB], zero, zero),
            (near[ORB:], rest[ORB:] + head, tail, zero),
            (zero, jnp.where(low, 0.0, ahead), beside, jnp.where(low, ahead, 0.0)),
        )
        for r in range(3):
            for q in range(4):
                value = jnp.where(even, got_even[r][q], got_odd[r][q])
                if q in (1, 2):
                    value = value + own_ref[which, ORB * r : ORB * r + ORB, 128 * q - 128 : 128 * q]
                if which == 0:
                    value = value + extra_ref[ORB * r : ORB * r + ORB, 128 * q : 128 * q + 128]
                value = value * keep_ref[r : r + 1, 128 * q : 128 * q + 128]
                if which == 1:
                    on = iota((ORB, 128), 0) + (ORB * (r + 2) - 128 * q) == iota((ORB, 128), 1)
                    value = jnp.where(on, 2.0, 0.0) - value
                band_ref[ORB * r : ORB * r + ORB, 128 * q : 128 * q + 128] = value
    ham, inv = split(ham_ref[...]), split(inv_ref[...])
    theta_ref[...] = fine_product(ham, inv)
    for which, (high, _) in enumerate((ham, inv)):
        quarter = [high[:, 128 * q : 128 * q + 128].astype(F32) for q in range(4)]
        window_ref[which, :, 0:128] = jnp.where(even, quarter[2], quarter[0]).astype(BF16)
        last = jnp.where(even, jnp.where(low, quarter[3], quarter[1]), quarter[1])
        window_ref[which, :, 128:256] = last.astype(BF16)


def gradient_kernel(
    keep_ref, relayed_ref, bands_ref, base_ref,
    edge_ref, edge_energy_ref, edge_mask_ref,
    edge_grad_ref, theta_ref, mate_ref, across_ref,
    window_ref, total_ref,
):
    even = is_even()
    low = low_half()
    more = []
    kept_even = (keep_ref[2:3, 256:384], jnp.where(low, keep_ref[2:3, 384:512], keep_ref[2:3, 128:256]))
    kept_odd = (keep_ref[0:1, 0:128], keep_ref[0:1, 128:256])
    for which in range(2):
        tiles = []
        for q in range(2):
            value = relayed_ref[2 * which + q].astype(F32)
            tiles.append(value * jnp.where(even, kept_even[q], kept_odd[q]))
        more.append(jnp.concatenate(tiles, axis=1))
    first, third = slice(0, ORB), slice(2 * ORB, ROWS)
    window_ref[...] = bands_ref[0]
    window_ref[first] = (bands_ref[0, first].astype(F32) + jnp.where(even, 0.0, more[0])).astype(BF16)
    window_ref[third] = (bands_ref[0, third].astype(F32) + jnp.where(even, more[0], 0.0)).astype(BF16)
    more = [value.astype(BF16) for value in more]
    column = rows_product(window_ref[...], more[1])
    row = rows_product(more[0], bands_ref[1])
    total_ref[...] = base_ref[...]
    total_ref[first] += jnp.where(even, 0.0, row)
    total_ref[third] += jnp.where(even, row, 0.0)
    total_ref[:, first] -= jnp.where(even, 0.0, column)
    total_ref[:, third] -= jnp.where(even, column, 0.0)
    theta = total_ref[...].astype(BF16)
    theta_ref[...] = theta
    put_gradient(theta, edge_ref, edge_energy_ref, edge_mask_ref, edge_grad_ref)
    put_messages(edge_grad_ref, mate_ref, across_ref)


def smooth_kernel(
    theta_ref, phi_ref, energy_ref, edge_ref, mask_ref, edge_mask_ref,
    out_ref, part_ref,
    grad_ref, done_ref, rest_ref, sems,
):
    put_gradient(theta_ref[...], phi_ref, energy_ref, mask_ref, grad_ref)
    weights = in_plane(8, 1)
    copies = []

    def send(source, rows, start, sem):
        copies.append(pltpu.make_async_copy(source, out_ref.at[rows, start : start + TILE], sem))
        copies[-1].start()

    for t in range(PLANE // TILE):
        lanes = slice(TILE * t, TILE * t + TILE)
        edge = edge_ref[:, :, lanes].astype(F32)
        mid = grad_ref[:, :, lanes].astype(F32)
        inner = plane_product(grad_ref, weights, 1.0, t)
        outer = plane_product(edge_ref, weights, 1.0, t)
        for i in range(2):
            value = (inner[i] + (edge[i] + mid[1 - i])) * (1.0 / 32.0)
            done_ref[i, :, lanes] = value.astype(BF16) * mask_ref[i, :, lanes]
            value = outer[i] + mid[i]
            part_ref[i, :, lanes] = value
            rest = rest_rows(i)
            value = value[rest] * (1.0 / 32.0)
            rest_ref[i, :, lanes] = value.astype(BF16) * edge_mask_ref[i, rest, lanes]
        for i in range(2):
            send(done_ref.at[i, :, lanes], slice(0, ROWS), PLANE * (1 + i) + TILE * t, sems.at[t, i])
            send(rest_ref.at[i, :, lanes], rest_rows(i), PLANE * (CX - 1) * i + TILE * t, sems.at[t, 2 + i])
    for copy in copies:
        copy.wait()


def finish_kernel(across_ref, mate_ref, part_ref, mask_ref, inner_ref, out_ref, done_ref, sems):
    halos = [
        side_by_side(unfold(side), i)
        for i, side in enumerate(sides(mate_ref[...].astype(F32), across_ref[...].astype(F32)))
    ]
    copies = []
    for i in range(2):
        start = PLANE * (CX - 1) * i
        for half in range(2):
            rows = slice(ORB * (half + i), ORB * (half + i) + ORB)
            got = slice(ORB * half, ORB * half + ORB)
            for t in range(PLANE // 128):
                lanes = slice(128 * t, 128 * t + 128)
                value = (part_ref[i, rows, lanes] + halos[i][t][got]) * (1.0 / 32.0)
                done_ref[i, got, lanes] = value.astype(BF16) * mask_ref[i, rows, lanes]
            copies.append(
                pltpu.make_async_copy(
                    done_ref.at[i, got], out_ref.at[rows, start : start + PLANE], sems.at[i, half]
                )
            )
            copies[-1].start()
    for copy in copies:
        copy.wait()


def shape(*dims, dtype=BF16):
    return jax.ShapeDtypeStruct(dims, dtype)


def cost(flops, moved):
    return pl.CostEstimate(flops=flops, bytes_accessed=moved, transcendentals=0)


PARAMS = pltpu.CompilerParams(vmem_limit_bytes=32 * 1024 * 1024)
WHOLE = pl.BlockSpec(memory_space=pltpu.VMEM)
FAR = pl.BlockSpec(memory_space=pltpu.HBM)


def far(value):
    return pltpu.with_memory_space_constraint(value, pltpu.HBM)


def per_device(pieces, potential, centers, pattern):
    count = lax.axis_size("sx")
    mates = [(i, i ^ 1) for i in range(count)]
    others = [(i, i + 1 if i % 2 else i - 1) for i in range(1, count - 1)]
    groups = lax.axis_size("grp")
    pairs = [[g * count + i, g * count + i + 1] for g in range(groups) for i in range(1, count - 1, 2)]
    ends = [g * count + end for g in range(groups) for end in (0, count - 1)]
    pairs += [[ends[i], ends[i + 2]] for i in range(len(ends)) if i % 4 < 2] if groups % 2 == 0 else [
        [ends[2 * i], ends[2 * i + 1]] for i in range(groups)
    ]

    def to_mate(value):
        return lax.ppermute(value, "sx", mates)

    def across(value):
        return lax.ppermute(value, "sx", others)

    def gathered(value):
        return lax.all_gather(value, ("grp", "sx"), axis_index_groups=pairs)

    table = centers.T
    patterns = pattern.T
    pair = shape(2, ROWS, PLANE)

    edge, edge_mask, rows, reach, keep, for_mate, face = pl.pallas_call(
        edges_kernel,
        out_shape=(
            pair, pair, shape(5 * ORB, 16), shape(ROWS, PLANE, dtype=F32), shape(3, 8 * ORB, dtype=F32),
            shape(2 * ORB, 128), shape(FACE, 128),
        ),
        in_specs=[FAR, FAR, FAR],
        out_specs=(WHOLE,) * 7,
        scratch_shapes=[
            pltpu.VMEM((4, WINDOW), jnp.int32),
            pltpu.VMEM((2, ROWS, PLANE), BF16),
            pltpu.SMEM(patterns.shape, jnp.int32),
            pltpu.SemaphoreType.DMA((4,)),
        ],
        compiler_params=PARAMS,
        cost_estimate=cost(10**8, 10**6),
        name="edges",
    )(far(table), far(patterns), far(pieces))
    mate_side = to_mate(for_mate)

    mid, mid_mask, mid_energy, part, rest_energy, corr, ham = pl.pallas_call(
        energy_kernel,
        out_shape=(
            pair, pair, pair, shape(2, ROWS, PLANE, dtype=F32), pair,
            shape(ROWS, ROWS, dtype=F32), shape(ROWS, ROWS, dtype=F32),
        ),
        in_specs=[WHOLE] * 6,
        out_specs=(WHOLE,) * 7,
        compiler_params=PARAMS,
        cost_estimate=cost(4 * 10**9, 10**7),
        name="energy",
    )(rows, reach, pieces, potential, edge, edge_mask)

    edge_energy, own, for_mate = pl.pallas_call(
        bands_kernel,
        out_shape=(pair, shape(2, ROWS, TILE, dtype=F32), shape(3, 2 * ORB, 128)),
        in_specs=[WHOLE] * 7,
        out_specs=(WHOLE,) * 3,
        input_output_aliases={6: 0},
        compiler_params=PARAMS,
        cost_estimate=cost(10**9, 10**7),
        name="bands",
    )(mate_side, part, edge_mask, edge, corr, ham, rest_energy)
    mate_rows = to_mate(for_mate)
    around = pl.pallas_call(
        around_kernel,
        out_shape=shape(ROWS, PLANE),
        in_specs=[WHOLE],
        out_specs=WHOLE,
        compiler_params=PARAMS,
        cost_estimate=cost(10**8, 10**6),
        name="around",
    )(rows)
    for_other = pl.pallas_call(
        relay_kernel,
        out_shape=shape(7 * ORB + FACE, 128),
        in_specs=[WHOLE] * 3,
        out_specs=WHOLE,
        compiler_params=PARAMS,
        cost_estimate=cost(10**6, 10**6),
        name="relay",
    )(own, mate_rows, face)
    edge_energy, other_rows, extra, forward = pl.pallas_call(
        face_kernel,
        out_shape=(pair, shape(7, ORB, 128), shape(ROWS, 8 * ORB, dtype=F32), shape(4, ORB, 128)),
        in_specs=[WHOLE] * 6,
        out_specs=(WHOLE,) * 4,
        scratch_shapes=[
            pltpu.VMEM((ROWS, PLANE), BF16),
            pltpu.VMEM((2 * ORB, PLANE), BF16),
            pltpu.VMEM((2 * ORB, PLANE), BF16),
            pltpu.VMEM((2, 2 * ORB, TILE), F32),
        ],
        input_output_aliases={5: 0},
        compiler_params=PARAMS,
        cost_estimate=cost(10**8, 10**6),
        name="face",
    )(gathered(for_other), around, edge, edge_mask, part, edge_energy)
    relayed = to_mate(forward)

    bands, base = pl.pallas_call(
        theta_kernel,
        out_shape=(shape(2, ROWS, TILE), shape(ROWS, ROWS, dtype=F32)),
        in_specs=[WHOLE] * 5,
        out_specs=(WHOLE,) * 2,
        scratch_shapes=[pltpu.VMEM((ROWS, 8 * ORB), F32), pltpu.VMEM((ROWS, 8 * ORB), F32)],
        compiler_params=PARAMS,
        cost_estimate=cost(10**9, 4 * 10**6),
        name="theta",
    )(keep, own, mate_rows, other_rows, extra)
    edge_grad, theta, for_mate, for_other = pl.pallas_call(
        gradient_kernel,
        out_shape=(pair, shape(ROWS, ROWS), shape(2 * ORB, 128), shape(2 * ORB, 128)),
        in_specs=[WHOLE] * 7,
        out_specs=(WHOLE,) * 4,
        scratch_shapes=[pltpu.VMEM((ROWS, TILE), BF16), pltpu.VMEM((ROWS, ROWS), F32)],
        compiler_params=PARAMS,
        cost_estimate=cost(10**9, 10**7),
        name="gradient",
    )(keep, relayed, bands, base, edge, edge_energy, edge_mask)
    other_side = across(for_other)
    mate_side = to_mate(for_mate)

    inner, part = pl.pallas_call(
        smooth_kernel,
        out_shape=(pltpu.HBM((ROWS, CX * PLANE), BF16), shape(2, ROWS, PLANE, dtype=F32)),
        in_specs=[WHOLE] * 6,
        out_specs=(FAR, WHOLE),
        scratch_shapes=[
            pltpu.VMEM((2, ROWS, PLANE), BF16),
            pltpu.VMEM((2, ROWS, PLANE), BF16),
            pltpu.VMEM((2, ORB, PLANE), BF16),
            pltpu.SemaphoreType.DMA((PLANE // TILE, 4)),
        ],
        compiler_params=PARAMS,
        cost_estimate=cost(2 * 10**9, 10**7),
        name="smooth",
    )(theta, mid, mid_energy, edge_grad, mid_mask, edge_mask)

    return pl.pallas_call(
        finish_kernel,
        out_shape=pltpu.HBM((ROWS, CX * PLANE), BF16),
        in_specs=[WHOLE] * 4 + [FAR],
        out_specs=FAR,
        scratch_shapes=[pltpu.VMEM((2, 2 * ORB, PLANE), BF16), pltpu.SemaphoreType.DMA((2, 2))],
        input_output_aliases={4: 0},
        compiler_params=PARAMS,
        cost_estimate=cost(10**7, 10**7),
        name="finish",
    )(other_side, mate_side, part, edge_mask, inner)


def solution(mesh):
    return jax.shard_map(
        per_device,
        mesh=mesh,
        in_specs=(P(("grp", "sx"), None), P(("grp", "sx"), None), P("grp", None), P("grp", None)),
        out_specs=P(("grp", "sx"), None),
        check_vma=False,
    )
```

```python
import functools

import jax
import jax.numpy as jnp
from jax import lax
from jax.experimental import pallas as pl
from jax.experimental.pallas import tpu as pltpu
from jax.sharding import PartitionSpec as P

ORB = 64
CX = 4
NY = 32
NZ = 32
ROWS = 3 * ORB
PLANE = NY * NZ
TILE = 256
WINDOW = 6 * ORB
FACE = 2 * ORB + ORB // 4
F32 = jnp.float32
BF16 = jnp.bfloat16


def iota(shape, dim):
    return lax.broadcasted_iota(jnp.int32, shape, dim)


def window_start(width):
    slab = lax.axis_index("sx")
    first = jnp.clip(slab * ORB - 2 * ORB, 0, width - WINDOW) // 128 * 128
    return pl.multiple_of(first, 128)


def row_features(window_ref, first):
    slab = lax.axis_index("sx")
    count = lax.axis_size("sx")
    window = window_ref[...]
    shift = slab * ORB - 2 * ORB - first
    window = pltpu.roll(jnp.concatenate([window, window], axis=0), lax.rem(WINDOW - shift, WINDOW), 1)
    lane = iota((1, WINDOW), 1)
    block = slab - 2 + lane // ORB
    valid = (block >= 0) & (block < count)
    cx = window[0:1] - slab * CX
    cy = window[1:2]
    cz = window[2:3]
    r = window[3:4]
    const = cx * cx + cy * cy + cz * cz - r * r
    const = jnp.where(valid, const, 65535)
    cx = jnp.where(valid, cx, 0)
    cy = jnp.where(valid, cy, 0)
    cz = jnp.where(valid, cz, 0)
    k = iota((16, WINDOW), 0)
    feats = jnp.where(k == 0, 1, 0)
    feats = jnp.where(k == 1, 256, feats)
    feats = jnp.where(k == 2, cy, feats)
    feats = jnp.where(k == 3, cz, feats)
    feats = jnp.where(k == 4, const & 255, feats)
    feats = jnp.where(k == 5, const >> 8, feats)
    feats = jnp.where(k == 6, cx, feats)
    return jnp.transpose(feats.astype(F32))[: 5 * ORB].astype(BF16)


def cell_features():
    k = iota((16, PLANE), 0)
    cell = iota((16, PLANE), 1)
    y = cell >> 5
    z = cell & 31
    sq = y * y + z * z
    feats = jnp.where(k == 0, sq & 255, 0)
    feats = jnp.where(k == 1, sq >> 8, feats)
    feats = jnp.where(k == 2, -2 * y, feats)
    feats = jnp.where(k == 3, -2 * z, feats)
    feats = jnp.where(k == 4, 1, feats)
    feats = jnp.where(k == 5, 256, feats)
    return feats.astype(F32).astype(BF16)


def sphere(reach, rows, plane):
    bound = rows[:, 6:7].astype(F32) * (2.0 * plane) - float(plane * plane)
    return jnp.where(reach <= bound, 1.0, 0.0).astype(BF16)


def in_plane(center, beside):
    k = iota((TILE, TILE), 0)
    n = iota((TILE, TILE), 1)
    diff = k - n
    near_y = (diff == NZ) | (diff == -NZ)
    near_z = ((diff == 1) | (diff == -1)) & ((k >> 5) == (n >> 5))
    w = jnp.where(near_y | near_z, float(beside), 0.0)
    return jnp.where(diff == 0, float(center), w).astype(BF16)


def plane_product(ref, weights, beside, t):
    start = TILE * t
    values = ref[:, :, start : start + TILE].reshape(2 * ROWS, TILE)
    out = jnp.dot(values, weights, preferred_element_type=F32).reshape(2, ROWS, TILE)
    lane = iota((1, 1, 128), 2)
    first, last = out[:, :, :128], out[:, :, 128:]
    if t > 0:
        turned = pltpu.roll(ref[:, :, start - 128 : start].astype(F32), NZ, 2)
        turned = jnp.where(lane < NZ, turned, 0.0)
        first = first + turned if beside > 0 else first - turned
    if start + TILE < PLANE:
        turned = pltpu.roll(ref[:, :, start + TILE : start + TILE + 128].astype(F32), 128 - NZ, 2)
        turned = jnp.where(lane >= 128 - NZ, turned, 0.0)
        last = last + turned if beside > 0 else last - turned
    return jnp.concatenate([first, last], axis=2)


def low_lanes(width):
    return (iota((1, 128), 1) & (2 * width - 1)) < width


def pack(first, second, width):
    return jnp.where(
        low_lanes(width),
        first + pltpu.roll(first, 128 - width, 1),
        second + pltpu.roll(second, width, 1),
    )


def unpack(packed, width):
    low = low_lanes(width)
    return (
        jnp.where(low, packed, pltpu.roll(packed, width, 1)),
        jnp.where(low, pltpu.roll(packed, 128 - width, 1), packed),
    )


def lane_tiles(values):
    return [values[:, 128 * t : 128 * t + 128] for t in range(PLANE // 128)]


def halves(values):
    half = values.shape[0] // 2
    return values[:half], values[half:]


def fold(full, side):
    tiles = lane_tiles(full)
    a, b, c = (sum(tiles[t::3][1:], tiles[t]) for t in range(3))
    tiles = lane_tiles(side)
    d, e = (sum(tiles[t::2][1:], tiles[t]) for t in range(2))
    return pack(a, b, 16), pack(*halves(c), 16), pack(*halves(pack(d, e, 16)), 8)


def unfold(packed):
    a, b = unpack(packed[:ORB], 16)
    c = jnp.concatenate(unpack(packed[ORB : ORB + ORB // 2], 16), axis=0)
    d, e = unpack(jnp.concatenate(unpack(packed[ORB + ORB // 2 : 2 * ORB], 8), axis=0), 16)
    return (a, b, c), (d, e)


def fold_far(values):
    tiles = lane_tiles(values)
    return pack(*halves(pack(*halves(sum(tiles[1:], tiles[0])), 16)), 8)


def unfold_far(packed):
    half = jnp.concatenate(unpack(packed, 8), axis=0)
    return jnp.concatenate(unpack(half, 16), axis=0)


def put_fold(ref, parts):
    start = 0
    for part in parts:
        ref[start : start + part.shape[0]] = part.astype(BF16)
        start += part.shape[0]


def side_by_side(unfolded, i):
    full, side = unfolded
    tiles = []
    for t in range(PLANE // 128):
        pair = [full[t % 3], side[t % 2]]
        tiles.append(jnp.concatenate(pair if i == 0 else pair[::-1], axis=0))
    return tiles


def is_even():
    return lax.rem(lax.axis_index("sx"), 2) == 0


def put_messages(planes, mate_ref, across_ref):
    own = slice(ORB, 2 * ORB)
    down = fold(planes[0, own].astype(F32), planes[0, :ORB].astype(F32))
    up = fold(planes[1, own].astype(F32), planes[1, 2 * ORB :].astype(F32))
    even = is_even()
    put_fold(mate_ref, [jnp.where(even, u, d) for u, d in zip(up, down)])
    put_fold(across_ref, [jnp.where(even, d, u) for u, d in zip(up, down)])


def sides(mate, across):
    even = is_even()
    return (jnp.where(even, across, mate), jnp.where(even, mate, across))


def at_end():
    slab = lax.axis_index("sx")
    return (slab == 0) | (slab == lax.axis_size("sx") - 1)


def kept(pattern_ref, r, q):
    slab = lax.axis_index("sx")
    last = pattern_ref.shape[1] - 1
    values = []
    for col in (2 * q, 2 * q + 1):
        apart = abs(col - r - 2)
        if apart == 0:
            values.append(1.0)
        elif apart > 2:
            values.append(0.0)
        else:
            at = jnp.clip(slab - 3 + min(col, r + 2), 0, last)
            values.append(pattern_ref[apart - 1, at].astype(F32))
    return jnp.where(low_half(), values[0], values[1])


def edges_kernel(
    table_ref, pieces_ref,
    phi_ref, mask_ref, rows_ref, reach_ref, mate_ref,
    window_ref, raw_ref, sems,
):
    first = window_start(table_ref.shape[1])
    table_copy = pltpu.make_async_copy(table_ref.at[:, pl.ds(first, WINDOW)], window_ref, sems.at[2])
    table_copy.start()
    copies = []
    for i in range(2):
        start = (CX - 1) * PLANE * i
        copies.append(
            pltpu.make_async_copy(pieces_ref.at[:, start : start + PLANE], raw_ref.at[i], sems.at[i])
        )
        copies[i].start()
    cells = cell_features()
    table_copy.wait()
    blocks = row_features(window_ref, first)
    rows_ref[...] = blocks
    rows = blocks[ORB : 4 * ORB]
    reach = jnp.dot(rows, cells, preferred_element_type=F32)
    reach_ref[...] = reach
    for i in range(2):
        mask_ref[i] = sphere(reach, rows, (CX - 1) * i)
    for i in range(2):
        copies[i].wait()
        phi_ref[i] = raw_ref[i] * mask_ref[i]
    even = is_even()
    own = slice(ORB, 2 * ORB)
    lower, upper = phi_ref[0].astype(F32), phi_ref[1].astype(F32)
    put_fold(mate_ref, fold(jnp.where(even, upper[own], lower[own]), jnp.where(even, upper[2 * ORB :], lower[:ORB])))


def rows_product(a, b):
    return lax.dot_general(a, b, (((1,), (1,)), ((), ())), preferred_element_type=F32)


def energy_kernel(
    rows_ref, reach_ref, pieces_ref, pot_ref, edge_ref, edge_mask_ref,
    phi_ref, mask_ref, energy_ref, part_ref, edge_energy_ref, corr_ref, ham_ref,
):
    rows = rows_ref[ORB : 4 * ORB]
    for i in range(2):
        mask = sphere(reach_ref[...], rows, 1 + i)
        mask_ref[i] = mask
        phi_ref[i] = pieces_ref[:, PLANE * (1 + i) : PLANE * (2 + i)] * mask
    weights = in_plane(6, -1)
    for t in range(PLANE // TILE):
        lanes = slice(TILE * t, TILE * t + TILE)
        edge = edge_ref[:, :, lanes].astype(F32)
        mid = phi_ref[:, :, lanes].astype(F32)
        inner = plane_product(phi_ref, weights, -1.0, t)
        outer = plane_product(edge_ref, weights, -1.0, t)
        for i in range(2):
            value = 0.5 * (inner[i] - (edge[i] + mid[1 - i])) + pot_ref[1 + i : 2 + i, lanes] * mid[i]
            energy_ref[i, :, lanes] = value.astype(BF16) * mask_ref[i, :, lanes]
            plane = (CX - 1) * i
            value = 0.5 * (outer[i] - mid[i]) + pot_ref[plane : plane + 1, lanes] * edge[i]
            part_ref[i, :, lanes] = value
            rest = rest_rows(i)
            edge_energy_ref[i, rest, lanes] = value[rest].astype(BF16) * edge_mask_ref[i, rest, lanes]
    mid = jnp.concatenate([phi_ref[0], phi_ref[1]], axis=1)
    both = jnp.concatenate([energy_ref[0], energy_ref[1]], axis=1)
    gram = rows_product(jnp.concatenate([mid, both], axis=0), mid)
    corr = gram[:ROWS]
    ham_ref[...] = gram[ROWS:]
    for i in range(2):
        rest = rest_rows(i)
        gram = rows_product(jnp.concatenate([edge_ref[i], edge_energy_ref[i, rest]], axis=0), edge_ref[i])
        corr = corr + gram[:ROWS]
        ham_ref[rest] += gram[ROWS:]
    corr_ref[...] = corr


def halo_rows(i):
    return slice(0, 2 * ORB) if i == 0 else slice(ORB, ROWS)


def rest_rows(i):
    return slice(2 * ORB, ROWS) if i == 0 else slice(0, ORB)


def bands_kernel(
    mate_ref, part_ref, mask_ref, phi_ref, corr_ref, ham_ref, rest_ref,
    energy_ref, own_ref, rows_ref,
):
    volume = 1.0 / (4.0 * CX**3)
    gram = []
    mate = mate_ref[...].astype(F32)
    for i, side in enumerate(sides(mate, jnp.zeros_like(mate))):
        tiles = side_by_side(unfold(side), i)
        for t in range(PLANE // 128):
            lanes = slice(128 * t, 128 * t + 128)
            value = part_ref[i, halo_rows(i), lanes] - 0.5 * tiles[t]
            energy_ref[i, halo_rows(i), lanes] = value.astype(BF16) * mask_ref[i, halo_rows(i), lanes]
        gram.append(rows_product(energy_ref[i, halo_rows(i)], phi_ref[i]))
    own_ref[:, :, ROWS:] = jnp.zeros((2, ROWS, TILE - ROWS), F32)
    own_ref[0, :ORB, :ROWS] = (ham_ref[:ORB] + gram[0][:ORB]) * volume
    own_ref[0, ORB : 2 * ORB, :ROWS] = (ham_ref[ORB : 2 * ORB] + gram[0][ORB:] + gram[1][:ORB]) * volume
    own_ref[0, 2 * ORB :, :ROWS] = (ham_ref[2 * ORB :] + gram[1][ORB:]) * volume
    own_ref[1, :, :ROWS] = corr_ref[...] * volume
    tail = jnp.where(low_half(), own_ref[0, :, 128:256], swapped(own_ref[1, :, 128:256]))
    even = is_even()
    for i, value in enumerate((own_ref[0, :, 0:128], own_ref[1, :, 0:128], tail)):
        rows_ref[i] = jnp.where(even, value[ORB:], value[: 2 * ORB]).astype(BF16)


def low_half():
    return iota((1, 128), 1) < 64


def swapped(value):
    return pltpu.roll(value, 64, 1)


def mate_blocks(rows_ref, which):
    tail = rows_ref[2].astype(F32)
    if which == 1:
        tail = swapped(tail)
    return rows_ref[which].astype(F32), jnp.where(low_half(), tail, 0.0)


def shifted(c01, c2x):
    low = low_half()
    turned = swapped(c01)
    return jnp.where(low, 0.0, turned), jnp.where(low, turned, swapped(c2x))


def relay_kernel(own_ref, rows_ref, face_ref, out_ref):
    even = is_even()
    heads = []

    def put(i, value):
        out_ref[ORB * i : ORB * i + ORB] = value.astype(BF16)

    for which in range(2):
        head, rest = shifted(own_ref[which, :, 0:128], own_ref[which, :, 128:256])
        c01, c2x = mate_blocks(rows_ref, which)
        c01 = jnp.where(even, c01[:ORB], c01[ORB:])
        c2x = jnp.where(even, c2x[:ORB], c2x[ORB:])
        own = slice(ORB, 2 * ORB)
        put(2 * which, head[own] + jnp.where(even, c2x, c01))
        put(2 * which + 1, rest[own] + jnp.where(even, c01, c2x))
        put(5 + which, jnp.where(even, rest[:ORB], rest[2 * ORB :]))
        heads.append(jnp.where(even, head[:ORB], head[2 * ORB :]))
    put(4, jnp.where(low_half(), swapped(heads[1]), heads[0]))
    out_ref[7 * ORB :] = face_ref[...]


def around_kernel(pattern_ref, rows_ref, phi_ref, mask_ref, keep_ref, face_ref, scalar_ref, sem):
    pattern_copy = pltpu.make_async_copy(pattern_ref, scalar_ref, sem)
    pattern_copy.start()
    even = is_even()
    own = slice(ORB, 2 * ORB)
    lower, upper = phi_ref[0].astype(F32), phi_ref[1].astype(F32)
    parts = fold(jnp.where(even, lower[own], upper[own]), jnp.where(even, lower[:ORB], upper[2 * ORB :]))
    put_fold(face_ref, parts + (fold_far(jnp.where(even, lower[2 * ORB :], upper[:ORB])),))
    rows = jnp.where(even, rows_ref[:ROWS].astype(F32), rows_ref[2 * ORB :].astype(F32))
    reach = jnp.dot(rows.astype(BF16), cell_features(), preferred_element_type=F32)
    plane = jnp.where(even, -1.0, float(CX))
    bound = rows[:, 6:7] * (2.0 * plane) - plane * plane
    mask_ref[...] = jnp.where(reach <= bound, 1.0, 0.0).astype(BF16)
    pattern_copy.wait()
    for r in range(3):
        for q in range(4):
            keep_ref[r : r + 1, 128 * q : 128 * q + 128] = kept(scalar_ref, r, q)


def shared_head(tile, which):
    tile = tile.astype(F32)
    if which == 1:
        tile = swapped(tile)
    return jnp.where(low_half(), 0.0, tile)


def face_kernel(
    both_ref, around_ref, phi_ref, mask_ref,
    halo_ref, other_ref, extra_ref, forward_ref,
    beyond_ref, back_ref, work_ref,
):
    even = is_even()
    low = low_half()
    scale = -0.5 / (4.0 * CX**3)

    def got(start, size):
        rows = slice(start, start + size)
        value = jnp.where(even, both_ref[0, rows].astype(F32), both_ref[1, rows].astype(F32))
        return jnp.where(at_end(), 0.0, value)

    tiles = [got(ORB * i, ORB) for i in range(7)]
    for i in range(7):
        other_ref[i] = tiles[i].astype(BF16)
    beside = unfold(got(7 * ORB, 2 * ORB))
    far_off = unfold_far(got(9 * ORB, ORB // 4)).astype(BF16)
    extra_ref[...] = jnp.zeros((ROWS, 8 * ORB), F32)
    work_ref[:, :, ROWS:] = jnp.zeros((2, 2 * ORB, TILE - ROWS), F32)
    head, tail = shared_head(tiles[4], 1), tiles[6]
    forward_ref[2] = jnp.where(low, swapped(head), swapped(tail)).astype(BF16)
    forward_ref[3] = jnp.where(low, swapped(tail), 0.0).astype(BF16)

    def add_face(i):
        here = halo_rows(i)
        there = slice(ORB, ROWS) if i == 0 else slice(0, 2 * ORB)
        outer = slice(0, ORB) if i == 0 else slice(2 * ORB, ROWS)
        for t, value in enumerate(side_by_side(beside, i)):
            lanes = slice(128 * t, 128 * t + 128)
            beyond_ref[there, lanes] = value.astype(BF16) * around_ref[there, lanes]
            beyond_ref[outer, lanes] = far_off * around_ref[outer, lanes]
            halo_ref[:, lanes] = value.astype(BF16) * mask_ref[i, here, lanes]
            back_ref[:, lanes] = phi_ref[i, here, lanes] * around_ref[there, lanes]
        work_ref[0, :, :ROWS] = rows_product(halo_ref[...], phi_ref[i]) * scale
        work_ref[1, :, :ROWS] = rows_product(back_ref[...], beyond_ref[...]) * scale
        x, y = work_ref[0, :, 0:128], work_ref[0, :, 128:256]
        a, b = shifted(work_ref[1, :, 0:128], work_ref[1, :, 128:256])
        if i == 0:
            extra_ref[here, 0:128] = a
            extra_ref[here, 128:256] = b + x
            extra_ref[here, 256:384] = y
            own = slice(ORB, 2 * ORB)
        else:
            extra_ref[here, 128:256] = a + x
            extra_ref[here, 256:384] = b + y
            own = slice(0, ORB)
        a = swapped(shared_head(tiles[4], 0) + a[own])
        b = swapped(tiles[5] + b[own])
        x, y = swapped(x[own]), swapped(y[own])
        if i == 0:
            forward_ref[0] = jnp.where(low, a, b + x).astype(BF16)
            forward_ref[1] = jnp.where(low, b + x, y).astype(BF16)
        else:
            forward_ref[0] = jnp.where(low, a + x, b + y).astype(BF16)
            forward_ref[1] = jnp.where(low, b, x).astype(BF16)

    pl.when(even)(lambda: add_face(0))
    pl.when(jnp.logical_not(even))(lambda: add_face(1))


def add_halo(i, halo_ref, part_ref, mask_ref, energy_ref):
    here = halo_rows(i)
    value = part_ref[i, here] - 0.5 * halo_ref[...].astype(F32)
    energy_ref[i, here] = value.astype(BF16) * mask_ref[i, here]


def put_gradient(theta, orbital_ref, energy_ref, mask_ref, out_ref):
    for i in range(2):
        for t in range(PLANE // TILE):
            lanes = slice(TILE * t, TILE * t + TILE)
            fix = jnp.dot(theta, orbital_ref[i, :, lanes], preferred_element_type=F32)
            value = energy_ref[i, :, lanes].astype(F32) - fix
            out_ref[i, :, lanes] = value.astype(BF16) * mask_ref[i, :, lanes]


def split(value):
    high = value.astype(BF16)
    return high, (value - high.astype(F32)).astype(BF16)


def fine_product(a, b):
    return rows_product(a[0], b[0]) + (rows_product(a[0], b[1]) + rows_product(a[1], b[0]))


def theta_kernel(
    keep_ref, own_ref, rows_ref, other_ref, extra_ref, halo_ref, part_ref, edge_mask_ref, energy_in_ref,
    window_ref, theta_ref, energy_ref,
    ham_ref, inv_ref,
):
    even = is_even()
    low = low_half()
    zero = jnp.zeros((ORB, 128), F32)
    for which, band_ref in enumerate((ham_ref, inv_ref)):
        near, rest = shifted(*mate_blocks(rows_ref, which))
        ahead = other_ref[2 * which].astype(F32)
        beside = other_ref[2 * which + 1].astype(F32)
        head = shared_head(other_ref[4], which)
        tail = other_ref[5 + which].astype(F32)
        got_even = (
            (ahead, beside, zero, zero),
            (head, tail + near[:ORB], rest[:ORB], zero),
            (zero, near[ORB:], rest[ORB:], zero),
        )
        got_odd = (
            (near[:ORB], rest[:ORB], zero, zero),
            (near[ORB:], rest[ORB:] + head, tail, zero),
            (zero, jnp.where(low, 0.0, ahead), beside, jnp.where(low, ahead, 0.0)),
        )
        for r in range(3):
            for q in range(4):
                value = jnp.where(even, got_even[r][q], got_odd[r][q])
                if q in (1, 2):
                    value = value + own_ref[which, ORB * r : ORB * r + ORB, 128 * q - 128 : 128 * q]
                if which == 0:
                    value = value + extra_ref[ORB * r : ORB * r + ORB, 128 * q : 128 * q + 128]
                value = value * keep_ref[r : r + 1, 128 * q : 128 * q + 128]
                if which == 1:
                    on = iota((ORB, 128), 0) + (ORB * (r + 2) - 128 * q) == iota((ORB, 128), 1)
                    value = jnp.where(on, 2.0, 0.0) - value
                band_ref[ORB * r : ORB * r + ORB, 128 * q : 128 * q + 128] = value
    ham, inv = split(ham_ref[...]), split(inv_ref[...])
    theta_ref[...] = fine_product(ham, inv)
    for which, (high, _) in enumerate((ham, inv)):
        quarter = [high[:, 128 * q : 128 * q + 128].astype(F32) for q in range(4)]
        window_ref[which, :, 0:128] = jnp.where(even, quarter[2], quarter[0]).astype(BF16)
        last = jnp.where(even, jnp.where(low, quarter[3], quarter[1]), quarter[1])
        window_ref[which, :, 128:256] = last.astype(BF16)
    pl.when(even)(lambda: add_halo(0, halo_ref, part_ref, edge_mask_ref, energy_ref))
    pl.when(jnp.logical_not(even))(lambda: add_halo(1, halo_ref, part_ref, edge_mask_ref, energy_ref))


def gradient_kernel(
    keep_ref, relayed_ref, bands_ref, base_ref,
    edge_ref, edge_energy_ref, edge_mask_ref,
    edge_grad_ref, theta_ref, mate_ref, across_ref,
    window_ref, total_ref,
):
    even = is_even()
    low = low_half()
    more = []
    kept_even = (keep_ref[2:3, 256:384], jnp.where(low, keep_ref[2:3, 384:512], keep_ref[2:3, 128:256]))
    kept_odd = (keep_ref[0:1, 0:128], keep_ref[0:1, 128:256])
    for which in range(2):
        tiles = []
        for q in range(2):
            value = relayed_ref[2 * which + q].astype(F32)
            tiles.append(value * jnp.where(even, kept_even[q], kept_odd[q]))
        more.append(jnp.concatenate(tiles, axis=1))
    first, third = slice(0, ORB), slice(2 * ORB, ROWS)
    window_ref[...] = bands_ref[0]
    window_ref[first] = (bands_ref[0, first].astype(F32) + jnp.where(even, 0.0, more[0])).astype(BF16)
    window_ref[third] = (bands_ref[0, third].astype(F32) + jnp.where(even, more[0], 0.0)).astype(BF16)
    more = [value.astype(BF16) for value in more]
    column = rows_product(window_ref[...], more[1])
    row = rows_product(more[0], bands_ref[1])
    total_ref[...] = base_ref[...]
    total_ref[first] += jnp.where(even, 0.0, row)
    total_ref[third] += jnp.where(even, row, 0.0)
    total_ref[:, first] -= jnp.where(even, 0.0, column)
    total_ref[:, third] -= jnp.where(even, column, 0.0)
    theta = total_ref[...].astype(BF16)
    theta_ref[...] = theta
    put_gradient(theta, edge_ref, edge_energy_ref, edge_mask_ref, edge_grad_ref)
    put_messages(edge_grad_ref, mate_ref, across_ref)


def smooth_kernel(
    theta_ref, phi_ref, energy_ref, edge_ref, mask_ref, edge_mask_ref,
    out_ref, part_ref,
    grad_ref, done_ref, rest_ref, sems,
):
    put_gradient(theta_ref[...], phi_ref, energy_ref, mask_ref, grad_ref)
    weights = in_plane(8, 1)
    copies = []

    def send(source, rows, start, sem):
        copies.append(pltpu.make_async_copy(source, out_ref.at[rows, start : start + TILE], sem))
        copies[-1].start()

    for t in range(PLANE // TILE):
        lanes = slice(TILE * t, TILE * t + TILE)
        edge = edge_ref[:, :, lanes].astype(F32)
        mid = grad_ref[:, :, lanes].astype(F32)
        inner = plane_product(grad_ref, weights, 1.0, t)
        outer = plane_product(edge_ref, weights, 1.0, t)
        for i in range(2):
            value = (inner[i] + (edge[i] + mid[1 - i])) * (1.0 / 32.0)
            done_ref[i, :, lanes] = value.astype(BF16) * mask_ref[i, :, lanes]
            value = outer[i] + mid[i]
            part_ref[i, :, lanes] = value
            rest = rest_rows(i)
            value = value[rest] * (1.0 / 32.0)
            rest_ref[i, :, lanes] = value.astype(BF16) * edge_mask_ref[i, rest, lanes]
        for i in range(2):
            send(done_ref.at[i, :, lanes], slice(0, ROWS), PLANE * (1 + i) + TILE * t, sems.at[t, i])
            send(rest_ref.at[i, :, lanes], rest_rows(i), PLANE * (CX - 1) * i + TILE * t, sems.at[t, 2 + i])
    for copy in copies:
        copy.wait()


def finish_kernel(across_ref, mate_ref, part_ref, mask_ref, inner_ref, out_ref, done_ref, sems):
    halos = [
        side_by_side(unfold(side), i)
        for i, side in enumerate(sides(mate_ref[...].astype(F32), across_ref[...].astype(F32)))
    ]
    copies = []
    for i in range(2):
        start = PLANE * (CX - 1) * i
        for half in range(2):
            rows = slice(ORB * (half + i), ORB * (half + i) + ORB)
            got = slice(ORB * half, ORB * half + ORB)
            for t in range(PLANE // 128):
                lanes = slice(128 * t, 128 * t + 128)
                value = (part_ref[i, rows, lanes] + halos[i][t][got]) * (1.0 / 32.0)
                done_ref[i, got, lanes] = value.astype(BF16) * mask_ref[i, rows, lanes]
            copies.append(
                pltpu.make_async_copy(
                    done_ref.at[i, got], out_ref.at[rows, start : start + PLANE], sems.at[i, half]
                )
            )
            copies[-1].start()
    for copy in copies:
        copy.wait()


def shape(*dims, dtype=BF16):
    return jax.ShapeDtypeStruct(dims, dtype)


def cost(flops, moved):
    return pl.CostEstimate(flops=flops, bytes_accessed=moved, transcendentals=0)


PARAMS = pltpu.CompilerParams(vmem_limit_bytes=32 * 1024 * 1024)
WHOLE = pl.BlockSpec(memory_space=pltpu.VMEM)
FAR = pl.BlockSpec(memory_space=pltpu.HBM)


def far(value):
    return pltpu.with_memory_space_constraint(value, pltpu.HBM)


def per_device(pieces, potential, centers, pattern):
    count = lax.axis_size("sx")
    mates = [(i, i ^ 1) for i in range(count)]
    others = [(i, i + 1 if i % 2 else i - 1) for i in range(1, count - 1)]
    groups = lax.axis_size("grp")
    pairs = [[g * count + i, g * count + i + 1] for g in range(groups) for i in range(1, count - 1, 2)]
    ends = [g * count + end for g in range(groups) for end in (0, count - 1)]
    pairs += [[ends[i], ends[i + 2]] for i in range(len(ends)) if i % 4 < 2] if groups % 2 == 0 else [
        [ends[2 * i], ends[2 * i + 1]] for i in range(groups)
    ]

    def to_mate(value):
        return lax.ppermute(value, "sx", mates)

    def across(value):
        return lax.ppermute(value, "sx", others)

    def gathered(value):
        return lax.all_gather(value, ("grp", "sx"), axis_index_groups=pairs)

    table = centers.T
    patterns = pattern.T
    pair = shape(2, ROWS, PLANE)

    edge, edge_mask, rows, reach, for_mate = pl.pallas_call(
        edges_kernel,
        out_shape=(
            pair, pair, shape(5 * ORB, 16), shape(ROWS, PLANE, dtype=F32), shape(2 * ORB, 128),
        ),
        in_specs=[FAR, FAR],
        out_specs=(WHOLE,) * 5,
        scratch_shapes=[
            pltpu.VMEM((4, WINDOW), jnp.int32),
            pltpu.VMEM((2, ROWS, PLANE), BF16),
            pltpu.SemaphoreType.DMA((3,)),
        ],
        compiler_params=PARAMS,
        cost_estimate=cost(10**8, 10**6),
        name="edges",
    )(far(table), far(pieces))
    mate_side = to_mate(for_mate)

    mid, mid_mask, mid_energy, part, rest_energy, corr, ham = pl.pallas_call(
        energy_kernel,
        out_shape=(
            pair, pair, pair, shape(2, ROWS, PLANE, dtype=F32), pair,
            shape(ROWS, ROWS, dtype=F32), shape(ROWS, ROWS, dtype=F32),
        ),
        in_specs=[WHOLE] * 6,
        out_specs=(WHOLE,) * 7,
        compiler_params=PARAMS,
        cost_estimate=cost(4 * 10**9, 10**7),
        name="energy",
    )(rows, reach, pieces, potential, edge, edge_mask)

    edge_energy, own, for_mate = pl.pallas_call(
        bands_kernel,
        out_shape=(pair, shape(2, ROWS, TILE, dtype=F32), shape(3, 2 * ORB, 128)),
        in_specs=[WHOLE] * 7,
        out_specs=(WHOLE,) * 3,
        input_output_aliases={6: 0},
        compiler_params=PARAMS,
        cost_estimate=cost(10**9, 10**7),
        name="bands",
    )(mate_side, part, edge_mask, edge, corr, ham, rest_energy)
    mate_rows = to_mate(for_mate)
    around, keep, face = pl.pallas_call(
        around_kernel,
        out_shape=(shape(ROWS, PLANE), shape(3, 8 * ORB, dtype=F32), shape(FACE, 128)),
        in_specs=[FAR, WHOLE, WHOLE],
        out_specs=(WHOLE,) * 3,
        scratch_shapes=[pltpu.SMEM(patterns.shape, jnp.int32), pltpu.SemaphoreType.DMA],
        compiler_params=PARAMS,
        cost_estimate=cost(10**8, 10**6),
        name="around",
    )(far(patterns), rows, edge)
    for_other = pl.pallas_call(
        relay_kernel,
        out_shape=shape(7 * ORB + FACE, 128),
        in_specs=[WHOLE] * 3,
        out_specs=WHOLE,
        compiler_params=PARAMS,
        cost_estimate=cost(10**6, 10**6),
        name="relay",
    )(own, mate_rows, face)
    halo, other_rows, extra, forward = pl.pallas_call(
        face_kernel,
        out_shape=(
            shape(2 * ORB, PLANE), shape(7, ORB, 128), shape(ROWS, 8 * ORB, dtype=F32), shape(4, ORB, 128),
        ),
        in_specs=[WHOLE] * 4,
        out_specs=(WHOLE,) * 4,
        scratch_shapes=[
            pltpu.VMEM((ROWS, PLANE), BF16),
            pltpu.VMEM((2 * ORB, PLANE), BF16),
            pltpu.VMEM((2, 2 * ORB, TILE), F32),
        ],
        compiler_params=PARAMS,
        cost_estimate=cost(10**8, 10**6),
        name="face",
    )(gathered(for_other), around, edge, edge_mask)
    relayed = to_mate(forward)

    bands, base, edge_energy = pl.pallas_call(
        theta_kernel,
        out_shape=(shape(2, ROWS, TILE), shape(ROWS, ROWS, dtype=F32), pair),
        in_specs=[WHOLE] * 9,
        out_specs=(WHOLE,) * 3,
        scratch_shapes=[pltpu.VMEM((ROWS, 8 * ORB), F32), pltpu.VMEM((ROWS, 8 * ORB), F32)],
        input_output_aliases={8: 2},
        compiler_params=PARAMS,
        cost_estimate=cost(10**9, 4 * 10**6),
        name="theta",
    )(keep, own, mate_rows, other_rows, extra, halo, part, edge_mask, edge_energy)
    edge_grad, theta, for_mate, for_other = pl.pallas_call(
        gradient_kernel,
        out_shape=(pair, shape(ROWS, ROWS), shape(2 * ORB, 128), shape(2 * ORB, 128)),
        in_specs=[WHOLE] * 7,
        out_specs=(WHOLE,) * 4,
        scratch_shapes=[pltpu.VMEM((ROWS, TILE), BF16), pltpu.VMEM((ROWS, ROWS), F32)],
        compiler_params=PARAMS,
        cost_estimate=cost(10**9, 10**7),
        name="gradient",
    )(keep, relayed, bands, base, edge, edge_energy, edge_mask)
    other_side = across(for_other)
    mate_side = to_mate(for_mate)

    inner, part = pl.pallas_call(
        smooth_kernel,
        out_shape=(pltpu.HBM((ROWS, CX * PLANE), BF16), shape(2, ROWS, PLANE, dtype=F32)),
        in_specs=[WHOLE] * 6,
        out_specs=(FAR, WHOLE),
        scratch_shapes=[
            pltpu.VMEM((2, ROWS, PLANE), BF16),
            pltpu.VMEM((2, ROWS, PLANE), BF16),
            pltpu.VMEM((2, ORB, PLANE), BF16),
            pltpu.SemaphoreType.DMA((PLANE // TILE, 4)),
        ],
        compiler_params=PARAMS,
        cost_estimate=cost(2 * 10**9, 10**7),
        name="smooth",
    )(theta, mid, mid_energy, edge_grad, mid_mask, edge_mask)

    return pl.pallas_call(
        finish_kernel,
        out_shape=pltpu.HBM((ROWS, CX * PLANE), BF16),
        in_specs=[WHOLE] * 4 + [FAR],
        out_specs=FAR,
        scratch_shapes=[pltpu.VMEM((2, 2 * ORB, PLANE), BF16), pltpu.SemaphoreType.DMA((2, 2))],
        input_output_aliases={4: 0},
        compiler_params=PARAMS,
        cost_estimate=cost(10**7, 10**7),
        name="finish",
    )(other_side, mate_side, part, edge_mask, inner)


def solution(mesh):
    return jax.shard_map(
        per_device,
        mesh=mesh,
        in_specs=(P(("grp", "sx"), None), P(("grp", "sx"), None), P("grp", None), P("grp", None)),
        out_specs=P(("grp", "sx"), None),
        check_vma=False,
    )
```

```python
import functools

import jax
import jax.numpy as jnp
from jax import lax
from jax.experimental import pallas as pl
from jax.experimental.pallas import tpu as pltpu
from jax.sharding import PartitionSpec as P

ORB = 64
CX = 4
NY = 32
NZ = 32
ROWS = 3 * ORB
PLANE = NY * NZ
TILE = 256
WINDOW = 6 * ORB
FACE = 2 * ORB + ORB // 4
F32 = jnp.float32
BF16 = jnp.bfloat16


def iota(shape, dim):
    return lax.broadcasted_iota(jnp.int32, shape, dim)


def window_start(width):
    slab = lax.axis_index("sx")
    first = jnp.clip(slab * ORB - 2 * ORB, 0, width - WINDOW) // 128 * 128
    return pl.multiple_of(first, 128)


def row_features(window_ref, first):
    slab = lax.axis_index("sx")
    count = lax.axis_size("sx")
    window = window_ref[...]
    shift = slab * ORB - 2 * ORB - first
    window = pltpu.roll(jnp.concatenate([window, window], axis=0), lax.rem(WINDOW - shift, WINDOW), 1)
    lane = iota((1, WINDOW), 1)
    block = slab - 2 + lane // ORB
    valid = (block >= 0) & (block < count)
    cx = window[0:1] - slab * CX
    cy = window[1:2]
    cz = window[2:3]
    r = window[3:4]
    const = cx * cx + cy * cy + cz * cz - r * r
    const = jnp.where(valid, const, 65535)
    cx = jnp.where(valid, cx, 0)
    cy = jnp.where(valid, cy, 0)
    cz = jnp.where(valid, cz, 0)
    k = iota((16, WINDOW), 0)
    feats = jnp.where(k == 0, 1, 0)
    feats = jnp.where(k == 1, 256, feats)
    feats = jnp.where(k == 2, cy, feats)
    feats = jnp.where(k == 3, cz, feats)
    feats = jnp.where(k == 4, const & 255, feats)
    feats = jnp.where(k == 5, const >> 8, feats)
    feats = jnp.where(k == 6, cx, feats)
    return jnp.transpose(feats.astype(F32))[: 5 * ORB].astype(BF16)


def cell_features():
    k = iota((16, PLANE), 0)
    cell = iota((16, PLANE), 1)
    y = cell >> 5
    z = cell & 31
    sq = y * y + z * z
    feats = jnp.where(k == 0, sq & 255, 0)
    feats = jnp.where(k == 1, sq >> 8, feats)
    feats = jnp.where(k == 2, -2 * y, feats)
    feats = jnp.where(k == 3, -2 * z, feats)
    feats = jnp.where(k == 4, 1, feats)
    feats = jnp.where(k == 5, 256, feats)
    return feats.astype(F32).astype(BF16)


def sphere(reach, rows, plane):
    bound = rows[:, 6:7].astype(F32) * (2.0 * plane) - float(plane * plane)
    return jnp.where(reach <= bound, 1.0, 0.0).astype(BF16)


def in_plane(center, beside):
    k = iota((TILE, TILE), 0)
    n = iota((TILE, TILE), 1)
    diff = k - n
    near_y = (diff == NZ) | (diff == -NZ)
    near_z = ((diff == 1) | (diff == -1)) & ((k >> 5) == (n >> 5))
    w = jnp.where(near_y | near_z, float(beside), 0.0)
    return jnp.where(diff == 0, float(center), w).astype(BF16)


def plane_product(ref, weights, beside, t):
    start = TILE * t
    values = ref[:, :, start : start + TILE].reshape(2 * ROWS, TILE)
    out = jnp.dot(values, weights, preferred_element_type=F32).reshape(2, ROWS, TILE)
    lane = iota((1, 1, 128), 2)
    first, last = out[:, :, :128], out[:, :, 128:]
    if t > 0:
        turned = pltpu.roll(ref[:, :, start - 128 : start].astype(F32), NZ, 2)
        turned = jnp.where(lane < NZ, turned, 0.0)
        first = first + turned if beside > 0 else first - turned
    if start + TILE < PLANE:
        turned = pltpu.roll(ref[:, :, start + TILE : start + TILE + 128].astype(F32), 128 - NZ, 2)
        turned = jnp.where(lane >= 128 - NZ, turned, 0.0)
        last = last + turned if beside > 0 else last - turned
    return jnp.concatenate([first, last], axis=2)


def low_lanes(width):
    return (iota((1, 128), 1) & (2 * width - 1)) < width


def pack(first, second, width):
    return jnp.where(
        low_lanes(width),
        first + pltpu.roll(first, 128 - width, 1),
        second + pltpu.roll(second, width, 1),
    )


def unpack(packed, width):
    low = low_lanes(width)
    return (
        jnp.where(low, packed, pltpu.roll(packed, width, 1)),
        jnp.where(low, pltpu.roll(packed, 128 - width, 1), packed),
    )


def lane_tiles(values):
    return [values[:, 128 * t : 128 * t + 128] for t in range(PLANE // 128)]


def halves(values):
    half = values.shape[0] // 2
    return values[:half], values[half:]


def fold(full, side):
    tiles = lane_tiles(full)
    a, b, c = (sum(tiles[t::3][1:], tiles[t]) for t in range(3))
    tiles = lane_tiles(side)
    d, e = (sum(tiles[t::2][1:], tiles[t]) for t in range(2))
    return pack(a, b, 16), pack(*halves(c), 16), pack(*halves(pack(d, e, 16)), 8)


def unfold(packed):
    a, b = unpack(packed[:ORB], 16)
    c = jnp.concatenate(unpack(packed[ORB : ORB + ORB // 2], 16), axis=0)
    d, e = unpack(jnp.concatenate(unpack(packed[ORB + ORB // 2 : 2 * ORB], 8), axis=0), 16)
    return (a, b, c), (d, e)


def fold_far(values):
    tiles = lane_tiles(values)
    return pack(*halves(pack(*halves(sum(tiles[1:], tiles[0])), 16)), 8)


def unfold_far(packed):
    half = jnp.concatenate(unpack(packed, 8), axis=0)
    return jnp.concatenate(unpack(half, 16), axis=0)


def put_fold(ref, parts):
    start = 0
    for part in parts:
        ref[start : start + part.shape[0]] = part.astype(BF16)
        start += part.shape[0]


def side_by_side(unfolded, i):
    full, side = unfolded
    tiles = []
    for t in range(PLANE // 128):
        pair = [full[t % 3], side[t % 2]]
        tiles.append(jnp.concatenate(pair if i == 0 else pair[::-1], axis=0))
    return tiles


def is_even():
    return lax.rem(lax.axis_index("sx"), 2) == 0


def put_messages(planes, mate_ref, across_ref):
    own = slice(ORB, 2 * ORB)
    down = fold(planes[0, own].astype(F32), planes[0, :ORB].astype(F32))
    up = fold(planes[1, own].astype(F32), planes[1, 2 * ORB :].astype(F32))
    even = is_even()
    put_fold(mate_ref, [jnp.where(even, u, d) for u, d in zip(up, down)])
    put_fold(across_ref, [jnp.where(even, d, u) for u, d in zip(up, down)])


def sides(mate, across):
    even = is_even()
    return (jnp.where(even, across, mate), jnp.where(even, mate, across))


def at_end():
    slab = lax.axis_index("sx")
    return (slab == 0) | (slab == lax.axis_size("sx") - 1)


def kept(pattern_ref, r, q):
    slab = lax.axis_index("sx")
    last = pattern_ref.shape[1] - 1
    values = []
    for col in (2 * q, 2 * q + 1):
        apart = abs(col - r - 2)
        if apart == 0:
            values.append(1.0)
        elif apart > 2:
            values.append(0.0)
        else:
            at = jnp.clip(slab - 3 + min(col, r + 2), 0, last)
            values.append(pattern_ref[apart - 1, at].astype(F32))
    return jnp.where(low_half(), values[0], values[1])


def edges_kernel(
    table_ref, pieces_ref,
    phi_ref, mask_ref, rows_ref, reach_ref, mate_ref,
    window_ref, raw_ref, sems,
):
    first = window_start(table_ref.shape[1])
    table_copy = pltpu.make_async_copy(table_ref.at[:, pl.ds(first, WINDOW)], window_ref, sems.at[6])
    table_copy.start()
    copies = []
    for i in range(2):
        start = (CX - 1) * PLANE * i
        for j in range(3):
            rows = slice(ORB * j, ORB * j + ORB)
            copies.append(
                pltpu.make_async_copy(
                    pieces_ref.at[rows, start : start + PLANE], raw_ref.at[i, rows], sems.at[3 * i + j]
                )
            )
            copies[-1].start()
    cells = cell_features()
    table_copy.wait()
    blocks = row_features(window_ref, first)
    rows_ref[...] = blocks
    rows = blocks[ORB : 4 * ORB]
    reach = jnp.dot(rows, cells, preferred_element_type=F32)
    reach_ref[...] = reach
    for i in range(2):
        mask_ref[i] = sphere(reach, rows, (CX - 1) * i)
    for i in range(2):
        for j in range(3):
            copies[3 * i + j].wait()
        phi_ref[i] = raw_ref[i] * mask_ref[i]
    even = is_even()
    own = slice(ORB, 2 * ORB)
    lower, upper = phi_ref[0].astype(F32), phi_ref[1].astype(F32)
    put_fold(mate_ref, fold(jnp.where(even, upper[own], lower[own]), jnp.where(even, upper[2 * ORB :], lower[:ORB])))


def rows_product(a, b):
    return lax.dot_general(a, b, (((1,), (1,)), ((), ())), preferred_element_type=F32)


def energy_kernel(
    rows_ref, reach_ref, pieces_ref, pot_ref, edge_ref, edge_mask_ref,
    phi_ref, mask_ref, energy_ref, part_ref, edge_energy_ref, corr_ref, ham_ref,
):
    rows = rows_ref[ORB : 4 * ORB]
    for i in range(2):
        mask = sphere(reach_ref[...], rows, 1 + i)
        mask_ref[i] = mask
        phi_ref[i] = pieces_ref[:, PLANE * (1 + i) : PLANE * (2 + i)] * mask
    weights = in_plane(6, -1)
    for t in range(PLANE // TILE):
        lanes = slice(TILE * t, TILE * t + TILE)
        edge = edge_ref[:, :, lanes].astype(F32)
        mid = phi_ref[:, :, lanes].astype(F32)
        inner = plane_product(phi_ref, weights, -1.0, t)
        outer = plane_product(edge_ref, weights, -1.0, t)
        for i in range(2):
            value = 0.5 * (inner[i] - (edge[i] + mid[1 - i])) + pot_ref[1 + i : 2 + i, lanes] * mid[i]
            energy_ref[i, :, lanes] = value.astype(BF16) * mask_ref[i, :, lanes]
            plane = (CX - 1) * i
            value = 0.5 * (outer[i] - mid[i]) + pot_ref[plane : plane + 1, lanes] * edge[i]
            part_ref[i, :, lanes] = value
            rest = rest_rows(i)
            edge_energy_ref[i, rest, lanes] = value[rest].astype(BF16) * edge_mask_ref[i, rest, lanes]
    mid = jnp.concatenate([phi_ref[0], phi_ref[1]], axis=1)
    both = jnp.concatenate([energy_ref[0], energy_ref[1]], axis=1)
    gram = rows_product(jnp.concatenate([mid, both], axis=0), mid)
    corr = gram[:ROWS]
    ham_ref[...] = gram[ROWS:]
    for i in range(2):
        rest = rest_rows(i)
        gram = rows_product(jnp.concatenate([edge_ref[i], edge_energy_ref[i, rest]], axis=0), edge_ref[i])
        corr = corr + gram[:ROWS]
        ham_ref[rest] += gram[ROWS:]
    corr_ref[...] = corr


def halo_rows(i):
    return slice(0, 2 * ORB) if i == 0 else slice(ORB, ROWS)


def rest_rows(i):
    return slice(2 * ORB, ROWS) if i == 0 else slice(0, ORB)


def bands_kernel(
    mate_ref, part_ref, mask_ref, phi_ref, corr_ref, ham_ref, rest_ref,
    energy_ref, own_ref, rows_ref,
):
    volume = 1.0 / (4.0 * CX**3)
    gram = []
    unfolded = unfold(mate_ref[...].astype(F32))
    for i in range(2):
        factor = jnp.where(is_even() == (i == 1), 0.5, 0.0)
        tiles = side_by_side(unfolded, i)
        for t in range(PLANE // 128):
            lanes = slice(128 * t, 128 * t + 128)
            value = part_ref[i, halo_rows(i), lanes] - factor * tiles[t]
            energy_ref[i, halo_rows(i), lanes] = value.astype(BF16) * mask_ref[i, halo_rows(i), lanes]
        gram.append(rows_product(energy_ref[i, halo_rows(i)], phi_ref[i]))
    own_ref[:, :, ROWS:] = jnp.zeros((2, ROWS, TILE - ROWS), F32)
    own_ref[0, :ORB, :ROWS] = (ham_ref[:ORB] + gram[0][:ORB]) * volume
    own_ref[0, ORB : 2 * ORB, :ROWS] = (ham_ref[ORB : 2 * ORB] + gram[0][ORB:] + gram[1][:ORB]) * volume
    own_ref[0, 2 * ORB :, :ROWS] = (ham_ref[2 * ORB :] + gram[1][ORB:]) * volume
    own_ref[1, :, :ROWS] = corr_ref[...] * volume
    tail = jnp.where(low_half(), own_ref[0, :, 128:256], swapped(own_ref[1, :, 128:256]))
    even = is_even()
    for i, value in enumerate((own_ref[0, :, 0:128], own_ref[1, :, 0:128], tail)):
        rows_ref[i] = jnp.where(even, value[ORB:], value[: 2 * ORB]).astype(BF16)


def low_half():
    return iota((1, 128), 1) < 64


def swapped(value):
    return pltpu.roll(value, 64, 1)


def mate_blocks(rows_ref, which):
    tail = rows_ref[2].astype(F32)
    if which == 1:
        tail = swapped(tail)
    return rows_ref[which].astype(F32), jnp.where(low_half(), tail, 0.0)


def shifted(c01, c2x):
    low = low_half()
    turned = swapped(c01)
    return jnp.where(low, 0.0, turned), jnp.where(low, turned, swapped(c2x))


def relay_kernel(own_ref, rows_ref, face_ref, out_ref):
    even = is_even()
    heads = []

    def put(i, value):
        out_ref[ORB * i : ORB * i + ORB] = value.astype(BF16)

    for which in range(2):
        head, rest = shifted(own_ref[which, :, 0:128], own_ref[which, :, 128:256])
        c01, c2x = mate_blocks(rows_ref, which)
        c01 = jnp.where(even, c01[:ORB], c01[ORB:])
        c2x = jnp.where(even, c2x[:ORB], c2x[ORB:])
        own = slice(ORB, 2 * ORB)
        put(2 * which, head[own] + jnp.where(even, c2x, c01))
        put(2 * which + 1, rest[own] + jnp.where(even, c01, c2x))
        put(5 + which, jnp.where(even, rest[:ORB], rest[2 * ORB :]))
        heads.append(jnp.where(even, head[:ORB], head[2 * ORB :]))
    put(4, jnp.where(low_half(), swapped(heads[1]), heads[0]))
    out_ref[7 * ORB :] = face_ref[...]


def around_kernel(pattern_ref, rows_ref, phi_ref, mask_ref, keep_ref, face_ref, scalar_ref, sem):
    pattern_copy = pltpu.make_async_copy(pattern_ref, scalar_ref, sem)
    pattern_copy.start()
    even = is_even()
    own = slice(ORB, 2 * ORB)
    lower, upper = phi_ref[0].astype(F32), phi_ref[1].astype(F32)
    parts = fold(jnp.where(even, lower[own], upper[own]), jnp.where(even, lower[:ORB], upper[2 * ORB :]))
    put_fold(face_ref, parts + (fold_far(jnp.where(even, lower[2 * ORB :], upper[:ORB])),))
    rows = jnp.where(even, rows_ref[:ROWS].astype(F32), rows_ref[2 * ORB :].astype(F32))
    reach = jnp.dot(rows.astype(BF16), cell_features(), preferred_element_type=F32)
    plane = jnp.where(even, -1.0, float(CX))
    bound = rows[:, 6:7] * (2.0 * plane) - plane * plane
    mask_ref[...] = jnp.where(reach <= bound, 1.0, 0.0).astype(BF16)
    pattern_copy.wait()
    for r in range(3):
        for q in range(4):
            keep_ref[r : r + 1, 128 * q : 128 * q + 128] = kept(scalar_ref, r, q)


def shared_head(tile, which):
    tile = tile.astype(F32)
    if which == 1:
        tile = swapped(tile)
    return jnp.where(low_half(), 0.0, tile)


def face_kernel(
    both_ref, around_ref, phi_ref, mask_ref,
    halo_ref, other_ref, extra_ref, forward_ref,
    beyond_ref, back_ref, work_ref,
):
    even = is_even()
    low = low_half()
    scale = -0.5 / (4.0 * CX**3)

    def got(start, size):
        rows = slice(start, start + size)
        value = jnp.where(even, both_ref[0, rows].astype(F32), both_ref[1, rows].astype(F32))
        return jnp.where(at_end(), 0.0, value)

    tiles = [got(ORB * i, ORB) for i in range(7)]
    for i in range(7):
        other_ref[i] = tiles[i].astype(BF16)
    beside = unfold(got(7 * ORB, 2 * ORB))
    far_off = unfold_far(got(9 * ORB, ORB // 4)).astype(BF16)
    extra_ref[...] = jnp.zeros((ROWS, 8 * ORB), F32)
    work_ref[:, :, ROWS:] = jnp.zeros((2, 2 * ORB, TILE - ROWS), F32)
    head, tail = shared_head(tiles[4], 1), tiles[6]
    forward_ref[2] = jnp.where(low, swapped(head), swapped(tail)).astype(BF16)
    forward_ref[3] = jnp.where(low, swapped(tail), 0.0).astype(BF16)

    def add_face(i):
        here = halo_rows(i)
        there = slice(ORB, ROWS) if i == 0 else slice(0, 2 * ORB)
        outer = slice(0, ORB) if i == 0 else slice(2 * ORB, ROWS)
        for t, value in enumerate(side_by_side(beside, i)):
            lanes = slice(128 * t, 128 * t + 128)
            beyond_ref[there, lanes] = value.astype(BF16) * around_ref[there, lanes]
            beyond_ref[outer, lanes] = far_off * around_ref[outer, lanes]
            halo_ref[:, lanes] = value.astype(BF16) * mask_ref[i, here, lanes]
            back_ref[:, lanes] = phi_ref[i, here, lanes] * around_ref[there, lanes]
        work_ref[0, :, :ROWS] = rows_product(halo_ref[...], phi_ref[i]) * scale
        work_ref[1, :, :ROWS] = rows_product(back_ref[...], beyond_ref[...]) * scale
        x, y = work_ref[0, :, 0:128], work_ref[0, :, 128:256]
        a, b = shifted(work_ref[1, :, 0:128], work_ref[1, :, 128:256])
        if i == 0:
            extra_ref[here, 0:128] = a
            extra_ref[here, 128:256] = b + x
            extra_ref[here, 256:384] = y
            own = slice(ORB, 2 * ORB)
        else:
            extra_ref[here, 128:256] = a + x
            extra_ref[here, 256:384] = b + y
            own = slice(0, ORB)
        a = swapped(shared_head(tiles[4], 0) + a[own])
        b = swapped(tiles[5] + b[own])
        x, y = swapped(x[own]), swapped(y[own])
        if i == 0:
            forward_ref[0] = jnp.where(low, a, b + x).astype(BF16)
            forward_ref[1] = jnp.where(low, b + x, y).astype(BF16)
        else:
            forward_ref[0] = jnp.where(low, a + x, b + y).astype(BF16)
            forward_ref[1] = jnp.where(low, b, x).astype(BF16)

    pl.when(even)(lambda: add_face(0))
    pl.when(jnp.logical_not(even))(lambda: add_face(1))


def add_halo(i, halo_ref, part_ref, mask_ref, energy_ref):
    here = halo_rows(i)
    value = part_ref[i, here] - 0.5 * halo_ref[...].astype(F32)
    energy_ref[i, here] = value.astype(BF16) * mask_ref[i, here]


def put_gradient(theta, orbital_ref, energy_ref, mask_ref, out_ref):
    for i in range(2):
        for t in range(PLANE // TILE):
            lanes = slice(TILE * t, TILE * t + TILE)
            fix = jnp.dot(theta, orbital_ref[i, :, lanes], preferred_element_type=F32)
            value = energy_ref[i, :, lanes].astype(F32) - fix
            out_ref[i, :, lanes] = value.astype(BF16) * mask_ref[i, :, lanes]


def split(value):
    high = value.astype(BF16)
    return high, (value - high.astype(F32)).astype(BF16)


def fine_product(a, b):
    return rows_product(a[0], b[0]) + (rows_product(a[0], b[1]) + rows_product(a[1], b[0]))


def theta_kernel(
    keep_ref, own_ref, rows_ref, other_ref, extra_ref, halo_ref, part_ref, edge_mask_ref, energy_in_ref,
    window_ref, theta_ref, energy_ref,
    ham_ref, inv_ref,
):
    even = is_even()
    low = low_half()
    zero = jnp.zeros((ORB, 128), F32)
    for which, band_ref in enumerate((ham_ref, inv_ref)):
        near, rest = shifted(*mate_blocks(rows_ref, which))
        ahead = other_ref[2 * which].astype(F32)
        beside = other_ref[2 * which + 1].astype(F32)
        head = shared_head(other_ref[4], which)
        tail = other_ref[5 + which].astype(F32)
        got_even = (
            (ahead, beside, zero, zero),
            (head, tail + near[:ORB], rest[:ORB], zero),
            (zero, near[ORB:], rest[ORB:], zero),
        )
        got_odd = (
            (near[:ORB], rest[:ORB], zero, zero),
            (near[ORB:], rest[ORB:] + head, tail, zero),
            (zero, jnp.where(low, 0.0, ahead), beside, jnp.where(low, ahead, 0.0)),
        )
        for r in range(3):
            for q in range(4):
                value = jnp.where(even, got_even[r][q], got_odd[r][q])
                if q in (1, 2):
                    value = value + own_ref[which, ORB * r : ORB * r + ORB, 128 * q - 128 : 128 * q]
                if which == 0:
                    value = value + extra_ref[ORB * r : ORB * r + ORB, 128 * q : 128 * q + 128]
                value = value * keep_ref[r : r + 1, 128 * q : 128 * q + 128]
                if which == 1:
                    on = iota((ORB, 128), 0) + (ORB * (r + 2) - 128 * q) == iota((ORB, 128), 1)
                    value = jnp.where(on, 2.0, 0.0) - value
                band_ref[ORB * r : ORB * r + ORB, 128 * q : 128 * q + 128] = value
    ham, inv = split(ham_ref[...]), split(inv_ref[...])
    theta_ref[...] = fine_product(ham, inv)
    for which, (high, _) in enumerate((ham, inv)):
        quarter = [high[:, 128 * q : 128 * q + 128].astype(F32) for q in range(4)]
        window_ref[which, :, 0:128] = jnp.where(even, quarter[2], quarter[0]).astype(BF16)
        last = jnp.where(even, jnp.where(low, quarter[3], quarter[1]), quarter[1])
        window_ref[which, :, 128:256] = last.astype(BF16)
    pl.when(even)(lambda: add_halo(0, halo_ref, part_ref, edge_mask_ref, energy_ref))
    pl.when(jnp.logical_not(even))(lambda: add_halo(1, halo_ref, part_ref, edge_mask_ref, energy_ref))


def gradient_kernel(
    keep_ref, relayed_ref, bands_ref, base_ref,
    edge_ref, edge_energy_ref, edge_mask_ref,
    edge_grad_ref, theta_ref, mate_ref, across_ref,
    window_ref, total_ref,
):
    even = is_even()
    low = low_half()
    more = []
    kept_even = (keep_ref[2:3, 256:384], jnp.where(low, keep_ref[2:3, 384:512], keep_ref[2:3, 128:256]))
    kept_odd = (keep_ref[0:1, 0:128], keep_ref[0:1, 128:256])
    for which in range(2):
        tiles = []
        for q in range(2):
            value = relayed_ref[2 * which + q].astype(F32)
            tiles.append(value * jnp.where(even, kept_even[q], kept_odd[q]))
        more.append(jnp.concatenate(tiles, axis=1))
    first, third = slice(0, ORB), slice(2 * ORB, ROWS)
    window_ref[...] = bands_ref[0]
    window_ref[first] = (bands_ref[0, first].astype(F32) + jnp.where(even, 0.0, more[0])).astype(BF16)
    window_ref[third] = (bands_ref[0, third].astype(F32) + jnp.where(even, more[0], 0.0)).astype(BF16)
    more = [value.astype(BF16) for value in more]
    column = rows_product(window_ref[...], more[1])
    row = rows_product(more[0], bands_ref[1])
    total_ref[...] = base_ref[...]
    total_ref[first] += jnp.where(even, 0.0, row)
    total_ref[third] += jnp.where(even, row, 0.0)
    total_ref[:, first] -= jnp.where(even, 0.0, column)
    total_ref[:, third] -= jnp.where(even, column, 0.0)
    theta = total_ref[...].astype(BF16)
    theta_ref[...] = theta
    put_gradient(theta, edge_ref, edge_energy_ref, edge_mask_ref, edge_grad_ref)
    put_messages(edge_grad_ref, mate_ref, across_ref)


def smooth_kernel(
    theta_ref, phi_ref, energy_ref, edge_ref, mask_ref, edge_mask_ref,
    out_ref, part_ref,
    grad_ref, done_ref, rest_ref, sems,
):
    put_gradient(theta_ref[...], phi_ref, energy_ref, mask_ref, grad_ref)
    weights = in_plane(8, 1)
    copies = []

    def send(source, rows, start, sem):
        copies.append(pltpu.make_async_copy(source, out_ref.at[rows, start : start + TILE], sem))
        copies[-1].start()

    for t in range(PLANE // TILE):
        lanes = slice(TILE * t, TILE * t + TILE)
        edge = edge_ref[:, :, lanes].astype(F32)
        mid = grad_ref[:, :, lanes].astype(F32)
        inner = plane_product(grad_ref, weights, 1.0, t)
        outer = plane_product(edge_ref, weights, 1.0, t)
        for i in range(2):
            value = (inner[i] + (edge[i] + mid[1 - i])) * (1.0 / 32.0)
            done_ref[i, :, lanes] = value.astype(BF16) * mask_ref[i, :, lanes]
            value = outer[i] + mid[i]
            part_ref[i, :, lanes] = value
            rest = rest_rows(i)
            value = value[rest] * (1.0 / 32.0)
            rest_ref[i, :, lanes] = value.astype(BF16) * edge_mask_ref[i, rest, lanes]
        for i in range(2):
            send(done_ref.at[i, :, lanes], slice(0, ROWS), PLANE * (1 + i) + TILE * t, sems.at[t, i])
            send(rest_ref.at[i, :, lanes], rest_rows(i), PLANE * (CX - 1) * i + TILE * t, sems.at[t, 2 + i])
    for copy in copies:
        copy.wait()


def finish_kernel(across_ref, mate_ref, part_ref, mask_ref, inner_ref, out_ref, done_ref, sems):
    halos = [
        side_by_side(unfold(side), i)
        for i, side in enumerate(sides(mate_ref[...].astype(F32), across_ref[...].astype(F32)))
    ]
    copies = []
    for i in range(2):
        start = PLANE * (CX - 1) * i
        for half in range(2):
            rows = slice(ORB * (half + i), ORB * (half + i) + ORB)
            got = slice(ORB * half, ORB * half + ORB)
            for t in range(PLANE // 128):
                lanes = slice(128 * t, 128 * t + 128)
                value = (part_ref[i, rows, lanes] + halos[i][t][got]) * (1.0 / 32.0)
                done_ref[i, got, lanes] = value.astype(BF16) * mask_ref[i, rows, lanes]
            copies.append(
                pltpu.make_async_copy(
                    done_ref.at[i, got], out_ref.at[rows, start : start + PLANE], sems.at[i, half]
                )
            )
            copies[-1].start()
    for copy in copies:
        copy.wait()


def shape(*dims, dtype=BF16):
    return jax.ShapeDtypeStruct(dims, dtype)


def cost(flops, moved):
    return pl.CostEstimate(flops=flops, bytes_accessed=moved, transcendentals=0)


PARAMS = pltpu.CompilerParams(vmem_limit_bytes=32 * 1024 * 1024)
WHOLE = pl.BlockSpec(memory_space=pltpu.VMEM)
FAR = pl.BlockSpec(memory_space=pltpu.HBM)


def far(value):
    return pltpu.with_memory_space_constraint(value, pltpu.HBM)


def per_device(pieces, potential, centers, pattern):
    count = lax.axis_size("sx")
    mates = [(i, i ^ 1) for i in range(count)]
    others = [(i, i + 1 if i % 2 else i - 1) for i in range(1, count - 1)]
    groups = lax.axis_size("grp")
    pairs = [[g * count + i, g * count + i + 1] for g in range(groups) for i in range(1, count - 1, 2)]
    ends = [g * count + end for g in range(groups) for end in (0, count - 1)]
    pairs += [[ends[i], ends[i + 2]] for i in range(len(ends)) if i % 4 < 2] if groups % 2 == 0 else [
        [ends[2 * i], ends[2 * i + 1]] for i in range(groups)
    ]

    def to_mate(value):
        return lax.ppermute(value, "sx", mates)

    def across(value):
        return lax.ppermute(value, "sx", others)

    def gathered(value):
        return lax.all_gather(value, ("grp", "sx"), axis_index_groups=pairs)

    table = centers.T
    patterns = pattern.T
    pair = shape(2, ROWS, PLANE)

    edge, edge_mask, rows, reach, for_mate = pl.pallas_call(
        edges_kernel,
        out_shape=(
            pair, pair, shape(5 * ORB, 16), shape(ROWS, PLANE, dtype=F32), shape(2 * ORB, 128),
        ),
        in_specs=[FAR, FAR],
        out_specs=(WHOLE,) * 5,
        scratch_shapes=[
            pltpu.VMEM((4, WINDOW), jnp.int32),
            pltpu.VMEM((2, ROWS, PLANE), BF16),
            pltpu.SemaphoreType.DMA((7,)),
        ],
        compiler_params=PARAMS,
        cost_estimate=cost(10**8, 10**6),
        name="edges",
    )(far(table), far(pieces))
    mate_side = to_mate(for_mate)

    mid, mid_mask, mid_energy, part, rest_energy, corr, ham = pl.pallas_call(
        energy_kernel,
        out_shape=(
            pair, pair, pair, shape(2, ROWS, PLANE, dtype=F32), pair,
            shape(ROWS, ROWS, dtype=F32), shape(ROWS, ROWS, dtype=F32),
        ),
        in_specs=[WHOLE] * 6,
        out_specs=(WHOLE,) * 7,
        compiler_params=PARAMS,
        cost_estimate=cost(4 * 10**9, 10**7),
        name="energy",
    )(rows, reach, pieces, potential, edge, edge_mask)

    edge_energy, own, for_mate = pl.pallas_call(
        bands_kernel,
        out_shape=(pair, shape(2, ROWS, TILE, dtype=F32), shape(3, 2 * ORB, 128)),
        in_specs=[WHOLE] * 7,
        out_specs=(WHOLE,) * 3,
        input_output_aliases={6: 0},
        compiler_params=PARAMS,
        cost_estimate=cost(10**9, 10**7),
        name="bands",
    )(mate_side, part, edge_mask, edge, corr, ham, rest_energy)
    mate_rows = to_mate(for_mate)
    around, keep, face = pl.pallas_call(
        around_kernel,
        out_shape=(shape(ROWS, PLANE), shape(3, 8 * ORB, dtype=F32), shape(FACE, 128)),
        in_specs=[FAR, WHOLE, WHOLE],
        out_specs=(WHOLE,) * 3,
        scratch_shapes=[pltpu.SMEM(patterns.shape, jnp.int32), pltpu.SemaphoreType.DMA],
        compiler_params=PARAMS,
        cost_estimate=cost(10**8, 10**6),
        name="around",
    )(far(patterns), rows, edge)
    for_other = pl.pallas_call(
        relay_kernel,
        out_shape=shape(7 * ORB + FACE, 128),
        in_specs=[WHOLE] * 3,
        out_specs=WHOLE,
        compiler_params=PARAMS,
        cost_estimate=cost(10**6, 10**6),
        name="relay",
    )(own, mate_rows, face)
    halo, other_rows, extra, forward = pl.pallas_call(
        face_kernel,
        out_shape=(
            shape(2 * ORB, PLANE), shape(7, ORB, 128), shape(ROWS, 8 * ORB, dtype=F32), shape(4, ORB, 128),
        ),
        in_specs=[WHOLE] * 4,
        out_specs=(WHOLE,) * 4,
        scratch_shapes=[
            pltpu.VMEM((ROWS, PLANE), BF16),
            pltpu.VMEM((2 * ORB, PLANE), BF16),
            pltpu.VMEM((2, 2 * ORB, TILE), F32),
        ],
        compiler_params=PARAMS,
        cost_estimate=cost(10**8, 10**6),
        name="face",
    )(gathered(for_other), around, edge, edge_mask)
    relayed = to_mate(forward)

    bands, base, edge_energy = pl.pallas_call(
        theta_kernel,
        out_shape=(shape(2, ROWS, TILE), shape(ROWS, ROWS, dtype=F32), pair),
        in_specs=[WHOLE] * 9,
        out_specs=(WHOLE,) * 3,
        scratch_shapes=[pltpu.VMEM((ROWS, 8 * ORB), F32), pltpu.VMEM((ROWS, 8 * ORB), F32)],
        input_output_aliases={8: 2},
        compiler_params=PARAMS,
        cost_estimate=cost(10**9, 4 * 10**6),
        name="theta",
    )(keep, own, mate_rows, other_rows, extra, halo, part, edge_mask, edge_energy)
    edge_grad, theta, for_mate, for_other = pl.pallas_call(
        gradient_kernel,
        out_shape=(pair, shape(ROWS, ROWS), shape(2 * ORB, 128), shape(2 * ORB, 128)),
        in_specs=[WHOLE] * 7,
        out_specs=(WHOLE,) * 4,
        scratch_shapes=[pltpu.VMEM((ROWS, TILE), BF16), pltpu.VMEM((ROWS, ROWS), F32)],
        compiler_params=PARAMS,
        cost_estimate=cost(10**9, 10**7),
        name="gradient",
    )(keep, relayed, bands, base, edge, edge_energy, edge_mask)
    other_side = across(for_other)
    mate_side = to_mate(for_mate)

    inner, part = pl.pallas_call(
        smooth_kernel,
        out_shape=(pltpu.HBM((ROWS, CX * PLANE), BF16), shape(2, ROWS, PLANE, dtype=F32)),
        in_specs=[WHOLE] * 6,
        out_specs=(FAR, WHOLE),
        scratch_shapes=[
            pltpu.VMEM((2, ROWS, PLANE), BF16),
            pltpu.VMEM((2, ROWS, PLANE), BF16),
            pltpu.VMEM((2, ORB, PLANE), BF16),
            pltpu.SemaphoreType.DMA((PLANE // TILE, 4)),
        ],
        compiler_params=PARAMS,
        cost_estimate=cost(2 * 10**9, 10**7),
        name="smooth",
    )(theta, mid, mid_energy, edge_grad, mid_mask, edge_mask)

    return pl.pallas_call(
        finish_kernel,
        out_shape=pltpu.HBM((ROWS, CX * PLANE), BF16),
        in_specs=[WHOLE] * 4 + [FAR],
        out_specs=FAR,
        scratch_shapes=[pltpu.VMEM((2, 2 * ORB, PLANE), BF16), pltpu.SemaphoreType.DMA((2, 2))],
        input_output_aliases={4: 0},
        compiler_params=PARAMS,
        cost_estimate=cost(10**7, 10**7),
        name="finish",
    )(other_side, mate_side, part, edge_mask, inner)


def solution(mesh):
    return jax.shard_map(
        per_device,
        mesh=mesh,
        in_specs=(P(("grp", "sx"), None), P(("grp", "sx"), None), P("grp", None), P("grp", None)),
        out_specs=P(("grp", "sx"), None),
        check_vma=False,
    )
```

```python
import functools

import jax
import jax.numpy as jnp
from jax import lax
from jax.experimental import pallas as pl
from jax.experimental.pallas import tpu as pltpu
from jax.sharding import PartitionSpec as P

ORB = 64
CX = 4
NY = 32
NZ = 32
ROWS = 3 * ORB
PLANE = NY * NZ
TILE = 256
WINDOW = 6 * ORB
FACE = 2 * ORB + ORB // 4
F32 = jnp.float32
BF16 = jnp.bfloat16


def iota(shape, dim):
    return lax.broadcasted_iota(jnp.int32, shape, dim)


def window_start(width):
    slab = lax.axis_index("sx")
    first = jnp.clip(slab * ORB - 2 * ORB, 0, width - WINDOW) // 128 * 128
    return pl.multiple_of(first, 128)


def row_features(window_ref, first):
    slab = lax.axis_index("sx")
    count = lax.axis_size("sx")
    window = window_ref[...]
    shift = slab * ORB - 2 * ORB - first
    window = pltpu.roll(jnp.concatenate([window, window], axis=0), lax.rem(WINDOW - shift, WINDOW), 1)
    lane = iota((1, WINDOW), 1)
    block = slab - 2 + lane // ORB
    valid = (block >= 0) & (block < count)
    cx = window[0:1] - slab * CX
    cy = window[1:2]
    cz = window[2:3]
    r = window[3:4]
    const = cx * cx + cy * cy + cz * cz - r * r
    const = jnp.where(valid, const, 65535)
    cx = jnp.where(valid, cx, 0)
    cy = jnp.where(valid, cy, 0)
    cz = jnp.where(valid, cz, 0)
    k = iota((16, WINDOW), 0)
    feats = jnp.where(k == 0, 1, 0)
    feats = jnp.where(k == 1, 256, feats)
    feats = jnp.where(k == 2, cy, feats)
    feats = jnp.where(k == 3, cz, feats)
    feats = jnp.where(k == 4, const & 255, feats)
    feats = jnp.where(k == 5, const >> 8, feats)
    feats = jnp.where(k == 6, cx, feats)
    return jnp.transpose(feats.astype(F32))[: 5 * ORB].astype(BF16)


def cell_features():
    k = iota((16, PLANE), 0)
    cell = iota((16, PLANE), 1)
    y = cell >> 5
    z = cell & 31
    sq = y * y + z * z
    feats = jnp.where(k == 0, sq & 255, 0)
    feats = jnp.where(k == 1, sq >> 8, feats)
    feats = jnp.where(k == 2, -2 * y, feats)
    feats = jnp.where(k == 3, -2 * z, feats)
    feats = jnp.where(k == 4, 1, feats)
    feats = jnp.where(k == 5, 256, feats)
    return feats.astype(F32).astype(BF16)


def sphere(reach, rows, plane):
    bound = rows[:, 6:7].astype(F32) * (2.0 * plane) - float(plane * plane)
    return jnp.where(reach <= bound, 1.0, 0.0).astype(BF16)


def in_plane(center, beside):
    k = iota((TILE, TILE), 0)
    n = iota((TILE, TILE), 1)
    diff = k - n
    near_y = (diff == NZ) | (diff == -NZ)
    near_z = ((diff == 1) | (diff == -1)) & ((k >> 5) == (n >> 5))
    w = jnp.where(near_y | near_z, float(beside), 0.0)
    return jnp.where(diff == 0, float(center), w).astype(BF16)


def plane_product(ref, weights, beside, t):
    start = TILE * t
    values = ref[:, :, start : start + TILE].reshape(2 * ROWS, TILE)
    out = jnp.dot(values, weights, preferred_element_type=F32).reshape(2, ROWS, TILE)
    lane = iota((1, 1, 128), 2)
    first, last = out[:, :, :128], out[:, :, 128:]
    if t > 0:
        turned = pltpu.roll(ref[:, :, start - 128 : start].astype(F32), NZ, 2)
        turned = jnp.where(lane < NZ, turned, 0.0)
        first = first + turned if beside > 0 else first - turned
    if start + TILE < PLANE:
        turned = pltpu.roll(ref[:, :, start + TILE : start + TILE + 128].astype(F32), 128 - NZ, 2)
        turned = jnp.where(lane >= 128 - NZ, turned, 0.0)
        last = last + turned if beside > 0 else last - turned
    return jnp.concatenate([first, last], axis=2)


def low_lanes(width):
    return (iota((1, 128), 1) & (2 * width - 1)) < width


def pack(first, second, width):
    return jnp.where(
        low_lanes(width),
        first + pltpu.roll(first, 128 - width, 1),
        second + pltpu.roll(second, width, 1),
    )


def unpack(packed, width):
    low = low_lanes(width)
    return (
        jnp.where(low, packed, pltpu.roll(packed, width, 1)),
        jnp.where(low, pltpu.roll(packed, 128 - width, 1), packed),
    )


def lane_tiles(values):
    return [values[:, 128 * t : 128 * t + 128] for t in range(PLANE // 128)]


def halves(values):
    half = values.shape[0] // 2
    return values[:half], values[half:]


def fold(full, side):
    tiles = lane_tiles(full)
    a, b, c = (sum(tiles[t::3][1:], tiles[t]) for t in range(3))
    tiles = lane_tiles(side)
    d, e = (sum(tiles[t::2][1:], tiles[t]) for t in range(2))
    return pack(a, b, 16), pack(*halves(c), 16), pack(*halves(pack(d, e, 16)), 8)


def unfold(packed):
    a, b = unpack(packed[:ORB], 16)
    c = jnp.concatenate(unpack(packed[ORB : ORB + ORB // 2], 16), axis=0)
    d, e = unpack(jnp.concatenate(unpack(packed[ORB + ORB // 2 : 2 * ORB], 8), axis=0), 16)
    return (a, b, c), (d, e)


def fold_far(values):
    tiles = lane_tiles(values)
    return pack(*halves(pack(*halves(sum(tiles[1:], tiles[0])), 16)), 8)


def unfold_far(packed):
    half = jnp.concatenate(unpack(packed, 8), axis=0)
    return jnp.concatenate(unpack(half, 16), axis=0)


def put_fold(ref, parts):
    start = 0
    for part in parts:
        ref[start : start + part.shape[0]] = part.astype(BF16)
        start += part.shape[0]


def side_by_side(unfolded, i):
    full, side = unfolded
    tiles = []
    for t in range(PLANE // 128):
        pair = [full[t % 3], side[t % 2]]
        tiles.append(jnp.concatenate(pair if i == 0 else pair[::-1], axis=0))
    return tiles


def is_even():
    return lax.rem(lax.axis_index("sx"), 2) == 0


def put_messages(planes, mate_ref, across_ref):
    own = slice(ORB, 2 * ORB)
    down = fold(planes[0, own].astype(F32), planes[0, :ORB].astype(F32))
    up = fold(planes[1, own].astype(F32), planes[1, 2 * ORB :].astype(F32))
    even = is_even()
    put_fold(mate_ref, [jnp.where(even, u, d) for u, d in zip(up, down)])
    put_fold(across_ref, [jnp.where(even, d, u) for u, d in zip(up, down)])


def sides(mate, across):
    even = is_even()
    return (jnp.where(even, across, mate), jnp.where(even, mate, across))


def at_end():
    slab = lax.axis_index("sx")
    return (slab == 0) | (slab == lax.axis_size("sx") - 1)


def kept(pattern_ref, r, q):
    slab = lax.axis_index("sx")
    last = pattern_ref.shape[1] - 1
    values = []
    for col in (2 * q, 2 * q + 1):
        apart = abs(col - r - 2)
        if apart == 0:
            values.append(1.0)
        elif apart > 2:
            values.append(0.0)
        else:
            at = jnp.clip(slab - 3 + min(col, r + 2), 0, last)
            values.append(pattern_ref[apart - 1, at].astype(F32))
    return jnp.where(low_half(), values[0], values[1])


def edges_kernel(
    table_ref, pieces_ref,
    phi_ref, mask_ref, rows_ref, mid_mask_ref, mate_ref,
    window_ref, raw_ref, sems,
):
    first = window_start(table_ref.shape[1])
    table_copy = pltpu.make_async_copy(table_ref.at[:, pl.ds(first, WINDOW)], window_ref, sems.at[2])
    table_copy.start()
    copies = []
    for i in range(2):
        start = (CX - 1) * PLANE * i
        copies.append(
            pltpu.make_async_copy(pieces_ref.at[:, start : start + PLANE], raw_ref.at[i], sems.at[i])
        )
        copies[i].start()
    cells = cell_features()
    table_copy.wait()
    blocks = row_features(window_ref, first)
    rows_ref[...] = blocks
    rows = blocks[ORB : 4 * ORB]
    reach = jnp.dot(rows, cells, preferred_element_type=F32)
    for i in range(2):
        mask_ref[i] = sphere(reach, rows, (CX - 1) * i)
        mid_mask_ref[i] = sphere(reach, rows, 1 + i)
    for i in range(2):
        copies[i].wait()
        phi_ref[i] = raw_ref[i] * mask_ref[i]
    even = is_even()
    own = slice(ORB, 2 * ORB)
    lower, upper = phi_ref[0].astype(F32), phi_ref[1].astype(F32)
    put_fold(mate_ref, fold(jnp.where(even, upper[own], lower[own]), jnp.where(even, upper[2 * ORB :], lower[:ORB])))


def rows_product(a, b):
    return lax.dot_general(a, b, (((1,), (1,)), ((), ())), preferred_element_type=F32)


def energy_kernel(
    mask_ref, pieces_ref, pot_ref, edge_ref, edge_mask_ref,
    phi_ref, energy_ref, part_ref, edge_energy_ref, corr_ref, ham_ref,
):
    for i in range(2):
        phi_ref[i] = pieces_ref[:, PLANE * (1 + i) : PLANE * (2 + i)] * mask_ref[i]
    weights = in_plane(6, -1)
    for t in range(PLANE // TILE):
        lanes = slice(TILE * t, TILE * t + TILE)
        edge = edge_ref[:, :, lanes].astype(F32)
        mid = phi_ref[:, :, lanes].astype(F32)
        inner = plane_product(phi_ref, weights, -1.0, t)
        outer = plane_product(edge_ref, weights, -1.0, t)
        for i in range(2):
            value = 0.5 * (inner[i] - (edge[i] + mid[1 - i])) + pot_ref[1 + i : 2 + i, lanes] * mid[i]
            energy_ref[i, :, lanes] = value.astype(BF16) * mask_ref[i, :, lanes]
            plane = (CX - 1) * i
            value = 0.5 * (outer[i] - mid[i]) + pot_ref[plane : plane + 1, lanes] * edge[i]
            part_ref[i, :, lanes] = value
            rest = rest_rows(i)
            edge_energy_ref[i, rest, lanes] = value[rest].astype(BF16) * edge_mask_ref[i, rest, lanes]
    mid = jnp.concatenate([phi_ref[0], phi_ref[1]], axis=1)
    both = jnp.concatenate([energy_ref[0], energy_ref[1]], axis=1)
    gram = rows_product(jnp.concatenate([mid, both], axis=0), mid)
    corr = gram[:ROWS]
    ham_ref[...] = gram[ROWS:]
    for i in range(2):
        rest = rest_rows(i)
        gram = rows_product(jnp.concatenate([edge_ref[i], edge_energy_ref[i, rest]], axis=0), edge_ref[i])
        corr = corr + gram[:ROWS]
        ham_ref[rest] += gram[ROWS:]
    corr_ref[...] = corr


def halo_rows(i):
    return slice(0, 2 * ORB) if i == 0 else slice(ORB, ROWS)


def rest_rows(i):
    return slice(2 * ORB, ROWS) if i == 0 else slice(0, ORB)


def bands_kernel(
    mate_ref, part_ref, mask_ref, phi_ref, corr_ref, ham_ref, rest_ref,
    energy_ref, own_ref, rows_ref,
):
    volume = 1.0 / (4.0 * CX**3)
    gram = []
    unfolded = unfold(mate_ref[...].astype(F32))
    for i in range(2):
        factor = jnp.where(is_even() == (i == 1), 0.5, 0.0)
        tiles = side_by_side(unfolded, i)
        for t in range(PLANE // 128):
            lanes = slice(128 * t, 128 * t + 128)
            value = part_ref[i, halo_rows(i), lanes] - factor * tiles[t]
            energy_ref[i, halo_rows(i), lanes] = value.astype(BF16) * mask_ref[i, halo_rows(i), lanes]
        gram.append(rows_product(energy_ref[i, halo_rows(i)], phi_ref[i]))
    own_ref[:, :, ROWS:] = jnp.zeros((2, ROWS, TILE - ROWS), F32)
    own_ref[0, :ORB, :ROWS] = (ham_ref[:ORB] + gram[0][:ORB]) * volume
    own_ref[0, ORB : 2 * ORB, :ROWS] = (ham_ref[ORB : 2 * ORB] + gram[0][ORB:] + gram[1][:ORB]) * volume
    own_ref[0, 2 * ORB :, :ROWS] = (ham_ref[2 * ORB :] + gram[1][ORB:]) * volume
    own_ref[1, :, :ROWS] = corr_ref[...] * volume
    tail = jnp.where(low_half(), own_ref[0, :, 128:256], swapped(own_ref[1, :, 128:256]))
    even = is_even()
    for i, value in enumerate((own_ref[0, :, 0:128], own_ref[1, :, 0:128], tail)):
        rows_ref[i] = jnp.where(even, value[ORB:], value[: 2 * ORB]).astype(BF16)


def low_half():
    return iota((1, 128), 1) < 64


def swapped(value):
    return pltpu.roll(value, 64, 1)


def mate_blocks(rows_ref, which):
    tail = rows_ref[2].astype(F32)
    if which == 1:
        tail = swapped(tail)
    return rows_ref[which].astype(F32), jnp.where(low_half(), tail, 0.0)


def shifted(c01, c2x):
    low = low_half()
    turned = swapped(c01)
    return jnp.where(low, 0.0, turned), jnp.where(low, turned, swapped(c2x))


def relay_kernel(own_ref, rows_ref, face_ref, out_ref):
    even = is_even()
    heads = []

    def put(i, value):
        out_ref[ORB * i : ORB * i + ORB] = value.astype(BF16)

    for which in range(2):
        head, rest = shifted(own_ref[which, :, 0:128], own_ref[which, :, 128:256])
        c01, c2x = mate_blocks(rows_ref, which)
        c01 = jnp.where(even, c01[:ORB], c01[ORB:])
        c2x = jnp.where(even, c2x[:ORB], c2x[ORB:])
        own = slice(ORB, 2 * ORB)
        put(2 * which, head[own] + jnp.where(even, c2x, c01))
        put(2 * which + 1, rest[own] + jnp.where(even, c01, c2x))
        put(5 + which, jnp.where(even, rest[:ORB], rest[2 * ORB :]))
        heads.append(jnp.where(even, head[:ORB], head[2 * ORB :]))
    put(4, jnp.where(low_half(), swapped(heads[1]), heads[0]))
    out_ref[7 * ORB :] = face_ref[...]


def around_kernel(pattern_ref, rows_ref, phi_ref, mask_ref, keep_ref, face_ref, scalar_ref, sem):
    pattern_copy = pltpu.make_async_copy(pattern_ref, scalar_ref, sem)
    pattern_copy.start()
    even = is_even()
    own = slice(ORB, 2 * ORB)
    lower, upper = phi_ref[0].astype(F32), phi_ref[1].astype(F32)
    parts = fold(jnp.where(even, lower[own], upper[own]), jnp.where(even, lower[:ORB], upper[2 * ORB :]))
    put_fold(face_ref, parts + (fold_far(jnp.where(even, lower[2 * ORB :], upper[:ORB])),))
    rows = jnp.where(even, rows_ref[:ROWS].astype(F32), rows_ref[2 * ORB :].astype(F32))
    reach = jnp.dot(rows.astype(BF16), cell_features(), preferred_element_type=F32)
    plane = jnp.where(even, -1.0, float(CX))
    bound = rows[:, 6:7] * (2.0 * plane) - plane * plane
    mask_ref[...] = jnp.where(reach <= bound, 1.0, 0.0).astype(BF16)
    pattern_copy.wait()
    for r in range(3):
        for q in range(4):
            keep_ref[r : r + 1, 128 * q : 128 * q + 128] = kept(scalar_ref, r, q)


def shared_head(tile, which):
    tile = tile.astype(F32)
    if which == 1:
        tile = swapped(tile)
    return jnp.where(low_half(), 0.0, tile)


def face_kernel(
    both_ref, around_ref, phi_ref, mask_ref,
    halo_ref, other_ref, work_ref, forward_ref,
    beyond_ref, back_ref,
):
    even = is_even()
    low = low_half()
    scale = -0.5 / (4.0 * CX**3)

    def got(start, size):
        rows = slice(start, start + size)
        value = jnp.where(even, both_ref[0, rows].astype(F32), both_ref[1, rows].astype(F32))
        return jnp.where(at_end(), 0.0, value)

    tiles = [got(ORB * i, ORB) for i in range(7)]
    for i in range(7):
        other_ref[i] = tiles[i].astype(BF16)
    beside = unfold(got(7 * ORB, 2 * ORB))
    far_off = unfold_far(got(9 * ORB, ORB // 4)).astype(BF16)
    work_ref[:, :, ROWS:] = jnp.zeros((2, 2 * ORB, TILE - ROWS), F32)
    head, tail = shared_head(tiles[4], 1), tiles[6]
    forward_ref[2] = jnp.where(low, swapped(head), swapped(tail)).astype(BF16)
    forward_ref[3] = jnp.where(low, swapped(tail), 0.0).astype(BF16)

    def add_face(i):
        here = halo_rows(i)
        there = slice(ORB, ROWS) if i == 0 else slice(0, 2 * ORB)
        outer = slice(0, ORB) if i == 0 else slice(2 * ORB, ROWS)
        for t, value in enumerate(side_by_side(beside, i)):
            lanes = slice(128 * t, 128 * t + 128)
            beyond_ref[there, lanes] = value.astype(BF16) * around_ref[there, lanes]
            beyond_ref[outer, lanes] = far_off * around_ref[outer, lanes]
            halo_ref[:, lanes] = value.astype(BF16) * mask_ref[i, here, lanes]
            back_ref[:, lanes] = phi_ref[i, here, lanes] * around_ref[there, lanes]
        work_ref[0, :, :ROWS] = rows_product(halo_ref[...], phi_ref[i]) * scale
        work_ref[1, :, :ROWS] = rows_product(back_ref[...], beyond_ref[...]) * scale
        x, y = work_ref[0, :, 0:128], work_ref[0, :, 128:256]
        a, b = shifted(work_ref[1, :, 0:128], work_ref[1, :, 128:256])
        own = slice(ORB, 2 * ORB) if i == 0 else slice(0, ORB)
        a = swapped(shared_head(tiles[4], 0) + a[own])
        b = swapped(tiles[5] + b[own])
        x, y = swapped(x[own]), swapped(y[own])
        if i == 0:
            forward_ref[0] = jnp.where(low, a, b + x).astype(BF16)
            forward_ref[1] = jnp.where(low, b + x, y).astype(BF16)
        else:
            forward_ref[0] = jnp.where(low, a + x, b + y).astype(BF16)
            forward_ref[1] = jnp.where(low, b, x).astype(BF16)

    pl.when(even)(lambda: add_face(0))
    pl.when(jnp.logical_not(even))(lambda: add_face(1))


def add_terms(i, work_ref, extra_ref):
    here = halo_rows(i)
    x, y = work_ref[0, :, 0:128], work_ref[0, :, 128:256]
    a, b = shifted(work_ref[1, :, 0:128], work_ref[1, :, 128:256])
    if i == 0:
        extra_ref[here, 0:128] = a
        extra_ref[here, 128:256] = b + x
        extra_ref[here, 256:384] = y
    else:
        extra_ref[here, 128:256] = a + x
        extra_ref[here, 256:384] = b + y


def add_halo(i, halo_ref, part_ref, mask_ref, energy_ref):
    here = halo_rows(i)
    value = part_ref[i, here] - 0.5 * halo_ref[...].astype(F32)
    energy_ref[i, here] = value.astype(BF16) * mask_ref[i, here]


def put_gradient(theta, orbital_ref, energy_ref, mask_ref, out_ref):
    for i in range(2):
        for t in range(PLANE // TILE):
            lanes = slice(TILE * t, TILE * t + TILE)
            fix = jnp.dot(theta, orbital_ref[i, :, lanes], preferred_element_type=F32)
            value = energy_ref[i, :, lanes].astype(F32) - fix
            out_ref[i, :, lanes] = value.astype(BF16) * mask_ref[i, :, lanes]


def split(value):
    high = value.astype(BF16)
    return high, (value - high.astype(F32)).astype(BF16)


def fine_product(a, b):
    return rows_product(a[0], b[0]) + (rows_product(a[0], b[1]) + rows_product(a[1], b[0]))


def theta_kernel(
    keep_ref, own_ref, rows_ref, other_ref, work_ref, halo_ref, part_ref, edge_mask_ref, energy_in_ref,
    window_ref, theta_ref, energy_ref,
    ham_ref, inv_ref, extra_ref,
):
    even = is_even()
    extra_ref[...] = jnp.zeros((ROWS, 8 * ORB), F32)
    pl.when(even)(lambda: add_terms(0, work_ref, extra_ref))
    pl.when(jnp.logical_not(even))(lambda: add_terms(1, work_ref, extra_ref))
    low = low_half()
    zero = jnp.zeros((ORB, 128), F32)
    for which, band_ref in enumerate((ham_ref, inv_ref)):
        near, rest = shifted(*mate_blocks(rows_ref, which))
        ahead = other_ref[2 * which].astype(F32)
        beside = other_ref[2 * which + 1].astype(F32)
        head = shared_head(other_ref[4], which)
        tail = other_ref[5 + which].astype(F32)
        got_even = (
            (ahead, beside, zero, zero),
            (head, tail + near[:ORB], rest[:ORB], zero),
            (zero, near[ORB:], rest[ORB:], zero),
        )
        got_odd = (
            (near[:ORB], rest[:ORB], zero, zero),
            (near[ORB:], rest[ORB:] + head, tail, zero),
            (zero, jnp.where(low, 0.0, ahead), beside, jnp.where(low, ahead, 0.0)),
        )
        for r in range(3):
            for q in range(4):
                value = jnp.where(even, got_even[r][q], got_odd[r][q])
                if q in (1, 2):
                    value = value + own_ref[which, ORB * r : ORB * r + ORB, 128 * q - 128 : 128 * q]
                if which == 0:
                    value = value + extra_ref[ORB * r : ORB * r + ORB, 128 * q : 128 * q + 128]
                value = value * keep_ref[r : r + 1, 128 * q : 128 * q + 128]
                if which == 1:
                    on = iota((ORB, 128), 0) + (ORB * (r + 2) - 128 * q) == iota((ORB, 128), 1)
                    value = jnp.where(on, 2.0, 0.0) - value
                band_ref[ORB * r : ORB * r + ORB, 128 * q : 128 * q + 128] = value
    ham, inv = split(ham_ref[...]), split(inv_ref[...])
    theta_ref[...] = fine_product(ham, inv)
    for which, (high, _) in enumerate((ham, inv)):
        quarter = [high[:, 128 * q : 128 * q + 128].astype(F32) for q in range(4)]
        window_ref[which, :, 0:128] = jnp.where(even, quarter[2], quarter[0]).astype(BF16)
        last = jnp.where(even, jnp.where(low, quarter[3], quarter[1]), quarter[1])
        window_ref[which, :, 128:256] = last.astype(BF16)
    pl.when(even)(lambda: add_halo(0, halo_ref, part_ref, edge_mask_ref, energy_ref))
    pl.when(jnp.logical_not(even))(lambda: add_halo(1, halo_ref, part_ref, edge_mask_ref, energy_ref))


def gradient_kernel(
    keep_ref, relayed_ref, bands_ref, base_ref,
    edge_ref, edge_energy_ref, edge_mask_ref,
    edge_grad_ref, theta_ref, mate_ref, across_ref,
    window_ref, total_ref,
):
    even = is_even()
    low = low_half()
    more = []
    kept_even = (keep_ref[2:3, 256:384], jnp.where(low, keep_ref[2:3, 384:512], keep_ref[2:3, 128:256]))
    kept_odd = (keep_ref[0:1, 0:128], keep_ref[0:1, 128:256])
    for which in range(2):
        tiles = []
        for q in range(2):
            value = relayed_ref[2 * which + q].astype(F32)
            tiles.append(value * jnp.where(even, kept_even[q], kept_odd[q]))
        more.append(jnp.concatenate(tiles, axis=1))
    first, third = slice(0, ORB), slice(2 * ORB, ROWS)
    window_ref[...] = bands_ref[0]
    window_ref[first] = (bands_ref[0, first].astype(F32) + jnp.where(even, 0.0, more[0])).astype(BF16)
    window_ref[third] = (bands_ref[0, third].astype(F32) + jnp.where(even, more[0], 0.0)).astype(BF16)
    more = [value.astype(BF16) for value in more]
    column = rows_product(window_ref[...], more[1])
    row = rows_product(more[0], bands_ref[1])
    total_ref[...] = base_ref[...]
    total_ref[first] += jnp.where(even, 0.0, row)
    total_ref[third] += jnp.where(even, row, 0.0)
    total_ref[:, first] -= jnp.where(even, 0.0, column)
    total_ref[:, third] -= jnp.where(even, column, 0.0)
    theta = total_ref[...].astype(BF16)
    theta_ref[...] = theta
    put_gradient(theta, edge_ref, edge_energy_ref, edge_mask_ref, edge_grad_ref)
    put_messages(edge_grad_ref, mate_ref, across_ref)


def smooth_kernel(
    theta_ref, phi_ref, energy_ref, edge_ref, mask_ref, edge_mask_ref,
    out_ref, part_ref,
    grad_ref, done_ref, rest_ref, sems,
):
    put_gradient(theta_ref[...], phi_ref, energy_ref, mask_ref, grad_ref)
    weights = in_plane(8, 1)
    copies = []

    def send(source, rows, start, sem):
        copies.append(pltpu.make_async_copy(source, out_ref.at[rows, start : start + TILE], sem))
        copies[-1].start()

    for t in range(PLANE // TILE):
        lanes = slice(TILE * t, TILE * t + TILE)
        edge = edge_ref[:, :, lanes].astype(F32)
        mid = grad_ref[:, :, lanes].astype(F32)
        inner = plane_product(grad_ref, weights, 1.0, t)
        outer = plane_product(edge_ref, weights, 1.0, t)
        for i in range(2):
            value = (inner[i] + (edge[i] + mid[1 - i])) * (1.0 / 32.0)
            done_ref[i, :, lanes] = value.astype(BF16) * mask_ref[i, :, lanes]
            value = outer[i] + mid[i]
            part_ref[i, :, lanes] = value
            rest = rest_rows(i)
            value = value[rest] * (1.0 / 32.0)
            rest_ref[i, :, lanes] = value.astype(BF16) * edge_mask_ref[i, rest, lanes]
        for i in range(2):
            send(done_ref.at[i, :, lanes], slice(0, ROWS), PLANE * (1 + i) + TILE * t, sems.at[t, i])
            send(rest_ref.at[i, :, lanes], rest_rows(i), PLANE * (CX - 1) * i + TILE * t, sems.at[t, 2 + i])
    for copy in copies:
        copy.wait()


def finish_kernel(across_ref, mate_ref, part_ref, mask_ref, inner_ref, out_ref, done_ref, sems):
    halos = [
        side_by_side(unfold(side), i)
        for i, side in enumerate(sides(mate_ref[...].astype(F32), across_ref[...].astype(F32)))
    ]
    copies = []
    for i in range(2):
        start = PLANE * (CX - 1) * i
        for half in range(2):
            rows = slice(ORB * (half + i), ORB * (half + i) + ORB)
            got = slice(ORB * half, ORB * half + ORB)
            for t in range(PLANE // 128):
                lanes = slice(128 * t, 128 * t + 128)
                value = (part_ref[i, rows, lanes] + halos[i][t][got]) * (1.0 / 32.0)
                done_ref[i, got, lanes] = value.astype(BF16) * mask_ref[i, rows, lanes]
            copies.append(
                pltpu.make_async_copy(
                    done_ref.at[i, got], out_ref.at[rows, start : start + PLANE], sems.at[i, half]
                )
            )
            copies[-1].start()
    for copy in copies:
        copy.wait()


def shape(*dims, dtype=BF16):
    return jax.ShapeDtypeStruct(dims, dtype)


def cost(flops, moved):
    return pl.CostEstimate(flops=flops, bytes_accessed=moved, transcendentals=0)


PARAMS = pltpu.CompilerParams(vmem_limit_bytes=32 * 1024 * 1024)
WHOLE = pl.BlockSpec(memory_space=pltpu.VMEM)
FAR = pl.BlockSpec(memory_space=pltpu.HBM)


def far(value):
    return pltpu.with_memory_space_constraint(value, pltpu.HBM)


def per_device(pieces, potential, centers, pattern):
    count = lax.axis_size("sx")
    mates = [(i, i ^ 1) for i in range(count)]
    others = [(i, i + 1 if i % 2 else i - 1) for i in range(1, count - 1)]
    groups = lax.axis_size("grp")
    pairs = [[g * count + i, g * count + i + 1] for g in range(groups) for i in range(1, count - 1, 2)]
    ends = [g * count + end for g in range(groups) for end in (0, count - 1)]
    pairs += [[ends[i], ends[i + 2]] for i in range(len(ends)) if i % 4 < 2] if groups % 2 == 0 else [
        [ends[2 * i], ends[2 * i + 1]] for i in range(groups)
    ]

    def to_mate(value):
        return lax.ppermute(value, "sx", mates)

    def across(value):
        return lax.ppermute(value, "sx", others)

    def gathered(value):
        return lax.all_gather(value, ("grp", "sx"), axis_index_groups=pairs)

    table = centers.T
    patterns = pattern.T
    pair = shape(2, ROWS, PLANE)

    edge, edge_mask, rows, mid_mask, for_mate = pl.pallas_call(
        edges_kernel,
        out_shape=(
            pair, pair, shape(5 * ORB, 16), pair, shape(2 * ORB, 128),
        ),
        in_specs=[FAR, FAR],
        out_specs=(WHOLE,) * 5,
        scratch_shapes=[
            pltpu.VMEM((4, WINDOW), jnp.int32),
            pltpu.VMEM((2, ROWS, PLANE), BF16),
            pltpu.SemaphoreType.DMA((3,)),
        ],
        compiler_params=PARAMS,
        cost_estimate=cost(10**8, 10**6),
        name="edges",
    )(far(table), far(pieces))
    mate_side = to_mate(for_mate)

    mid, mid_energy, part, rest_energy, corr, ham = pl.pallas_call(
        energy_kernel,
        out_shape=(
            pair, pair, shape(2, ROWS, PLANE, dtype=F32), pair,
            shape(ROWS, ROWS, dtype=F32), shape(ROWS, ROWS, dtype=F32),
        ),
        in_specs=[WHOLE] * 5,
        out_specs=(WHOLE,) * 6,
        compiler_params=PARAMS,
        cost_estimate=cost(4 * 10**9, 10**7),
        name="energy",
    )(mid_mask, pieces, potential, edge, edge_mask)

    edge_energy, own, for_mate = pl.pallas_call(
        bands_kernel,
        out_shape=(pair, shape(2, ROWS, TILE, dtype=F32), shape(3, 2 * ORB, 128)),
        in_specs=[WHOLE] * 7,
        out_specs=(WHOLE,) * 3,
        input_output_aliases={6: 0},
        compiler_params=PARAMS,
        cost_estimate=cost(10**9, 10**7),
        name="bands",
    )(mate_side, part, edge_mask, edge, corr, ham, rest_energy)
    mate_rows = to_mate(for_mate)
    around, keep, face = pl.pallas_call(
        around_kernel,
        out_shape=(shape(ROWS, PLANE), shape(3, 8 * ORB, dtype=F32), shape(FACE, 128)),
        in_specs=[FAR, WHOLE, WHOLE],
        out_specs=(WHOLE,) * 3,
        scratch_shapes=[pltpu.SMEM(patterns.shape, jnp.int32), pltpu.SemaphoreType.DMA],
        compiler_params=PARAMS,
        cost_estimate=cost(10**8, 10**6),
        name="around",
    )(far(patterns), rows, edge)
    for_other = pl.pallas_call(
        relay_kernel,
        out_shape=shape(7 * ORB + FACE, 128),
        in_specs=[WHOLE] * 3,
        out_specs=WHOLE,
        compiler_params=PARAMS,
        cost_estimate=cost(10**6, 10**6),
        name="relay",
    )(own, mate_rows, face)
    halo, other_rows, face_terms, forward = pl.pallas_call(
        face_kernel,
        out_shape=(
            shape(2 * ORB, PLANE), shape(7, ORB, 128), shape(2, 2 * ORB, TILE, dtype=F32), shape(4, ORB, 128),
        ),
        in_specs=[WHOLE] * 4,
        out_specs=(WHOLE,) * 4,
        scratch_shapes=[
            pltpu.VMEM((ROWS, PLANE), BF16),
            pltpu.VMEM((2 * ORB, PLANE), BF16),
        ],
        compiler_params=PARAMS,
        cost_estimate=cost(10**8, 10**6),
        name="face",
    )(gathered(for_other), around, edge, edge_mask)
    relayed = to_mate(forward)

    bands, base, edge_energy = pl.pallas_call(
        theta_kernel,
        out_shape=(shape(2, ROWS, TILE), shape(ROWS, ROWS, dtype=F32), pair),
        in_specs=[WHOLE] * 9,
        out_specs=(WHOLE,) * 3,
        scratch_shapes=[pltpu.VMEM((ROWS, 8 * ORB), F32)] * 3,
        input_output_aliases={8: 2},
        compiler_params=PARAMS,
        cost_estimate=cost(10**9, 4 * 10**6),
        name="theta",
    )(keep, own, mate_rows, other_rows, face_terms, halo, part, edge_mask, edge_energy)
    edge_grad, theta, for_mate, for_other = pl.pallas_call(
        gradient_kernel,
        out_shape=(pair, shape(ROWS, ROWS), shape(2 * ORB, 128), shape(2 * ORB, 128)),
        in_specs=[WHOLE] * 7,
        out_specs=(WHOLE,) * 4,
        scratch_shapes=[pltpu.VMEM((ROWS, TILE), BF16), pltpu.VMEM((ROWS, ROWS), F32)],
        compiler_params=PARAMS,
        cost_estimate=cost(10**9, 10**7),
        name="gradient",
    )(keep, relayed, bands, base, edge, edge_energy, edge_mask)
    other_side = across(for_other)
    mate_side = to_mate(for_mate)

    inner, part = pl.pallas_call(
        smooth_kernel,
        out_shape=(pltpu.HBM((ROWS, CX * PLANE), BF16), shape(2, ROWS, PLANE, dtype=F32)),
        in_specs=[WHOLE] * 6,
        out_specs=(FAR, WHOLE),
        scratch_shapes=[
            pltpu.VMEM((2, ROWS, PLANE), BF16),
            pltpu.VMEM((2, ROWS, PLANE), BF16),
            pltpu.VMEM((2, ORB, PLANE), BF16),
            pltpu.SemaphoreType.DMA((PLANE // TILE, 4)),
        ],
        compiler_params=PARAMS,
        cost_estimate=cost(2 * 10**9, 10**7),
        name="smooth",
    )(theta, mid, mid_energy, edge_grad, mid_mask, edge_mask)

    return pl.pallas_call(
        finish_kernel,
        out_shape=pltpu.HBM((ROWS, CX * PLANE), BF16),
        in_specs=[WHOLE] * 4 + [FAR],
        out_specs=FAR,
        scratch_shapes=[pltpu.VMEM((2, 2 * ORB, PLANE), BF16), pltpu.SemaphoreType.DMA((2, 2))],
        input_output_aliases={4: 0},
        compiler_params=PARAMS,
        cost_estimate=cost(10**7, 10**7),
        name="finish",
    )(other_side, mate_side, part, edge_mask, inner)


def solution(mesh):
    return jax.shard_map(
        per_device,
        mesh=mesh,
        in_specs=(P(("grp", "sx"), None), P(("grp", "sx"), None), P("grp", None), P("grp", None)),
        out_specs=P(("grp", "sx"), None),
        check_vma=False,
    )
```

```python
import functools

import jax
import jax.numpy as jnp
from jax import lax
from jax.experimental import pallas as pl
from jax.experimental.pallas import tpu as pltpu
from jax.sharding import PartitionSpec as P

ORB = 64
CX = 4
NY = 32
NZ = 32
ROWS = 3 * ORB
PLANE = NY * NZ
TILE = 256
WINDOW = 6 * ORB
FACE = 2 * ORB + ORB // 4
F32 = jnp.float32
BF16 = jnp.bfloat16


def iota(shape, dim):
    return lax.broadcasted_iota(jnp.int32, shape, dim)


def window_start(width):
    slab = lax.axis_index("sx")
    first = jnp.clip(slab * ORB - 2 * ORB, 0, width - WINDOW) // 128 * 128
    return pl.multiple_of(first, 128)


def row_features(window_ref, first):
    slab = lax.axis_index("sx")
    count = lax.axis_size("sx")
    window = window_ref[...]
    shift = slab * ORB - 2 * ORB - first
    window = pltpu.roll(jnp.concatenate([window, window], axis=0), lax.rem(WINDOW - shift, WINDOW), 1)
    lane = iota((1, WINDOW), 1)
    block = slab - 2 + lane // ORB
    valid = (block >= 0) & (block < count)
    cx = window[0:1] - slab * CX
    cy = window[1:2]
    cz = window[2:3]
    r = window[3:4]
    const = cx * cx + cy * cy + cz * cz - r * r
    const = jnp.where(valid, const, 65535)
    cx = jnp.where(valid, cx, 0)
    cy = jnp.where(valid, cy, 0)
    cz = jnp.where(valid, cz, 0)
    k = iota((16, WINDOW), 0)
    feats = jnp.where(k == 0, 1, 0)
    feats = jnp.where(k == 1, 256, feats)
    feats = jnp.where(k == 2, cy, feats)
    feats = jnp.where(k == 3, cz, feats)
    feats = jnp.where(k == 4, const & 255, feats)
    feats = jnp.where(k == 5, const >> 8, feats)
    feats = jnp.where(k == 6, cx, feats)
    return jnp.transpose(feats.astype(F32))[: 5 * ORB].astype(BF16)


def cell_features():
    k = iota((16, PLANE), 0)
    cell = iota((16, PLANE), 1)
    y = cell >> 5
    z = cell & 31
    sq = y * y + z * z
    feats = jnp.where(k == 0, sq & 255, 0)
    feats = jnp.where(k == 1, sq >> 8, feats)
    feats = jnp.where(k == 2, -2 * y, feats)
    feats = jnp.where(k == 3, -2 * z, feats)
    feats = jnp.where(k == 4, 1, feats)
    feats = jnp.where(k == 5, 256, feats)
    return feats.astype(F32).astype(BF16)


def sphere(reach, rows, plane):
    bound = rows[:, 6:7].astype(F32) * (2.0 * plane) - float(plane * plane)
    return jnp.where(reach <= bound, 1.0, 0.0).astype(BF16)


def in_plane(center, beside):
    k = iota((TILE, TILE), 0)
    n = iota((TILE, TILE), 1)
    diff = k - n
    near_y = (diff == NZ) | (diff == -NZ)
    near_z = ((diff == 1) | (diff == -1)) & ((k >> 5) == (n >> 5))
    w = jnp.where(near_y | near_z, float(beside), 0.0)
    return jnp.where(diff == 0, float(center), w).astype(BF16)


def plane_product(ref, weights, beside, t):
    start = TILE * t
    values = ref[:, :, start : start + TILE].reshape(2 * ROWS, TILE)
    out = jnp.dot(values, weights, preferred_element_type=F32).reshape(2, ROWS, TILE)
    lane = iota((1, 1, 128), 2)
    first, last = out[:, :, :128], out[:, :, 128:]
    if t > 0:
        turned = pltpu.roll(ref[:, :, start - 128 : start].astype(F32), NZ, 2)
        turned = jnp.where(lane < NZ, turned, 0.0)
        first = first + turned if beside > 0 else first - turned
    if start + TILE < PLANE:
        turned = pltpu.roll(ref[:, :, start + TILE : start + TILE + 128].astype(F32), 128 - NZ, 2)
        turned = jnp.where(lane >= 128 - NZ, turned, 0.0)
        last = last + turned if beside > 0 else last - turned
    return jnp.concatenate([first, last], axis=2)


def low_lanes(width):
    return (iota((1, 128), 1) & (2 * width - 1)) < width


def pack(first, second, width):
    return jnp.where(
        low_lanes(width),
        first + pltpu.roll(first, 128 - width, 1),
        second + pltpu.roll(second, width, 1),
    )


def unpack(packed, width):
    low = low_lanes(width)
    return (
        jnp.where(low, packed, pltpu.roll(packed, width, 1)),
        jnp.where(low, pltpu.roll(packed, 128 - width, 1), packed),
    )


def lane_tiles(values):
    return [values[:, 128 * t : 128 * t + 128] for t in range(PLANE // 128)]


def halves(values):
    half = values.shape[0] // 2
    return values[:half], values[half:]


def fold(full, side):
    tiles = lane_tiles(full)
    a, b, c = (sum(tiles[t::3][1:], tiles[t]) for t in range(3))
    tiles = lane_tiles(side)
    d, e = (sum(tiles[t::2][1:], tiles[t]) for t in range(2))
    return pack(a, b, 16), pack(*halves(c), 16), pack(*halves(pack(d, e, 16)), 8)


def unfold(packed):
    a, b = unpack(packed[:ORB], 16)
    c = jnp.concatenate(unpack(packed[ORB : ORB + ORB // 2], 16), axis=0)
    d, e = unpack(jnp.concatenate(unpack(packed[ORB + ORB // 2 : 2 * ORB], 8), axis=0), 16)
    return (a, b, c), (d, e)


def fold_far(values):
    tiles = lane_tiles(values)
    return pack(*halves(pack(*halves(sum(tiles[1:], tiles[0])), 16)), 8)


def unfold_far(packed):
    half = jnp.concatenate(unpack(packed, 8), axis=0)
    return jnp.concatenate(unpack(half, 16), axis=0)


def put_fold(ref, parts):
    start = 0
    for part in parts:
        ref[start : start + part.shape[0]] = part.astype(BF16)
        start += part.shape[0]


def side_by_side(unfolded, i):
    full, side = unfolded
    tiles = []
    for t in range(PLANE // 128):
        pair = [full[t % 3], side[t % 2]]
        tiles.append(jnp.concatenate(pair if i == 0 else pair[::-1], axis=0))
    return tiles


def is_even():
    return lax.rem(lax.axis_index("sx"), 2) == 0


def put_messages(planes, mate_ref, across_ref):
    own = slice(ORB, 2 * ORB)
    down = fold(planes[0, own].astype(F32), planes[0, :ORB].astype(F32))
    up = fold(planes[1, own].astype(F32), planes[1, 2 * ORB :].astype(F32))
    even = is_even()
    put_fold(mate_ref, [jnp.where(even, u, d) for u, d in zip(up, down)])
    put_fold(across_ref, [jnp.where(even, d, u) for u, d in zip(up, down)])


def sides(mate, across):
    even = is_even()
    return (jnp.where(even, across, mate), jnp.where(even, mate, across))


def at_end():
    slab = lax.axis_index("sx")
    return (slab == 0) | (slab == lax.axis_size("sx") - 1)


def kept(pattern_ref, r, q):
    slab = lax.axis_index("sx")
    last = pattern_ref.shape[1] - 1
    values = []
    for col in (2 * q, 2 * q + 1):
        apart = abs(col - r - 2)
        if apart == 0:
            values.append(1.0)
        elif apart > 2:
            values.append(0.0)
        else:
            at = jnp.clip(slab - 3 + min(col, r + 2), 0, last)
            values.append(pattern_ref[apart - 1, at].astype(F32))
    return jnp.where(low_half(), values[0], values[1])


def edges_kernel(
    table_ref, pieces_ref,
    phi_ref, mask_ref, rows_ref, reach_ref, mate_ref,
    window_ref, raw_ref, sems,
):
    first = window_start(table_ref.shape[1])
    table_copy = pltpu.make_async_copy(table_ref.at[:, pl.ds(first, WINDOW)], window_ref, sems.at[2])
    table_copy.start()
    copies = []
    for i in range(2):
        start = (CX - 1) * PLANE * i
        copies.append(
            pltpu.make_async_copy(pieces_ref.at[:, start : start + PLANE], raw_ref.at[i], sems.at[i])
        )
        copies[i].start()
    cells = cell_features()
    table_copy.wait()
    blocks = row_features(window_ref, first)
    rows_ref[...] = blocks
    rows = blocks[ORB : 4 * ORB]
    reach = jnp.dot(rows, cells, preferred_element_type=F32)
    reach_ref[...] = reach
    for i in range(2):
        mask_ref[i] = sphere(reach, rows, (CX - 1) * i)
    for i in range(2):
        copies[i].wait()
        phi_ref[i] = raw_ref[i] * mask_ref[i]
    even = is_even()
    own = slice(ORB, 2 * ORB)
    lower, upper = phi_ref[0].astype(F32), phi_ref[1].astype(F32)
    put_fold(mate_ref, fold(jnp.where(even, upper[own], lower[own]), jnp.where(even, upper[2 * ORB :], lower[:ORB])))


def rows_product(a, b):
    return lax.dot_general(a, b, (((1,), (1,)), ((), ())), preferred_element_type=F32)


def energy_kernel(
    rows_ref, reach_ref, pieces_ref, pot_ref, edge_ref, edge_mask_ref,
    phi_ref, mask_ref, energy_ref, part_ref, edge_energy_ref, corr_ref, ham_ref,
):
    rows = rows_ref[ORB : 4 * ORB]
    for i in range(2):
        mask = sphere(reach_ref[...], rows, 1 + i)
        mask_ref[i] = mask
        phi_ref[i] = pieces_ref[:, PLANE * (1 + i) : PLANE * (2 + i)] * mask
    weights = in_plane(6, -1)
    for t in range(PLANE // TILE):
        lanes = slice(TILE * t, TILE * t + TILE)
        edge = edge_ref[:, :, lanes].astype(F32)
        mid = phi_ref[:, :, lanes].astype(F32)
        inner = plane_product(phi_ref, weights, -1.0, t)
        outer = plane_product(edge_ref, weights, -1.0, t)
        for i in range(2):
            value = 0.5 * (inner[i] - (edge[i] + mid[1 - i])) + pot_ref[1 + i : 2 + i, lanes] * mid[i]
            energy_ref[i, :, lanes] = value.astype(BF16) * mask_ref[i, :, lanes]
            plane = (CX - 1) * i
            value = 0.5 * (outer[i] - mid[i]) + pot_ref[plane : plane + 1, lanes] * edge[i]
            part_ref[i, :, lanes] = value
            edge_energy_ref[i, :, lanes] = value.astype(BF16) * edge_mask_ref[i, :, lanes]
    mid = jnp.concatenate([phi_ref[0], phi_ref[1]], axis=1)
    both = jnp.concatenate([energy_ref[0], energy_ref[1]], axis=1)
    gram = rows_product(jnp.concatenate([mid, both], axis=0), mid)
    corr = gram[:ROWS]
    ham = gram[ROWS:]
    for i in range(2):
        gram = rows_product(jnp.concatenate([edge_ref[i], edge_energy_ref[i]], axis=0), edge_ref[i])
        corr = corr + gram[:ROWS]
        ham = ham + gram[ROWS:]
    corr_ref[...] = corr
    ham_ref[...] = ham


def halo_rows(i):
    return slice(0, 2 * ORB) if i == 0 else slice(ORB, ROWS)


def rest_rows(i):
    return slice(2 * ORB, ROWS) if i == 0 else slice(0, ORB)


def bands_kernel(
    mate_ref, part_ref, mask_ref, phi_ref, corr_ref, ham_ref, rest_ref,
    energy_ref, own_ref, rows_ref,
    halo_ref,
):
    volume = 1.0 / (4.0 * CX**3)
    unfolded = unfold(mate_ref[...].astype(F32))
    own_ref[0, :, :ROWS] = ham_ref[...] * volume

    def add_mate(i):
        here = halo_rows(i)
        for t, value in enumerate(side_by_side(unfolded, i)):
            lanes = slice(128 * t, 128 * t + 128)
            mask = mask_ref[i, here, lanes]
            halo_ref[:, lanes] = value.astype(BF16) * mask
            energy_ref[i, here, lanes] = (part_ref[i, here, lanes] - 0.5 * value).astype(BF16) * mask
        own_ref[0, here, :ROWS] += rows_product(halo_ref[...], phi_ref[i]) * (-0.5 * volume)

    pl.when(is_even())(lambda: add_mate(1))
    pl.when(jnp.logical_not(is_even()))(lambda: add_mate(0))
    own_ref[:, :, ROWS:] = jnp.zeros((2, ROWS, TILE - ROWS), F32)
    own_ref[1, :, :ROWS] = corr_ref[...] * volume
    tail = jnp.where(low_half(), own_ref[0, :, 128:256], swapped(own_ref[1, :, 128:256]))
    even = is_even()
    for i, value in enumerate((own_ref[0, :, 0:128], own_ref[1, :, 0:128], tail)):
        rows_ref[i] = jnp.where(even, value[ORB:], value[: 2 * ORB]).astype(BF16)


def low_half():
    return iota((1, 128), 1) < 64


def swapped(value):
    return pltpu.roll(value, 64, 1)


def mate_blocks(rows_ref, which):
    tail = rows_ref[2].astype(F32)
    if which == 1:
        tail = swapped(tail)
    return rows_ref[which].astype(F32), jnp.where(low_half(), tail, 0.0)


def shifted(c01, c2x):
    low = low_half()
    turned = swapped(c01)
    return jnp.where(low, 0.0, turned), jnp.where(low, turned, swapped(c2x))


def relay_kernel(own_ref, rows_ref, face_ref, out_ref):
    even = is_even()
    heads = []

    def put(i, value):
        out_ref[ORB * i : ORB * i + ORB] = value.astype(BF16)

    for which in range(2):
        head, rest = shifted(own_ref[which, :, 0:128], own_ref[which, :, 128:256])
        c01, c2x = mate_blocks(rows_ref, which)
        c01 = jnp.where(even, c01[:ORB], c01[ORB:])
        c2x = jnp.where(even, c2x[:ORB], c2x[ORB:])
        own = slice(ORB, 2 * ORB)
        put(2 * which, head[own] + jnp.where(even, c2x, c01))
        put(2 * which + 1, rest[own] + jnp.where(even, c01, c2x))
        put(5 + which, jnp.where(even, rest[:ORB], rest[2 * ORB :]))
        heads.append(jnp.where(even, head[:ORB], head[2 * ORB :]))
    put(4, jnp.where(low_half(), swapped(heads[1]), heads[0]))
    out_ref[7 * ORB :] = face_ref[...]


def around_kernel(pattern_ref, rows_ref, phi_ref, mask_ref, keep_ref, face_ref, scalar_ref, sem):
    pattern_copy = pltpu.make_async_copy(pattern_ref, scalar_ref, sem)
    pattern_copy.start()
    even = is_even()
    own = slice(ORB, 2 * ORB)
    lower, upper = phi_ref[0].astype(F32), phi_ref[1].astype(F32)
    parts = fold(jnp.where(even, lower[own], upper[own]), jnp.where(even, lower[:ORB], upper[2 * ORB :]))
    put_fold(face_ref, parts + (fold_far(jnp.where(even, lower[2 * ORB :], upper[:ORB])),))
    rows = jnp.where(even, rows_ref[:ROWS].astype(F32), rows_ref[2 * ORB :].astype(F32))
    reach = jnp.dot(rows.astype(BF16), cell_features(), preferred_element_type=F32)
    plane = jnp.where(even, -1.0, float(CX))
    bound = rows[:, 6:7] * (2.0 * plane) - plane * plane
    mask_ref[...] = jnp.where(reach <= bound, 1.0, 0.0).astype(BF16)
    pattern_copy.wait()
    for r in range(3):
        for q in range(4):
            keep_ref[r : r + 1, 128 * q : 128 * q + 128] = kept(scalar_ref, r, q)


def shared_head(tile, which):
    tile = tile.astype(F32)
    if which == 1:
        tile = swapped(tile)
    return jnp.where(low_half(), 0.0, tile)


def face_kernel(
    both_ref, around_ref, phi_ref, mask_ref,
    halo_ref, other_ref, extra_ref, forward_ref,
    beyond_ref, back_ref, work_ref,
):
    even = is_even()
    low = low_half()
    scale = -0.5 / (4.0 * CX**3)

    def got(start, size):
        rows = slice(start, start + size)
        value = jnp.where(even, both_ref[0, rows].astype(F32), both_ref[1, rows].astype(F32))
        return jnp.where(at_end(), 0.0, value)

    tiles = [got(ORB * i, ORB) for i in range(7)]
    for i in range(7):
        other_ref[i] = tiles[i].astype(BF16)
    beside = unfold(got(7 * ORB, 2 * ORB))
    far_off = unfold_far(got(9 * ORB, ORB // 4)).astype(BF16)
    extra_ref[...] = jnp.zeros((ROWS, 8 * ORB), F32)
    work_ref[:, :, ROWS:] = jnp.zeros((2, 2 * ORB, TILE - ROWS), F32)
    head, tail = shared_head(tiles[4], 1), tiles[6]
    forward_ref[2] = jnp.where(low, swapped(head), swapped(tail)).astype(BF16)
    forward_ref[3] = jnp.where(low, swapped(tail), 0.0).astype(BF16)

    def add_face(i):
        here = halo_rows(i)
        there = slice(ORB, ROWS) if i == 0 else slice(0, 2 * ORB)
        outer = slice(0, ORB) if i == 0 else slice(2 * ORB, ROWS)
        for t, value in enumerate(side_by_side(beside, i)):
            lanes = slice(128 * t, 128 * t + 128)
            beyond_ref[there, lanes] = value.astype(BF16) * around_ref[there, lanes]
            beyond_ref[outer, lanes] = far_off * around_ref[outer, lanes]
            halo_ref[:, lanes] = value.astype(BF16) * mask_ref[i, here, lanes]
            back_ref[:, lanes] = phi_ref[i, here, lanes] * around_ref[there, lanes]
        work_ref[0, :, :ROWS] = rows_product(halo_ref[...], phi_ref[i]) * scale
        work_ref[1, :, :ROWS] = rows_product(back_ref[...], beyond_ref[...]) * scale
        x, y = work_ref[0, :, 0:128], work_ref[0, :, 128:256]
        a, b = shifted(work_ref[1, :, 0:128], work_ref[1, :, 128:256])
        if i == 0:
            extra_ref[here, 0:128] = a
            extra_ref[here, 128:256] = b + x
            extra_ref[here, 256:384] = y
            own = slice(ORB, 2 * ORB)
        else:
            extra_ref[here, 128:256] = a + x
            extra_ref[here, 256:384] = b + y
            own = slice(0, ORB)
        a = swapped(shared_head(tiles[4], 0) + a[own])
        b = swapped(tiles[5] + b[own])
        x, y = swapped(x[own]), swapped(y[own])
        if i == 0:
            forward_ref[0] = jnp.where(low, a, b + x).astype(BF16)
            forward_ref[1] = jnp.where(low, b + x, y).astype(BF16)
        else:
            forward_ref[0] = jnp.where(low, a + x, b + y).astype(BF16)
            forward_ref[1] = jnp.where(low, b, x).astype(BF16)

    pl.when(even)(lambda: add_face(0))
    pl.when(jnp.logical_not(even))(lambda: add_face(1))


def add_halo(i, halo_ref, part_ref, mask_ref, energy_ref):
    here = halo_rows(i)
    value = part_ref[i, here] - 0.5 * halo_ref[...].astype(F32)
    energy_ref[i, here] = value.astype(BF16) * mask_ref[i, here]


def put_gradient(theta, orbital_ref, energy_ref, mask_ref, out_ref):
    for i in range(2):
        for t in range(PLANE // TILE):
            lanes = slice(TILE * t, TILE * t + TILE)
            fix = jnp.dot(theta, orbital_ref[i, :, lanes], preferred_element_type=F32)
            value = energy_ref[i, :, lanes].astype(F32) - fix
            out_ref[i, :, lanes] = value.astype(BF16) * mask_ref[i, :, lanes]


def split(value):
    high = value.astype(BF16)
    return high, (value - high.astype(F32)).astype(BF16)


def fine_product(a, b):
    return rows_product(a[0], b[0]) + (rows_product(a[0], b[1]) + rows_product(a[1], b[0]))


def theta_kernel(
    keep_ref, own_ref, rows_ref, other_ref, extra_ref, halo_ref, part_ref, edge_mask_ref, energy_in_ref,
    window_ref, theta_ref, energy_ref,
    ham_ref, inv_ref,
):
    even = is_even()
    low = low_half()
    zero = jnp.zeros((ORB, 128), F32)
    for which, band_ref in enumerate((ham_ref, inv_ref)):
        near, rest = shifted(*mate_blocks(rows_ref, which))
        ahead = other_ref[2 * which].astype(F32)
        beside = other_ref[2 * which + 1].astype(F32)
        head = shared_head(other_ref[4], which)
        tail = other_ref[5 + which].astype(F32)
        got_even = (
            (ahead, beside, zero, zero),
            (head, tail + near[:ORB], rest[:ORB], zero),
            (zero, near[ORB:], rest[ORB:], zero),
        )
        got_odd = (
            (near[:ORB], rest[:ORB], zero, zero),
            (near[ORB:], rest[ORB:] + head, tail, zero),
            (zero, jnp.where(low, 0.0, ahead), beside, jnp.where(low, ahead, 0.0)),
        )
        for r in range(3):
            for q in range(4):
                value = jnp.where(even, got_even[r][q], got_odd[r][q])
                if q in (1, 2):
                    value = value + own_ref[which, ORB * r : ORB * r + ORB, 128 * q - 128 : 128 * q]
                if which == 0:
                    value = value + extra_ref[ORB * r : ORB * r + ORB, 128 * q : 128 * q + 128]
                value = value * keep_ref[r : r + 1, 128 * q : 128 * q + 128]
                if which == 1:
                    on = iota((ORB, 128), 0) + (ORB * (r + 2) - 128 * q) == iota((ORB, 128), 1)
                    value = jnp.where(on, 2.0, 0.0) - value
                band_ref[ORB * r : ORB * r + ORB, 128 * q : 128 * q + 128] = value
    ham, inv = split(ham_ref[...]), split(inv_ref[...])
    theta_ref[...] = fine_product(ham, inv)
    for which, (high, _) in enumerate((ham, inv)):
        quarter = [high[:, 128 * q : 128 * q + 128].astype(F32) for q in range(4)]
        window_ref[which, :, 0:128] = jnp.where(even, quarter[2], quarter[0]).astype(BF16)
        last = jnp.where(even, jnp.where(low, quarter[3], quarter[1]), quarter[1])
        window_ref[which, :, 128:256] = last.astype(BF16)
    pl.when(even)(lambda: add_halo(0, halo_ref, part_ref, edge_mask_ref, energy_ref))
    pl.when(jnp.logical_not(even))(lambda: add_halo(1, halo_ref, part_ref, edge_mask_ref, energy_ref))


def gradient_kernel(
    keep_ref, relayed_ref, bands_ref, base_ref,
    edge_ref, edge_energy_ref, edge_mask_ref,
    edge_grad_ref, theta_ref, mate_ref, across_ref,
    window_ref, total_ref,
):
    even = is_even()
    low = low_half()
    more = []
    kept_even = (keep_ref[2:3, 256:384], jnp.where(low, keep_ref[2:3, 384:512], keep_ref[2:3, 128:256]))
    kept_odd = (keep_ref[0:1, 0:128], keep_ref[0:1, 128:256])
    for which in range(2):
        tiles = []
        for q in range(2):
            value = relayed_ref[2 * which + q].astype(F32)
            tiles.append(value * jnp.where(even, kept_even[q], kept_odd[q]))
        more.append(jnp.concatenate(tiles, axis=1))
    first, third = slice(0, ORB), slice(2 * ORB, ROWS)
    window_ref[...] = bands_ref[0]
    window_ref[first] = (bands_ref[0, first].astype(F32) + jnp.where(even, 0.0, more[0])).astype(BF16)
    window_ref[third] = (bands_ref[0, third].astype(F32) + jnp.where(even, more[0], 0.0)).astype(BF16)
    more = [value.astype(BF16) for value in more]
    column = rows_product(window_ref[...], more[1])
    row = rows_product(more[0], bands_ref[1])
    total_ref[...] = base_ref[...]
    total_ref[first] += jnp.where(even, 0.0, row)
    total_ref[third] += jnp.where(even, row, 0.0)
    total_ref[:, first] -= jnp.where(even, 0.0, column)
    total_ref[:, third] -= jnp.where(even, column, 0.0)
    theta = total_ref[...].astype(BF16)
    theta_ref[...] = theta
    put_gradient(theta, edge_ref, edge_energy_ref, edge_mask_ref, edge_grad_ref)
    put_messages(edge_grad_ref, mate_ref, across_ref)


def smooth_kernel(
    theta_ref, phi_ref, energy_ref, edge_ref, mask_ref, edge_mask_ref,
    out_ref, part_ref,
    grad_ref, done_ref, rest_ref, sems,
):
    put_gradient(theta_ref[...], phi_ref, energy_ref, mask_ref, grad_ref)
    weights = in_plane(8, 1)
    copies = []

    def send(source, rows, start, sem):
        copies.append(pltpu.make_async_copy(source, out_ref.at[rows, start : start + TILE], sem))
        copies[-1].start()

    for t in range(PLANE // TILE):
        lanes = slice(TILE * t, TILE * t + TILE)
        edge = edge_ref[:, :, lanes].astype(F32)
        mid = grad_ref[:, :, lanes].astype(F32)
        inner = plane_product(grad_ref, weights, 1.0, t)
        outer = plane_product(edge_ref, weights, 1.0, t)
        for i in range(2):
            value = (inner[i] + (edge[i] + mid[1 - i])) * (1.0 / 32.0)
            done_ref[i, :, lanes] = value.astype(BF16) * mask_ref[i, :, lanes]
            value = outer[i] + mid[i]
            part_ref[i, :, lanes] = value
            rest = rest_rows(i)
            value = value[rest] * (1.0 / 32.0)
            rest_ref[i, :, lanes] = value.astype(BF16) * edge_mask_ref[i, rest, lanes]
        for i in range(2):
            send(done_ref.at[i, :, lanes], slice(0, ROWS), PLANE * (1 + i) + TILE * t, sems.at[t, i])
            send(rest_ref.at[i, :, lanes], rest_rows(i), PLANE * (CX - 1) * i + TILE * t, sems.at[t, 2 + i])
    for copy in copies:
        copy.wait()


def finish_kernel(across_ref, mate_ref, part_ref, mask_ref, inner_ref, out_ref, done_ref, sems):
    halos = [
        side_by_side(unfold(side), i)
        for i, side in enumerate(sides(mate_ref[...].astype(F32), across_ref[...].astype(F32)))
    ]
    copies = []
    for i in range(2):
        start = PLANE * (CX - 1) * i
        for half in range(2):
            rows = slice(ORB * (half + i), ORB * (half + i) + ORB)
            got = slice(ORB * half, ORB * half + ORB)
            for t in range(PLANE // 128):
                lanes = slice(128 * t, 128 * t + 128)
                value = (part_ref[i, rows, lanes] + halos[i][t][got]) * (1.0 / 32.0)
                done_ref[i, got, lanes] = value.astype(BF16) * mask_ref[i, rows, lanes]
            copies.append(
                pltpu.make_async_copy(
                    done_ref.at[i, got], out_ref.at[rows, start : start + PLANE], sems.at[i, half]
                )
            )
            copies[-1].start()
    for copy in copies:
        copy.wait()


def shape(*dims, dtype=BF16):
    return jax.ShapeDtypeStruct(dims, dtype)


def cost(flops, moved):
    return pl.CostEstimate(flops=flops, bytes_accessed=moved, transcendentals=0)


PARAMS = pltpu.CompilerParams(vmem_limit_bytes=32 * 1024 * 1024)
WHOLE = pl.BlockSpec(memory_space=pltpu.VMEM)
FAR = pl.BlockSpec(memory_space=pltpu.HBM)


def far(value):
    return pltpu.with_memory_space_constraint(value, pltpu.HBM)


def per_device(pieces, potential, centers, pattern):
    count = lax.axis_size("sx")
    mates = [(i, i ^ 1) for i in range(count)]
    others = [(i, i + 1 if i % 2 else i - 1) for i in range(1, count - 1)]
    groups = lax.axis_size("grp")
    pairs = [[g * count + i, g * count + i + 1] for g in range(groups) for i in range(1, count - 1, 2)]
    ends = [g * count + end for g in range(groups) for end in (0, count - 1)]
    pairs += [[ends[i], ends[i + 2]] for i in range(len(ends)) if i % 4 < 2] if groups % 2 == 0 else [
        [ends[2 * i], ends[2 * i + 1]] for i in range(groups)
    ]

    def to_mate(value):
        return lax.ppermute(value, "sx", mates)

    def across(value):
        return lax.ppermute(value, "sx", others)

    def gathered(value):
        return lax.all_gather(value, ("grp", "sx"), axis_index_groups=pairs)

    table = centers.T
    patterns = pattern.T
    pair = shape(2, ROWS, PLANE)

    edge, edge_mask, rows, reach, for_mate = pl.pallas_call(
        edges_kernel,
        out_shape=(
            pair, pair, shape(5 * ORB, 16), shape(ROWS, PLANE, dtype=F32), shape(2 * ORB, 128),
        ),
        in_specs=[FAR, FAR],
        out_specs=(WHOLE,) * 5,
        scratch_shapes=[
            pltpu.VMEM((4, WINDOW), jnp.int32),
            pltpu.VMEM((2, ROWS, PLANE), BF16),
            pltpu.SemaphoreType.DMA((3,)),
        ],
        compiler_params=PARAMS,
        cost_estimate=cost(10**8, 10**6),
        name="edges",
    )(far(table), far(pieces))
    mate_side = to_mate(for_mate)

    mid, mid_mask, mid_energy, part, rest_energy, corr, ham = pl.pallas_call(
        energy_kernel,
        out_shape=(
            pair, pair, pair, shape(2, ROWS, PLANE, dtype=F32), pair,
            shape(ROWS, ROWS, dtype=F32), shape(ROWS, ROWS, dtype=F32),
        ),
        in_specs=[WHOLE] * 6,
        out_specs=(WHOLE,) * 7,
        compiler_params=PARAMS,
        cost_estimate=cost(4 * 10**9, 10**7),
        name="energy",
    )(rows, reach, pieces, potential, edge, edge_mask)

    edge_energy, own, for_mate = pl.pallas_call(
        bands_kernel,
        out_shape=(pair, shape(2, ROWS, TILE, dtype=F32), shape(3, 2 * ORB, 128)),
        in_specs=[WHOLE] * 7,
        out_specs=(WHOLE,) * 3,
        scratch_shapes=[pltpu.VMEM((2 * ORB, PLANE), BF16)],
        input_output_aliases={6: 0},
        compiler_params=PARAMS,
        cost_estimate=cost(10**9, 10**7),
        name="bands",
    )(mate_side, part, edge_mask, edge, corr, ham, rest_energy)
    mate_rows = to_mate(for_mate)
    around, keep, face = pl.pallas_call(
        around_kernel,
        out_shape=(shape(ROWS, PLANE), shape(3, 8 * ORB, dtype=F32), shape(FACE, 128)),
        in_specs=[FAR, WHOLE, WHOLE],
        out_specs=(WHOLE,) * 3,
        scratch_shapes=[pltpu.SMEM(patterns.shape, jnp.int32), pltpu.SemaphoreType.DMA],
        compiler_params=PARAMS,
        cost_estimate=cost(10**8, 10**6),
        name="around",
    )(far(patterns), rows, edge)
    for_other = pl.pallas_call(
        relay_kernel,
        out_shape=shape(7 * ORB + FACE, 128),
        in_specs=[WHOLE] * 3,
        out_specs=WHOLE,
        compiler_params=PARAMS,
        cost_estimate=cost(10**6, 10**6),
        name="relay",
    )(own, mate_rows, face)
    halo, other_rows, extra, forward = pl.pallas_call(
        face_kernel,
        out_shape=(
            shape(2 * ORB, PLANE), shape(7, ORB, 128), shape(ROWS, 8 * ORB, dtype=F32), shape(4, ORB, 128),
        ),
        in_specs=[WHOLE] * 4,
        out_specs=(WHOLE,) * 4,
        scratch_shapes=[
            pltpu.VMEM((ROWS, PLANE), BF16),
            pltpu.VMEM((2 * ORB, PLANE), BF16),
            pltpu.VMEM((2, 2 * ORB, TILE), F32),
        ],
        compiler_params=PARAMS,
        cost_estimate=cost(10**8, 10**6),
        name="face",
    )(gathered(for_other), around, edge, edge_mask)
    relayed = to_mate(forward)

    bands, base, edge_energy = pl.pallas_call(
        theta_kernel,
        out_shape=(shape(2, ROWS, TILE), shape(ROWS, ROWS, dtype=F32), pair),
        in_specs=[WHOLE] * 9,
        out_specs=(WHOLE,) * 3,
        scratch_shapes=[pltpu.VMEM((ROWS, 8 * ORB), F32), pltpu.VMEM((ROWS, 8 * ORB), F32)],
        input_output_aliases={8: 2},
        compiler_params=PARAMS,
        cost_estimate=cost(10**9, 4 * 10**6),
        name="theta",
    )(keep, own, mate_rows, other_rows, extra, halo, part, edge_mask, edge_energy)
    edge_grad, theta, for_mate, for_other = pl.pallas_call(
        gradient_kernel,
        out_shape=(pair, shape(ROWS, ROWS), shape(2 * ORB, 128), shape(2 * ORB, 128)),
        in_specs=[WHOLE] * 7,
        out_specs=(WHOLE,) * 4,
        scratch_shapes=[pltpu.VMEM((ROWS, TILE), BF16), pltpu.VMEM((ROWS, ROWS), F32)],
        compiler_params=PARAMS,
        cost_estimate=cost(10**9, 10**7),
        name="gradient",
    )(keep, relayed, bands, base, edge, edge_energy, edge_mask)
    other_side = across(for_other)
    mate_side = to_mate(for_mate)

    inner, part = pl.pallas_call(
        smooth_kernel,
        out_shape=(pltpu.HBM((ROWS, CX * PLANE), BF16), shape(2, ROWS, PLANE, dtype=F32)),
        in_specs=[WHOLE] * 6,
        out_specs=(FAR, WHOLE),
        scratch_shapes=[
            pltpu.VMEM((2, ROWS, PLANE), BF16),
            pltpu.VMEM((2, ROWS, PLANE), BF16),
            pltpu.VMEM((2, ORB, PLANE), BF16),
            pltpu.SemaphoreType.DMA((PLANE // TILE, 4)),
        ],
        compiler_params=PARAMS,
        cost_estimate=cost(2 * 10**9, 10**7),
        name="smooth",
    )(theta, mid, mid_energy, edge_grad, mid_mask, edge_mask)

    return pl.pallas_call(
        finish_kernel,
        out_shape=pltpu.HBM((ROWS, CX * PLANE), BF16),
        in_specs=[WHOLE] * 4 + [FAR],
        out_specs=FAR,
        scratch_shapes=[pltpu.VMEM((2, 2 * ORB, PLANE), BF16), pltpu.SemaphoreType.DMA((2, 2))],
        input_output_aliases={4: 0},
        compiler_params=PARAMS,
        cost_estimate=cost(10**7, 10**7),
        name="finish",
    )(other_side, mate_side, part, edge_mask, inner)


def solution(mesh):
    return jax.shard_map(
        per_device,
        mesh=mesh,
        in_specs=(P(("grp", "sx"), None), P(("grp", "sx"), None), P("grp", None), P("grp", None)),
        out_specs=P(("grp", "sx"), None),
        check_vma=False,
    )
```

```python
import functools

import jax
import jax.numpy as jnp
from jax import lax
from jax.experimental import pallas as pl
from jax.experimental.pallas import tpu as pltpu
from jax.sharding import PartitionSpec as P

ORB = 64
CX = 4
NY = 32
NZ = 32
ROWS = 3 * ORB
PLANE = NY * NZ
TILE = 256
WINDOW = 6 * ORB
FACE = 2 * ORB + ORB // 4
F32 = jnp.float32
BF16 = jnp.bfloat16


def iota(shape, dim):
    return lax.broadcasted_iota(jnp.int32, shape, dim)


def window_start(width):
    slab = lax.axis_index("sx")
    first = jnp.clip(slab * ORB - 2 * ORB, 0, width - WINDOW) // 128 * 128
    return pl.multiple_of(first, 128)


def row_features(window_ref, first):
    slab = lax.axis_index("sx")
    count = lax.axis_size("sx")
    window = window_ref[...]
    shift = slab * ORB - 2 * ORB - first
    window = pltpu.roll(jnp.concatenate([window, window], axis=0), lax.rem(WINDOW - shift, WINDOW), 1)
    lane = iota((1, WINDOW), 1)
    block = slab - 2 + lane // ORB
    valid = (block >= 0) & (block < count)
    cx = window[0:1] - slab * CX
    cy = window[1:2]
    cz = window[2:3]
    r = window[3:4]
    const = cx * cx + cy * cy + cz * cz - r * r
    const = jnp.where(valid, const, 65535)
    cx = jnp.where(valid, cx, 0)
    cy = jnp.where(valid, cy, 0)
    cz = jnp.where(valid, cz, 0)
    k = iota((16, WINDOW), 0)
    feats = jnp.where(k == 0, 1, 0)
    feats = jnp.where(k == 1, 256, feats)
    feats = jnp.where(k == 2, cy, feats)
    feats = jnp.where(k == 3, cz, feats)
    feats = jnp.where(k == 4, const & 255, feats)
    feats = jnp.where(k == 5, const >> 8, feats)
    feats = jnp.where(k == 6, cx, feats)
    return jnp.transpose(feats.astype(F32))[: 5 * ORB].astype(BF16)


def cell_features():
    k = iota((16, PLANE), 0)
    cell = iota((16, PLANE), 1)
    y = cell >> 5
    z = cell & 31
    sq = y * y + z * z
    feats = jnp.where(k == 0, sq & 255, 0)
    feats = jnp.where(k == 1, sq >> 8, feats)
    feats = jnp.where(k == 2, -2 * y, feats)
    feats = jnp.where(k == 3, -2 * z, feats)
    feats = jnp.where(k == 4, 1, feats)
    feats = jnp.where(k == 5, 256, feats)
    return feats.astype(F32).astype(BF16)


def sphere(reach, rows, plane):
    bound = rows[:, 6:7].astype(F32) * (2.0 * plane) - float(plane * plane)
    return jnp.where(reach <= bound, 1.0, 0.0).astype(BF16)


def in_plane(center, beside):
    k = iota((TILE, TILE), 0)
    n = iota((TILE, TILE), 1)
    diff = k - n
    near_y = (diff == NZ) | (diff == -NZ)
    near_z = ((diff == 1) | (diff == -1)) & ((k >> 5) == (n >> 5))
    w = jnp.where(near_y | near_z, float(beside), 0.0)
    return jnp.where(diff == 0, float(center), w).astype(BF16)


def plane_product(ref, weights, beside, t):
    start = TILE * t
    values = ref[:, :, start : start + TILE].reshape(2 * ROWS, TILE)
    out = jnp.dot(values, weights, preferred_element_type=F32).reshape(2, ROWS, TILE)
    lane = iota((1, 1, 128), 2)
    first, last = out[:, :, :128], out[:, :, 128:]
    if t > 0:
        turned = pltpu.roll(ref[:, :, start - 128 : start].astype(F32), NZ, 2)
        turned = jnp.where(lane < NZ, turned, 0.0)
        first = first + turned if beside > 0 else first - turned
    if start + TILE < PLANE:
        turned = pltpu.roll(ref[:, :, start + TILE : start + TILE + 128].astype(F32), 128 - NZ, 2)
        turned = jnp.where(lane >= 128 - NZ, turned, 0.0)
        last = last + turned if beside > 0 else last - turned
    return jnp.concatenate([first, last], axis=2)


def low_lanes(width):
    return (iota((1, 128), 1) & (2 * width - 1)) < width


def pack(first, second, width):
    return jnp.where(
        low_lanes(width),
        first + pltpu.roll(first, 128 - width, 1),
        second + pltpu.roll(second, width, 1),
    )


def unpack(packed, width):
    low = low_lanes(width)
    return (
        jnp.where(low, packed, pltpu.roll(packed, width, 1)),
        jnp.where(low, pltpu.roll(packed, 128 - width, 1), packed),
    )


def lane_tiles(values):
    return [values[:, 128 * t : 128 * t + 128] for t in range(PLANE // 128)]


def halves(values):
    half = values.shape[0] // 2
    return values[:half], values[half:]


def fold(full, side):
    tiles = lane_tiles(full)
    a, b, c = (sum(tiles[t::3][1:], tiles[t]) for t in range(3))
    tiles = lane_tiles(side)
    d, e = (sum(tiles[t::2][1:], tiles[t]) for t in range(2))
    return pack(a, b, 16), pack(*halves(c), 16), pack(*halves(pack(d, e, 16)), 8)


def unfold(packed):
    a, b = unpack(packed[:ORB], 16)
    c = jnp.concatenate(unpack(packed[ORB : ORB + ORB // 2], 16), axis=0)
    d, e = unpack(jnp.concatenate(unpack(packed[ORB + ORB // 2 : 2 * ORB], 8), axis=0), 16)
    return (a, b, c), (d, e)


def fold_far(values):
    tiles = lane_tiles(values)
    return pack(*halves(pack(*halves(sum(tiles[1:], tiles[0])), 16)), 8)


def unfold_far(packed):
    half = jnp.concatenate(unpack(packed, 8), axis=0)
    return jnp.concatenate(unpack(half, 16), axis=0)


def put_fold(ref, parts):
    start = 0
    for part in parts:
        ref[start : start + part.shape[0]] = part.astype(BF16)
        start += part.shape[0]


def side_by_side(unfolded, i):
    full, side = unfolded
    tiles = []
    for t in range(PLANE // 128):
        pair = [full[t % 3], side[t % 2]]
        tiles.append(jnp.concatenate(pair if i == 0 else pair[::-1], axis=0))
    return tiles


def is_even():
    return lax.rem(lax.axis_index("sx"), 2) == 0


def put_messages(planes, mate_ref, across_ref):
    own = slice(ORB, 2 * ORB)
    down = fold(planes[0, own].astype(F32), planes[0, :ORB].astype(F32))
    up = fold(planes[1, own].astype(F32), planes[1, 2 * ORB :].astype(F32))
    even = is_even()
    put_fold(mate_ref, [jnp.where(even, u, d) for u, d in zip(up, down)])
    put_fold(across_ref, [jnp.where(even, d, u) for u, d in zip(up, down)])


def sides(mate, across):
    even = is_even()
    return (jnp.where(even, across, mate), jnp.where(even, mate, across))


def at_end():
    slab = lax.axis_index("sx")
    return (slab == 0) | (slab == lax.axis_size("sx") - 1)


def kept(pattern_ref, r, q):
    slab = lax.axis_index("sx")
    last = pattern_ref.shape[1] - 1
    values = []
    for col in (2 * q, 2 * q + 1):
        apart = abs(col - r - 2)
        if apart == 0:
            values.append(1.0)
        elif apart > 2:
            values.append(0.0)
        else:
            at = jnp.clip(slab - 3 + min(col, r + 2), 0, last)
            values.append(pattern_ref[apart - 1, at].astype(F32))
    return jnp.where(low_half(), values[0], values[1])


def edges_kernel(
    table_ref, pieces_ref,
    phi_ref, mask_ref, rows_ref, reach_ref, mate_ref,
    window_ref, raw_ref, sems,
):
    first = window_start(table_ref.shape[1])
    table_copy = pltpu.make_async_copy(table_ref.at[:, pl.ds(first, WINDOW)], window_ref, sems.at[2])
    table_copy.start()
    copies = []
    for i in range(2):
        start = (CX - 1) * PLANE * i
        copies.append(
            pltpu.make_async_copy(pieces_ref.at[:, start : start + PLANE], raw_ref.at[i], sems.at[i])
        )
        copies[i].start()
    cells = cell_features()
    table_copy.wait()
    blocks = row_features(window_ref, first)
    rows_ref[...] = blocks
    rows = blocks[ORB : 4 * ORB]
    reach = jnp.dot(rows, cells, preferred_element_type=F32)
    reach_ref[...] = reach
    for i in range(2):
        mask_ref[i] = sphere(reach, rows, (CX - 1) * i)
    for i in range(2):
        copies[i].wait()
        phi_ref[i] = raw_ref[i] * mask_ref[i]
    even = is_even()
    own = slice(ORB, 2 * ORB)
    lower, upper = phi_ref[0].astype(F32), phi_ref[1].astype(F32)
    put_fold(mate_ref, fold(jnp.where(even, upper[own], lower[own]), jnp.where(even, upper[2 * ORB :], lower[:ORB])))


def rows_product(a, b):
    return lax.dot_general(a, b, (((1,), (1,)), ((), ())), preferred_element_type=F32)


def energy_kernel(
    rows_ref, reach_ref, pieces_ref, pot_ref, edge_ref, edge_mask_ref,
    phi_ref, mask_ref, energy_ref, part_ref, edge_energy_ref, corr_ref, ham_ref,
):
    rows = rows_ref[ORB : 4 * ORB]
    for i in range(2):
        mask = sphere(reach_ref[...], rows, 1 + i)
        mask_ref[i] = mask
        phi_ref[i] = pieces_ref[:, PLANE * (1 + i) : PLANE * (2 + i)] * mask
    weights = in_plane(6, -1)
    for t in range(PLANE // TILE):
        lanes = slice(TILE * t, TILE * t + TILE)
        edge = edge_ref[:, :, lanes].astype(F32)
        mid = phi_ref[:, :, lanes].astype(F32)
        inner = plane_product(phi_ref, weights, -1.0, t)
        outer = plane_product(edge_ref, weights, -1.0, t)
        for i in range(2):
            value = 0.5 * (inner[i] - (edge[i] + mid[1 - i])) + pot_ref[1 + i : 2 + i, lanes] * mid[i]
            energy_ref[i, :, lanes] = value.astype(BF16) * mask_ref[i, :, lanes]
            plane = (CX - 1) * i
            value = 0.5 * (outer[i] - mid[i]) + pot_ref[plane : plane + 1, lanes] * edge[i]
            part_ref[i, :, lanes] = value
            edge_energy_ref[i, :, lanes] = value.astype(BF16) * edge_mask_ref[i, :, lanes]
    orbitals = jnp.concatenate([phi_ref[0], phi_ref[1], edge_ref[0], edge_ref[1]], axis=1)
    energies = jnp.concatenate([energy_ref[0], energy_ref[1], edge_energy_ref[0], edge_energy_ref[1]], axis=1)
    gram = rows_product(jnp.concatenate([orbitals, energies], axis=0), orbitals)
    corr_ref[...] = gram[:ROWS]
    ham_ref[...] = gram[ROWS:]


def halo_rows(i):
    return slice(0, 2 * ORB) if i == 0 else slice(ORB, ROWS)


def rest_rows(i):
    return slice(2 * ORB, ROWS) if i == 0 else slice(0, ORB)


def bands_kernel(
    mate_ref, part_ref, mask_ref, phi_ref, corr_ref, ham_ref, rest_ref,
    energy_ref, own_ref, rows_ref,
    halo_ref,
):
    volume = 1.0 / (4.0 * CX**3)
    unfolded = unfold(mate_ref[...].astype(F32))
    own_ref[0, :, :ROWS] = ham_ref[...] * volume

    def add_mate(i):
        here = halo_rows(i)
        for t, value in enumerate(side_by_side(unfolded, i)):
            lanes = slice(128 * t, 128 * t + 128)
            mask = mask_ref[i, here, lanes]
            halo_ref[:, lanes] = value.astype(BF16) * mask
            energy_ref[i, here, lanes] = (part_ref[i, here, lanes] - 0.5 * value).astype(BF16) * mask
        own_ref[0, here, :ROWS] += rows_product(halo_ref[...], phi_ref[i]) * (-0.5 * volume)

    pl.when(is_even())(lambda: add_mate(1))
    pl.when(jnp.logical_not(is_even()))(lambda: add_mate(0))
    own_ref[:, :, ROWS:] = jnp.zeros((2, ROWS, TILE - ROWS), F32)
    own_ref[1, :, :ROWS] = corr_ref[...] * volume
    tail = jnp.where(low_half(), own_ref[0, :, 128:256], swapped(own_ref[1, :, 128:256]))
    even = is_even()
    for i, value in enumerate((own_ref[0, :, 0:128], own_ref[1, :, 0:128], tail)):
        rows_ref[i] = jnp.where(even, value[ORB:], value[: 2 * ORB]).astype(BF16)


def low_half():
    return iota((1, 128), 1) < 64


def swapped(value):
    return pltpu.roll(value, 64, 1)


def mate_blocks(rows_ref, which):
    tail = rows_ref[2].astype(F32)
    if which == 1:
        tail = swapped(tail)
    return rows_ref[which].astype(F32), jnp.where(low_half(), tail, 0.0)


def shifted(c01, c2x):
    low = low_half()
    turned = swapped(c01)
    return jnp.where(low, 0.0, turned), jnp.where(low, turned, swapped(c2x))


def relay_kernel(own_ref, rows_ref, face_ref, out_ref):
    even = is_even()
    heads = []

    def put(i, value):
        out_ref[ORB * i : ORB * i + ORB] = value.astype(BF16)

    for which in range(2):
        head, rest = shifted(own_ref[which, :, 0:128], own_ref[which, :, 128:256])
        c01, c2x = mate_blocks(rows_ref, which)
        c01 = jnp.where(even, c01[:ORB], c01[ORB:])
        c2x = jnp.where(even, c2x[:ORB], c2x[ORB:])
        own = slice(ORB, 2 * ORB)
        put(2 * which, head[own] + jnp.where(even, c2x, c01))
        put(2 * which + 1, rest[own] + jnp.where(even, c01, c2x))
        put(5 + which, jnp.where(even, rest[:ORB], rest[2 * ORB :]))
        heads.append(jnp.where(even, head[:ORB], head[2 * ORB :]))
    put(4, jnp.where(low_half(), swapped(heads[1]), heads[0]))
    out_ref[7 * ORB :] = face_ref[...]


def around_kernel(pattern_ref, rows_ref, phi_ref, mask_ref, keep_ref, face_ref, scalar_ref, sem):
    pattern_copy = pltpu.make_async_copy(pattern_ref, scalar_ref, sem)
    pattern_copy.start()
    even = is_even()
    own = slice(ORB, 2 * ORB)
    lower, upper = phi_ref[0].astype(F32), phi_ref[1].astype(F32)
    parts = fold(jnp.where(even, lower[own], upper[own]), jnp.where(even, lower[:ORB], upper[2 * ORB :]))
    put_fold(face_ref, parts + (fold_far(jnp.where(even, lower[2 * ORB :], upper[:ORB])),))
    rows = jnp.where(even, rows_ref[:ROWS].astype(F32), rows_ref[2 * ORB :].astype(F32))
    reach = jnp.dot(rows.astype(BF16), cell_features(), preferred_element_type=F32)
    plane = jnp.where(even, -1.0, float(CX))
    bound = rows[:, 6:7] * (2.0 * plane) - plane * plane
    mask_ref[...] = jnp.where(reach <= bound, 1.0, 0.0).astype(BF16)
    pattern_copy.wait()
    for r in range(3):
        for q in range(4):
            keep_ref[r : r + 1, 128 * q : 128 * q + 128] = kept(scalar_ref, r, q)


def shared_head(tile, which):
    tile = tile.astype(F32)
    if which == 1:
        tile = swapped(tile)
    return jnp.where(low_half(), 0.0, tile)


def face_kernel(
    both_ref, around_ref, phi_ref, mask_ref,
    halo_ref, other_ref, extra_ref, forward_ref,
    beyond_ref, back_ref, work_ref,
):
    even = is_even()
    low = low_half()
    scale = -0.5 / (4.0 * CX**3)

    def got(start, size):
        rows = slice(start, start + size)
        value = jnp.where(even, both_ref[0, rows].astype(F32), both_ref[1, rows].astype(F32))
        return jnp.where(at_end(), 0.0, value)

    tiles = [got(ORB * i, ORB) for i in range(7)]
    for i in range(7):
        other_ref[i] = tiles[i].astype(BF16)
    beside = unfold(got(7 * ORB, 2 * ORB))
    far_off = unfold_far(got(9 * ORB, ORB // 4)).astype(BF16)
    extra_ref[...] = jnp.zeros((ROWS, 8 * ORB), F32)
    work_ref[:, :, ROWS:] = jnp.zeros((2, 2 * ORB, TILE - ROWS), F32)
    head, tail = shared_head(tiles[4], 1), tiles[6]
    forward_ref[2] = jnp.where(low, swapped(head), swapped(tail)).astype(BF16)
    forward_ref[3] = jnp.where(low, swapped(tail), 0.0).astype(BF16)

    def add_face(i):
        here = halo_rows(i)
        there = slice(ORB, ROWS) if i == 0 else slice(0, 2 * ORB)
        outer = slice(0, ORB) if i == 0 else slice(2 * ORB, ROWS)
        for t, value in enumerate(side_by_side(beside, i)):
            lanes = slice(128 * t, 128 * t + 128)
            beyond_ref[there, lanes] = value.astype(BF16) * around_ref[there, lanes]
            beyond_ref[outer, lanes] = far_off * around_ref[outer, lanes]
            halo_ref[:, lanes] = value.astype(BF16) * mask_ref[i, here, lanes]
            back_ref[:, lanes] = phi_ref[i, here, lanes] * around_ref[there, lanes]
        work_ref[0, :, :ROWS] = rows_product(halo_ref[...], phi_ref[i]) * scale
        work_ref[1, :, :ROWS] = rows_product(back_ref[...], beyond_ref[...]) * scale
        x, y = work_ref[0, :, 0:128], work_ref[0, :, 128:256]
        a, b = shifted(work_ref[1, :, 0:128], work_ref[1, :, 128:256])
        if i == 0:
            extra_ref[here, 0:128] = a
            extra_ref[here, 128:256] = b + x
            extra_ref[here, 256:384] = y
            own = slice(ORB, 2 * ORB)
        else:
            extra_ref[here, 128:256] = a + x
            extra_ref[here, 256:384] = b + y
            own = slice(0, ORB)
        a = swapped(shared_head(tiles[4], 0) + a[own])
        b = swapped(tiles[5] + b[own])
        x, y = swapped(x[own]), swapped(y[own])
        if i == 0:
            forward_ref[0] = jnp.where(low, a, b + x).astype(BF16)
            forward_ref[1] = jnp.where(low, b + x, y).astype(BF16)
        else:
            forward_ref[0] = jnp.where(low, a + x, b + y).astype(BF16)
            forward_ref[1] = jnp.where(low, b, x).astype(BF16)

    pl.when(even)(lambda: add_face(0))
    pl.when(jnp.logical_not(even))(lambda: add_face(1))


def add_halo(i, halo_ref, part_ref, mask_ref, energy_ref):
    here = halo_rows(i)
    value = part_ref[i, here] - 0.5 * halo_ref[...].astype(F32)
    energy_ref[i, here] = value.astype(BF16) * mask_ref[i, here]


def put_gradient(theta, orbital_ref, energy_ref, mask_ref, out_ref):
    for i in range(2):
        for t in range(PLANE // TILE):
            lanes = slice(TILE * t, TILE * t + TILE)
            fix = jnp.dot(theta, orbital_ref[i, :, lanes], preferred_element_type=F32)
            value = energy_ref[i, :, lanes].astype(F32) - fix
            out_ref[i, :, lanes] = value.astype(BF16) * mask_ref[i, :, lanes]


def split(value):
    high = value.astype(BF16)
    return high, (value - high.astype(F32)).astype(BF16)


def fine_product(a, b):
    return rows_product(a[0], b[0]) + (rows_product(a[0], b[1]) + rows_product(a[1], b[0]))


def theta_kernel(
    keep_ref, own_ref, rows_ref, other_ref, extra_ref, halo_ref, part_ref, edge_mask_ref, energy_in_ref,
    window_ref, theta_ref, energy_ref,
    ham_ref, inv_ref,
):
    even = is_even()
    low = low_half()
    zero = jnp.zeros((ORB, 128), F32)
    for which, band_ref in enumerate((ham_ref, inv_ref)):
        near, rest = shifted(*mate_blocks(rows_ref, which))
        ahead = other_ref[2 * which].astype(F32)
        beside = other_ref[2 * which + 1].astype(F32)
        head = shared_head(other_ref[4], which)
        tail = other_ref[5 + which].astype(F32)
        got_even = (
            (ahead, beside, zero, zero),
            (head, tail + near[:ORB], rest[:ORB], zero),
            (zero, near[ORB:], rest[ORB:], zero),
        )
        got_odd = (
            (near[:ORB], rest[:ORB], zero, zero),
            (near[ORB:], rest[ORB:] + head, tail, zero),
            (zero, jnp.where(low, 0.0, ahead), beside, jnp.where(low, ahead, 0.0)),
        )
        for r in range(3):
            for q in range(4):
                value = jnp.where(even, got_even[r][q], got_odd[r][q])
                if q in (1, 2):
                    value = value + own_ref[which, ORB * r : ORB * r + ORB, 128 * q - 128 : 128 * q]
                if which == 0:
                    value = value + extra_ref[ORB * r : ORB * r + ORB, 128 * q : 128 * q + 128]
                value = value * keep_ref[r : r + 1, 128 * q : 128 * q + 128]
                if which == 1:
                    on = iota((ORB, 128), 0) + (ORB * (r + 2) - 128 * q) == iota((ORB, 128), 1)
                    value = jnp.where(on, 2.0, 0.0) - value
                band_ref[ORB * r : ORB * r + ORB, 128 * q : 128 * q + 128] = value
    ham, inv = split(ham_ref[...]), split(inv_ref[...])
    theta_ref[...] = fine_product(ham, inv)
    for which, (high, _) in enumerate((ham, inv)):
        quarter = [high[:, 128 * q : 128 * q + 128].astype(F32) for q in range(4)]
        window_ref[which, :, 0:128] = jnp.where(even, quarter[2], quarter[0]).astype(BF16)
        last = jnp.where(even, jnp.where(low, quarter[3], quarter[1]), quarter[1])
        window_ref[which, :, 128:256] = last.astype(BF16)
    pl.when(even)(lambda: add_halo(0, halo_ref, part_ref, edge_mask_ref, energy_ref))
    pl.when(jnp.logical_not(even))(lambda: add_halo(1, halo_ref, part_ref, edge_mask_ref, energy_ref))


def gradient_kernel(
    keep_ref, relayed_ref, bands_ref, base_ref,
    edge_ref, edge_energy_ref, edge_mask_ref,
    edge_grad_ref, theta_ref, mate_ref, across_ref,
    window_ref, total_ref,
):
    even = is_even()
    low = low_half()
    more = []
    kept_even = (keep_ref[2:3, 256:384], jnp.where(low, keep_ref[2:3, 384:512], keep_ref[2:3, 128:256]))
    kept_odd = (keep_ref[0:1, 0:128], keep_ref[0:1, 128:256])
    for which in range(2):
        tiles = []
        for q in range(2):
            value = relayed_ref[2 * which + q].astype(F32)
            tiles.append(value * jnp.where(even, kept_even[q], kept_odd[q]))
        more.append(jnp.concatenate(tiles, axis=1))
    first, third = slice(0, ORB), slice(2 * ORB, ROWS)
    window_ref[...] = bands_ref[0]
    window_ref[first] = (bands_ref[0, first].astype(F32) + jnp.where(even, 0.0, more[0])).astype(BF16)
    window_ref[third] = (bands_ref[0, third].astype(F32) + jnp.where(even, more[0], 0.0)).astype(BF16)
    more = [value.astype(BF16) for value in more]
    column = rows_product(window_ref[...], more[1])
    row = rows_product(more[0], bands_ref[1])
    total_ref[...] = base_ref[...]
    total_ref[first] += jnp.where(even, 0.0, row)
    total_ref[third] += jnp.where(even, row, 0.0)
    total_ref[:, first] -= jnp.where(even, 0.0, column)
    total_ref[:, third] -= jnp.where(even, column, 0.0)
    theta = total_ref[...].astype(BF16)
    theta_ref[...] = theta
    put_gradient(theta, edge_ref, edge_energy_ref, edge_mask_ref, edge_grad_ref)
    put_messages(edge_grad_ref, mate_ref, across_ref)


def smooth_kernel(
    theta_ref, phi_ref, energy_ref, edge_ref, mask_ref, edge_mask_ref,
    out_ref, part_ref,
    grad_ref, done_ref, rest_ref, sems,
):
    put_gradient(theta_ref[...], phi_ref, energy_ref, mask_ref, grad_ref)
    weights = in_plane(8, 1)
    copies = []

    def send(source, rows, start, sem):
        copies.append(pltpu.make_async_copy(source, out_ref.at[rows, start : start + TILE], sem))
        copies[-1].start()

    for t in range(PLANE // TILE):
        lanes = slice(TILE * t, TILE * t + TILE)
        edge = edge_ref[:, :, lanes].astype(F32)
        mid = grad_ref[:, :, lanes].astype(F32)
        inner = plane_product(grad_ref, weights, 1.0, t)
        outer = plane_product(edge_ref, weights, 1.0, t)
        for i in range(2):
            value = (inner[i] + (edge[i] + mid[1 - i])) * (1.0 / 32.0)
            done_ref[i, :, lanes] = value.astype(BF16) * mask_ref[i, :, lanes]
            value = outer[i] + mid[i]
            part_ref[i, :, lanes] = value
            rest = rest_rows(i)
            value = value[rest] * (1.0 / 32.0)
            rest_ref[i, :, lanes] = value.astype(BF16) * edge_mask_ref[i, rest, lanes]
        for i in range(2):
            send(done_ref.at[i, :, lanes], slice(0, ROWS), PLANE * (1 + i) + TILE * t, sems.at[t, i])
            send(rest_ref.at[i, :, lanes], rest_rows(i), PLANE * (CX - 1) * i + TILE * t, sems.at[t, 2 + i])
    for copy in copies:
        copy.wait()


def finish_kernel(across_ref, mate_ref, part_ref, mask_ref, inner_ref, out_ref, done_ref, sems):
    halos = [
        side_by_side(unfold(side), i)
        for i, side in enumerate(sides(mate_ref[...].astype(F32), across_ref[...].astype(F32)))
    ]
    copies = []
    for i in range(2):
        start = PLANE * (CX - 1) * i
        for half in range(2):
            rows = slice(ORB * (half + i), ORB * (half + i) + ORB)
            got = slice(ORB * half, ORB * half + ORB)
            for t in range(PLANE // 128):
                lanes = slice(128 * t, 128 * t + 128)
                value = (part_ref[i, rows, lanes] + halos[i][t][got]) * (1.0 / 32.0)
                done_ref[i, got, lanes] = value.astype(BF16) * mask_ref[i, rows, lanes]
            copies.append(
                pltpu.make_async_copy(
                    done_ref.at[i, got], out_ref.at[rows, start : start + PLANE], sems.at[i, half]
                )
            )
            copies[-1].start()
    for copy in copies:
        copy.wait()


def shape(*dims, dtype=BF16):
    return jax.ShapeDtypeStruct(dims, dtype)


def cost(flops, moved):
    return pl.CostEstimate(flops=flops, bytes_accessed=moved, transcendentals=0)


PARAMS = pltpu.CompilerParams(vmem_limit_bytes=32 * 1024 * 1024)
WHOLE = pl.BlockSpec(memory_space=pltpu.VMEM)
FAR = pl.BlockSpec(memory_space=pltpu.HBM)


def far(value):
    return pltpu.with_memory_space_constraint(value, pltpu.HBM)


def per_device(pieces, potential, centers, pattern):
    count = lax.axis_size("sx")
    mates = [(i, i ^ 1) for i in range(count)]
    others = [(i, i + 1 if i % 2 else i - 1) for i in range(1, count - 1)]
    groups = lax.axis_size("grp")
    pairs = [[g * count + i, g * count + i + 1] for g in range(groups) for i in range(1, count - 1, 2)]
    ends = [g * count + end for g in range(groups) for end in (0, count - 1)]
    pairs += [[ends[i], ends[i + 2]] for i in range(len(ends)) if i % 4 < 2] if groups % 2 == 0 else [
        [ends[2 * i], ends[2 * i + 1]] for i in range(groups)
    ]

    def to_mate(value):
        return lax.ppermute(value, "sx", mates)

    def across(value):
        return lax.ppermute(value, "sx", others)

    def gathered(value):
        return lax.all_gather(value, ("grp", "sx"), axis_index_groups=pairs)

    table = centers.T
    patterns = pattern.T
    pair = shape(2, ROWS, PLANE)

    edge, edge_mask, rows, reach, for_mate = pl.pallas_call(
        edges_kernel,
        out_shape=(
            pair, pair, shape(5 * ORB, 16), shape(ROWS, PLANE, dtype=F32), shape(2 * ORB, 128),
        ),
        in_specs=[FAR, FAR],
        out_specs=(WHOLE,) * 5,
        scratch_shapes=[
            pltpu.VMEM((4, WINDOW), jnp.int32),
            pltpu.VMEM((2, ROWS, PLANE), BF16),
            pltpu.SemaphoreType.DMA((3,)),
        ],
        compiler_params=PARAMS,
        cost_estimate=cost(10**8, 10**6),
        name="edges",
    )(far(table), far(pieces))
    mate_side = to_mate(for_mate)

    mid, mid_mask, mid_energy, part, rest_energy, corr, ham = pl.pallas_call(
        energy_kernel,
        out_shape=(
            pair, pair, pair, shape(2, ROWS, PLANE, dtype=F32), pair,
            shape(ROWS, ROWS, dtype=F32), shape(ROWS, ROWS, dtype=F32),
        ),
        in_specs=[WHOLE] * 6,
        out_specs=(WHOLE,) * 7,
        compiler_params=PARAMS,
        cost_estimate=cost(4 * 10**9, 10**7),
        name="energy",
    )(rows, reach, pieces, potential, edge, edge_mask)

    edge_energy, own, for_mate = pl.pallas_call(
        bands_kernel,
        out_shape=(pair, shape(2, ROWS, TILE, dtype=F32), shape(3, 2 * ORB, 128)),
        in_specs=[WHOLE] * 7,
        out_specs=(WHOLE,) * 3,
        scratch_shapes=[pltpu.VMEM((2 * ORB, PLANE), BF16)],
        input_output_aliases={6: 0},
        compiler_params=PARAMS,
        cost_estimate=cost(10**9, 10**7),
        name="bands",
    )(mate_side, part, edge_mask, edge, corr, ham, rest_energy)
    mate_rows = to_mate(for_mate)
    around, keep, face = pl.pallas_call(
        around_kernel,
        out_shape=(shape(ROWS, PLANE), shape(3, 8 * ORB, dtype=F32), shape(FACE, 128)),
        in_specs=[FAR, WHOLE, WHOLE],
        out_specs=(WHOLE,) * 3,
        scratch_shapes=[pltpu.SMEM(patterns.shape, jnp.int32), pltpu.SemaphoreType.DMA],
        compiler_params=PARAMS,
        cost_estimate=cost(10**8, 10**6),
        name="around",
    )(far(patterns), rows, edge)
    for_other = pl.pallas_call(
        relay_kernel,
        out_shape=shape(7 * ORB + FACE, 128),
        in_specs=[WHOLE] * 3,
        out_specs=WHOLE,
        compiler_params=PARAMS,
        cost_estimate=cost(10**6, 10**6),
        name="relay",
    )(own, mate_rows, face)
    halo, other_rows, extra, forward = pl.pallas_call(
        face_kernel,
        out_shape=(
            shape(2 * ORB, PLANE), shape(7, ORB, 128), shape(ROWS, 8 * ORB, dtype=F32), shape(4, ORB, 128),
        ),
        in_specs=[WHOLE] * 4,
        out_specs=(WHOLE,) * 4,
        scratch_shapes=[
            pltpu.VMEM((ROWS, PLANE), BF16),
            pltpu.VMEM((2 * ORB, PLANE), BF16),
            pltpu.VMEM((2, 2 * ORB, TILE), F32),
        ],
        compiler_params=PARAMS,
        cost_estimate=cost(10**8, 10**6),
        name="face",
    )(gathered(for_other), around, edge, edge_mask)
    relayed = to_mate(forward)

    bands, base, edge_energy = pl.pallas_call(
        theta_kernel,
        out_shape=(shape(2, ROWS, TILE), shape(ROWS, ROWS, dtype=F32), pair),
        in_specs=[WHOLE] * 9,
        out_specs=(WHOLE,) * 3,
        scratch_shapes=[pltpu.VMEM((ROWS, 8 * ORB), F32), pltpu.VMEM((ROWS, 8 * ORB), F32)],
        input_output_aliases={8: 2},
        compiler_params=PARAMS,
        cost_estimate=cost(10**9, 4 * 10**6),
        name="theta",
    )(keep, own, mate_rows, other_rows, extra, halo, part, edge_mask, edge_energy)
    edge_grad, theta, for_mate, for_other = pl.pallas_call(
        gradient_kernel,
        out_shape=(pair, shape(ROWS, ROWS), shape(2 * ORB, 128), shape(2 * ORB, 128)),
        in_specs=[WHOLE] * 7,
        out_specs=(WHOLE,) * 4,
        scratch_shapes=[pltpu.VMEM((ROWS, TILE), BF16), pltpu.VMEM((ROWS, ROWS), F32)],
        compiler_params=PARAMS,
        cost_estimate=cost(10**9, 10**7),
        name="gradient",
    )(keep, relayed, bands, base, edge, edge_energy, edge_mask)
    other_side = across(for_other)
    mate_side = to_mate(for_mate)

    inner, part = pl.pallas_call(
        smooth_kernel,
        out_shape=(pltpu.HBM((ROWS, CX * PLANE), BF16), shape(2, ROWS, PLANE, dtype=F32)),
        in_specs=[WHOLE] * 6,
        out_specs=(FAR, WHOLE),
        scratch_shapes=[
            pltpu.VMEM((2, ROWS, PLANE), BF16),
            pltpu.VMEM((2, ROWS, PLANE), BF16),
            pltpu.VMEM((2, ORB, PLANE), BF16),
            pltpu.SemaphoreType.DMA((PLANE // TILE, 4)),
        ],
        compiler_params=PARAMS,
        cost_estimate=cost(2 * 10**9, 10**7),
        name="smooth",
    )(theta, mid, mid_energy, edge_grad, mid_mask, edge_mask)

    return pl.pallas_call(
        finish_kernel,
        out_shape=pltpu.HBM((ROWS, CX * PLANE), BF16),
        in_specs=[WHOLE] * 4 + [FAR],
        out_specs=FAR,
        scratch_shapes=[pltpu.VMEM((2, 2 * ORB, PLANE), BF16), pltpu.SemaphoreType.DMA((2, 2))],
        input_output_aliases={4: 0},
        compiler_params=PARAMS,
        cost_estimate=cost(10**7, 10**7),
        name="finish",
    )(other_side, mate_side, part, edge_mask, inner)


def solution(mesh):
    return jax.shard_map(
        per_device,
        mesh=mesh,
        in_specs=(P(("grp", "sx"), None), P(("grp", "sx"), None), P("grp", None), P("grp", None)),
        out_specs=P(("grp", "sx"), None),
        check_vma=False,
    )
```

```python
import functools

import jax
import jax.numpy as jnp
from jax import lax
from jax.experimental import pallas as pl
from jax.experimental.pallas import tpu as pltpu
from jax.sharding import PartitionSpec as P

ORB = 64
CX = 4
NY = 32
NZ = 32
ROWS = 3 * ORB
PLANE = NY * NZ
TILE = 256
WINDOW = 6 * ORB
FACE = 2 * ORB + ORB // 4
F32 = jnp.float32
BF16 = jnp.bfloat16


def iota(shape, dim):
    return lax.broadcasted_iota(jnp.int32, shape, dim)


def window_start(width):
    slab = lax.axis_index("sx")
    first = jnp.clip(slab * ORB - 2 * ORB, 0, width - WINDOW) // 128 * 128
    return pl.multiple_of(first, 128)


def row_features(window_ref, first):
    slab = lax.axis_index("sx")
    count = lax.axis_size("sx")
    window = window_ref[...]
    shift = slab * ORB - 2 * ORB - first
    window = pltpu.roll(jnp.concatenate([window, window], axis=0), lax.rem(WINDOW - shift, WINDOW), 1)
    lane = iota((1, WINDOW), 1)
    block = slab - 2 + lane // ORB
    valid = (block >= 0) & (block < count)
    cx = window[0:1] - slab * CX
    cy = window[1:2]
    cz = window[2:3]
    r = window[3:4]
    const = cx * cx + cy * cy + cz * cz - r * r
    const = jnp.where(valid, const, 65535)
    cx = jnp.where(valid, cx, 0)
    cy = jnp.where(valid, cy, 0)
    cz = jnp.where(valid, cz, 0)
    k = iota((16, WINDOW), 0)
    feats = jnp.where(k == 0, 1, 0)
    feats = jnp.where(k == 1, 256, feats)
    feats = jnp.where(k == 2, cy, feats)
    feats = jnp.where(k == 3, cz, feats)
    feats = jnp.where(k == 4, const & 255, feats)
    feats = jnp.where(k == 5, const >> 8, feats)
    feats = jnp.where(k == 6, cx, feats)
    return jnp.transpose(feats.astype(F32))[: 5 * ORB].astype(BF16)


def cell_features():
    k = iota((16, PLANE), 0)
    cell = iota((16, PLANE), 1)
    y = cell >> 5
    z = cell & 31
    sq = y * y + z * z
    feats = jnp.where(k == 0, sq & 255, 0)
    feats = jnp.where(k == 1, sq >> 8, feats)
    feats = jnp.where(k == 2, -2 * y, feats)
    feats = jnp.where(k == 3, -2 * z, feats)
    feats = jnp.where(k == 4, 1, feats)
    feats = jnp.where(k == 5, 256, feats)
    return feats.astype(F32).astype(BF16)


def sphere(reach, rows, plane):
    bound = rows[:, 6:7].astype(F32) * (2.0 * plane) - float(plane * plane)
    return jnp.where(reach <= bound, 1.0, 0.0).astype(BF16)


def in_plane(center, beside):
    k = iota((TILE, TILE), 0)
    n = iota((TILE, TILE), 1)
    diff = k - n
    near_y = (diff == NZ) | (diff == -NZ)
    near_z = ((diff == 1) | (diff == -1)) & ((k >> 5) == (n >> 5))
    w = jnp.where(near_y | near_z, float(beside), 0.0)
    return jnp.where(diff == 0, float(center), w).astype(BF16)


def plane_product(ref, weights, beside, t):
    start = TILE * t
    values = ref[:, :, start : start + TILE].reshape(2 * ROWS, TILE)
    out = jnp.dot(values, weights, preferred_element_type=F32).reshape(2, ROWS, TILE)
    lane = iota((1, 1, 128), 2)
    first, last = out[:, :, :128], out[:, :, 128:]
    if t > 0:
        turned = pltpu.roll(ref[:, :, start - 128 : start].astype(F32), NZ, 2)
        turned = jnp.where(lane < NZ, turned, 0.0)
        first = first + turned if beside > 0 else first - turned
    if start + TILE < PLANE:
        turned = pltpu.roll(ref[:, :, start + TILE : start + TILE + 128].astype(F32), 128 - NZ, 2)
        turned = jnp.where(lane >= 128 - NZ, turned, 0.0)
        last = last + turned if beside > 0 else last - turned
    return jnp.concatenate([first, last], axis=2)


def low_lanes(width):
    return (iota((1, 128), 1) & (2 * width - 1)) < width


def pack(first, second, width):
    return jnp.where(
        low_lanes(width),
        first + pltpu.roll(first, 128 - width, 1),
        second + pltpu.roll(second, width, 1),
    )


def unpack(packed, width):
    low = low_lanes(width)
    return (
        jnp.where(low, packed, pltpu.roll(packed, width, 1)),
        jnp.where(low, pltpu.roll(packed, 128 - width, 1), packed),
    )


def lane_tiles(values):
    return [values[:, 128 * t : 128 * t + 128] for t in range(PLANE // 128)]


def halves(values):
    half = values.shape[0] // 2
    return values[:half], values[half:]


def fold(full, side):
    tiles = lane_tiles(full)
    a, b, c = (sum(tiles[t::3][1:], tiles[t]) for t in range(3))
    tiles = lane_tiles(side)
    d, e = (sum(tiles[t::2][1:], tiles[t]) for t in range(2))
    return pack(a, b, 16), pack(*halves(c), 16), pack(*halves(pack(d, e, 16)), 8)


def unfold(packed):
    a, b = unpack(packed[:ORB], 16)
    c = jnp.concatenate(unpack(packed[ORB : ORB + ORB // 2], 16), axis=0)
    d, e = unpack(jnp.concatenate(unpack(packed[ORB + ORB // 2 : 2 * ORB], 8), axis=0), 16)
    return (a, b, c), (d, e)


def fold_far(values):
    tiles = lane_tiles(values)
    return pack(*halves(pack(*halves(sum(tiles[1:], tiles[0])), 16)), 8)


def unfold_far(packed):
    half = jnp.concatenate(unpack(packed, 8), axis=0)
    return jnp.concatenate(unpack(half, 16), axis=0)


def put_fold(ref, parts):
    start = 0
    for part in parts:
        ref[start : start + part.shape[0]] = part.astype(BF16)
        start += part.shape[0]


def side_by_side(unfolded, i):
    full, side = unfolded
    tiles = []
    for t in range(PLANE // 128):
        pair = [full[t % 3], side[t % 2]]
        tiles.append(jnp.concatenate(pair if i == 0 else pair[::-1], axis=0))
    return tiles


def is_even():
    return lax.rem(lax.axis_index("sx"), 2) == 0


def put_messages(planes, mate_ref, across_ref):
    own = slice(ORB, 2 * ORB)
    down = fold(planes[0, own].astype(F32), planes[0, :ORB].astype(F32))
    up = fold(planes[1, own].astype(F32), planes[1, 2 * ORB :].astype(F32))
    even = is_even()
    put_fold(mate_ref, [jnp.where(even, u, d) for u, d in zip(up, down)])
    put_fold(across_ref, [jnp.where(even, d, u) for u, d in zip(up, down)])


def sides(mate, across):
    even = is_even()
    return (jnp.where(even, across, mate), jnp.where(even, mate, across))


def at_end():
    slab = lax.axis_index("sx")
    return (slab == 0) | (slab == lax.axis_size("sx") - 1)


def kept(pattern_ref, r, q):
    slab = lax.axis_index("sx")
    last = pattern_ref.shape[1] - 1
    values = []
    for col in (2 * q, 2 * q + 1):
        apart = abs(col - r - 2)
        if apart == 0:
            values.append(1.0)
        elif apart > 2:
            values.append(0.0)
        else:
            at = jnp.clip(slab - 3 + min(col, r + 2), 0, last)
            values.append(pattern_ref[apart - 1, at].astype(F32))
    return jnp.where(low_half(), values[0], values[1])


def edges_kernel(
    table_ref, pieces_ref,
    phi_ref, mask_ref, rows_ref, reach_ref, mate_ref,
    window_ref, raw_ref, sems,
):
    first = window_start(table_ref.shape[1])
    table_copy = pltpu.make_async_copy(table_ref.at[:, pl.ds(first, WINDOW)], window_ref, sems.at[2])
    table_copy.start()
    copies = []
    for i in range(2):
        start = (CX - 1) * PLANE * i
        copies.append(
            pltpu.make_async_copy(pieces_ref.at[:, start : start + PLANE], raw_ref.at[i], sems.at[i])
        )
        copies[i].start()
    cells = cell_features()
    table_copy.wait()
    blocks = row_features(window_ref, first)
    rows_ref[...] = blocks
    rows = blocks[ORB : 4 * ORB]
    reach = jnp.dot(rows, cells, preferred_element_type=F32)
    reach_ref[...] = reach
    for i in range(2):
        mask_ref[i] = sphere(reach, rows, (CX - 1) * i)
    for i in range(2):
        copies[i].wait()
        phi_ref[i] = raw_ref[i] * mask_ref[i]
    even = is_even()
    own = slice(ORB, 2 * ORB)
    lower, upper = phi_ref[0].astype(F32), phi_ref[1].astype(F32)
    put_fold(mate_ref, fold(jnp.where(even, upper[own], lower[own]), jnp.where(even, upper[2 * ORB :], lower[:ORB])))


def rows_product(a, b):
    return lax.dot_general(a, b, (((1,), (1,)), ((), ())), preferred_element_type=F32)


def energy_kernel(
    rows_ref, reach_ref, pieces_ref, pot_ref, edge_ref, edge_mask_ref,
    phi_ref, mask_ref, energy_ref, part_ref, edge_energy_ref, corr_ref, ham_ref,
):
    rows = rows_ref[ORB : 4 * ORB]
    for i in range(2):
        mask = sphere(reach_ref[...], rows, 1 + i)
        mask_ref[i] = mask
        phi_ref[i] = pieces_ref[:, PLANE * (1 + i) : PLANE * (2 + i)] * mask
    weights = in_plane(6, -1)
    for t in range(PLANE // TILE):
        lanes = slice(TILE * t, TILE * t + TILE)
        edge = edge_ref[:, :, lanes].astype(F32)
        mid = phi_ref[:, :, lanes].astype(F32)
        inner = plane_product(phi_ref, weights, -1.0, t)
        outer = plane_product(edge_ref, weights, -1.0, t)
        for i in range(2):
            value = 0.5 * (inner[i] - (edge[i] + mid[1 - i])) + pot_ref[1 + i : 2 + i, lanes] * mid[i]
            energy_ref[i, :, lanes] = value.astype(BF16) * mask_ref[i, :, lanes]
            plane = (CX - 1) * i
            value = 0.5 * (outer[i] - mid[i]) + pot_ref[plane : plane + 1, lanes] * edge[i]
            part_ref[i, :, lanes] = value
            rest = rest_rows(i)
            edge_energy_ref[i, rest, lanes] = value[rest].astype(BF16) * edge_mask_ref[i, rest, lanes]
    mid = jnp.concatenate([phi_ref[0], phi_ref[1]], axis=1)
    both = jnp.concatenate([energy_ref[0], energy_ref[1]], axis=1)
    gram = rows_product(jnp.concatenate([mid, both], axis=0), mid)
    corr = gram[:ROWS]
    ham_ref[...] = gram[ROWS:]
    for i in range(2):
        rest = rest_rows(i)
        gram = rows_product(jnp.concatenate([edge_ref[i], edge_energy_ref[i, rest]], axis=0), edge_ref[i])
        corr = corr + gram[:ROWS]
        ham_ref[rest] += gram[ROWS:]
    corr_ref[...] = corr


def halo_rows(i):
    return slice(0, 2 * ORB) if i == 0 else slice(ORB, ROWS)


def rest_rows(i):
    return slice(2 * ORB, ROWS) if i == 0 else slice(0, ORB)


def bands_kernel(
    mate_ref, part_ref, mask_ref, phi_ref, corr_ref, ham_ref, rest_ref,
    energy_ref, own_ref, rows_ref,
):
    volume = 1.0 / (4.0 * CX**3)
    gram = []
    unfolded = unfold(mate_ref[...].astype(F32))
    for i in range(2):
        factor = jnp.where(is_even() == (i == 1), 0.5, 0.0)
        tiles = side_by_side(unfolded, i)
        for t in range(PLANE // 128):
            lanes = slice(128 * t, 128 * t + 128)
            value = part_ref[i, halo_rows(i), lanes] - factor * tiles[t]
            energy_ref[i, halo_rows(i), lanes] = value.astype(BF16) * mask_ref[i, halo_rows(i), lanes]
        gram.append(rows_product(energy_ref[i, halo_rows(i)], phi_ref[i]))
    own_ref[:, :, ROWS:] = jnp.zeros((2, ROWS, TILE - ROWS), F32)
    own_ref[0, :ORB, :ROWS] = (ham_ref[:ORB] + gram[0][:ORB]) * volume
    own_ref[0, ORB : 2 * ORB, :ROWS] = (ham_ref[ORB : 2 * ORB] + gram[0][ORB:] + gram[1][:ORB]) * volume
    own_ref[0, 2 * ORB :, :ROWS] = (ham_ref[2 * ORB :] + gram[1][ORB:]) * volume
    own_ref[1, :, :ROWS] = corr_ref[...] * volume
    tail = jnp.where(low_half(), own_ref[0, :, 128:256], swapped(own_ref[1, :, 128:256]))
    even = is_even()
    for i, value in enumerate((own_ref[0, :, 0:128], own_ref[1, :, 0:128], tail)):
        rows_ref[i] = jnp.where(even, value[ORB:], value[: 2 * ORB]).astype(BF16)


def low_half():
    return iota((1, 128), 1) < 64


def swapped(value):
    return pltpu.roll(value, 64, 1)


def mate_blocks(rows_ref, which):
    tail = rows_ref[2].astype(F32)
    if which == 1:
        tail = swapped(tail)
    return rows_ref[which].astype(F32), jnp.where(low_half(), tail, 0.0)


def shifted(c01, c2x):
    low = low_half()
    turned = swapped(c01)
    return jnp.where(low, 0.0, turned), jnp.where(low, turned, swapped(c2x))


def relay_kernel(own_ref, rows_ref, face_ref, out_ref):
    even = is_even()
    heads = []

    def put(i, value):
        out_ref[ORB * i : ORB * i + ORB] = value.astype(BF16)

    for which in range(2):
        head, rest = shifted(own_ref[which, :, 0:128], own_ref[which, :, 128:256])
        c01, c2x = mate_blocks(rows_ref, which)
        c01 = jnp.where(even, c01[:ORB], c01[ORB:])
        c2x = jnp.where(even, c2x[:ORB], c2x[ORB:])
        own = slice(ORB, 2 * ORB)
        put(2 * which, head[own] + jnp.where(even, c2x, c01))
        put(2 * which + 1, rest[own] + jnp.where(even, c01, c2x))
        put(5 + which, jnp.where(even, rest[:ORB], rest[2 * ORB :]))
        heads.append(jnp.where(even, head[:ORB], head[2 * ORB :]))
    put(4, jnp.where(low_half(), swapped(heads[1]), heads[0]))
    out_ref[7 * ORB :] = face_ref[...]


def around_kernel(pattern_ref, rows_ref, phi_ref, mask_ref, keep_ref, face_ref, scalar_ref, sem):
    pattern_copy = pltpu.make_async_copy(pattern_ref, scalar_ref, sem)
    pattern_copy.start()
    even = is_even()
    own = slice(ORB, 2 * ORB)
    lower, upper = phi_ref[0].astype(F32), phi_ref[1].astype(F32)
    parts = fold(jnp.where(even, lower[own], upper[own]), jnp.where(even, lower[:ORB], upper[2 * ORB :]))
    put_fold(face_ref, parts + (fold_far(jnp.where(even, lower[2 * ORB :], upper[:ORB])),))
    rows = jnp.where(even, rows_ref[:ROWS].astype(F32), rows_ref[2 * ORB :].astype(F32))
    reach = jnp.dot(rows.astype(BF16), cell_features(), preferred_element_type=F32)
    plane = jnp.where(even, -1.0, float(CX))
    bound = rows[:, 6:7] * (2.0 * plane) - plane * plane
    mask_ref[...] = jnp.where(reach <= bound, 1.0, 0.0).astype(BF16)
    pattern_copy.wait()
    for r in range(3):
        for q in range(4):
            keep_ref[r : r + 1, 128 * q : 128 * q + 128] = kept(scalar_ref, r, q)


def shared_head(tile, which):
    tile = tile.astype(F32)
    if which == 1:
        tile = swapped(tile)
    return jnp.where(low_half(), 0.0, tile)


def face_kernel(
    both_ref, around_ref, phi_ref, mask_ref,
    halo_ref, other_ref, extra_ref, forward_ref,
    beyond_ref, back_ref, work_ref,
):
    even = is_even()
    low = low_half()
    scale = -0.5 / (4.0 * CX**3)

    def got(start, size):
        rows = slice(start, start + size)
        value = jnp.where(even, both_ref[0, rows].astype(F32), both_ref[1, rows].astype(F32))
        return jnp.where(at_end(), 0.0, value)

    tiles = [got(ORB * i, ORB) for i in range(7)]
    for i in range(7):
        other_ref[i] = tiles[i].astype(BF16)
    beside = unfold(got(7 * ORB, 2 * ORB))
    far_off = unfold_far(got(9 * ORB, ORB // 4)).astype(BF16)
    extra_ref[...] = jnp.zeros((ROWS, 8 * ORB), F32)
    work_ref[:, :, ROWS:] = jnp.zeros((2, 2 * ORB, TILE - ROWS), F32)
    head, tail = shared_head(tiles[4], 1), tiles[6]
    forward_ref[2] = jnp.where(low, swapped(head), swapped(tail)).astype(BF16)
    forward_ref[3] = jnp.where(low, swapped(tail), 0.0).astype(BF16)

    def add_face(i):
        here = halo_rows(i)
        there = slice(ORB, ROWS) if i == 0 else slice(0, 2 * ORB)
        outer = slice(0, ORB) if i == 0 else slice(2 * ORB, ROWS)
        for t, value in enumerate(side_by_side(beside, i)):
            lanes = slice(128 * t, 128 * t + 128)
            beyond_ref[there, lanes] = value.astype(BF16) * around_ref[there, lanes]
            beyond_ref[outer, lanes] = far_off * around_ref[outer, lanes]
            halo_ref[:, lanes] = value.astype(BF16) * mask_ref[i, here, lanes]
            back_ref[:, lanes] = phi_ref[i, here, lanes] * around_ref[there, lanes]
        work_ref[0, :, :ROWS] = rows_product(halo_ref[...], phi_ref[i]) * scale
        work_ref[1, :, :ROWS] = rows_product(back_ref[...], beyond_ref[...]) * scale
        x, y = work_ref[0, :, 0:128], work_ref[0, :, 128:256]
        a, b = shifted(work_ref[1, :, 0:128], work_ref[1, :, 128:256])
        if i == 0:
            extra_ref[here, 0:128] = a
            extra_ref[here, 128:256] = b + x
            extra_ref[here, 256:384] = y
            own = slice(ORB, 2 * ORB)
        else:
            extra_ref[here, 128:256] = a + x
            extra_ref[here, 256:384] = b + y
            own = slice(0, ORB)
        a = swapped(shared_head(tiles[4], 0) + a[own])
        b = swapped(tiles[5] + b[own])
        x, y = swapped(x[own]), swapped(y[own])
        if i == 0:
            forward_ref[0] = jnp.where(low, a, b + x).astype(BF16)
            forward_ref[1] = jnp.where(low, b + x, y).astype(BF16)
        else:
            forward_ref[0] = jnp.where(low, a + x, b + y).astype(BF16)
            forward_ref[1] = jnp.where(low, b, x).astype(BF16)

    pl.when(even)(lambda: add_face(0))
    pl.when(jnp.logical_not(even))(lambda: add_face(1))


def add_halo(i, halo_ref, part_ref, mask_ref, energy_ref):
    here = halo_rows(i)
    value = part_ref[i, here] - 0.5 * halo_ref[...].astype(F32)
    energy_ref[i, here] = value.astype(BF16) * mask_ref[i, here]


def put_gradient(theta, orbital_ref, energy_ref, mask_ref, out_ref):
    for i in range(2):
        for t in range(PLANE // TILE):
            lanes = slice(TILE * t, TILE * t + TILE)
            fix = jnp.dot(theta, orbital_ref[i, :, lanes], preferred_element_type=F32)
            value = energy_ref[i, :, lanes].astype(F32) - fix
            out_ref[i, :, lanes] = value.astype(BF16) * mask_ref[i, :, lanes]


def split(value):
    high = value.astype(BF16)
    return high, (value - high.astype(F32)).astype(BF16)


def fine_product(a, b):
    return rows_product(a[0], b[0]) + (rows_product(a[0], b[1]) + rows_product(a[1], b[0]))


def theta_kernel(
    keep_ref, own_ref, rows_ref, other_ref, extra_ref, halo_ref, part_ref, edge_mask_ref, energy_in_ref,
    window_ref, theta_ref, energy_ref,
    ham_ref, inv_ref,
):
    even = is_even()
    low = low_half()
    zero = jnp.zeros((ORB, 128), F32)
    for which, band_ref in enumerate((ham_ref, inv_ref)):
        near, rest = shifted(*mate_blocks(rows_ref, which))
        ahead = other_ref[2 * which].astype(F32)
        beside = other_ref[2 * which + 1].astype(F32)
        head = shared_head(other_ref[4], which)
        tail = other_ref[5 + which].astype(F32)
        got_even = (
            (ahead, beside, zero, zero),
            (head, tail + near[:ORB], rest[:ORB], zero),
            (zero, near[ORB:], rest[ORB:], zero),
        )
        got_odd = (
            (near[:ORB], rest[:ORB], zero, zero),
            (near[ORB:], rest[ORB:] + head, tail, zero),
            (zero, jnp.where(low, 0.0, ahead), beside, jnp.where(low, ahead, 0.0)),
        )
        for r in range(3):
            for q in range(4):
                value = jnp.where(even, got_even[r][q], got_odd[r][q])
                if q in (1, 2):
                    value = value + own_ref[which, ORB * r : ORB * r + ORB, 128 * q - 128 : 128 * q]
                if which == 0:
                    value = value + extra_ref[ORB * r : ORB * r + ORB, 128 * q : 128 * q + 128]
                value = value * keep_ref[r : r + 1, 128 * q : 128 * q + 128]
                if which == 1:
                    on = iota((ORB, 128), 0) + (ORB * (r + 2) - 128 * q) == iota((ORB, 128), 1)
                    value = jnp.where(on, 2.0, 0.0) - value
                band_ref[ORB * r : ORB * r + ORB, 128 * q : 128 * q + 128] = value
    ham, inv = split(ham_ref[...]), split(inv_ref[...])
    theta_ref[...] = fine_product(ham, inv)
    for which, (high, _) in enumerate((ham, inv)):
        quarter = [high[:, 128 * q : 128 * q + 128].astype(F32) for q in range(4)]
        window_ref[which, :, 0:128] = jnp.where(even, quarter[2], quarter[0]).astype(BF16)
        last = jnp.where(even, jnp.where(low, quarter[3], quarter[1]), quarter[1])
        window_ref[which, :, 128:256] = last.astype(BF16)
    pl.when(even)(lambda: add_halo(0, halo_ref, part_ref, edge_mask_ref, energy_ref))
    pl.when(jnp.logical_not(even))(lambda: add_halo(1, halo_ref, part_ref, edge_mask_ref, energy_ref))


def gradient_kernel(
    keep_ref, relayed_ref, bands_ref, base_ref,
    edge_ref, edge_energy_ref, edge_mask_ref,
    edge_grad_ref, theta_ref, mate_ref, across_ref,
    window_ref, total_ref,
):
    even = is_even()
    low = low_half()
    more = []
    kept_even = (keep_ref[2:3, 256:384], jnp.where(low, keep_ref[2:3, 384:512], keep_ref[2:3, 128:256]))
    kept_odd = (keep_ref[0:1, 0:128], keep_ref[0:1, 128:256])
    for which in range(2):
        tiles = []
        for q in range(2):
            value = relayed_ref[2 * which + q].astype(F32)
            tiles.append(value * jnp.where(even, kept_even[q], kept_odd[q]))
        more.append(jnp.concatenate(tiles, axis=1))
    first, third = slice(0, ORB), slice(2 * ORB, ROWS)
    window_ref[...] = bands_ref[0]
    window_ref[first] = (bands_ref[0, first].astype(F32) + jnp.where(even, 0.0, more[0])).astype(BF16)
    window_ref[third] = (bands_ref[0, third].astype(F32) + jnp.where(even, more[0], 0.0)).astype(BF16)
    more = [value.astype(BF16) for value in more]
    column = rows_product(window_ref[...], more[1])
    row = rows_product(more[0], bands_ref[1])
    total_ref[...] = base_ref[...]
    total_ref[first] += jnp.where(even, 0.0, row)
    total_ref[third] += jnp.where(even, row, 0.0)
    total_ref[:, first] -= jnp.where(even, 0.0, column)
    total_ref[:, third] -= jnp.where(even, column, 0.0)
    theta = total_ref[...].astype(BF16)
    theta_ref[...] = theta
    put_gradient(theta, edge_ref, edge_energy_ref, edge_mask_ref, edge_grad_ref)
    put_messages(edge_grad_ref, mate_ref, across_ref)


def smooth_kernel(
    theta_ref, phi_ref, energy_ref, edge_ref, mask_ref, edge_mask_ref,
    out_ref, part_ref,
    grad_ref, done_ref, rest_ref, sems,
):
    put_gradient(theta_ref[...], phi_ref, energy_ref, mask_ref, grad_ref)
    weights = in_plane(8, 1)
    copies = []

    def send(source, rows, start, sem):
        copies.append(pltpu.make_async_copy(source, out_ref.at[rows, start : start + TILE], sem))
        copies[-1].start()

    for t in range(PLANE // TILE):
        lanes = slice(TILE * t, TILE * t + TILE)
        edge = edge_ref[:, :, lanes].astype(F32)
        mid = grad_ref[:, :, lanes].astype(F32)
        inner = plane_product(grad_ref, weights, 1.0, t)
        outer = plane_product(edge_ref, weights, 1.0, t)
        for i in range(2):
            value = (inner[i] + (edge[i] + mid[1 - i])) * (1.0 / 32.0)
            done_ref[i, :, lanes] = value.astype(BF16) * mask_ref[i, :, lanes]
            value = outer[i] + mid[i]
            part_ref[i, :, lanes] = value
            rest = rest_rows(i)
            value = value[rest] * (1.0 / 32.0)
            rest_ref[i, :, lanes] = value.astype(BF16) * edge_mask_ref[i, rest, lanes]
        for i in range(2):
            send(done_ref.at[i, :, lanes], slice(0, ROWS), PLANE * (1 + i) + TILE * t, sems.at[t, i])
            send(rest_ref.at[i, :, lanes], rest_rows(i), PLANE * (CX - 1) * i + TILE * t, sems.at[t, 2 + i])
    for copy in copies:
        copy.wait()


def finish_kernel(across_ref, mate_ref, part_ref, mask_ref, inner_ref, out_ref, done_ref, sems):
    halos = [
        side_by_side(unfold(side), i)
        for i, side in enumerate(sides(mate_ref[...].astype(F32), across_ref[...].astype(F32)))
    ]
    copies = []
    for i in range(2):
        start = PLANE * (CX - 1) * i
        for half in range(2):
            rows = slice(ORB * (half + i), ORB * (half + i) + ORB)
            got = slice(ORB * half, ORB * half + ORB)
            for t in range(PLANE // 128):
                lanes = slice(128 * t, 128 * t + 128)
                value = (part_ref[i, rows, lanes] + halos[i][t][got]) * (1.0 / 32.0)
                done_ref[i, got, lanes] = value.astype(BF16) * mask_ref[i, rows, lanes]
            copies.append(
                pltpu.make_async_copy(
                    done_ref.at[i, got], out_ref.at[rows, start : start + PLANE], sems.at[i, half]
                )
            )
            copies[-1].start()
    for copy in copies:
        copy.wait()


def shape(*dims, dtype=BF16):
    return jax.ShapeDtypeStruct(dims, dtype)


def cost(flops, moved):
    return pl.CostEstimate(flops=flops, bytes_accessed=moved, transcendentals=0)


PARAMS = pltpu.CompilerParams(vmem_limit_bytes=32 * 1024 * 1024)
WHOLE = pl.BlockSpec(memory_space=pltpu.VMEM)
FAR = pl.BlockSpec(memory_space=pltpu.HBM)


def far(value):
    return pltpu.with_memory_space_constraint(value, pltpu.HBM)


def per_device(pieces, potential, centers, pattern):
    count = lax.axis_size("sx")
    mates = [(i, i ^ 1) for i in range(count)]
    others = [(i, i + 1 if i % 2 else i - 1) for i in range(1, count - 1)]
    groups = lax.axis_size("grp")
    pairs = [[g * count + i, g * count + i + 1] for g in range(groups) for i in range(1, count - 1, 2)]
    ends = [g * count + end for g in range(groups) for end in (0, count - 1)]
    pairs += [[ends[i], ends[i + 2]] for i in range(len(ends)) if i % 4 < 2] if groups % 2 == 0 else [
        [ends[2 * i], ends[2 * i + 1]] for i in range(groups)
    ]

    def to_mate(value):
        return lax.ppermute(value, "sx", mates)

    def across(value):
        return lax.ppermute(value, "sx", others)

    def gathered(value):
        return lax.all_gather(value, ("grp", "sx"), axis_index_groups=pairs)

    table = centers.T
    patterns = pattern.T
    pair = shape(2, ROWS, PLANE)

    edge, edge_mask, rows, reach, for_mate = pl.pallas_call(
        edges_kernel,
        out_shape=(
            pair, pair, shape(5 * ORB, 16), shape(ROWS, PLANE, dtype=F32), shape(2 * ORB, 128),
        ),
        in_specs=[FAR, FAR],
        out_specs=(WHOLE,) * 5,
        scratch_shapes=[
            pltpu.VMEM((4, WINDOW), jnp.int32),
            pltpu.VMEM((2, ROWS, PLANE), BF16),
            pltpu.SemaphoreType.DMA((3,)),
        ],
        compiler_params=PARAMS,
        cost_estimate=cost(10**8, 10**6),
        name="edges",
    )(far(table), far(pieces))
    mate_side = to_mate(for_mate)

    mid, mid_mask, mid_energy, part, rest_energy, corr, ham = pl.pallas_call(
        energy_kernel,
        out_shape=(
            pair, pair, pair, shape(2, ROWS, PLANE, dtype=F32), pair,
            shape(ROWS, ROWS, dtype=F32), shape(ROWS, ROWS, dtype=F32),
        ),
        in_specs=[WHOLE] * 6,
        out_specs=(WHOLE,) * 7,
        compiler_params=PARAMS,
        cost_estimate=cost(4 * 10**9, 10**7),
        name="energy",
    )(rows, reach, pieces, potential, edge, edge_mask)

    edge_energy, own, for_mate = pl.pallas_call(
        bands_kernel,
        out_shape=(pair, shape(2, ROWS, TILE, dtype=F32), shape(3, 2 * ORB, 128)),
        in_specs=[WHOLE] * 7,
        out_specs=(WHOLE,) * 3,
        input_output_aliases={6: 0},
        compiler_params=PARAMS,
        cost_estimate=cost(10**9, 10**7),
        name="bands",
    )(mate_side, part, edge_mask, edge, corr, ham, rest_energy)
    mate_rows = to_mate(for_mate)
    around, keep, face = pl.pallas_call(
        around_kernel,
        out_shape=(shape(ROWS, PLANE), shape(3, 8 * ORB, dtype=F32), shape(FACE, 128)),
        in_specs=[FAR, WHOLE, WHOLE],
        out_specs=(WHOLE,) * 3,
        scratch_shapes=[pltpu.SMEM(patterns.shape, jnp.int32), pltpu.SemaphoreType.DMA],
        compiler_params=PARAMS,
        cost_estimate=cost(10**8, 10**6),
        name="around",
    )(far(patterns), rows, edge)
    for_other = pl.pallas_call(
        relay_kernel,
        out_shape=shape(7 * ORB + FACE, 128),
        in_specs=[WHOLE] * 3,
        out_specs=WHOLE,
        compiler_params=PARAMS,
        cost_estimate=cost(10**6, 10**6),
        name="relay",
    )(own, mate_rows, face)
    halo, other_rows, extra, forward = pl.pallas_call(
        face_kernel,
        out_shape=(
            shape(2 * ORB, PLANE), shape(7, ORB, 128), shape(ROWS, 8 * ORB, dtype=F32), shape(4, ORB, 128),
        ),
        in_specs=[WHOLE] * 4,
        out_specs=(WHOLE,) * 4,
        scratch_shapes=[
            pltpu.VMEM((ROWS, PLANE), BF16),
            pltpu.VMEM((2 * ORB, PLANE), BF16),
            pltpu.VMEM((2, 2 * ORB, TILE), F32),
        ],
        compiler_params=PARAMS,
        cost_estimate=cost(10**8, 10**6),
        name="face",
    )(gathered(for_other), around, edge, edge_mask)
    relayed = to_mate(forward)

    bands, base, edge_energy = pl.pallas_call(
        theta_kernel,
        out_shape=(shape(2, ROWS, TILE), shape(ROWS, ROWS, dtype=F32), pair),
        in_specs=[WHOLE] * 9,
        out_specs=(WHOLE,) * 3,
        scratch_shapes=[pltpu.VMEM((ROWS, 8 * ORB), F32), pltpu.VMEM((ROWS, 8 * ORB), F32)],
        input_output_aliases={8: 2},
        compiler_params=PARAMS,
        cost_estimate=cost(10**9, 4 * 10**6),
        name="theta",
    )(keep, own, mate_rows, other_rows, extra, halo, part, edge_mask, edge_energy)
    edge_grad, theta, for_mate, for_other = pl.pallas_call(
        gradient_kernel,
        out_shape=(pair, shape(ROWS, ROWS), shape(2 * ORB, 128), shape(2 * ORB, 128)),
        in_specs=[WHOLE] * 7,
        out_specs=(WHOLE,) * 4,
        scratch_shapes=[pltpu.VMEM((ROWS, TILE), BF16), pltpu.VMEM((ROWS, ROWS), F32)],
        compiler_params=PARAMS,
        cost_estimate=cost(10**9, 10**7),
        name="gradient",
    )(keep, relayed, bands, base, edge, edge_energy, edge_mask)
    other_side = across(for_other)
    mate_side = to_mate(for_mate)

    inner, part = pl.pallas_call(
        smooth_kernel,
        out_shape=(pltpu.HBM((ROWS, CX * PLANE), BF16), shape(2, ROWS, PLANE, dtype=F32)),
        in_specs=[WHOLE] * 6,
        out_specs=(FAR, WHOLE),
        scratch_shapes=[
            pltpu.VMEM((2, ROWS, PLANE), BF16),
            pltpu.VMEM((2, ROWS, PLANE), BF16),
            pltpu.VMEM((2, ORB, PLANE), BF16),
            pltpu.SemaphoreType.DMA((PLANE // TILE, 4)),
        ],
        compiler_params=PARAMS,
        cost_estimate=cost(2 * 10**9, 10**7),
        name="smooth",
    )(theta, mid, mid_energy, edge_grad, mid_mask, edge_mask)

    return pl.pallas_call(
        finish_kernel,
        out_shape=pltpu.HBM((ROWS, CX * PLANE), BF16),
        in_specs=[WHOLE] * 4 + [FAR],
        out_specs=FAR,
        scratch_shapes=[pltpu.VMEM((2, 2 * ORB, PLANE), BF16), pltpu.SemaphoreType.DMA((2, 2))],
        input_output_aliases={4: 0},
        compiler_params=PARAMS,
        cost_estimate=cost(10**7, 10**7),
        name="finish",
    )(other_side, mate_side, part, edge_mask, inner)


def solution(mesh):
    return jax.shard_map(
        per_device,
        mesh=mesh,
        in_specs=(P(("grp", "sx"), None), P(("grp", "sx"), None), P("grp", None), P("grp", None)),
        out_specs=P(("grp", "sx"), None),
        check_vma=False,
    )
```

```python
import functools

import jax
import jax.numpy as jnp
from jax import lax
from jax.experimental import pallas as pl
from jax.experimental.pallas import tpu as pltpu
from jax.sharding import PartitionSpec as P

ORB = 64
CX = 4
NY = 32
NZ = 32
ROWS = 3 * ORB
PLANE = NY * NZ
TILE = 256
WINDOW = 6 * ORB
FACE = 2 * ORB + ORB // 4
F32 = jnp.float32
BF16 = jnp.bfloat16


def iota(shape, dim):
    return lax.broadcasted_iota(jnp.int32, shape, dim)


def window_start(width):
    slab = lax.axis_index("sx")
    first = jnp.clip(slab * ORB - 2 * ORB, 0, width - WINDOW) // 128 * 128
    return pl.multiple_of(first, 128)


def row_features(window_ref, first):
    slab = lax.axis_index("sx")
    count = lax.axis_size("sx")
    window = window_ref[...]
    shift = slab * ORB - 2 * ORB - first
    window = pltpu.roll(jnp.concatenate([window, window], axis=0), lax.rem(WINDOW - shift, WINDOW), 1)
    lane = iota((1, WINDOW), 1)
    block = slab - 2 + lane // ORB
    valid = (block >= 0) & (block < count)
    cx = window[0:1] - slab * CX
    cy = window[1:2]
    cz = window[2:3]
    r = window[3:4]
    const = cx * cx + cy * cy + cz * cz - r * r
    const = jnp.where(valid, const, 65535)
    cx = jnp.where(valid, cx, 0)
    cy = jnp.where(valid, cy, 0)
    cz = jnp.where(valid, cz, 0)
    k = iota((16, WINDOW), 0)
    feats = jnp.where(k == 0, 1, 0)
    feats = jnp.where(k == 1, 256, feats)
    feats = jnp.where(k == 2, cy, feats)
    feats = jnp.where(k == 3, cz, feats)
    feats = jnp.where(k == 4, const & 255, feats)
    feats = jnp.where(k == 5, const >> 8, feats)
    feats = jnp.where(k == 6, cx, feats)
    return jnp.transpose(feats.astype(F32))[: 5 * ORB].astype(BF16)


def cell_features():
    k = iota((16, PLANE), 0)
    cell = iota((16, PLANE), 1)
    y = cell >> 5
    z = cell & 31
    sq = y * y + z * z
    feats = jnp.where(k == 0, sq & 255, 0)
    feats = jnp.where(k == 1, sq >> 8, feats)
    feats = jnp.where(k == 2, -2 * y, feats)
    feats = jnp.where(k == 3, -2 * z, feats)
    feats = jnp.where(k == 4, 1, feats)
    feats = jnp.where(k == 5, 256, feats)
    return feats.astype(F32).astype(BF16)


def sphere(reach, rows, plane):
    bound = rows[:, 6:7].astype(F32) * (2.0 * plane) - float(plane * plane)
    return jnp.where(reach <= bound, 1.0, 0.0).astype(BF16)


def in_plane(center, beside):
    k = iota((TILE, TILE), 0)
    n = iota((TILE, TILE), 1)
    diff = k - n
    near_y = (diff == NZ) | (diff == -NZ)
    near_z = ((diff == 1) | (diff == -1)) & ((k >> 5) == (n >> 5))
    w = jnp.where(near_y | near_z, float(beside), 0.0)
    return jnp.where(diff == 0, float(center), w).astype(BF16)


def plane_product(ref, weights, beside, t):
    start = TILE * t
    values = ref[:, :, start : start + TILE].reshape(2 * ROWS, TILE)
    out = jnp.dot(values, weights, preferred_element_type=F32).reshape(2, ROWS, TILE)
    lane = iota((1, 1, 128), 2)
    first, last = out[:, :, :128], out[:, :, 128:]
    if t > 0:
        turned = pltpu.roll(ref[:, :, start - 128 : start].astype(F32), NZ, 2)
        turned = jnp.where(lane < NZ, turned, 0.0)
        first = first + turned if beside > 0 else first - turned
    if start + TILE < PLANE:
        turned = pltpu.roll(ref[:, :, start + TILE : start + TILE + 128].astype(F32), 128 - NZ, 2)
        turned = jnp.where(lane >= 128 - NZ, turned, 0.0)
        last = last + turned if beside > 0 else last - turned
    return jnp.concatenate([first, last], axis=2)


def low_lanes(width):
    return (iota((1, 128), 1) & (2 * width - 1)) < width


def pack(first, second, width):
    return jnp.where(
        low_lanes(width),
        first + pltpu.roll(first, 128 - width, 1),
        second + pltpu.roll(second, width, 1),
    )


def unpack(packed, width):
    low = low_lanes(width)
    return (
        jnp.where(low, packed, pltpu.roll(packed, width, 1)),
        jnp.where(low, pltpu.roll(packed, 128 - width, 1), packed),
    )


def lane_tiles(values):
    return [values[:, 128 * t : 128 * t + 128] for t in range(PLANE // 128)]


def halves(values):
    half = values.shape[0] // 2
    return values[:half], values[half:]


def fold(full, side):
    tiles = lane_tiles(full)
    a, b, c = (sum(tiles[t::3][1:], tiles[t]) for t in range(3))
    tiles = lane_tiles(side)
    d, e = (sum(tiles[t::2][1:], tiles[t]) for t in range(2))
    return pack(a, b, 16), pack(*halves(c), 16), pack(*halves(pack(d, e, 16)), 8)


def unfold(packed):
    a, b = unpack(packed[:ORB], 16)
    c = jnp.concatenate(unpack(packed[ORB : ORB + ORB // 2], 16), axis=0)
    d, e = unpack(jnp.concatenate(unpack(packed[ORB + ORB // 2 : 2 * ORB], 8), axis=0), 16)
    return (a, b, c), (d, e)


def fold_far(values):
    tiles = lane_tiles(values)
    return pack(*halves(pack(*halves(sum(tiles[1:], tiles[0])), 16)), 8)


def unfold_far(packed):
    half = jnp.concatenate(unpack(packed, 8), axis=0)
    return jnp.concatenate(unpack(half, 16), axis=0)


def put_fold(ref, parts):
    start = 0
    for part in parts:
        ref[start : start + part.shape[0]] = part.astype(BF16)
        start += part.shape[0]


def side_by_side(unfolded, i):
    full, side = unfolded
    tiles = []
    for t in range(PLANE // 128):
        pair = [full[t % 3], side[t % 2]]
        tiles.append(jnp.concatenate(pair if i == 0 else pair[::-1], axis=0))
    return tiles


def is_even():
    return lax.rem(lax.axis_index("sx"), 2) == 0


def put_messages(planes, mate_ref, across_ref):
    own = slice(ORB, 2 * ORB)
    down = fold(planes[0, own].astype(F32), planes[0, :ORB].astype(F32))
    up = fold(planes[1, own].astype(F32), planes[1, 2 * ORB :].astype(F32))
    even = is_even()
    put_fold(mate_ref, [jnp.where(even, u, d) for u, d in zip(up, down)])
    put_fold(across_ref, [jnp.where(even, d, u) for u, d in zip(up, down)])


def sides(mate, across):
    even = is_even()
    return (jnp.where(even, across, mate), jnp.where(even, mate, across))


def at_end():
    slab = lax.axis_index("sx")
    return (slab == 0) | (slab == lax.axis_size("sx") - 1)


def kept(pattern_ref, r, q):
    slab = lax.axis_index("sx")
    last = pattern_ref.shape[1] - 1
    values = []
    for col in (2 * q, 2 * q + 1):
        apart = abs(col - r - 2)
        if apart == 0:
            values.append(1.0)
        elif apart > 2:
            values.append(0.0)
        else:
            at = jnp.clip(slab - 3 + min(col, r + 2), 0, last)
            values.append(pattern_ref[apart - 1, at].astype(F32))
    return jnp.where(low_half(), values[0], values[1])


def edges_kernel(
    table_ref, pieces_ref,
    phi_ref, mask_ref, rows_ref, reach_ref, mate_ref,
    window_ref, raw_ref, sems,
):
    first = window_start(table_ref.shape[1])
    table_copy = pltpu.make_async_copy(table_ref.at[:, pl.ds(first, WINDOW)], window_ref, sems.at[2])
    table_copy.start()
    copies = []
    for i in range(2):
        start = (CX - 1) * PLANE * i
        copies.append(
            pltpu.make_async_copy(pieces_ref.at[:, start : start + PLANE], raw_ref.at[i], sems.at[i])
        )
        copies[i].start(priority=1)
    cells = cell_features()
    table_copy.wait()
    blocks = row_features(window_ref, first)
    rows_ref[...] = blocks
    rows = blocks[ORB : 4 * ORB]
    reach = jnp.dot(rows, cells, preferred_element_type=F32)
    reach_ref[...] = reach
    for i in range(2):
        mask_ref[i] = sphere(reach, rows, (CX - 1) * i)
    for i in range(2):
        copies[i].wait()
        phi_ref[i] = raw_ref[i] * mask_ref[i]
    even = is_even()
    own = slice(ORB, 2 * ORB)
    lower, upper = phi_ref[0].astype(F32), phi_ref[1].astype(F32)
    put_fold(mate_ref, fold(jnp.where(even, upper[own], lower[own]), jnp.where(even, upper[2 * ORB :], lower[:ORB])))


def rows_product(a, b):
    return lax.dot_general(a, b, (((1,), (1,)), ((), ())), preferred_element_type=F32)


def energy_kernel(
    rows_ref, reach_ref, pieces_ref, pot_ref, edge_ref, edge_mask_ref,
    phi_ref, mask_ref, energy_ref, part_ref, edge_energy_ref, corr_ref, ham_ref,
):
    rows = rows_ref[ORB : 4 * ORB]
    for i in range(2):
        mask = sphere(reach_ref[...], rows, 1 + i)
        mask_ref[i] = mask
        phi_ref[i] = pieces_ref[:, PLANE * (1 + i) : PLANE * (2 + i)] * mask
    weights = in_plane(6, -1)
    for t in range(PLANE // TILE):
        lanes = slice(TILE * t, TILE * t + TILE)
        edge = edge_ref[:, :, lanes].astype(F32)
        mid = phi_ref[:, :, lanes].astype(F32)
        inner = plane_product(phi_ref, weights, -1.0, t)
        outer = plane_product(edge_ref, weights, -1.0, t)
        for i in range(2):
            value = 0.5 * (inner[i] - (edge[i] + mid[1 - i])) + pot_ref[1 + i : 2 + i, lanes] * mid[i]
            energy_ref[i, :, lanes] = value.astype(BF16) * mask_ref[i, :, lanes]
            plane = (CX - 1) * i
            value = 0.5 * (outer[i] - mid[i]) + pot_ref[plane : plane + 1, lanes] * edge[i]
            part_ref[i, :, lanes] = value
            rest = rest_rows(i)
            edge_energy_ref[i, rest, lanes] = value[rest].astype(BF16) * edge_mask_ref[i, rest, lanes]
    mid = jnp.concatenate([phi_ref[0], phi_ref[1]], axis=1)
    both = jnp.concatenate([energy_ref[0], energy_ref[1]], axis=1)
    gram = rows_product(jnp.concatenate([mid, both], axis=0), mid)
    corr = gram[:ROWS]
    ham_ref[...] = gram[ROWS:]
    for i in range(2):
        rest = rest_rows(i)
        gram = rows_product(jnp.concatenate([edge_ref[i], edge_energy_ref[i, rest]], axis=0), edge_ref[i])
        corr = corr + gram[:ROWS]
        ham_ref[rest] += gram[ROWS:]
    corr_ref[...] = corr


def halo_rows(i):
    return slice(0, 2 * ORB) if i == 0 else slice(ORB, ROWS)


def rest_rows(i):
    return slice(2 * ORB, ROWS) if i == 0 else slice(0, ORB)


def bands_kernel(
    mate_ref, part_ref, mask_ref, phi_ref, corr_ref, ham_ref, rest_ref,
    energy_ref, own_ref, rows_ref,
):
    volume = 1.0 / (4.0 * CX**3)
    gram = []
    unfolded = unfold(mate_ref[...].astype(F32))
    for i in range(2):
        factor = jnp.where(is_even() == (i == 1), 0.5, 0.0)
        tiles = side_by_side(unfolded, i)
        for t in range(PLANE // 128):
            lanes = slice(128 * t, 128 * t + 128)
            value = part_ref[i, halo_rows(i), lanes] - factor * tiles[t]
            energy_ref[i, halo_rows(i), lanes] = value.astype(BF16) * mask_ref[i, halo_rows(i), lanes]
        gram.append(rows_product(energy_ref[i, halo_rows(i)], phi_ref[i]))
    own_ref[:, :, ROWS:] = jnp.zeros((2, ROWS, TILE - ROWS), F32)
    own_ref[0, :ORB, :ROWS] = (ham_ref[:ORB] + gram[0][:ORB]) * volume
    own_ref[0, ORB : 2 * ORB, :ROWS] = (ham_ref[ORB : 2 * ORB] + gram[0][ORB:] + gram[1][:ORB]) * volume
    own_ref[0, 2 * ORB :, :ROWS] = (ham_ref[2 * ORB :] + gram[1][ORB:]) * volume
    own_ref[1, :, :ROWS] = corr_ref[...] * volume
    tail = jnp.where(low_half(), own_ref[0, :, 128:256], swapped(own_ref[1, :, 128:256]))
    even = is_even()
    for i, value in enumerate((own_ref[0, :, 0:128], own_ref[1, :, 0:128], tail)):
        rows_ref[i] = jnp.where(even, value[ORB:], value[: 2 * ORB]).astype(BF16)


def low_half():
    return iota((1, 128), 1) < 64


def swapped(value):
    return pltpu.roll(value, 64, 1)


def mate_blocks(rows_ref, which):
    tail = rows_ref[2].astype(F32)
    if which == 1:
        tail = swapped(tail)
    return rows_ref[which].astype(F32), jnp.where(low_half(), tail, 0.0)


def shifted(c01, c2x):
    low = low_half()
    turned = swapped(c01)
    return jnp.where(low, 0.0, turned), jnp.where(low, turned, swapped(c2x))


def relay_kernel(own_ref, rows_ref, face_ref, out_ref):
    even = is_even()
    heads = []

    def put(i, value):
        out_ref[ORB * i : ORB * i + ORB] = value.astype(BF16)

    for which in range(2):
        head, rest = shifted(own_ref[which, :, 0:128], own_ref[which, :, 128:256])
        c01, c2x = mate_blocks(rows_ref, which)
        c01 = jnp.where(even, c01[:ORB], c01[ORB:])
        c2x = jnp.where(even, c2x[:ORB], c2x[ORB:])
        own = slice(ORB, 2 * ORB)
        put(2 * which, head[own] + jnp.where(even, c2x, c01))
        put(2 * which + 1, rest[own] + jnp.where(even, c01, c2x))
        put(5 + which, jnp.where(even, rest[:ORB], rest[2 * ORB :]))
        heads.append(jnp.where(even, head[:ORB], head[2 * ORB :]))
    put(4, jnp.where(low_half(), swapped(heads[1]), heads[0]))
    out_ref[7 * ORB :] = face_ref[...]


def around_kernel(pattern_ref, rows_ref, phi_ref, mask_ref, keep_ref, face_ref, scalar_ref, sem):
    pattern_copy = pltpu.make_async_copy(pattern_ref, scalar_ref, sem)
    pattern_copy.start()
    even = is_even()
    own = slice(ORB, 2 * ORB)
    lower, upper = phi_ref[0].astype(F32), phi_ref[1].astype(F32)
    parts = fold(jnp.where(even, lower[own], upper[own]), jnp.where(even, lower[:ORB], upper[2 * ORB :]))
    put_fold(face_ref, parts + (fold_far(jnp.where(even, lower[2 * ORB :], upper[:ORB])),))
    rows = jnp.where(even, rows_ref[:ROWS].astype(F32), rows_ref[2 * ORB :].astype(F32))
    reach = jnp.dot(rows.astype(BF16), cell_features(), preferred_element_type=F32)
    plane = jnp.where(even, -1.0, float(CX))
    bound = rows[:, 6:7] * (2.0 * plane) - plane * plane
    mask_ref[...] = jnp.where(reach <= bound, 1.0, 0.0).astype(BF16)
    pattern_copy.wait()
    for r in range(3):
        for q in range(4):
            keep_ref[r : r + 1, 128 * q : 128 * q + 128] = kept(scalar_ref, r, q)


def shared_head(tile, which):
    tile = tile.astype(F32)
    if which == 1:
        tile = swapped(tile)
    return jnp.where(low_half(), 0.0, tile)


def face_kernel(
    both_ref, around_ref, phi_ref, mask_ref,
    halo_ref, other_ref, extra_ref, forward_ref,
    beyond_ref, back_ref, work_ref,
):
    even = is_even()
    low = low_half()
    scale = -0.5 / (4.0 * CX**3)

    def got(start, size):
        rows = slice(start, start + size)
        value = jnp.where(even, both_ref[0, rows].astype(F32), both_ref[1, rows].astype(F32))
        return jnp.where(at_end(), 0.0, value)

    tiles = [got(ORB * i, ORB) for i in range(7)]
    for i in range(7):
        other_ref[i] = tiles[i].astype(BF16)
    beside = unfold(got(7 * ORB, 2 * ORB))
    far_off = unfold_far(got(9 * ORB, ORB // 4)).astype(BF16)
    extra_ref[...] = jnp.zeros((ROWS, 8 * ORB), F32)
    work_ref[:, :, ROWS:] = jnp.zeros((2, 2 * ORB, TILE - ROWS), F32)
    head, tail = shared_head(tiles[4], 1), tiles[6]
    forward_ref[2] = jnp.where(low, swapped(head), swapped(tail)).astype(BF16)
    forward_ref[3] = jnp.where(low, swapped(tail), 0.0).astype(BF16)

    def add_face(i):
        here = halo_rows(i)
        there = slice(ORB, ROWS) if i == 0 else slice(0, 2 * ORB)
        outer = slice(0, ORB) if i == 0 else slice(2 * ORB, ROWS)
        for t, value in enumerate(side_by_side(beside, i)):
            lanes = slice(128 * t, 128 * t + 128)
            beyond_ref[there, lanes] = value.astype(BF16) * around_ref[there, lanes]
            beyond_ref[outer, lanes] = far_off * around_ref[outer, lanes]
            halo_ref[:, lanes] = value.astype(BF16) * mask_ref[i, here, lanes]
            back_ref[:, lanes] = phi_ref[i, here, lanes] * around_ref[there, lanes]
        work_ref[0, :, :ROWS] = rows_product(halo_ref[...], phi_ref[i]) * scale
        work_ref[1, :, :ROWS] = rows_product(back_ref[...], beyond_ref[...]) * scale
        x, y = work_ref[0, :, 0:128], work_ref[0, :, 128:256]
        a, b = shifted(work_ref[1, :, 0:128], work_ref[1, :, 128:256])
        if i == 0:
            extra_ref[here, 0:128] = a
            extra_ref[here, 128:256] = b + x
            extra_ref[here, 256:384] = y
            own = slice(ORB, 2 * ORB)
        else:
            extra_ref[here, 128:256] = a + x
            extra_ref[here, 256:384] = b + y
            own = slice(0, ORB)
        a = swapped(shared_head(tiles[4], 0) + a[own])
        b = swapped(tiles[5] + b[own])
        x, y = swapped(x[own]), swapped(y[own])
        if i == 0:
            forward_ref[0] = jnp.where(low, a, b + x).astype(BF16)
            forward_ref[1] = jnp.where(low, b + x, y).astype(BF16)
        else:
            forward_ref[0] = jnp.where(low, a + x, b + y).astype(BF16)
            forward_ref[1] = jnp.where(low, b, x).astype(BF16)

    pl.when(even)(lambda: add_face(0))
    pl.when(jnp.logical_not(even))(lambda: add_face(1))


def add_halo(i, halo_ref, part_ref, mask_ref, energy_ref):
    here = halo_rows(i)
    value = part_ref[i, here] - 0.5 * halo_ref[...].astype(F32)
    energy_ref[i, here] = value.astype(BF16) * mask_ref[i, here]


def put_gradient(theta, orbital_ref, energy_ref, mask_ref, out_ref):
    for i in range(2):
        for t in range(PLANE // TILE):
            lanes = slice(TILE * t, TILE * t + TILE)
            fix = jnp.dot(theta, orbital_ref[i, :, lanes], preferred_element_type=F32)
            value = energy_ref[i, :, lanes].astype(F32) - fix
            out_ref[i, :, lanes] = value.astype(BF16) * mask_ref[i, :, lanes]


def split(value):
    high = value.astype(BF16)
    return high, (value - high.astype(F32)).astype(BF16)


def fine_product(a, b):
    return rows_product(a[0], b[0]) + (rows_product(a[0], b[1]) + rows_product(a[1], b[0]))


def theta_kernel(
    keep_ref, own_ref, rows_ref, other_ref, extra_ref, halo_ref, part_ref, edge_mask_ref, energy_in_ref,
    window_ref, theta_ref, energy_ref,
    ham_ref, inv_ref,
):
    even = is_even()
    low = low_half()
    zero = jnp.zeros((ORB, 128), F32)
    for which, band_ref in enumerate((ham_ref, inv_ref)):
        near, rest = shifted(*mate_blocks(rows_ref, which))
        ahead = other_ref[2 * which].astype(F32)
        beside = other_ref[2 * which + 1].astype(F32)
        head = shared_head(other_ref[4], which)
        tail = other_ref[5 + which].astype(F32)
        got_even = (
            (ahead, beside, zero, zero),
            (head, tail + near[:ORB], rest[:ORB], zero),
            (zero, near[ORB:], rest[ORB:], zero),
        )
        got_odd = (
            (near[:ORB], rest[:ORB], zero, zero),
            (near[ORB:], rest[ORB:] + head, tail, zero),
            (zero, jnp.where(low, 0.0, ahead), beside, jnp.where(low, ahead, 0.0)),
        )
        for r in range(3):
            for q in range(4):
                value = jnp.where(even, got_even[r][q], got_odd[r][q])
                if q in (1, 2):
                    value = value + own_ref[which, ORB * r : ORB * r + ORB, 128 * q - 128 : 128 * q]
                if which == 0:
                    value = value + extra_ref[ORB * r : ORB * r + ORB, 128 * q : 128 * q + 128]
                value = value * keep_ref[r : r + 1, 128 * q : 128 * q + 128]
                if which == 1:
                    on = iota((ORB, 128), 0) + (ORB * (r + 2) - 128 * q) == iota((ORB, 128), 1)
                    value = jnp.where(on, 2.0, 0.0) - value
                band_ref[ORB * r : ORB * r + ORB, 128 * q : 128 * q + 128] = value
    ham, inv = split(ham_ref[...]), split(inv_ref[...])
    theta_ref[...] = fine_product(ham, inv)
    for which, (high, _) in enumerate((ham, inv)):
        quarter = [high[:, 128 * q : 128 * q + 128].astype(F32) for q in range(4)]
        window_ref[which, :, 0:128] = jnp.where(even, quarter[2], quarter[0]).astype(BF16)
        last = jnp.where(even, jnp.where(low, quarter[3], quarter[1]), quarter[1])
        window_ref[which, :, 128:256] = last.astype(BF16)
    pl.when(even)(lambda: add_halo(0, halo_ref, part_ref, edge_mask_ref, energy_ref))
    pl.when(jnp.logical_not(even))(lambda: add_halo(1, halo_ref, part_ref, edge_mask_ref, energy_ref))


def gradient_kernel(
    keep_ref, relayed_ref, bands_ref, base_ref,
    edge_ref, edge_energy_ref, edge_mask_ref,
    edge_grad_ref, theta_ref, mate_ref, across_ref,
    window_ref, total_ref,
):
    even = is_even()
    low = low_half()
    more = []
    kept_even = (keep_ref[2:3, 256:384], jnp.where(low, keep_ref[2:3, 384:512], keep_ref[2:3, 128:256]))
    kept_odd = (keep_ref[0:1, 0:128], keep_ref[0:1, 128:256])
    for which in range(2):
        tiles = []
        for q in range(2):
            value = relayed_ref[2 * which + q].astype(F32)
            tiles.append(value * jnp.where(even, kept_even[q], kept_odd[q]))
        more.append(jnp.concatenate(tiles, axis=1))
    first, third = slice(0, ORB), slice(2 * ORB, ROWS)
    window_ref[...] = bands_ref[0]
    window_ref[first] = (bands_ref[0, first].astype(F32) + jnp.where(even, 0.0, more[0])).astype(BF16)
    window_ref[third] = (bands_ref[0, third].astype(F32) + jnp.where(even, more[0], 0.0)).astype(BF16)
    more = [value.astype(BF16) for value in more]
    column = rows_product(window_ref[...], more[1])
    row = rows_product(more[0], bands_ref[1])
    total_ref[...] = base_ref[...]
    total_ref[first] += jnp.where(even, 0.0, row)
    total_ref[third] += jnp.where(even, row, 0.0)
    total_ref[:, first] -= jnp.where(even, 0.0, column)
    total_ref[:, third] -= jnp.where(even, column, 0.0)
    theta = total_ref[...].astype(BF16)
    theta_ref[...] = theta
    put_gradient(theta, edge_ref, edge_energy_ref, edge_mask_ref, edge_grad_ref)
    put_messages(edge_grad_ref, mate_ref, across_ref)


def smooth_kernel(
    theta_ref, phi_ref, energy_ref, edge_ref, mask_ref, edge_mask_ref,
    out_ref, part_ref,
    grad_ref, done_ref, rest_ref, sems,
):
    put_gradient(theta_ref[...], phi_ref, energy_ref, mask_ref, grad_ref)
    weights = in_plane(8, 1)
    copies = []

    def send(source, rows, start, sem):
        copies.append(pltpu.make_async_copy(source, out_ref.at[rows, start : start + TILE], sem))
        copies[-1].start()

    for t in range(PLANE // TILE):
        lanes = slice(TILE * t, TILE * t + TILE)
        edge = edge_ref[:, :, lanes].astype(F32)
        mid = grad_ref[:, :, lanes].astype(F32)
        inner = plane_product(grad_ref, weights, 1.0, t)
        outer = plane_product(edge_ref, weights, 1.0, t)
        for i in range(2):
            value = (inner[i] + (edge[i] + mid[1 - i])) * (1.0 / 32.0)
            done_ref[i, :, lanes] = value.astype(BF16) * mask_ref[i, :, lanes]
            value = outer[i] + mid[i]
            part_ref[i, :, lanes] = value
            rest = rest_rows(i)
            value = value[rest] * (1.0 / 32.0)
            rest_ref[i, :, lanes] = value.astype(BF16) * edge_mask_ref[i, rest, lanes]
        for i in range(2):
            send(done_ref.at[i, :, lanes], slice(0, ROWS), PLANE * (1 + i) + TILE * t, sems.at[t, i])
            send(rest_ref.at[i, :, lanes], rest_rows(i), PLANE * (CX - 1) * i + TILE * t, sems.at[t, 2 + i])
    for copy in copies:
        copy.wait()


def finish_kernel(across_ref, mate_ref, part_ref, mask_ref, inner_ref, out_ref, done_ref, sems):
    halos = [
        side_by_side(unfold(side), i)
        for i, side in enumerate(sides(mate_ref[...].astype(F32), across_ref[...].astype(F32)))
    ]
    copies = []
    for i in range(2):
        start = PLANE * (CX - 1) * i
        for half in range(2):
            rows = slice(ORB * (half + i), ORB * (half + i) + ORB)
            got = slice(ORB * half, ORB * half + ORB)
            for t in range(PLANE // 128):
                lanes = slice(128 * t, 128 * t + 128)
                value = (part_ref[i, rows, lanes] + halos[i][t][got]) * (1.0 / 32.0)
                done_ref[i, got, lanes] = value.astype(BF16) * mask_ref[i, rows, lanes]
            copies.append(
                pltpu.make_async_copy(
                    done_ref.at[i, got], out_ref.at[rows, start : start + PLANE], sems.at[i, half]
                )
            )
            copies[-1].start()
    for copy in copies:
        copy.wait()


def shape(*dims, dtype=BF16):
    return jax.ShapeDtypeStruct(dims, dtype)


def cost(flops, moved):
    return pl.CostEstimate(flops=flops, bytes_accessed=moved, transcendentals=0)


PARAMS = pltpu.CompilerParams(vmem_limit_bytes=32 * 1024 * 1024)
WHOLE = pl.BlockSpec(memory_space=pltpu.VMEM)
FAR = pl.BlockSpec(memory_space=pltpu.HBM)


def far(value):
    return pltpu.with_memory_space_constraint(value, pltpu.HBM)


def per_device(pieces, potential, centers, pattern):
    count = lax.axis_size("sx")
    mates = [(i, i ^ 1) for i in range(count)]
    others = [(i, i + 1 if i % 2 else i - 1) for i in range(1, count - 1)]
    groups = lax.axis_size("grp")
    pairs = [[g * count + i, g * count + i + 1] for g in range(groups) for i in range(1, count - 1, 2)]
    ends = [g * count + end for g in range(groups) for end in (0, count - 1)]
    pairs += [[ends[i], ends[i + 2]] for i in range(len(ends)) if i % 4 < 2] if groups % 2 == 0 else [
        [ends[2 * i], ends[2 * i + 1]] for i in range(groups)
    ]

    def to_mate(value):
        return lax.ppermute(value, "sx", mates)

    def across(value):
        return lax.ppermute(value, "sx", others)

    def gathered(value):
        return lax.all_gather(value, ("grp", "sx"), axis_index_groups=pairs)

    table = centers.T
    patterns = pattern.T
    pair = shape(2, ROWS, PLANE)

    edge, edge_mask, rows, reach, for_mate = pl.pallas_call(
        edges_kernel,
        out_shape=(
            pair, pair, shape(5 * ORB, 16), shape(ROWS, PLANE, dtype=F32), shape(2 * ORB, 128),
        ),
        in_specs=[FAR, FAR],
        out_specs=(WHOLE,) * 5,
        scratch_shapes=[
            pltpu.VMEM((4, WINDOW), jnp.int32),
            pltpu.VMEM((2, ROWS, PLANE), BF16),
            pltpu.SemaphoreType.DMA((3,)),
        ],
        compiler_params=PARAMS,
        cost_estimate=cost(10**8, 10**6),
        name="edges",
    )(far(table), far(pieces))
    mate_side = to_mate(for_mate)

    mid, mid_mask, mid_energy, part, rest_energy, corr, ham = pl.pallas_call(
        energy_kernel,
        out_shape=(
            pair, pair, pair, shape(2, ROWS, PLANE, dtype=F32), pair,
            shape(ROWS, ROWS, dtype=F32), shape(ROWS, ROWS, dtype=F32),
        ),
        in_specs=[WHOLE] * 6,
        out_specs=(WHOLE,) * 7,
        compiler_params=PARAMS,
        cost_estimate=cost(4 * 10**9, 10**7),
        name="energy",
    )(rows, reach, pieces, potential, edge, edge_mask)

    edge_energy, own, for_mate = pl.pallas_call(
        bands_kernel,
        out_shape=(pair, shape(2, ROWS, TILE, dtype=F32), shape(3, 2 * ORB, 128)),
        in_specs=[WHOLE] * 7,
        out_specs=(WHOLE,) * 3,
        input_output_aliases={6: 0},
        compiler_params=PARAMS,
        cost_estimate=cost(10**9, 10**7),
        name="bands",
    )(mate_side, part, edge_mask, edge, corr, ham, rest_energy)
    mate_rows = to_mate(for_mate)
    around, keep, face = pl.pallas_call(
        around_kernel,
        out_shape=(shape(ROWS, PLANE), shape(3, 8 * ORB, dtype=F32), shape(FACE, 128)),
        in_specs=[FAR, WHOLE, WHOLE],
        out_specs=(WHOLE,) * 3,
        scratch_shapes=[pltpu.SMEM(patterns.shape, jnp.int32), pltpu.SemaphoreType.DMA],
        compiler_params=PARAMS,
        cost_estimate=cost(10**8, 10**6),
        name="around",
    )(far(patterns), rows, edge)
    for_other = pl.pallas_call(
        relay_kernel,
        out_shape=shape(7 * ORB + FACE, 128),
        in_specs=[WHOLE] * 3,
        out_specs=WHOLE,
        compiler_params=PARAMS,
        cost_estimate=cost(10**6, 10**6),
        name="relay",
    )(own, mate_rows, face)
    halo, other_rows, extra, forward = pl.pallas_call(
        face_kernel,
        out_shape=(
            shape(2 * ORB, PLANE), shape(7, ORB, 128), shape(ROWS, 8 * ORB, dtype=F32), shape(4, ORB, 128),
        ),
        in_specs=[WHOLE] * 4,
        out_specs=(WHOLE,) * 4,
        scratch_shapes=[
            pltpu.VMEM((ROWS, PLANE), BF16),
            pltpu.VMEM((2 * ORB, PLANE), BF16),
            pltpu.VMEM((2, 2 * ORB, TILE), F32),
        ],
        compiler_params=PARAMS,
        cost_estimate=cost(10**8, 10**6),
        name="face",
    )(gathered(for_other), around, edge, edge_mask)
    relayed = to_mate(forward)

    bands, base, edge_energy = pl.pallas_call(
        theta_kernel,
        out_shape=(shape(2, ROWS, TILE), shape(ROWS, ROWS, dtype=F32), pair),
        in_specs=[WHOLE] * 9,
        out_specs=(WHOLE,) * 3,
        scratch_shapes=[pltpu.VMEM((ROWS, 8 * ORB), F32), pltpu.VMEM((ROWS, 8 * ORB), F32)],
        input_output_aliases={8: 2},
        compiler_params=PARAMS,
        cost_estimate=cost(10**9, 4 * 10**6),
        name="theta",
    )(keep, own, mate_rows, other_rows, extra, halo, part, edge_mask, edge_energy)
    edge_grad, theta, for_mate, for_other = pl.pallas_call(
        gradient_kernel,
        out_shape=(pair, shape(ROWS, ROWS), shape(2 * ORB, 128), shape(2 * ORB, 128)),
        in_specs=[WHOLE] * 7,
        out_specs=(WHOLE,) * 4,
        scratch_shapes=[pltpu.VMEM((ROWS, TILE), BF16), pltpu.VMEM((ROWS, ROWS), F32)],
        compiler_params=PARAMS,
        cost_estimate=cost(10**9, 10**7),
        name="gradient",
    )(keep, relayed, bands, base, edge, edge_energy, edge_mask)
    other_side = across(for_other)
    mate_side = to_mate(for_mate)

    inner, part = pl.pallas_call(
        smooth_kernel,
        out_shape=(pltpu.HBM((ROWS, CX * PLANE), BF16), shape(2, ROWS, PLANE, dtype=F32)),
        in_specs=[WHOLE] * 6,
        out_specs=(FAR, WHOLE),
        scratch_shapes=[
            pltpu.VMEM((2, ROWS, PLANE), BF16),
            pltpu.VMEM((2, ROWS, PLANE), BF16),
            pltpu.VMEM((2, ORB, PLANE), BF16),
            pltpu.SemaphoreType.DMA((PLANE // TILE, 4)),
        ],
        compiler_params=PARAMS,
        cost_estimate=cost(2 * 10**9, 10**7),
        name="smooth",
    )(theta, mid, mid_energy, edge_grad, mid_mask, edge_mask)

    return pl.pallas_call(
        finish_kernel,
        out_shape=pltpu.HBM((ROWS, CX * PLANE), BF16),
        in_specs=[WHOLE] * 4 + [FAR],
        out_specs=FAR,
        scratch_shapes=[pltpu.VMEM((2, 2 * ORB, PLANE), BF16), pltpu.SemaphoreType.DMA((2, 2))],
        input_output_aliases={4: 0},
        compiler_params=PARAMS,
        cost_estimate=cost(10**7, 10**7),
        name="finish",
    )(other_side, mate_side, part, edge_mask, inner)


def solution(mesh):
    return jax.shard_map(
        per_device,
        mesh=mesh,
        in_specs=(P(("grp", "sx"), None), P(("grp", "sx"), None), P("grp", None), P("grp", None)),
        out_specs=P(("grp", "sx"), None),
        check_vma=False,
    )
```
